32 devices in a mesh: band: 16 (over z, y, x), shell: 2 (over core).
Axes of the slice: x: 2, y: 2, z: 4, core: 2. Of those that a mesh axis runs over, the one named last changes fastest.
Arguments:
- spectrum: float32 [2, 3, 2, 512, 512], P('shell', None, None, 'band'), parts along dimension 0, may hold values from -6 to 6
- capture_rate: float32 [2, 1024, 2048], P('shell', 'band'), parts along dimension 0, may hold values from 0.5 to 1500, as said below
- row_latitude: int32 [1024], replicated, may hold values from 0 to 1023, each once
- slot_wavenumber: int32 [512], replicated, may hold values from 0 to 511, each once
Outputs:
- transport: float32 [2, 3, 2, 512, 512], P('shell', None, None, 'band'), parts along dimension 0
The draws below stay inside these ranges and needn't reach their ends.
There are 2 independent parts, one for each index of `shell`. The reference program is written for one: setup_inputs(seed, part) draws one part's arguments, and reference() takes and returns one part's arrays. A program takes and returns all parts, laid end to end along the dimension named above; an argument that names none is the same for every part. Nothing has to cross between parts.
Inputs may be any that keep to these rules, and one draw needn't show every extreme that they name: `row_latitude`: each latitude index appears once. `slot_wavenumber`: each wavenumber appears once. `capture_rate`: positive.
All inputs are finite; a program needn't handle non-finite values.
Results may differ from the reference program's by a relative error of at most 0.0013.
Values sent between devices are 32-bit elements; how exact they have to be, the bound alone decides.
No kernel may reach another device: no remote copies, remote signals or barrier semaphores. Data moves between devices by JAX's collectives and lax.ppermute only.
A program may use at most 128 MiB of HBM per device.

```python
import math
import jax
import jax.numpy as jnp
from jax import lax

DEG = 512
NLAT = 1024
NLON = 2048
FIELDS = 3
SHELLS = 1
MODES = 512


def draw_capture_rate(key, part):
    key = jax.random.fold_in(key, 7)
    row_key, col_key, cell_key = jax.random.split(key, 3)
    position = jnp.arange(NLAT, dtype=jnp.float32) / NLAT
    rising = jnp.exp(math.log(3.0) * position)[None, :, None]
    row_scale = jnp.exp(jax.random.uniform(row_key, (SHELLS, NLAT, 1), minval=0.0, maxval=math.log(10.0)))
    col_scale = jnp.exp(jax.random.uniform(col_key, (SHELLS, 1, NLON), minval=0.0, maxval=math.log(10.0)))
    roughness = jnp.exp(jax.random.uniform(cell_key, (SHELLS, NLAT, NLON), minval=math.log(0.5), maxval=math.log(2.0)))
    return (rising * row_scale * col_scale * roughness).astype(jnp.float32)


def shard_levels(own_key, extent, shards, low, top_value):
    def one(dim, parts):
        heights = jax.random.uniform(jax.random.fold_in(jax.random.fold_in(own_key, 6), dim), (parts,), jnp.float32, low / len(shards), top_value / len(shards))
        return jnp.repeat(jnp.exp(heights), extent[dim] // parts).reshape((-1,) + (1,) * (len(extent) - dim - 1))

    level = one(*shards[0])
    for cut in shards[1:]:
        level = level * one(*cut)
    return level


def normal_values(stream_key, dims, scale, limit, cuts=(), kind=jnp.bfloat16):
    values = jax.random.normal(stream_key, dims, jnp.float32) * scale
    if len(cuts) > 0:
        values = shard_levels(stream_key, dims, cuts, -0.22, 0.18) * values
    return jnp.clip(values, min=-limit, max=limit).astype(kind)


def setup_inputs(seed: int = 0, part: int = 0) -> dict:
    key_of = jax.random.split(jax.random.key(seed), 5)
    own_keys = jax.random.split(jax.random.fold_in(key_of[4], part), 5)
    spectrum = normal_values(own_keys[0], (SHELLS, FIELDS, 2, MODES, DEG), 1.0, 6.0, ((3, 16),), jnp.float32)
    capture_rate = draw_capture_rate(jax.random.fold_in(jax.random.fold_in(key_of[4], part), 71), part)
    row_latitude = jax.random.permutation(key_of[2], NLAT).astype(jnp.int32)
    slot_wavenumber = jax.random.permutation(key_of[3], MODES).astype(jnp.int32)
    return dict(spectrum=spectrum, capture_rate=capture_rate, row_latitude=row_latitude, slot_wavenumber=slot_wavenumber)


LOG_LARGE = 60.0 * math.log(2.0)

def legendre_halves(orders, cosine, log_sine, degree_count):
    order_float = orders.astype(jnp.float32)[:, None]
    indices = jnp.arange(1, degree_count, dtype=jnp.float32)
    log_terms = jnp.where(indices[None, :] <= order_float, 0.5 * jnp.log((2.0 * indices + 1.0) / (2.0 * indices))[None, :], jnp.float32(0.0))
    log_norm = jnp.where(order_float > 0, 0.5 * math.log(2.0) + lax.optimization_barrier(jnp.sum(log_terms, axis=1, keepdims=True)), jnp.float32(0.0))
    start_log = log_norm + order_float * log_sine[None, :]
    cos_row = cosine[None, :]
    order_sq = order_float * order_float

    def one_degree(carry, degree):
        current, previous, log_scale = carry
        denominator = degree * degree - order_sq
        safe_denom = jnp.where(denominator > 0, denominator, jnp.float32(1.0))
        alpha_coef = jnp.sqrt((4.0 * degree * degree - 1.0) / safe_denom)
        back_term = jnp.maximum((degree - 1.0) * (degree - 1.0) - order_sq, 0.0)
        beta_coef = jnp.sqrt(back_term * (2.0 * degree + 1.0) / (safe_denom * jnp.maximum(2.0 * degree - 3.0, 1.0)))
        recursed = alpha_coef * cos_row * current - beta_coef * previous
        newest = jnp.where(degree > order_float, recursed, jnp.where(degree == order_float, jnp.float32(1.0), jnp.float32(0.0)))
        too_large = jnp.abs(newest) > 2.0 ** 60
        newest = jnp.where(too_large, newest * 2.0 ** (-60), newest)
        older = jnp.where(too_large, current * 2.0 ** (-60), current)
        log_scale = jnp.where(too_large, log_scale + LOG_LARGE, log_scale)
        return ((newest, older, log_scale), newest * jnp.exp(log_scale))

    def two_degrees(carry, step_index):
        degree = 2.0 * step_index
        carry, even_value = one_degree(carry, degree)
        carry, odd_value = one_degree(carry, degree + 1.0)
        return (carry, (even_value, odd_value))
    zeros_start = jnp.zeros_like(start_log)
    steps = jnp.arange(degree_count // 2, dtype=jnp.float32)
    unused, tables = lax.scan(two_degrees, (zeros_start, zeros_start, start_log), steps)
    return tables

def synthesize(coeffs, even_table, odd_table, parity_sign):
    even_sum = jnp.einsum('kmj,cmk->cmj', even_table, coeffs[:, :, 0::2], precision=lax.Precision.HIGHEST)
    odd_sum = jnp.einsum('kmj,cmk->cmj', odd_table, coeffs[:, :, 1::2], precision=lax.Precision.HIGHEST)
    northern = even_sum + odd_sum
    southern = parity_sign[None, :, None] * (even_sum - odd_sum)
    return jnp.concatenate([northern, jnp.flip(southern, -1)], -1)

def analyze(by_latitude, even_table, odd_table, parity_sign):
    half_lat = by_latitude.shape[-1] // 2
    northern = by_latitude[..., :half_lat]
    southern = jnp.flip(by_latitude[..., half_lat:], -1) * parity_sign[None, :, None]
    even_out = jnp.einsum('kmj,cmj->cmk', even_table, northern + southern, precision=lax.Precision.HIGHEST)
    odd_out = jnp.einsum('kmj,cmj->cmk', odd_table, northern - southern, precision=lax.Precision.HIGHEST)
    channels, orders_here, half_deg = even_out.shape
    return jnp.stack([even_out, odd_out], -1).reshape(channels, orders_here, 2 * half_deg)

def reference(spectrum, capture_rate, row_latitude, slot_wavenumber):
    shells = spectrum.shape[0]
    channels = shells * FIELDS * 2
    half_lat = NLAT // 2
    north_theta = jnp.pi * (jnp.arange(half_lat, dtype=jnp.float32) + 0.5) / NLAT
    cosine = jnp.cos(north_theta)
    log_sine = jnp.log(jnp.sin(north_theta))
    block_count = 16
    block_width = MODES // block_count
    order_blocks = slot_wavenumber.reshape(block_count, block_width)
    sign_blocks = (1 - 2 * (order_blocks % 2)).astype(jnp.float32)
    coeff_blocks = spectrum.reshape(channels, block_count, block_width, DEG).transpose(1, 0, 2, 3)

    def synth_block(pieces):
        coeff_part, order_part, sign_part = pieces
        even_table, odd_table = legendre_halves(order_part, cosine, log_sine, DEG)
        return synthesize(coeff_part, even_table, odd_table, sign_part)
    fourier = lax.map(synth_block, (coeff_blocks, order_blocks, sign_blocks))
    fourier = fourier.transpose(1, 0, 2, 3).reshape(channels, MODES, NLAT)
    fourier = jnp.take(fourier, row_latitude, axis=2).reshape(shells, FIELDS, 2, MODES, NLAT)
    longitudes = jnp.arange(NLON, dtype=jnp.int32)
    phase_index = slot_wavenumber[:, None] * longitudes[None, :] % NLON
    phase_angle = phase_index.astype(jnp.float32) * (2.0 * math.pi / NLON)
    cos_tab = jnp.cos(phase_angle)
    sin_tab = jnp.sin(phase_angle)
    grid_fields = (jnp.einsum('sfmr,mk->sfrk', fourier[:, :, 0], cos_tab, precision=lax.Precision.HIGHEST) + jnp.einsum('sfmr,mk->sfrk', fourier[:, :, 1], sin_tab, precision=lax.Precision.HIGHEST)) / DEG
    row_theta = jnp.pi * (row_latitude.astype(jnp.float32) + 0.5) / NLAT
    row_sine = jnp.sin(row_theta)
    rate_mean = lax.optimization_barrier(jnp.sum(capture_rate * row_sine[None, :, None], axis=(1, 2))) * (math.pi / (2.0 * NLAT * NLON))
    concentration = grid_fields[:, 0]
    sink_term = capture_rate * concentration / rate_mean[:, None, None]
    products = jnp.stack([grid_fields[:, 1] * concentration, grid_fields[:, 2] * concentration, sink_term], 1)
    row_weight = DEG * math.pi * row_sine / (2.0 * NLAT * NLON)
    weighted = products * row_weight[None, None, :, None]
    spectral_rows = jnp.stack([jnp.einsum('sfrk,mk->sfmr', weighted, cos_tab, precision=lax.Precision.HIGHEST), jnp.einsum('sfrk,mk->sfmr', weighted, sin_tab, precision=lax.Precision.HIGHEST)], 2)
    lat_to_row = jnp.argsort(row_latitude).astype(jnp.int32)
    by_latitude = jnp.take(spectral_rows.reshape(channels, MODES, NLAT), lat_to_row, axis=2)
    lat_blocks = by_latitude.reshape(channels, block_count, block_width, NLAT).transpose(1, 0, 2, 3)

    def analyze_block(pieces):
        data_part, order_part, sign_part = pieces
        even_table, odd_table = legendre_halves(order_part, cosine, log_sine, DEG)
        return analyze(data_part, even_table, odd_table, sign_part)
    result = lax.map(analyze_block, (lat_blocks, order_blocks, sign_blocks))
    return result.transpose(1, 0, 2, 3).reshape(shells, FIELDS, 2, MODES, DEG)
```

```python
import math

import jax
import jax.numpy as jnp
import numpy as np
from jax import lax
from jax.experimental import pallas as pl
from jax.experimental.pallas import tpu as pltpu
from jax.sharding import PartitionSpec as P

DEG = 512
NLAT = 1024
NLON = 2048
FIELDS = 3
HALF = NLAT // 2
CHAN = 2 * FIELDS
BLK = 8
ROWS = CHAN * BLK
CHUNK = 64
LANES = 128
KTILE = 256
BF = jnp.bfloat16
F32 = jnp.float32


def split_two(value):
    high = value.astype(BF)
    low = (value - high.astype(F32)).astype(BF)
    return high, low


def dot(lhs, rhs, contract_rhs=0):
    return lax.dot_general(
        lhs, rhs, (((1,), (contract_rhs,)), ((), ())), preferred_element_type=F32
    )


def latitude_rows():
    theta = np.pi * (np.arange(HALF) + 0.5) / NLAT
    index = np.arange(DEG, dtype=np.float64)
    log_terms = np.zeros(DEG)
    log_terms[1:] = 0.5 * np.log2((2.0 * index[1:] + 1.0) / (2.0 * index[1:]))
    rows = np.zeros((8, DEG))
    rows[0], rows[1], rows[2] = np.cos(theta), np.log2(np.sin(theta)), log_terms
    return rows.astype(np.float32)


def spread_matrix():
    spread = np.zeros((LANES, 2, 2, CHUNK // 2, BLK), np.float32)
    for half in range(2):
        for parity in range(2):
            for step in range(CHUNK // 2):
                spread[half * CHUNK + 2 * step + parity, half, parity, step, :] = 1.0
    return spread.reshape(LANES, 2 * 2 * (CHUNK // 2) * BLK).astype(BF)


def block_orders(slots_ref, first):
    sublane = lax.broadcasted_iota(jnp.int32, (BLK, LANES), 0)
    orders = jnp.zeros((BLK, LANES), jnp.int32)
    lowest = jnp.int32(DEG)
    for i in range(BLK):
        order = slots_ref[first + i]
        orders = jnp.where(sublane == i, order, orders)
        lowest = jnp.minimum(lowest, order)
    return orders[:, :1], lowest


def recursion_tables(order, rows_ref, alpha_ref, beta_ref):
    degree = lax.broadcasted_iota(jnp.int32, (BLK, DEG), 1).astype(F32)
    order_sq = order * order
    denominator = degree * degree - order_sq
    safe = jnp.where(denominator > 0, denominator, 1.0)
    alpha = jnp.sqrt((4.0 * degree * degree - 1.0) / safe)
    back = jnp.maximum((degree - 1.0) * (degree - 1.0) - order_sq, 0.0)
    beta = jnp.sqrt(back * (2.0 * degree + 1.0) / (safe * jnp.maximum(2.0 * degree - 3.0, 1.0)))
    alpha_ref[...] = jnp.where(degree > order, alpha, 0.0)
    beta_ref[...] = jnp.where(degree > order, beta, -1.0)
    terms = jnp.where(degree <= order, rows_ref[2:3, :], 0.0)
    norm = jnp.where(order > 0, 0.5 + jnp.sum(terms, axis=1, keepdims=True), 0.0)
    return norm + order * rows_ref[1:2, :]


def run_chunk(step, carry, cosine, alpha_ref, beta_ref, emit):
    current, previous, log_scale = carry
    tile = pl.ds(pl.multiple_of(step // 2 * LANES, LANES), LANES)
    shift = (step % 2) * CHUNK
    alpha = pltpu.roll(alpha_ref[:, tile], shift, 1)
    beta = pltpu.roll(beta_ref[:, tile], shift, 1)
    scale = None
    for i in range(CHUNK):
        if i % 16 == 0:
            large = jnp.abs(current) > 2.0**60
            factor = jnp.where(large, 2.0**-60, 1.0)
            current = current * factor
            previous = previous * factor
            log_scale = jnp.where(large, log_scale + 60.0, log_scale)
            scale = jnp.exp2(jnp.maximum(log_scale, -200.0))
        newest = (alpha[:, i : i + 1] * cosine) * current - beta[:, i : i + 1] * previous
        current, previous = newest, current
        emit(i, newest * scale)
    return current, previous, log_scale


def start_state(log_start):
    ones = jnp.ones((BLK, HALF), F32)
    return ones, ones, log_start


def fold_matrix(latitude_ref, fold_ref):
    latitude = latitude_ref[...]
    north = jnp.where(latitude < HALF, latitude, NLAT - 1 - latitude)
    sublane = lax.broadcasted_iota(jnp.int32, (HALF, NLAT), 0)
    fold_ref[...] = jnp.where(sublane == north, 1.0, 0.0).astype(BF)


def synth_kernel(
    dims, slots_ref, spec_ref, rows_ref, spread_ref, latitude_ref, out_ref,
    alpha_ref, beta_ref, lhs_ref, high_ref, low_ref, acc_ref, fold_ref,
):
    bands, row_count, modes, first_block, blocks, tiles = dims
    fold_matrix(latitude_ref, fold_ref)
    base = lax.axis_index("band") * modes + first_block * BLK
    south = latitude_ref[...] >= HALF
    spread_width = 4 * (CHUNK // 2) * BLK
    lane = lax.broadcasted_iota(jnp.int32, (2 * ROWS, spread_width), 1)
    sub = lax.broadcasted_iota(jnp.int32, (2 * ROWS, spread_width), 0)
    diagonal = (lane % BLK) == (sub % BLK)
    width = (CHUNK // 2) * BLK

    def one_block(block, unused):
        orders, lowest = block_orders(slots_ref, base + block * BLK)
        order = orders.astype(F32)
        log_start = recursion_tables(order, rows_ref, alpha_ref, beta_ref)
        here = pl.ds(pl.multiple_of(block * BLK, BLK), BLK)
        degree = lax.broadcasted_iota(jnp.int32, (BLK, DEG), 1)
        coeffs = jnp.where((degree >= orders)[None], spec_ref[:, here, :], 0.0)
        coeff_high, coeff_low = split_two(coeffs.reshape(ROWS, DEG))
        stacked = jnp.concatenate([coeff_high, coeff_low], 0)
        for t in range(DEG // LANES):
            wide = dot(stacked[:, t * LANES : (t + 1) * LANES], spread_ref[...])
            wide = jnp.where(diagonal, wide, 0.0).astype(BF)
            for half in range(2):
                lhs_ref[2 * t + half] = wide[:, half * 2 * width : (half + 1) * 2 * width]
        acc_ref[...] = jnp.zeros_like(acc_ref)
        cosine = jnp.broadcast_to(rows_ref[0:1, :], (BLK, HALF))

        def one_chunk(step, carry):
            held = {}

            def emit(i, value):
                if i % 4 < 2:
                    held[i] = value
                else:
                    pair = jnp.concatenate([held.pop(i - 2), value], 0)
                    high, low = split_two(pair)
                    at = (i // 4) * 2 * BLK
                    high_ref[i % 2, at : at + 2 * BLK, :] = high
                    low_ref[i % 2, at : at + 2 * BLK, :] = low

            carry = run_chunk(step, carry, cosine, alpha_ref, beta_ref, emit)
            for parity in range(2):
                lhs = lhs_ref[step, :, parity * width : (parity + 1) * width]
                first = dot(lhs, high_ref[parity])
                second = dot(lhs[:ROWS], low_ref[parity])
                acc_ref[parity] += first[:ROWS] + first[ROWS:] + second
            return carry

        lax.fori_loop(lowest // CHUNK, DEG // CHUNK, one_chunk, start_state(log_start))
        both = acc_ref[...].reshape(2 * ROWS, HALF)
        high, low = split_two(both)
        moved = dot(jnp.concatenate([high, low], 0), fold_ref[...])
        moved = moved[: 2 * ROWS] + moved[2 * ROWS :]
        sign = jnp.tile(1.0 - 2.0 * (orders % 2).astype(F32), (CHAN, 1))
        even, odd = moved[:ROWS], moved[ROWS:]
        values = jnp.where(south, sign * (even - odd), even + odd)
        for d in range(bands):
            parts = []
            for kind in range(2):
                for field in range(FIELDS):
                    c = field * 2 + kind
                    parts.append(
                        values[c * BLK : (c + 1) * BLK, d * row_count : (d + 1) * row_count]
                    )
            if CHAN * row_count < tiles * LANES:
                parts.append(jnp.zeros((BLK, tiles * LANES - CHAN * row_count), F32))
            joined = jnp.concatenate(parts, 1)
            for t in range(tiles):
                at = pl.ds(pl.multiple_of(t * blocks * BLK + block * BLK, BLK), BLK)
                out_ref[d, at, :] = joined[:, t * LANES : (t + 1) * LANES]
        return unused

    lax.fori_loop(0, blocks, one_block, 0)


def analyze_kernel(
    dims, slots_ref, data_ref, total_ref, rows_ref, latitude_ref, out_ref,
    alpha_ref, beta_ref, high_ref, low_ref, weight_ref, result_ref, fold_ref,
):
    bands, row_count, modes, first_block, blocks, tiles = dims
    fold_matrix(latitude_ref, fold_ref)
    base = lax.axis_index("band") * modes + first_block * BLK
    south = latitude_ref[...] >= HALF
    total = total_ref[0]
    for d in range(1, bands):
        total = total + total_ref[d]
    inverse = (1.0 / total)[:, :1]
    lane = lax.broadcasted_iota(jnp.int32, (CHUNK * BLK, LANES), 1)
    sub = lax.broadcasted_iota(jnp.int32, (CHUNK * BLK, LANES), 0)
    keep = (lane % BLK == sub % BLK) & (lane // ROWS == sub // BLK % 2)

    def one_block(block, unused):
        orders, lowest = block_orders(slots_ref, base + block * BLK)
        order = orders.astype(F32)
        log_start = recursion_tables(order, rows_ref, alpha_ref, beta_ref)
        sign = 1.0 - 2.0 * (orders % 2).astype(F32)
        evens, odds = [], []
        for c in range(CHAN):
            offset = ((c % 2) * FIELDS + c // 2) * row_count
            t, at = offset // LANES, offset % LANES
            rows = pl.ds(pl.multiple_of(t * blocks * BLK + block * BLK, BLK), BLK)
            values = jnp.concatenate(
                [data_ref[d, rows, :][:, at : at + row_count] for d in range(bands)], 1
            )
            flipped = sign * values
            evens.append(jnp.where(south, flipped, values))
            odds.append(jnp.where(south, -flipped, values))
        high, low = split_two(jnp.concatenate(evens + odds, 0))
        folded = dot(jnp.concatenate([high, low], 0), fold_ref[...], 1)
        folded = folded[: 2 * ROWS] + folded[2 * ROWS :]
        padded = jnp.concatenate([folded, jnp.zeros((LANES - 2 * ROWS, HALF), F32)], 0)
        high, low = split_two(padded.T)
        weight_ref[:, :LANES] = high
        weight_ref[:, LANES:] = low
        result_ref[...] = jnp.zeros_like(result_ref)
        cosine = jnp.broadcast_to(rows_ref[0:1, :], (BLK, HALF))

        def one_chunk(step, carry):
            held = {}

            def emit(i, value):
                if i % 2 == 0:
                    held[i] = value
                else:
                    pair = jnp.concatenate([held.pop(i - 1), value], 0)
                    high, low = split_two(pair)
                    at = (i // 2) * 2 * BLK
                    high_ref[at : at + 2 * BLK, :] = high
                    low_ref[at : at + 2 * BLK, :] = low

            carry = run_chunk(step, carry, cosine, alpha_ref, beta_ref, emit)
            first = dot(high_ref[...], weight_ref[...])
            second = dot(low_ref[...], weight_ref[:, :LANES])
            full = first[:, :LANES] + first[:, LANES:] + second
            picked = jnp.where(keep, full, 0.0).reshape(CHUNK, BLK, LANES)
            at = pl.ds(pl.multiple_of(step * CHUNK, CHUNK), CHUNK)
            result_ref[at, :] = jnp.sum(picked, axis=1)
            return carry

        lax.fori_loop(lowest // CHUNK, DEG // CHUNK, one_chunk, start_state(log_start))
        turned = result_ref[...].T
        turned = turned[:ROWS] + turned[ROWS : 2 * ROWS]
        degree = lax.broadcasted_iota(jnp.int32, (BLK, DEG), 1)
        here = pl.ds(pl.multiple_of(block * BLK, BLK), BLK)
        for c in range(CHAN):
            part = jnp.where(degree >= orders, turned[c * BLK : (c + 1) * BLK], 0.0)
            if c // 2 == FIELDS - 1:
                part = part * inverse
            out_ref[c, here, :] = part
        return unused

    lax.fori_loop(0, blocks, one_block, 0)


def base_trig(order, first):
    lane = lax.broadcasted_iota(jnp.int32, order.shape, 1) + first
    phase = (order * lane) & (NLON - 1)
    quarter = (phase + NLON // 8) >> 9
    rest = (phase - quarter * (NLON // 4)).astype(F32) * (2.0 * math.pi / NLON)
    square = rest * rest
    sine = 1.0 / 362880.0
    for coef in (-1.0 / 5040.0, 1.0 / 120.0, -1.0 / 6.0, 1.0):
        sine = sine * square + coef
    sine = sine * rest
    cosine = 1.0 / 40320.0
    for coef in (-1.0 / 720.0, 1.0 / 24.0, -0.5, 1.0):
        cosine = cosine * square + coef
    swap = (quarter & 1) == 1
    cos_out = jnp.where(swap, sine, cosine)
    sin_out = jnp.where(swap, cosine, sine)
    cos_out = jnp.where(((quarter + 1) & 2) == 2, -cos_out, cos_out)
    sin_out = jnp.where((quarter & 2) == 2, -sin_out, sin_out)
    return cos_out, sin_out


def grid_kernel(
    dims, *refs,
):
    bands, row_count, modes, pieces, tiles, slots = dims
    data_refs = refs[:pieces]
    orders_ref, rate_ref, sine_ref = refs[pieces : pieces + 3]
    out_refs = refs[pieces + 3 : 2 * pieces + 3]
    total_ref = refs[2 * pieces + 3]
    (lhs_ref, cos_ref, sin_ref, turn_cos, turn_sin, high_ref, low_ref, weight_ref, acc_ref) = refs[
        2 * pieces + 4 :
    ]
    piece_modes = modes // pieces
    piece_slots = bands * piece_modes
    group = FIELDS * row_count
    padded = weight_ref.shape[0] // 2

    for p in range(pieces):
        columns = []
        for t in range(tiles):
            part = data_refs[p][:, t * piece_modes : (t + 1) * piece_modes, :]
            columns.append(part.reshape(piece_slots, LANES).T)
        turned = jnp.concatenate(columns, 0)
        for kind in range(2):
            high, low = split_two(turned[kind * group : (kind + 1) * group])
            at = kind * slots + p * piece_slots
            lhs_ref[:group, at : at + piece_slots] = high
            lhs_ref[group:, at : at + piece_slots] = low

    def prepare(step, unused):
        at = pl.ds(pl.multiple_of(step * 64, 64), 64)
        order = orders_ref[at, :]
        for t in range(KTILE // LANES):
            cosine, sine = base_trig(order, t * LANES)
            cos_ref[at, t * LANES : (t + 1) * LANES] = cosine
            sin_ref[at, t * LANES : (t + 1) * LANES] = sine
        eighth = order & 7
        root = math.sqrt(0.5)
        odd = (eighth & 1) == 1
        turned_cos = jnp.where(odd, root, jnp.where((eighth & 2) == 0, 1.0, 0.0))
        turned_sin = jnp.where(odd, root, jnp.where((eighth & 2) == 2, 1.0, 0.0))
        turn_cos[at, :] = jnp.where((eighth >= 3) & (eighth <= 5), -turned_cos, turned_cos)
        turn_sin[at, :] = jnp.where(eighth > 4, -turned_sin, turned_sin)
        return unused

    lax.fori_loop(0, slots // 64, prepare, 0)
    acc_ref[...] = jnp.zeros_like(acc_ref)
    weight_ref[...] = jnp.zeros_like(weight_ref)
    flux_scale = math.pi / (2.0 * NLAT * NLON * DEG)

    def one_tile(step, total):
        for s in range(0, slots, 64):
            rows_at = slice(s, s + 64)
            more_cos = jnp.tile(turn_cos[rows_at, :], (1, KTILE // LANES))
            more_sin = jnp.tile(turn_sin[rows_at, :], (1, KTILE // LANES))
            cosine, sine = cos_ref[rows_at, :], sin_ref[rows_at, :]
            cos_ref[rows_at, :] = cosine * more_cos - sine * more_sin
            sin_ref[rows_at, :] = sine * more_cos + cosine * more_sin
            high, low = split_two(cosine)
            high_ref[rows_at, :], low_ref[rows_at, :] = high, low
            high, low = split_two(sine)
            high_ref[slots + s : slots + s + 64, :] = high
            low_ref[slots + s : slots + s + 64, :] = low
        first = dot(lhs_ref[...], high_ref[...])
        second = dot(lhs_ref[:group, :], low_ref[...])
        fields = first[:group] + first[group:] + second
        weight = jnp.tile(sine_ref[...], (1, KTILE // LANES))
        columns = pl.ds(pl.multiple_of(step * KTILE, KTILE), KTILE)
        weighted_rate = rate_ref[:, columns] * weight
        scaled = fields[:row_count] * (weight * flux_scale)
        values = jnp.concatenate(
            [
                fields[row_count : 2 * row_count] * scaled,
                fields[2 * row_count :] * scaled,
                weighted_rate * fields[:row_count],
            ],
            0,
        )
        high, low = split_two(values)
        weight_ref[:group, :] = high
        weight_ref[padded : padded + group, :] = low
        first = dot(high_ref[...], weight_ref[...], 1)
        second = dot(low_ref[...], weight_ref[:padded, :], 1)
        acc_ref[...] += first[:, :padded] + first[:, padded:] + second
        return total + jnp.sum(weighted_rate.reshape(row_count // 8, 8, KTILE), axis=0)

    total = lax.fori_loop(0, NLON // KTILE, one_tile, jnp.zeros((8, KTILE), F32))
    total_ref[...] = jnp.broadcast_to(jnp.sum(total), (bands, 8, LANES))
    for p in range(pieces):
        at = p * piece_slots
        joined = [
            acc_ref[at : at + piece_slots, :group],
            acc_ref[slots + at : slots + at + piece_slots, :group],
        ]
        if 2 * group < tiles * LANES:
            joined.append(jnp.zeros((piece_slots, tiles * LANES - 2 * group), F32))
        joined = jnp.concatenate(joined, 1)
        for t in range(tiles):
            part = joined[:, t * LANES : (t + 1) * LANES]
            out_refs[p][:, t * piece_modes : (t + 1) * piece_modes, :] = part.reshape(
                bands, piece_modes, LANES
            )


VMEM = pl.BlockSpec(memory_space=pltpu.VMEM)
SMEM = pl.BlockSpec(memory_space=pltpu.SMEM)
PIECES = 1


def per_device(spectrum, capture_rate, row_latitude, slot_wavenumber):
    bands = lax.axis_size("band")
    modes = spectrum.shape[3]
    row_count = capture_rate.shape[1]
    slots = slot_wavenumber.shape[0]
    blocks = modes // BLK
    pieces = min(PIECES, blocks)
    per_piece = blocks // pieces
    tiles = -(-CHAN * row_count // LANES)
    band_index = lax.axis_index("band")
    rows = jnp.asarray(latitude_rows())
    spread = jnp.asarray(spread_matrix())
    latitude = row_latitude.reshape(1, NLAT)
    coeffs = spectrum.reshape(CHAN, modes, DEG)
    params = pltpu.CompilerParams(vmem_limit_bytes=48 * 2**20)
    chunk_rows = tiles * per_piece * BLK

    def synth(p):
        dims = (bands, row_count, modes, p * per_piece, per_piece, tiles)
        return pl.pallas_call(
            lambda *refs: synth_kernel(dims, *refs),
            out_shape=jax.ShapeDtypeStruct((bands, chunk_rows, LANES), F32),
            in_specs=[SMEM, VMEM, VMEM, VMEM, VMEM],
            out_specs=VMEM,
            scratch_shapes=[
                pltpu.VMEM((BLK, DEG), F32),
                pltpu.VMEM((BLK, DEG), F32),
                pltpu.VMEM((DEG // CHUNK, 2 * ROWS, CHUNK * BLK), BF),
                pltpu.VMEM((2, CHUNK // 2 * BLK, HALF), BF),
                pltpu.VMEM((2, CHUNK // 2 * BLK, HALF), BF),
                pltpu.VMEM((2, ROWS, HALF), F32),
                pltpu.VMEM((HALF, NLAT), BF),
            ],
            compiler_params=params,
            name="synth",
        )(
            slot_wavenumber,
            coeffs[:, p * per_piece * BLK : (p + 1) * per_piece * BLK],
            rows, spread, latitude,
        )

    def analyze(p, data, total):
        dims = (bands, row_count, modes, p * per_piece, per_piece, tiles)
        return pl.pallas_call(
            lambda *refs: analyze_kernel(dims, *refs),
            out_shape=jax.ShapeDtypeStruct((CHAN, per_piece * BLK, DEG), F32),
            in_specs=[SMEM, VMEM, VMEM, VMEM, VMEM],
            out_specs=VMEM,
            scratch_shapes=[
                pltpu.VMEM((BLK, DEG), F32),
                pltpu.VMEM((BLK, DEG), F32),
                pltpu.VMEM((CHUNK * BLK, HALF), BF),
                pltpu.VMEM((CHUNK * BLK, HALF), BF),
                pltpu.VMEM((HALF, 2 * LANES), BF),
                pltpu.VMEM((DEG, LANES), F32),
                pltpu.VMEM((HALF, NLAT), BF),
            ],
            compiler_params=params,
            name="analyze",
        )(slot_wavenumber, data, total, rows, latitude)

    def exchange(value):
        return lax.all_to_all(value, "band", split_axis=0, concat_axis=0, tiled=True)

    received = [exchange(synth(p)) for p in range(pieces)]

    my_latitudes = lax.dynamic_slice_in_dim(row_latitude, band_index * row_count, row_count)
    row_sine = jnp.sin(jnp.pi * (my_latitudes.astype(F32) + 0.5) / NLAT)
    row_sine = jnp.broadcast_to(row_sine[:, None], (row_count, LANES))
    orders = slot_wavenumber.reshape(bands, pieces, per_piece * BLK).transpose(1, 0, 2)
    orders = jnp.broadcast_to(orders.reshape(slots, 1), (slots, LANES))
    group = FIELDS * row_count
    padded = -(-group // LANES) * LANES
    dims = (bands, row_count, modes, pieces, tiles, slots)
    outs = pl.pallas_call(
        lambda *refs: grid_kernel(dims, *refs),
        out_shape=[jax.ShapeDtypeStruct((bands, chunk_rows, LANES), F32)] * pieces
        + [jax.ShapeDtypeStruct((bands, 8, LANES), F32)],
        in_specs=[VMEM] * (pieces + 3),
        out_specs=[VMEM] * (pieces + 1),
        scratch_shapes=[
            pltpu.VMEM((2 * group, 2 * slots), BF),
            pltpu.VMEM((slots, KTILE), F32),
            pltpu.VMEM((slots, KTILE), F32),
            pltpu.VMEM((slots, LANES), F32),
            pltpu.VMEM((slots, LANES), F32),
            pltpu.VMEM((2 * slots, KTILE), BF),
            pltpu.VMEM((2 * slots, KTILE), BF),
            pltpu.VMEM((2 * padded, KTILE), BF),
            pltpu.VMEM((2 * slots, padded), F32),
        ],
        compiler_params=params,
        name="grid",
    )(*received, orders, capture_rate.reshape(row_count, NLON), row_sine)
    total = exchange(outs[pieces])
    parts = [analyze(p, exchange(outs[p]), total) for p in range(pieces)]
    result = parts[0] if pieces == 1 else jnp.concatenate(parts, 1)
    return result.reshape(1, FIELDS, 2, modes, DEG)


def solution(mesh):
    return jax.shard_map(
        per_device,
        mesh=mesh,
        in_specs=(P("shell", None, None, "band", None), P("shell", "band", None), P(), P()),
        out_specs=P("shell", None, None, "band", None),
        check_vma=False,
    )
```

```python
import math

import jax
import jax.numpy as jnp
import numpy as np
from jax import lax
from jax.experimental import pallas as pl
from jax.experimental.pallas import tpu as pltpu
from jax.sharding import PartitionSpec as P

DEG = 512
NLAT = 1024
NLON = 2048
FIELDS = 3
HALF = NLAT // 2
CHAN = 2 * FIELDS
BLK = 8
ROWS = CHAN * BLK
CHUNK = 64
LANES = 128
KTILE = 256
BF = jnp.bfloat16
F32 = jnp.float32


def split_two(value):
    high = value.astype(BF)
    low = (value - high.astype(F32)).astype(BF)
    return high, low


def dot(lhs, rhs, contract_rhs=0):
    return lax.dot_general(
        lhs, rhs, (((1,), (contract_rhs,)), ((), ())), preferred_element_type=F32
    )


def latitude_rows():
    theta = np.pi * (np.arange(HALF) + 0.5) / NLAT
    index = np.arange(DEG, dtype=np.float64)
    log_terms = np.zeros(DEG)
    log_terms[1:] = 0.5 * np.log2((2.0 * index[1:] + 1.0) / (2.0 * index[1:]))
    rows = np.zeros((8, DEG))
    rows[0], rows[1], rows[2] = np.cos(theta), np.log2(np.sin(theta)), log_terms
    return rows.astype(np.float32)


def spread_matrix():
    spread = np.zeros((LANES, 2, 2, CHUNK // 2, BLK), np.float32)
    for half in range(2):
        for parity in range(2):
            for step in range(CHUNK // 2):
                spread[half * CHUNK + 2 * step + parity, half, parity, step, :] = 1.0
    return spread.reshape(LANES, 2 * 2 * (CHUNK // 2) * BLK).astype(BF)


def block_orders(slots_ref, first):
    sublane = lax.broadcasted_iota(jnp.int32, (BLK, LANES), 0)
    orders = jnp.zeros((BLK, LANES), jnp.int32)
    lowest = jnp.int32(DEG)
    for i in range(BLK):
        order = slots_ref[first + i]
        orders = jnp.where(sublane == i, order, orders)
        lowest = jnp.minimum(lowest, order)
    return orders[:, :1], lowest


def recursion_tables(order, rows_ref, alpha_ref, beta_ref):
    degree = lax.broadcasted_iota(jnp.int32, (BLK, DEG), 1).astype(F32)
    order_sq = order * order
    denominator = degree * degree - order_sq
    safe = jnp.where(denominator > 0, denominator, 1.0)
    alpha = jnp.sqrt((4.0 * degree * degree - 1.0) / safe)
    back = jnp.maximum((degree - 1.0) * (degree - 1.0) - order_sq, 0.0)
    beta = jnp.sqrt(back * (2.0 * degree + 1.0) / (safe * jnp.maximum(2.0 * degree - 3.0, 1.0)))
    alpha_ref[...] = jnp.where(degree > order, alpha, 0.0)
    beta_ref[...] = jnp.where(degree > order, beta, -1.0)
    terms = jnp.where(degree <= order, rows_ref[2:3, :], 0.0)
    norm = jnp.where(order > 0, 0.5 + jnp.sum(terms, axis=1, keepdims=True), 0.0)
    return norm + order * rows_ref[1:2, :]


def run_chunk(step, carry, cosine, alpha_ref, beta_ref, emit):
    current, previous, log_scale = carry
    tile = pl.ds(pl.multiple_of(step // 2 * LANES, LANES), LANES)
    shift = (step % 2) * CHUNK
    alpha = pltpu.roll(alpha_ref[:, tile], shift, 1)
    beta = pltpu.roll(beta_ref[:, tile], shift, 1)
    scale = None
    for i in range(CHUNK):
        if i % 16 == 0:
            large = jnp.abs(current) > 2.0**60
            factor = jnp.where(large, 2.0**-60, 1.0)
            current = current * factor
            previous = previous * factor
            log_scale = jnp.where(large, log_scale + 60.0, log_scale)
            scale = jnp.exp2(jnp.maximum(log_scale, -200.0))
        newest = (alpha[:, i : i + 1] * cosine) * current - beta[:, i : i + 1] * previous
        current, previous = newest, current
        emit(i, newest * scale)
    return current, previous, log_scale


def start_state(log_start):
    ones = jnp.ones((BLK, HALF), F32)
    return ones, ones, log_start


def fold_matrix(latitude_ref, fold_ref):
    latitude = latitude_ref[...]
    north = jnp.where(latitude < HALF, latitude, NLAT - 1 - latitude)
    sublane = lax.broadcasted_iota(jnp.int32, (HALF, NLAT), 0)
    fold_ref[...] = jnp.where(sublane == north, 1.0, 0.0).astype(BF)


def synth_kernel(
    dims, slots_ref, spec_ref, rows_ref, spread_ref, latitude_ref, out_ref,
    alpha_ref, beta_ref, lhs_ref, high_a, low_a, high_b, low_b, acc_ref, fold_ref,
):
    bands, row_count, modes, first_block, blocks, tiles = dims
    fold_matrix(latitude_ref, fold_ref)
    base = lax.axis_index("band") * modes + first_block * BLK
    south = latitude_ref[...] >= HALF
    spread_width = 4 * (CHUNK // 2) * BLK
    lane = lax.broadcasted_iota(jnp.int32, (2 * ROWS, spread_width), 1)
    sub = lax.broadcasted_iota(jnp.int32, (2 * ROWS, spread_width), 0)
    diagonal = (lane % BLK) == (sub % BLK)
    width = (CHUNK // 2) * BLK

    def one_block(block, unused):
        orders, lowest = block_orders(slots_ref, base + block * BLK)
        order = orders.astype(F32)
        log_start = recursion_tables(order, rows_ref, alpha_ref, beta_ref)
        here = pl.ds(pl.multiple_of(block * BLK, BLK), BLK)
        degree = lax.broadcasted_iota(jnp.int32, (BLK, DEG), 1)
        coeffs = jnp.where((degree >= orders)[None], spec_ref[:, here, :], 0.0)
        coeff_high, coeff_low = split_two(coeffs.reshape(ROWS, DEG))
        stacked = jnp.concatenate([coeff_high, coeff_low], 0)
        for t in range(DEG // LANES):
            wide = dot(stacked[:, t * LANES : (t + 1) * LANES], spread_ref[...])
            wide = jnp.where(diagonal, wide, 0.0).astype(BF)
            for half in range(2):
                lhs_ref[2 * t + half] = wide[:, half * 2 * width : (half + 1) * 2 * width]
        acc_ref[...] = jnp.zeros_like(acc_ref)
        cosine = jnp.broadcast_to(rows_ref[0:1, :], (BLK, HALF))

        def recur(step, carry, high_ref, low_ref):
            held = {}

            def emit(i, value):
                if i % 4 < 2:
                    held[i] = value
                else:
                    pair = jnp.concatenate([held.pop(i - 2), value], 0)
                    high, low = split_two(pair)
                    at = (i // 4) * 2 * BLK
                    high_ref[i % 2, at : at + 2 * BLK, :] = high
                    low_ref[i % 2, at : at + 2 * BLK, :] = low

            return run_chunk(step, carry, cosine, alpha_ref, beta_ref, emit)

        def add_products(step, high_ref, low_ref):
            for parity in range(2):
                lhs = lhs_ref[step, :, parity * width : (parity + 1) * width]
                first = dot(lhs, high_ref[parity])
                second = dot(lhs[:ROWS], low_ref[parity])
                acc_ref[parity] += first[:ROWS] + first[ROWS:] + second

        def two_chunks(pair, carry):
            step = 2 * pair
            carry = recur(step, carry, high_a, low_a)
            add_products(jnp.maximum(step - 1, 0), high_b, low_b)
            carry = recur(step + 1, carry, high_b, low_b)
            add_products(step, high_a, low_a)
            return carry

        high_b[...] = jnp.zeros_like(high_b)
        low_b[...] = jnp.zeros_like(low_b)
        chunks = DEG // CHUNK
        lax.fori_loop(lowest // (2 * CHUNK), chunks // 2, two_chunks, start_state(log_start))
        add_products(chunks - 1, high_b, low_b)
        both = acc_ref[...].reshape(2 * ROWS, HALF)
        high, low = split_two(both)
        moved = dot(jnp.concatenate([high, low], 0), fold_ref[...])
        moved = moved[: 2 * ROWS] + moved[2 * ROWS :]
        sign = jnp.tile(1.0 - 2.0 * (orders % 2).astype(F32), (CHAN, 1))
        even, odd = moved[:ROWS], moved[ROWS:]
        values = jnp.where(south, sign * (even - odd), even + odd)
        for d in range(bands):
            parts = []
            for kind in range(2):
                for field in range(FIELDS):
                    c = field * 2 + kind
                    parts.append(
                        values[c * BLK : (c + 1) * BLK, d * row_count : (d + 1) * row_count]
                    )
            if CHAN * row_count < tiles * LANES:
                parts.append(jnp.zeros((BLK, tiles * LANES - CHAN * row_count), F32))
            joined = jnp.concatenate(parts, 1)
            for t in range(tiles):
                at = pl.ds(pl.multiple_of(t * blocks * BLK + block * BLK, BLK), BLK)
                out_ref[d, at, :] = joined[:, t * LANES : (t + 1) * LANES]
        return unused

    lax.fori_loop(0, blocks, one_block, 0)


def analyze_kernel(
    dims, total_row, slots_ref, data_ref, total_ref, rows_ref, latitude_ref, out_ref,
    alpha_ref, beta_ref, high_a, low_a, high_b, low_b, weight_ref, result_ref, fold_ref,
):
    bands, row_count, modes, first_block, blocks, tiles = dims
    fold_matrix(latitude_ref, fold_ref)
    base = lax.axis_index("band") * modes + first_block * BLK
    south = latitude_ref[...] >= HALF
    total = total_ref[0, total_row : total_row + 8]
    for d in range(1, bands):
        total = total + total_ref[d, total_row : total_row + 8]
    inverse = (1.0 / total)[:, :1]
    lane = lax.broadcasted_iota(jnp.int32, (CHUNK * BLK, LANES), 1)
    sub = lax.broadcasted_iota(jnp.int32, (CHUNK * BLK, LANES), 0)
    keep = (lane % BLK == sub % BLK) & (lane // ROWS == sub // BLK % 2)

    def one_block(block, unused):
        orders, lowest = block_orders(slots_ref, base + block * BLK)
        order = orders.astype(F32)
        log_start = recursion_tables(order, rows_ref, alpha_ref, beta_ref)
        sign = 1.0 - 2.0 * (orders % 2).astype(F32)
        evens, odds = [], []
        for c in range(CHAN):
            offset = ((c % 2) * FIELDS + c // 2) * row_count
            t, at = offset // LANES, offset % LANES
            rows = pl.ds(pl.multiple_of(t * blocks * BLK + block * BLK, BLK), BLK)
            values = jnp.concatenate(
                [data_ref[d, rows, :][:, at : at + row_count] for d in range(bands)], 1
            )
            flipped = sign * values
            evens.append(jnp.where(south, flipped, values))
            odds.append(jnp.where(south, -flipped, values))
        high, low = split_two(jnp.concatenate(evens + odds, 0))
        folded = dot(jnp.concatenate([high, low], 0), fold_ref[...], 1)
        folded = folded[: 2 * ROWS] + folded[2 * ROWS :]
        padded = jnp.concatenate([folded, jnp.zeros((LANES - 2 * ROWS, HALF), F32)], 0)
        high, low = split_two(padded.T)
        weight_ref[:, :LANES] = high
        weight_ref[:, LANES:] = low
        result_ref[...] = jnp.zeros_like(result_ref)
        cosine = jnp.broadcast_to(rows_ref[0:1, :], (BLK, HALF))

        def recur(step, carry, high_ref, low_ref):
            held = {}

            def emit(i, value):
                if i % 2 == 0:
                    held[i] = value
                else:
                    pair = jnp.concatenate([held.pop(i - 1), value], 0)
                    high, low = split_two(pair)
                    at = (i // 2) * 2 * BLK
                    high_ref[at : at + 2 * BLK, :] = high
                    low_ref[at : at + 2 * BLK, :] = low

            return run_chunk(step, carry, cosine, alpha_ref, beta_ref, emit)

        def store_products(step, high_ref, low_ref):
            first = dot(high_ref[...], weight_ref[...])
            second = dot(low_ref[...], weight_ref[:, :LANES])
            full = first[:, :LANES] + first[:, LANES:] + second
            picked = jnp.where(keep, full, 0.0).reshape(CHUNK, BLK, LANES)
            at = pl.ds(pl.multiple_of(step * CHUNK, CHUNK), CHUNK)
            result_ref[at, :] = jnp.sum(picked, axis=1)

        def two_chunks(pair, carry):
            step = 2 * pair
            carry = recur(step, carry, high_a, low_a)
            store_products(jnp.maximum(step - 1, 0), high_b, low_b)
            carry = recur(step + 1, carry, high_b, low_b)
            store_products(step, high_a, low_a)
            return carry

        high_b[...] = jnp.zeros_like(high_b)
        low_b[...] = jnp.zeros_like(low_b)
        chunks = DEG // CHUNK
        lax.fori_loop(lowest // (2 * CHUNK), chunks // 2, two_chunks, start_state(log_start))
        store_products(chunks - 1, high_b, low_b)
        turned = result_ref[...].T
        turned = turned[:ROWS] + turned[ROWS : 2 * ROWS]
        degree = lax.broadcasted_iota(jnp.int32, (BLK, DEG), 1)
        here = pl.ds(pl.multiple_of(block * BLK, BLK), BLK)
        for c in range(CHAN):
            part = jnp.where(degree >= orders, turned[c * BLK : (c + 1) * BLK], 0.0)
            if c // 2 == FIELDS - 1:
                part = part * inverse
            out_ref[c, here, :] = part
        return unused

    lax.fori_loop(0, blocks, one_block, 0)


def base_trig(order, first):
    lane = lax.broadcasted_iota(jnp.int32, order.shape, 1) + first
    phase = (order * lane) & (NLON - 1)
    quarter = (phase + NLON // 8) >> 9
    rest = (phase - quarter * (NLON // 4)).astype(F32) * (2.0 * math.pi / NLON)
    square = rest * rest
    sine = 1.0 / 362880.0
    for coef in (-1.0 / 5040.0, 1.0 / 120.0, -1.0 / 6.0, 1.0):
        sine = sine * square + coef
    sine = sine * rest
    cosine = 1.0 / 40320.0
    for coef in (-1.0 / 720.0, 1.0 / 24.0, -0.5, 1.0):
        cosine = cosine * square + coef
    swap = (quarter & 1) == 1
    cos_out = jnp.where(swap, sine, cosine)
    sin_out = jnp.where(swap, cosine, sine)
    cos_out = jnp.where(((quarter + 1) & 2) == 2, -cos_out, cos_out)
    sin_out = jnp.where((quarter & 2) == 2, -sin_out, sin_out)
    return cos_out, sin_out


def grid_kernel(
    dims, *refs,
):
    bands, row_count, modes, pieces, tiles, slots = dims
    data_refs = refs[:pieces]
    orders_ref, rate_ref, sine_ref = refs[pieces : pieces + 3]
    out_refs = refs[pieces + 3 : 2 * pieces + 3]
    (lhs_ref, cos_ref, sin_ref, turn_cos, turn_sin, high_ref, low_ref, weight_ref, acc_ref) = refs[
        2 * pieces + 3 :
    ]
    piece_modes = modes // pieces
    piece_slots = bands * piece_modes
    group = FIELDS * row_count
    padded = weight_ref.shape[0] // 2

    for p in range(pieces):
        columns = []
        for t in range(tiles):
            part = data_refs[p][:, t * piece_modes : (t + 1) * piece_modes, :]
            columns.append(part.reshape(piece_slots, LANES).T)
        turned = jnp.concatenate(columns, 0)
        for kind in range(2):
            high, low = split_two(turned[kind * group : (kind + 1) * group])
            at = kind * slots + p * piece_slots
            lhs_ref[:group, at : at + piece_slots] = high
            lhs_ref[group:, at : at + piece_slots] = low

    def prepare(step, unused):
        at = pl.ds(pl.multiple_of(step * 64, 64), 64)
        order = orders_ref[at, :]
        for t in range(KTILE // LANES):
            cosine, sine = base_trig(order, t * LANES)
            cos_ref[at, t * LANES : (t + 1) * LANES] = cosine
            sin_ref[at, t * LANES : (t + 1) * LANES] = sine
        eighth = order & 7
        root = math.sqrt(0.5)
        odd = (eighth & 1) == 1
        turned_cos = jnp.where(odd, root, jnp.where((eighth & 2) == 0, 1.0, 0.0))
        turned_sin = jnp.where(odd, root, jnp.where((eighth & 2) == 2, 1.0, 0.0))
        turn_cos[at, :] = jnp.where((eighth >= 3) & (eighth <= 5), -turned_cos, turned_cos)
        turn_sin[at, :] = jnp.where(eighth > 4, -turned_sin, turned_sin)
        return unused

    lax.fori_loop(0, slots // 64, prepare, 0)
    acc_ref[...] = jnp.zeros_like(acc_ref)
    weight_ref[...] = jnp.zeros_like(weight_ref)
    flux_scale = math.pi / (2.0 * NLAT * NLON * DEG)

    def one_tile(step, total):
        for s in range(0, slots, 64):
            rows_at = slice(s, s + 64)
            more_cos = jnp.tile(turn_cos[rows_at, :], (1, KTILE // LANES))
            more_sin = jnp.tile(turn_sin[rows_at, :], (1, KTILE // LANES))
            cosine, sine = cos_ref[rows_at, :], sin_ref[rows_at, :]
            cos_ref[rows_at, :] = cosine * more_cos - sine * more_sin
            sin_ref[rows_at, :] = sine * more_cos + cosine * more_sin
            high, low = split_two(cosine)
            high_ref[rows_at, :], low_ref[rows_at, :] = high, low
            high, low = split_two(sine)
            high_ref[slots + s : slots + s + 64, :] = high
            low_ref[slots + s : slots + s + 64, :] = low
        first = dot(lhs_ref[...], high_ref[...])
        second = dot(lhs_ref[:group, :], low_ref[...])
        fields = first[:group] + first[group:] + second
        weight = jnp.tile(sine_ref[...], (1, KTILE // LANES))
        columns = pl.ds(pl.multiple_of(step * KTILE, KTILE), KTILE)
        weighted_rate = rate_ref[:, columns] * weight
        scaled = fields[:row_count] * (weight * flux_scale)
        values = jnp.concatenate(
            [
                fields[row_count : 2 * row_count] * scaled,
                fields[2 * row_count :] * scaled,
                weighted_rate * fields[:row_count],
            ],
            0,
        )
        high, low = split_two(values)
        weight_ref[:group, :] = high
        weight_ref[padded : padded + group, :] = low
        first = dot(high_ref[...], weight_ref[...], 1)
        second = dot(low_ref[...], weight_ref[:padded, :], 1)
        acc_ref[...] += first[:, :padded] + first[:, padded:] + second
        return total + jnp.sum(weighted_rate.reshape(row_count // 8, 8, KTILE), axis=0)

    total = lax.fori_loop(0, NLON // KTILE, one_tile, jnp.zeros((8, KTILE), F32))
    out_refs[0][:, tiles * piece_modes :, :] = jnp.broadcast_to(jnp.sum(total), (bands, 8, LANES))
    for p in range(pieces):
        at = p * piece_slots
        joined = [
            acc_ref[at : at + piece_slots, :group],
            acc_ref[slots + at : slots + at + piece_slots, :group],
        ]
        if 2 * group < tiles * LANES:
            joined.append(jnp.zeros((piece_slots, tiles * LANES - 2 * group), F32))
        joined = jnp.concatenate(joined, 1)
        for t in range(tiles):
            part = joined[:, t * LANES : (t + 1) * LANES]
            out_refs[p][:, t * piece_modes : (t + 1) * piece_modes, :] = part.reshape(
                bands, piece_modes, LANES
            )


VMEM = pl.BlockSpec(memory_space=pltpu.VMEM)
SMEM = pl.BlockSpec(memory_space=pltpu.SMEM)
PIECES = 4


def per_device(spectrum, capture_rate, row_latitude, slot_wavenumber):
    bands = lax.axis_size("band")
    modes = spectrum.shape[3]
    row_count = capture_rate.shape[1]
    slots = slot_wavenumber.shape[0]
    blocks = modes // BLK
    pieces = min(PIECES, blocks)
    per_piece = blocks // pieces
    tiles = -(-CHAN * row_count // LANES)
    band_index = lax.axis_index("band")
    rows = jnp.asarray(latitude_rows())
    spread = jnp.asarray(spread_matrix())
    latitude = row_latitude.reshape(1, NLAT)
    coeffs = spectrum.reshape(CHAN, modes, DEG)
    params = pltpu.CompilerParams(vmem_limit_bytes=40 * 2**20)
    cost = pl.CostEstimate(
        flops=6 * 10**9 * per_piece, bytes_accessed=2**20, transcendentals=0
    )
    chunk_rows = tiles * per_piece * BLK

    def synth(p):
        dims = (bands, row_count, modes, p * per_piece, per_piece, tiles)
        return pl.pallas_call(
            lambda *refs: synth_kernel(dims, *refs),
            out_shape=jax.ShapeDtypeStruct((bands, chunk_rows, LANES), F32),
            in_specs=[SMEM, VMEM, VMEM, VMEM, VMEM],
            out_specs=VMEM,
            scratch_shapes=[
                pltpu.VMEM((BLK, DEG), F32),
                pltpu.VMEM((BLK, DEG), F32),
                pltpu.VMEM((DEG // CHUNK, 2 * ROWS, CHUNK * BLK), BF),
                pltpu.VMEM((2, CHUNK // 2 * BLK, HALF), BF),
                pltpu.VMEM((2, CHUNK // 2 * BLK, HALF), BF),
                pltpu.VMEM((2, CHUNK // 2 * BLK, HALF), BF),
                pltpu.VMEM((2, CHUNK // 2 * BLK, HALF), BF),
                pltpu.VMEM((2, ROWS, HALF), F32),
                pltpu.VMEM((HALF, NLAT), BF),
            ],
            compiler_params=params,
            cost_estimate=cost,
            name="synth",
        )(
            slot_wavenumber,
            coeffs[:, p * per_piece * BLK : (p + 1) * per_piece * BLK],
            rows, spread, latitude,
        )

    def analyze(p, data, total):
        dims = (bands, row_count, modes, p * per_piece, per_piece, tiles)
        return pl.pallas_call(
            lambda *refs: analyze_kernel(dims, chunk_rows, *refs),
            out_shape=jax.ShapeDtypeStruct((CHAN, per_piece * BLK, DEG), F32),
            in_specs=[SMEM, VMEM, VMEM, VMEM, VMEM],
            out_specs=VMEM,
            scratch_shapes=[
                pltpu.VMEM((BLK, DEG), F32),
                pltpu.VMEM((BLK, DEG), F32),
                pltpu.VMEM((CHUNK * BLK, HALF), BF),
                pltpu.VMEM((CHUNK * BLK, HALF), BF),
                pltpu.VMEM((CHUNK * BLK, HALF), BF),
                pltpu.VMEM((CHUNK * BLK, HALF), BF),
                pltpu.VMEM((HALF, 2 * LANES), BF),
                pltpu.VMEM((DEG, LANES), F32),
                pltpu.VMEM((HALF, NLAT), BF),
            ],
            compiler_params=params,
            cost_estimate=cost,
            name="analyze",
        )(slot_wavenumber, data, total, rows, latitude)

    def exchange(value):
        return lax.all_to_all(value, "band", split_axis=0, concat_axis=0, tiled=True)

    received = [exchange(synth(p)) for p in range(pieces)]

    my_latitudes = lax.dynamic_slice_in_dim(row_latitude, band_index * row_count, row_count)
    row_sine = jnp.sin(jnp.pi * (my_latitudes.astype(F32) + 0.5) / NLAT)
    row_sine = jnp.broadcast_to(row_sine[:, None], (row_count, LANES))
    orders = slot_wavenumber.reshape(bands, pieces, per_piece * BLK).transpose(1, 0, 2)
    orders = jnp.broadcast_to(orders.reshape(slots, 1), (slots, LANES))
    group = FIELDS * row_count
    padded = -(-group // LANES) * LANES
    dims = (bands, row_count, modes, pieces, tiles, slots)
    outs = pl.pallas_call(
        lambda *refs: grid_kernel(dims, *refs),
        out_shape=[
            jax.ShapeDtypeStruct((bands, chunk_rows + (8 if p == 0 else 0), LANES), F32)
            for p in range(pieces)
        ],
        in_specs=[VMEM] * (pieces + 3),
        out_specs=[VMEM] * pieces,
        scratch_shapes=[
            pltpu.VMEM((2 * group, 2 * slots), BF),
            pltpu.VMEM((slots, KTILE), F32),
            pltpu.VMEM((slots, KTILE), F32),
            pltpu.VMEM((slots, LANES), F32),
            pltpu.VMEM((slots, LANES), F32),
            pltpu.VMEM((2 * slots, KTILE), BF),
            pltpu.VMEM((2 * slots, KTILE), BF),
            pltpu.VMEM((2 * padded, KTILE), BF),
            pltpu.VMEM((2 * slots, padded), F32),
        ],
        compiler_params=params,
        name="grid",
    )(*received, orders, capture_rate.reshape(row_count, NLON), row_sine)
    returned = [exchange(out) for out in outs]
    parts = [analyze(p, returned[p], returned[0]) for p in range(pieces)]
    result = parts[0] if pieces == 1 else jnp.concatenate(parts, 1)
    return result.reshape(1, FIELDS, 2, modes, DEG)


def solution(mesh):
    return jax.shard_map(
        per_device,
        mesh=mesh,
        in_specs=(P("shell", None, None, "band", None), P("shell", "band", None), P(), P()),
        out_specs=P("shell", None, None, "band", None),
        check_vma=False,
    )
```

```python
import functools
import math

import jax
import jax.numpy as jnp
import numpy as np
from jax import lax
from jax.experimental import pallas as pl
from jax.experimental.pallas import tpu as pltpu
from jax.sharding import PartitionSpec as P

DEG = 512
NLAT = 1024
NLON = 2048
FIELDS = 3
HALF = NLAT // 2
CHAN = 2 * FIELDS
BLK = 8
ROWS = CHAN * BLK
CHUNK = 64
LANES = 128
KTILE = 256
BF = jnp.bfloat16
F32 = jnp.float32


def split_two(value):
    high = value.astype(BF)
    low = (value - high.astype(F32)).astype(BF)
    return high, low


def dot(lhs, rhs, contract_rhs=0):
    return lax.dot_general(
        lhs, rhs, (((1,), (contract_rhs,)), ((), ())), preferred_element_type=F32
    )


def latitude_rows():
    theta = np.pi * (np.arange(HALF) + 0.5) / NLAT
    index = np.arange(DEG, dtype=np.float64)
    log_terms = np.zeros(DEG)
    log_terms[1:] = 0.5 * np.log2((2.0 * index[1:] + 1.0) / (2.0 * index[1:]))
    rows = np.zeros((8, DEG))
    rows[0], rows[1], rows[2] = np.cos(theta), np.log2(np.sin(theta)), log_terms
    return rows.astype(np.float32)


def spread_matrix():
    spread = np.zeros((LANES, 2, 2, CHUNK // 2, BLK), np.float32)
    for half in range(2):
        for parity in range(2):
            for step in range(CHUNK // 2):
                spread[half * CHUNK + 2 * step + parity, half, parity, step, :] = 1.0
    return spread.reshape(LANES, 2 * 2 * (CHUNK // 2) * BLK).astype(BF)


def block_orders(slots_ref, first):
    sublane = lax.broadcasted_iota(jnp.int32, (BLK, LANES), 0)
    orders = jnp.zeros((BLK, LANES), jnp.int32)
    lowest = jnp.int32(DEG)
    for i in range(BLK):
        order = slots_ref[first + i]
        orders = jnp.where(sublane == i, order, orders)
        lowest = jnp.minimum(lowest, order)
    return orders[:, :1], lowest


def recursion_tables(order, rows_ref, alpha_ref, beta_ref):
    degree = lax.broadcasted_iota(jnp.int32, (BLK, DEG), 1).astype(F32)
    order_sq = order * order
    denominator = degree * degree - order_sq
    safe = jnp.where(denominator > 0, denominator, 1.0)
    alpha = jnp.sqrt((4.0 * degree * degree - 1.0) / safe)
    back = jnp.maximum((degree - 1.0) * (degree - 1.0) - order_sq, 0.0)
    beta = jnp.sqrt(back * (2.0 * degree + 1.0) / (safe * jnp.maximum(2.0 * degree - 3.0, 1.0)))
    alpha_ref[...] = jnp.where(degree > order, alpha, 0.0)
    beta_ref[...] = jnp.where(degree > order, beta, -1.0)
    terms = jnp.where(degree <= order, rows_ref[2:3, :], 0.0)
    norm = jnp.where(order > 0, 0.5 + jnp.sum(terms, axis=1, keepdims=True), 0.0)
    return norm + order * rows_ref[1:2, :]


def run_chunk(step, carry, cosine, alpha_ref, beta_ref, emit, beside):
    current, previous, log_scale = carry
    tile = pl.ds(pl.multiple_of(step // 2 * LANES, LANES), LANES)
    shift = (step % 2) * CHUNK
    alpha = pltpu.roll(alpha_ref[:, tile], shift, 1)
    beta = pltpu.roll(beta_ref[:, tile], shift, 1)
    scale = None
    for i in range(CHUNK):
        if i % 16 == 0:
            large = jnp.abs(current) > 2.0**60
            factor = jnp.where(large, 2.0**-60, 1.0)
            current = current * factor
            previous = previous * factor
            log_scale = jnp.where(large, log_scale + 60.0, log_scale)
            scale = jnp.exp2(jnp.maximum(log_scale, -200.0))
        newest = (alpha[:, i : i + 1] * cosine) * current - beta[:, i : i + 1] * previous
        current, previous = newest, current
        emit(i, newest * scale)
        if i % (CHUNK // len(beside)) == 1:
            beside[i // (CHUNK // len(beside))]()
    return current, previous, log_scale


def start_state(log_start):
    ones = jnp.ones((BLK, HALF), F32)
    return ones, ones, log_start


def fold_matrix(latitude_ref, fold_ref):
    latitude = latitude_ref[...]
    north = jnp.where(latitude < HALF, latitude, NLAT - 1 - latitude)
    sublane = lax.broadcasted_iota(jnp.int32, (HALF, NLAT), 0)
    fold_ref[...] = jnp.where(sublane == north, 1.0, 0.0).astype(BF)


def synth_kernel(
    dims, slots_ref, place_ref, spec_ref, rows_ref, spread_ref, latitude_ref, out_ref,
    alpha_ref, beta_ref, lhs_ref, high_a, low_a, high_b, low_b, acc_ref, fold_ref, coeff_ref,
):
    bands, row_count, modes, first_block, blocks, tiles = dims
    fold_matrix(latitude_ref, fold_ref)
    base = lax.axis_index("band") * modes + first_block * BLK
    south = latitude_ref[...] >= HALF
    spread_width = 4 * (CHUNK // 2) * BLK
    lane = lax.broadcasted_iota(jnp.int32, (2 * ROWS, spread_width), 1)
    sub = lax.broadcasted_iota(jnp.int32, (2 * ROWS, spread_width), 0)
    diagonal = (lane % BLK) == (sub % BLK)
    width = (CHUNK // 2) * BLK

    def one_block(block, unused):
        orders, lowest = block_orders(slots_ref, base + block * BLK)
        order = orders.astype(F32)
        log_start = recursion_tables(order, rows_ref, alpha_ref, beta_ref)
        for i in range(BLK):
            source = pl.ds(place_ref[base + block * BLK + i], 1)
            coeff_ref[:, i : i + 1, :] = spec_ref[:, source, :]
        degree = lax.broadcasted_iota(jnp.int32, (BLK, DEG), 1)
        coeffs = jnp.where((degree >= orders)[None], coeff_ref[...], 0.0)
        coeff_high, coeff_low = split_two(coeffs.reshape(ROWS, DEG))
        stacked = jnp.concatenate([coeff_high, coeff_low], 0)
        for t in range(DEG // LANES):
            wide = dot(stacked[:, t * LANES : (t + 1) * LANES], spread_ref[...])
            wide = jnp.where(diagonal, wide, 0.0).astype(BF)
            for half in range(2):
                lhs_ref[2 * t + half] = wide[:, half * 2 * width : (half + 1) * 2 * width]
        acc_ref[...] = jnp.zeros_like(acc_ref)
        cosine = jnp.broadcast_to(rows_ref[0:1, :], (BLK, HALF))

        def recur(step, carry, high_ref, low_ref, beside):
            held = {}

            def emit(i, value):
                if i % 4 < 2:
                    held[i] = value
                else:
                    pair = jnp.concatenate([held.pop(i - 2), value], 0)
                    high, low = split_two(pair)
                    at = (i // 4) * 2 * BLK
                    high_ref[i % 2, at : at + 2 * BLK, :] = high
                    low_ref[i % 2, at : at + 2 * BLK, :] = low

            return run_chunk(step, carry, cosine, alpha_ref, beta_ref, emit, beside)

        def add_products(step, high_ref, low_ref):
            def part(parity, columns):
                lhs = lhs_ref[step, :, parity * width : (parity + 1) * width]
                first = dot(lhs, high_ref[parity, :, columns])
                second = dot(lhs[:ROWS], low_ref[parity, :, columns])
                acc_ref[parity, :, columns] += first[:ROWS] + first[ROWS:] + second

            return [
                functools.partial(part, parity, slice(at, at + KTILE))
                for parity in range(2)
                for at in range(0, HALF, KTILE)
            ]

        def two_chunks(pair, carry):
            step = 2 * pair
            beside = add_products(jnp.maximum(step - 1, 0), high_b, low_b)
            carry = recur(step, carry, high_a, low_a, beside)
            beside = add_products(step, high_a, low_a)
            return recur(step + 1, carry, high_b, low_b, beside)

        high_b[...] = jnp.zeros_like(high_b)
        low_b[...] = jnp.zeros_like(low_b)
        chunks = DEG // CHUNK
        lax.fori_loop(lowest // (2 * CHUNK), chunks // 2, two_chunks, start_state(log_start))
        for part in add_products(chunks - 1, high_b, low_b):
            part()
        both = acc_ref[...].reshape(2 * ROWS, HALF)
        high, low = split_two(both)
        moved = dot(jnp.concatenate([high, low], 0), fold_ref[...])
        moved = moved[: 2 * ROWS] + moved[2 * ROWS :]
        sign = jnp.tile(1.0 - 2.0 * (orders % 2).astype(F32), (CHAN, 1))
        even, odd = moved[:ROWS], moved[ROWS:]
        values = jnp.where(south, sign * (even - odd), even + odd)
        for d in range(bands):
            parts = []
            for kind in range(2):
                for field in range(FIELDS):
                    c = field * 2 + kind
                    parts.append(
                        values[c * BLK : (c + 1) * BLK, d * row_count : (d + 1) * row_count]
                    )
            if CHAN * row_count < tiles * LANES:
                parts.append(jnp.zeros((BLK, tiles * LANES - CHAN * row_count), F32))
            joined = jnp.concatenate(parts, 1)
            for t in range(tiles):
                at = pl.ds(pl.multiple_of(t * blocks * BLK + block * BLK, BLK), BLK)
                out_ref[d, at, :] = joined[:, t * LANES : (t + 1) * LANES]
        return unused

    lax.fori_loop(0, blocks, one_block, 0)


def analyze_kernel(
    dims, total_row, slots_ref, place_ref, data_ref, total_ref, rows_ref, latitude_ref, out_ref,
    alpha_ref, beta_ref, high_a, low_a, high_b, low_b, weight_ref, result_ref, fold_ref, coeff_ref,
):
    bands, row_count, modes, first_block, blocks, tiles = dims
    fold_matrix(latitude_ref, fold_ref)
    base = lax.axis_index("band") * modes + first_block * BLK
    south = latitude_ref[...] >= HALF
    total = total_ref[0, total_row : total_row + 8]
    for d in range(1, bands):
        total = total + total_ref[d, total_row : total_row + 8]
    inverse = (1.0 / total)[:, :1]
    lane = lax.broadcasted_iota(jnp.int32, (KTILE, LANES), 1)
    sub = lax.broadcasted_iota(jnp.int32, (KTILE, LANES), 0)
    keep = (lane % BLK == sub % BLK) & (lane // ROWS == sub // BLK % 2)

    def one_block(block, unused):
        orders, lowest = block_orders(slots_ref, base + block * BLK)
        order = orders.astype(F32)
        log_start = recursion_tables(order, rows_ref, alpha_ref, beta_ref)
        sign = 1.0 - 2.0 * (orders % 2).astype(F32)
        evens, odds = [], []
        for c in range(CHAN):
            offset = ((c % 2) * FIELDS + c // 2) * row_count
            t, at = offset // LANES, offset % LANES
            rows = pl.ds(pl.multiple_of(t * blocks * BLK + block * BLK, BLK), BLK)
            values = jnp.concatenate(
                [data_ref[d, rows, :][:, at : at + row_count] for d in range(bands)], 1
            )
            flipped = sign * values
            evens.append(jnp.where(south, flipped, values))
            odds.append(jnp.where(south, -flipped, values))
        high, low = split_two(jnp.concatenate(evens + odds, 0))
        folded = dot(jnp.concatenate([high, low], 0), fold_ref[...], 1)
        folded = folded[: 2 * ROWS] + folded[2 * ROWS :]
        padded = jnp.concatenate([folded, jnp.zeros((LANES - 2 * ROWS, HALF), F32)], 0)
        high, low = split_two(padded.T)
        weight_ref[:, :LANES] = high
        weight_ref[:, LANES:] = low
        result_ref[...] = jnp.zeros_like(result_ref)
        cosine = jnp.broadcast_to(rows_ref[0:1, :], (BLK, HALF))

        def recur(step, carry, high_ref, low_ref, beside):
            held = {}

            def emit(i, value):
                if i % 2 == 0:
                    held[i] = value
                else:
                    pair = jnp.concatenate([held.pop(i - 1), value], 0)
                    high, low = split_two(pair)
                    at = (i // 2) * 2 * BLK
                    high_ref[at : at + 2 * BLK, :] = high
                    low_ref[at : at + 2 * BLK, :] = low

            return run_chunk(step, carry, cosine, alpha_ref, beta_ref, emit, beside)

        def store_products(step, high_ref, low_ref):
            def part(at):
                rows = slice(at, at + KTILE)
                first = dot(high_ref[rows, :], weight_ref[...])
                second = dot(low_ref[rows, :], weight_ref[:, :LANES])
                full = first[:, :LANES] + first[:, LANES:] + second
                picked = jnp.where(keep, full, 0.0).reshape(KTILE // BLK, BLK, LANES)
                to = pl.ds(pl.multiple_of(step * CHUNK + at // BLK, KTILE // BLK), KTILE // BLK)
                result_ref[to, :] = jnp.sum(picked, axis=1)

            return [functools.partial(part, at) for at in range(0, CHUNK * BLK, KTILE)]

        def two_chunks(pair, carry):
            step = 2 * pair
            beside = store_products(jnp.maximum(step - 1, 0), high_b, low_b)
            carry = recur(step, carry, high_a, low_a, beside)
            beside = store_products(step, high_a, low_a)
            return recur(step + 1, carry, high_b, low_b, beside)

        high_b[...] = jnp.zeros_like(high_b)
        low_b[...] = jnp.zeros_like(low_b)
        chunks = DEG // CHUNK
        lax.fori_loop(lowest // (2 * CHUNK), chunks // 2, two_chunks, start_state(log_start))
        for part in store_products(chunks - 1, high_b, low_b):
            part()
        turned = result_ref[...].T
        turned = turned[:ROWS] + turned[ROWS : 2 * ROWS]
        degree = lax.broadcasted_iota(jnp.int32, (BLK, DEG), 1)
        for c in range(CHAN):
            part = jnp.where(degree >= orders, turned[c * BLK : (c + 1) * BLK], 0.0)
            if c // 2 == FIELDS - 1:
                part = part * inverse
            coeff_ref[c] = part
        for i in range(BLK):
            target = pl.ds(place_ref[base + block * BLK + i], 1)
            out_ref[:, target, :] = coeff_ref[:, i : i + 1, :]
        return unused

    lax.fori_loop(0, blocks, one_block, 0)


def base_trig(order, first):
    lane = lax.broadcasted_iota(jnp.int32, order.shape, 1) + first
    phase = (order * lane) & (NLON - 1)
    quarter = (phase + NLON // 8) >> 9
    rest = (phase - quarter * (NLON // 4)).astype(F32) * (2.0 * math.pi / NLON)
    square = rest * rest
    sine = 1.0 / 362880.0
    for coef in (-1.0 / 5040.0, 1.0 / 120.0, -1.0 / 6.0, 1.0):
        sine = sine * square + coef
    sine = sine * rest
    cosine = 1.0 / 40320.0
    for coef in (-1.0 / 720.0, 1.0 / 24.0, -0.5, 1.0):
        cosine = cosine * square + coef
    swap = (quarter & 1) == 1
    cos_out = jnp.where(swap, sine, cosine)
    sin_out = jnp.where(swap, cosine, sine)
    cos_out = jnp.where(((quarter + 1) & 2) == 2, -cos_out, cos_out)
    sin_out = jnp.where((quarter & 2) == 2, -sin_out, sin_out)
    return cos_out, sin_out


def grid_kernel(
    dims, *refs,
):
    bands, row_count, modes, pieces, tiles, slots = dims
    data_refs = refs[:pieces]
    orders_ref, rate_ref, sine_ref = refs[pieces : pieces + 3]
    out_refs = refs[pieces + 3 : 2 * pieces + 3]
    (lhs_ref, cos_ref, sin_ref, turn_cos, turn_sin, high_ref, low_ref, weight_ref, acc_ref) = refs[
        2 * pieces + 3 :
    ]
    piece_modes = modes // pieces
    piece_slots = bands * piece_modes
    group = FIELDS * row_count
    padded = weight_ref.shape[0] // 2

    for p in range(pieces):
        columns = []
        for t in range(tiles):
            part = data_refs[p][:, t * piece_modes : (t + 1) * piece_modes, :]
            columns.append(part.reshape(piece_slots, LANES).T)
        turned = jnp.concatenate(columns, 0)
        for kind in range(2):
            high, low = split_two(turned[kind * group : (kind + 1) * group])
            at = kind * slots + p * piece_slots
            lhs_ref[:group, at : at + piece_slots] = high
            lhs_ref[group:, at : at + piece_slots] = low

    def prepare(step, unused):
        at = pl.ds(pl.multiple_of(step * 64, 64), 64)
        order = orders_ref[at, :]
        for t in range(KTILE // LANES):
            cosine, sine = base_trig(order, t * LANES)
            cos_ref[at, t * LANES : (t + 1) * LANES] = cosine
            sin_ref[at, t * LANES : (t + 1) * LANES] = sine
        eighth = order & 7
        root = math.sqrt(0.5)
        odd = (eighth & 1) == 1
        turned_cos = jnp.where(odd, root, jnp.where((eighth & 2) == 0, 1.0, 0.0))
        turned_sin = jnp.where(odd, root, jnp.where((eighth & 2) == 2, 1.0, 0.0))
        turn_cos[at, :] = jnp.where((eighth >= 3) & (eighth <= 5), -turned_cos, turned_cos)
        turn_sin[at, :] = jnp.where(eighth > 4, -turned_sin, turned_sin)
        return unused

    lax.fori_loop(0, slots // 64, prepare, 0)
    acc_ref[...] = jnp.zeros_like(acc_ref)
    weight_ref[...] = jnp.zeros_like(weight_ref)
    flux_scale = math.pi / (2.0 * NLAT * NLON * DEG)

    def one_tile(step, total):
        for s in range(0, slots, 64):
            rows_at = slice(s, s + 64)
            more_cos = jnp.tile(turn_cos[rows_at, :], (1, KTILE // LANES))
            more_sin = jnp.tile(turn_sin[rows_at, :], (1, KTILE // LANES))
            cosine, sine = cos_ref[rows_at, :], sin_ref[rows_at, :]
            cos_ref[rows_at, :] = cosine * more_cos - sine * more_sin
            sin_ref[rows_at, :] = sine * more_cos + cosine * more_sin
            high, low = split_two(cosine)
            high_ref[rows_at, :], low_ref[rows_at, :] = high, low
            high, low = split_two(sine)
            high_ref[slots + s : slots + s + 64, :] = high
            low_ref[slots + s : slots + s + 64, :] = low
        first = dot(lhs_ref[...], high_ref[...])
        second = dot(lhs_ref[:group, :], low_ref[...])
        fields = first[:group] + first[group:] + second
        weight = jnp.tile(sine_ref[...], (1, KTILE // LANES))
        columns = pl.ds(pl.multiple_of(step * KTILE, KTILE), KTILE)
        weighted_rate = rate_ref[:, columns] * weight
        scaled = fields[:row_count] * (weight * flux_scale)
        values = jnp.concatenate(
            [
                fields[row_count : 2 * row_count] * scaled,
                fields[2 * row_count :] * scaled,
                weighted_rate * fields[:row_count],
            ],
            0,
        )
        high, low = split_two(values)
        weight_ref[:group, :] = high
        weight_ref[padded : padded + group, :] = low
        first = dot(high_ref[...], weight_ref[...], 1)
        second = dot(low_ref[...], weight_ref[:padded, :], 1)
        acc_ref[...] += first[:, :padded] + first[:, padded:] + second
        return total + jnp.sum(weighted_rate.reshape(row_count // 8, 8, KTILE), axis=0)

    total = lax.fori_loop(0, NLON // KTILE, one_tile, jnp.zeros((8, KTILE), F32))
    out_refs[0][:, tiles * piece_modes :, :] = jnp.broadcast_to(jnp.sum(total), (bands, 8, LANES))
    for p in range(pieces):
        at = p * piece_slots
        joined = [
            acc_ref[at : at + piece_slots, :group],
            acc_ref[slots + at : slots + at + piece_slots, :group],
        ]
        if 2 * group < tiles * LANES:
            joined.append(jnp.zeros((piece_slots, tiles * LANES - 2 * group), F32))
        joined = jnp.concatenate(joined, 1)
        for t in range(tiles):
            part = joined[:, t * LANES : (t + 1) * LANES]
            out_refs[p][:, t * piece_modes : (t + 1) * piece_modes, :] = part.reshape(
                bands, piece_modes, LANES
            )


VMEM = pl.BlockSpec(memory_space=pltpu.VMEM)
SMEM = pl.BlockSpec(memory_space=pltpu.SMEM)
PIECES = 1


def per_device(spectrum, capture_rate, row_latitude, slot_wavenumber):
    bands = lax.axis_size("band")
    modes = spectrum.shape[3]
    row_count = capture_rate.shape[1]
    slots = slot_wavenumber.shape[0]
    blocks = modes // BLK
    pieces = min(PIECES, blocks)
    per_piece = blocks // pieces
    tiles = -(-CHAN * row_count // LANES)
    band_index = lax.axis_index("band")
    table = slot_wavenumber.reshape(bands, modes)
    rank = jnp.sum((table[:, None, :] < table[:, :, None]).astype(jnp.int32), 2)
    match = rank[:, None, :] == jnp.arange(modes, dtype=jnp.int32)[None, :, None]
    ordered = jnp.sum(jnp.where(match, table[:, None, :], 0), 2).reshape(slots)
    place_row = jnp.arange(modes, dtype=jnp.int32)[None, None, :]
    places = jnp.sum(jnp.where(match, place_row, 0), 2).reshape(slots)
    rows = jnp.asarray(latitude_rows())
    spread = jnp.asarray(spread_matrix())
    latitude = row_latitude.reshape(1, NLAT)
    coeffs = spectrum.reshape(CHAN, modes, DEG)
    params = pltpu.CompilerParams(vmem_limit_bytes=40 * 2**20)
    cost = pl.CostEstimate(
        flops=6 * 10**9 * per_piece, bytes_accessed=2**20, transcendentals=0
    )
    chunk_rows = tiles * per_piece * BLK

    def synth(p):
        dims = (bands, row_count, modes, p * per_piece, per_piece, tiles)
        return pl.pallas_call(
            lambda *refs: synth_kernel(dims, *refs),
            out_shape=jax.ShapeDtypeStruct((bands, chunk_rows, LANES), F32),
            in_specs=[SMEM, SMEM, VMEM, VMEM, VMEM, VMEM],
            out_specs=VMEM,
            scratch_shapes=[
                pltpu.VMEM((BLK, DEG), F32),
                pltpu.VMEM((BLK, DEG), F32),
                pltpu.VMEM((DEG // CHUNK, 2 * ROWS, CHUNK * BLK), BF),
                pltpu.VMEM((2, CHUNK // 2 * BLK, HALF), BF),
                pltpu.VMEM((2, CHUNK // 2 * BLK, HALF), BF),
                pltpu.VMEM((2, CHUNK // 2 * BLK, HALF), BF),
                pltpu.VMEM((2, CHUNK // 2 * BLK, HALF), BF),
                pltpu.VMEM((2, ROWS, HALF), F32),
                pltpu.VMEM((HALF, NLAT), BF),
                pltpu.VMEM((CHAN, BLK, DEG), F32),
            ],
            compiler_params=params,
            cost_estimate=cost,
            name="synth",
        )(
            ordered, places, coeffs, rows, spread, latitude,
        )

    def analyze(p, data, total):
        dims = (bands, row_count, modes, p * per_piece, per_piece, tiles)
        return pl.pallas_call(
            lambda *refs: analyze_kernel(dims, chunk_rows, *refs),
            out_shape=jax.ShapeDtypeStruct((CHAN, per_piece * BLK, DEG), F32),
            in_specs=[SMEM, SMEM, VMEM, VMEM, VMEM, VMEM],
            out_specs=VMEM,
            scratch_shapes=[
                pltpu.VMEM((BLK, DEG), F32),
                pltpu.VMEM((BLK, DEG), F32),
                pltpu.VMEM((CHUNK * BLK, HALF), BF),
                pltpu.VMEM((CHUNK * BLK, HALF), BF),
                pltpu.VMEM((CHUNK * BLK, HALF), BF),
                pltpu.VMEM((CHUNK * BLK, HALF), BF),
                pltpu.VMEM((HALF, 2 * LANES), BF),
                pltpu.VMEM((DEG, LANES), F32),
                pltpu.VMEM((HALF, NLAT), BF),
                pltpu.VMEM((CHAN, BLK, DEG), F32),
            ],
            compiler_params=params,
            cost_estimate=cost,
            name="analyze",
        )(ordered, places, data, total, rows, latitude)

    def exchange(value):
        return lax.all_to_all(value, "band", split_axis=0, concat_axis=0, tiled=True)

    received = [exchange(synth(p)) for p in range(pieces)]

    my_latitudes = lax.dynamic_slice_in_dim(row_latitude, band_index * row_count, row_count)
    row_sine = jnp.sin(jnp.pi * (my_latitudes.astype(F32) + 0.5) / NLAT)
    row_sine = jnp.broadcast_to(row_sine[:, None], (row_count, LANES))
    orders = ordered.reshape(bands, pieces, per_piece * BLK).transpose(1, 0, 2)
    orders = jnp.broadcast_to(orders.reshape(slots, 1), (slots, LANES))
    group = FIELDS * row_count
    padded = -(-group // LANES) * LANES
    dims = (bands, row_count, modes, pieces, tiles, slots)
    outs = pl.pallas_call(
        lambda *refs: grid_kernel(dims, *refs),
        out_shape=[
            jax.ShapeDtypeStruct((bands, chunk_rows + (8 if p == 0 else 0), LANES), F32)
            for p in range(pieces)
        ],
        in_specs=[VMEM] * (pieces + 3),
        out_specs=[VMEM] * pieces,
        scratch_shapes=[
            pltpu.VMEM((2 * group, 2 * slots), BF),
            pltpu.VMEM((slots, KTILE), F32),
            pltpu.VMEM((slots, KTILE), F32),
            pltpu.VMEM((slots, LANES), F32),
            pltpu.VMEM((slots, LANES), F32),
            pltpu.VMEM((2 * slots, KTILE), BF),
            pltpu.VMEM((2 * slots, KTILE), BF),
            pltpu.VMEM((2 * padded, KTILE), BF),
            pltpu.VMEM((2 * slots, padded), F32),
        ],
        compiler_params=params,
        name="grid",
    )(*received, orders, capture_rate.reshape(row_count, NLON), row_sine)
    returned = [exchange(out) for out in outs]
    parts = [analyze(p, returned[p], returned[0]) for p in range(pieces)]
    result = parts[0] if pieces == 1 else jnp.concatenate(parts, 1)
    return result.reshape(1, FIELDS, 2, modes, DEG)


def solution(mesh):
    return jax.shard_map(
        per_device,
        mesh=mesh,
        in_specs=(P("shell", None, None, "band", None), P("shell", "band", None), P(), P()),
        out_specs=P("shell", None, None, "band", None),
        check_vma=False,
    )
```

```python
import functools
import math

import jax
import jax.numpy as jnp
import numpy as np
from jax import lax
from jax.experimental import pallas as pl
from jax.experimental.pallas import tpu as pltpu
from jax.sharding import PartitionSpec as P

DEG = 512
NLAT = 1024
NLON = 2048
FIELDS = 3
HALF = NLAT // 2
CHAN = 2 * FIELDS
BLK = 8
ROWS = CHAN * BLK
CHUNK = 64
LANES = 128
KTILE = 256
BF = jnp.bfloat16
F32 = jnp.float32


def split_two(value):
    high = value.astype(BF)
    low = (value - high.astype(F32)).astype(BF)
    return high, low


def dot(lhs, rhs, contract_rhs=0):
    return lax.dot_general(
        lhs, rhs, (((1,), (contract_rhs,)), ((), ())), preferred_element_type=F32
    )


def latitude_rows():
    theta = np.pi * (np.arange(HALF) + 0.5) / NLAT
    index = np.arange(DEG, dtype=np.float64)
    log_terms = np.zeros(DEG)
    log_terms[1:] = 0.5 * np.log2((2.0 * index[1:] + 1.0) / (2.0 * index[1:]))
    rows = np.zeros((8, DEG))
    rows[0], rows[1], rows[2] = np.cos(theta), np.log2(np.sin(theta)), log_terms
    return rows.astype(np.float32)


def spread_matrix():
    spread = np.zeros((LANES, 2, 2, CHUNK // 2, BLK), np.float32)
    for half in range(2):
        for parity in range(2):
            for step in range(CHUNK // 2):
                spread[half * CHUNK + 2 * step + parity, half, parity, step, :] = 1.0
    return spread.reshape(LANES, 2 * 2 * (CHUNK // 2) * BLK).astype(BF)


def block_orders(slots_ref, first):
    sublane = lax.broadcasted_iota(jnp.int32, (BLK, LANES), 0)
    orders = jnp.zeros((BLK, LANES), jnp.int32)
    lowest = jnp.int32(DEG)
    for i in range(BLK):
        order = slots_ref[first + i]
        orders = jnp.where(sublane == i, order, orders)
        lowest = jnp.minimum(lowest, order)
    return orders[:, :1], lowest


def recursion_tables(order, rows_ref, alpha_ref, beta_ref):
    degree = lax.broadcasted_iota(jnp.int32, (BLK, DEG), 1).astype(F32)
    order_sq = order * order
    denominator = degree * degree - order_sq
    safe = jnp.where(denominator > 0, denominator, 1.0)
    alpha = jnp.sqrt((4.0 * degree * degree - 1.0) / safe)
    back = jnp.maximum((degree - 1.0) * (degree - 1.0) - order_sq, 0.0)
    beta = jnp.sqrt(back * (2.0 * degree + 1.0) / (safe * jnp.maximum(2.0 * degree - 3.0, 1.0)))
    alpha_ref[...] = jnp.where(degree > order, alpha, 0.0)
    beta_ref[...] = jnp.where(degree > order, beta, -1.0)
    terms = jnp.where(degree <= order, rows_ref[2:3, :], 0.0)
    norm = jnp.where(order > 0, 0.5 + jnp.sum(terms, axis=1, keepdims=True), 0.0)
    return norm + order * rows_ref[1:2, :]


def run_chunk(step, carry, cosine, alpha_ref, beta_ref, emit, beside):
    current, previous, log_scale = carry
    tile = pl.ds(pl.multiple_of(step // 2 * LANES, LANES), LANES)
    shift = (step % 2) * CHUNK
    alpha = pltpu.roll(alpha_ref[:, tile], shift, 1)
    beta = pltpu.roll(beta_ref[:, tile], shift, 1)
    scale = None
    for i in range(CHUNK):
        if i % 16 == 0:
            large = jnp.abs(current) > 2.0**60
            factor = jnp.where(large, 2.0**-60, 1.0)
            current = current * factor
            previous = previous * factor
            log_scale = jnp.where(large, log_scale + 60.0, log_scale)
            scale = jnp.exp2(jnp.maximum(log_scale, -200.0))
        newest = (alpha[:, i : i + 1] * cosine) * current - beta[:, i : i + 1] * previous
        current, previous = newest, current
        emit(i, newest * scale)
        if i % (CHUNK // len(beside)) == 1:
            beside[i // (CHUNK // len(beside))]()
    return current, previous, log_scale


def start_state(log_start):
    ones = jnp.ones((BLK, HALF), F32)
    return ones, ones, log_start


def fold_matrix(latitude_ref, fold_ref):
    latitude = latitude_ref[...]
    north = jnp.where(latitude < HALF, latitude, NLAT - 1 - latitude)
    sublane = lax.broadcasted_iota(jnp.int32, (HALF, NLAT), 0)
    fold_ref[...] = jnp.where(sublane == north, 1.0, 0.0).astype(BF)


def synth_kernel(
    dims, slots_ref, place_ref, spec_ref, rows_ref, spread_ref, latitude_ref, out_refs,
    alpha_ref, beta_ref, lhs_ref, high_a, low_a, high_b, low_b, acc_ref, fold_ref, coeff_ref,
):
    bands, row_count, modes, first_block, blocks, tiles = dims
    fold_matrix(latitude_ref, fold_ref)
    base = lax.axis_index("band") * modes + first_block * BLK
    south = latitude_ref[...] >= HALF
    spread_width = 4 * (CHUNK // 2) * BLK
    lane = lax.broadcasted_iota(jnp.int32, (2 * ROWS, spread_width), 1)
    sub = lax.broadcasted_iota(jnp.int32, (2 * ROWS, spread_width), 0)
    diagonal = (lane % BLK) == (sub % BLK)
    width = (CHUNK // 2) * BLK

    def one_block(block, unused):
        orders, lowest = block_orders(slots_ref, base + block * BLK)
        order = orders.astype(F32)
        log_start = recursion_tables(order, rows_ref, alpha_ref, beta_ref)
        for i in range(BLK):
            source = pl.ds(place_ref[base + block * BLK + i], 1)
            coeff_ref[:, i : i + 1, :] = spec_ref[:, source, :]
        degree = lax.broadcasted_iota(jnp.int32, (BLK, DEG), 1)
        coeffs = jnp.where((degree >= orders)[None], coeff_ref[...], 0.0)
        coeff_high, coeff_low = split_two(coeffs.reshape(ROWS, DEG))
        stacked = jnp.concatenate([coeff_high, coeff_low], 0)
        for t in range(DEG // LANES):
            wide = dot(stacked[:, t * LANES : (t + 1) * LANES], spread_ref[...])
            wide = jnp.where(diagonal, wide, 0.0).astype(BF)
            for half in range(2):
                lhs_ref[2 * t + half] = wide[:, half * 2 * width : (half + 1) * 2 * width]
        acc_ref[...] = jnp.zeros_like(acc_ref)
        cosine = jnp.broadcast_to(rows_ref[0:1, :], (BLK, HALF))

        def recur(step, carry, high_ref, low_ref, beside):
            held = {}

            def emit(i, value):
                if i % 4 < 2:
                    held[i] = value
                else:
                    pair = jnp.concatenate([held.pop(i - 2), value], 0)
                    high, low = split_two(pair)
                    at = (i // 4) * 2 * BLK
                    high_ref[i % 2, at : at + 2 * BLK, :] = high
                    low_ref[i % 2, at : at + 2 * BLK, :] = low

            return run_chunk(step, carry, cosine, alpha_ref, beta_ref, emit, beside)

        def add_products(step, high_ref, low_ref):
            def part(parity, columns):
                lhs = lhs_ref[step, :, parity * width : (parity + 1) * width]
                first = dot(lhs, high_ref[parity, :, columns])
                second = dot(lhs[:ROWS], low_ref[parity, :, columns])
                acc_ref[parity, :, columns] += first[:ROWS] + first[ROWS:] + second

            return [
                functools.partial(part, parity, slice(at, at + KTILE))
                for parity in range(2)
                for at in range(0, HALF, KTILE)
            ]

        def two_chunks(pair, carry):
            step = 2 * pair
            beside = add_products(jnp.maximum(step - 1, 0), high_b, low_b)
            carry = recur(step, carry, high_a, low_a, beside)
            beside = add_products(step, high_a, low_a)
            return recur(step + 1, carry, high_b, low_b, beside)

        high_b[...] = jnp.zeros_like(high_b)
        low_b[...] = jnp.zeros_like(low_b)
        chunks = DEG // CHUNK
        lax.fori_loop(lowest // (2 * CHUNK), chunks // 2, two_chunks, start_state(log_start))
        for part in add_products(chunks - 1, high_b, low_b):
            part()
        both = acc_ref[...].reshape(2 * ROWS, HALF)
        high, low = split_two(both)
        moved = dot(jnp.concatenate([high, low], 0), fold_ref[...])
        moved = moved[: 2 * ROWS] + moved[2 * ROWS :]
        sign = jnp.tile(1.0 - 2.0 * (orders % 2).astype(F32), (CHAN, 1))
        even, odd = moved[:ROWS], moved[ROWS:]
        values = jnp.where(south, sign * (even - odd), even + odd)
        for d in range(bands):
            parts = []
            for kind in range(2):
                for field in range(FIELDS):
                    c = field * 2 + kind
                    parts.append(
                        values[c * BLK : (c + 1) * BLK, d * row_count : (d + 1) * row_count]
                    )
            if CHAN * row_count < tiles * LANES:
                parts.append(jnp.zeros((BLK, tiles * LANES - CHAN * row_count), F32))
            joined = jnp.concatenate(parts, 1)
            for t in range(tiles):
                at = pl.ds(pl.multiple_of(t * blocks * BLK + block * BLK, BLK), BLK)
                out_refs[d][at, :] = joined[:, t * LANES : (t + 1) * LANES]
        return unused

    lax.fori_loop(0, blocks, one_block, 0)


def analyze_kernel(
    dims, total_row, data_refs, slots_ref, place_ref, rows_ref, latitude_ref, out_ref,
    alpha_ref, beta_ref, high_a, low_a, high_b, low_b, weight_ref, result_ref, fold_ref, coeff_ref,
):
    bands, row_count, modes, first_block, blocks, tiles = dims
    fold_matrix(latitude_ref, fold_ref)
    base = lax.axis_index("band") * modes + first_block * BLK
    south = latitude_ref[...] >= HALF
    total = data_refs[0][total_row : total_row + 8]
    for d in range(1, bands):
        total = total + data_refs[d][total_row : total_row + 8]
    inverse = (1.0 / total)[:, :1]
    lane = lax.broadcasted_iota(jnp.int32, (KTILE, LANES), 1)
    sub = lax.broadcasted_iota(jnp.int32, (KTILE, LANES), 0)
    keep = (lane % BLK == sub % BLK) & (lane // ROWS == sub // BLK % 2)

    def one_block(block, unused):
        orders, lowest = block_orders(slots_ref, base + block * BLK)
        order = orders.astype(F32)
        log_start = recursion_tables(order, rows_ref, alpha_ref, beta_ref)
        sign = 1.0 - 2.0 * (orders % 2).astype(F32)
        evens, odds = [], []
        for c in range(CHAN):
            offset = ((c % 2) * FIELDS + c // 2) * row_count
            t, at = offset // LANES, offset % LANES
            rows = pl.ds(pl.multiple_of(t * blocks * BLK + block * BLK, BLK), BLK)
            values = jnp.concatenate(
                [data_refs[d][rows, :][:, at : at + row_count] for d in range(bands)], 1
            )
            flipped = sign * values
            evens.append(jnp.where(south, flipped, values))
            odds.append(jnp.where(south, -flipped, values))
        high, low = split_two(jnp.concatenate(evens + odds, 0))
        folded = dot(jnp.concatenate([high, low], 0), fold_ref[...], 1)
        folded = folded[: 2 * ROWS] + folded[2 * ROWS :]
        padded = jnp.concatenate([folded, jnp.zeros((LANES - 2 * ROWS, HALF), F32)], 0)
        high, low = split_two(padded.T)
        weight_ref[:, :LANES] = high
        weight_ref[:, LANES:] = low
        result_ref[...] = jnp.zeros_like(result_ref)
        cosine = jnp.broadcast_to(rows_ref[0:1, :], (BLK, HALF))

        def recur(step, carry, high_ref, low_ref, beside):
            held = {}

            def emit(i, value):
                if i % 2 == 0:
                    held[i] = value
                else:
                    pair = jnp.concatenate([held.pop(i - 1), value], 0)
                    high, low = split_two(pair)
                    at = (i // 2) * 2 * BLK
                    high_ref[at : at + 2 * BLK, :] = high
                    low_ref[at : at + 2 * BLK, :] = low

            return run_chunk(step, carry, cosine, alpha_ref, beta_ref, emit, beside)

        def store_products(step, high_ref, low_ref):
            def part(at):
                rows = slice(at, at + KTILE)
                first = dot(high_ref[rows, :], weight_ref[...])
                second = dot(low_ref[rows, :], weight_ref[:, :LANES])
                full = first[:, :LANES] + first[:, LANES:] + second
                picked = jnp.where(keep, full, 0.0).reshape(KTILE // BLK, BLK, LANES)
                to = pl.ds(pl.multiple_of(step * CHUNK + at // BLK, KTILE // BLK), KTILE // BLK)
                result_ref[to, :] = jnp.sum(picked, axis=1)

            return [functools.partial(part, at) for at in range(0, CHUNK * BLK, KTILE)]

        def two_chunks(pair, carry):
            step = 2 * pair
            beside = store_products(jnp.maximum(step - 1, 0), high_b, low_b)
            carry = recur(step, carry, high_a, low_a, beside)
            beside = store_products(step, high_a, low_a)
            return recur(step + 1, carry, high_b, low_b, beside)

        high_b[...] = jnp.zeros_like(high_b)
        low_b[...] = jnp.zeros_like(low_b)
        chunks = DEG // CHUNK
        lax.fori_loop(lowest // (2 * CHUNK), chunks // 2, two_chunks, start_state(log_start))
        for part in store_products(chunks - 1, high_b, low_b):
            part()
        turned = result_ref[...].T
        turned = turned[:ROWS] + turned[ROWS : 2 * ROWS]
        degree = lax.broadcasted_iota(jnp.int32, (BLK, DEG), 1)
        for c in range(CHAN):
            part = jnp.where(degree >= orders, turned[c * BLK : (c + 1) * BLK], 0.0)
            if c // 2 == FIELDS - 1:
                part = part * inverse
            coeff_ref[c] = part
        for i in range(BLK):
            target = pl.ds(place_ref[base + block * BLK + i], 1)
            out_ref[:, target, :] = coeff_ref[:, i : i + 1, :]
        return unused

    lax.fori_loop(0, blocks, one_block, 0)


def base_trig(order, first):
    lane = lax.broadcasted_iota(jnp.int32, order.shape, 1) + first
    phase = (order * lane) & (NLON - 1)
    quarter = (phase + NLON // 8) >> 9
    rest = (phase - quarter * (NLON // 4)).astype(F32) * (2.0 * math.pi / NLON)
    square = rest * rest
    sine = 1.0 / 362880.0
    for coef in (-1.0 / 5040.0, 1.0 / 120.0, -1.0 / 6.0, 1.0):
        sine = sine * square + coef
    sine = sine * rest
    cosine = 1.0 / 40320.0
    for coef in (-1.0 / 720.0, 1.0 / 24.0, -0.5, 1.0):
        cosine = cosine * square + coef
    swap = (quarter & 1) == 1
    cos_out = jnp.where(swap, sine, cosine)
    sin_out = jnp.where(swap, cosine, sine)
    cos_out = jnp.where(((quarter + 1) & 2) == 2, -cos_out, cos_out)
    sin_out = jnp.where((quarter & 2) == 2, -sin_out, sin_out)
    return cos_out, sin_out


def grid_kernel(
    dims, *refs,
):
    bands, row_count, modes, tiles, slots = dims
    data_refs = refs[:bands]
    orders_ref, rate_ref, sine_ref = refs[bands : bands + 3]
    out_refs = refs[bands + 3 : 2 * bands + 3]
    (lhs_ref, cos_ref, sin_ref, turn_cos, turn_sin, high_ref, low_ref, weight_ref, acc_ref) = refs[
        2 * bands + 3 :
    ]
    group = FIELDS * row_count
    padded = weight_ref.shape[0] // 2

    columns = []
    for t in range(tiles):
        part = [data_refs[d][t * modes : (t + 1) * modes, :] for d in range(bands)]
        columns.append(jnp.concatenate(part, 0).T)
    turned = jnp.concatenate(columns, 0)
    for kind in range(2):
        high, low = split_two(turned[kind * group : (kind + 1) * group])
        lhs_ref[:group, kind * slots : (kind + 1) * slots] = high
        lhs_ref[group:, kind * slots : (kind + 1) * slots] = low

    def prepare(step, unused):
        at = pl.ds(pl.multiple_of(step * 64, 64), 64)
        order = orders_ref[at, :]
        for t in range(KTILE // LANES):
            cosine, sine = base_trig(order, t * LANES)
            cos_ref[at, t * LANES : (t + 1) * LANES] = cosine
            sin_ref[at, t * LANES : (t + 1) * LANES] = sine
        eighth = order & 7
        root = math.sqrt(0.5)
        odd = (eighth & 1) == 1
        turned_cos = jnp.where(odd, root, jnp.where((eighth & 2) == 0, 1.0, 0.0))
        turned_sin = jnp.where(odd, root, jnp.where((eighth & 2) == 2, 1.0, 0.0))
        turn_cos[at, :] = jnp.where((eighth >= 3) & (eighth <= 5), -turned_cos, turned_cos)
        turn_sin[at, :] = jnp.where(eighth > 4, -turned_sin, turned_sin)
        return unused

    lax.fori_loop(0, slots // 64, prepare, 0)
    acc_ref[...] = jnp.zeros_like(acc_ref)
    weight_ref[...] = jnp.zeros_like(weight_ref)
    flux_scale = math.pi / (2.0 * NLAT * NLON * DEG)

    def one_tile(step, total):
        for s in range(0, slots, 64):
            rows_at = slice(s, s + 64)
            more_cos = jnp.tile(turn_cos[rows_at, :], (1, KTILE // LANES))
            more_sin = jnp.tile(turn_sin[rows_at, :], (1, KTILE // LANES))
            cosine, sine = cos_ref[rows_at, :], sin_ref[rows_at, :]
            cos_ref[rows_at, :] = cosine * more_cos - sine * more_sin
            sin_ref[rows_at, :] = sine * more_cos + cosine * more_sin
            high, low = split_two(cosine)
            high_ref[rows_at, :], low_ref[rows_at, :] = high, low
            high, low = split_two(sine)
            high_ref[slots + s : slots + s + 64, :] = high
            low_ref[slots + s : slots + s + 64, :] = low
        first = dot(lhs_ref[...], high_ref[...])
        second = dot(lhs_ref[:group, :], low_ref[...])
        fields = first[:group] + first[group:] + second
        weight = jnp.tile(sine_ref[...], (1, KTILE // LANES))
        columns = pl.ds(pl.multiple_of(step * KTILE, KTILE), KTILE)
        weighted_rate = rate_ref[:, columns] * weight
        scaled = fields[:row_count] * (weight * flux_scale)
        values = jnp.concatenate(
            [
                fields[row_count : 2 * row_count] * scaled,
                fields[2 * row_count :] * scaled,
                weighted_rate * fields[:row_count],
            ],
            0,
        )
        high, low = split_two(values)
        weight_ref[:group, :] = high
        weight_ref[padded : padded + group, :] = low
        first = dot(high_ref[...], weight_ref[...], 1)
        second = dot(low_ref[...], weight_ref[:padded, :], 1)
        acc_ref[...] += first[:, :padded] + first[:, padded:] + second
        return total + jnp.sum(weighted_rate.reshape(row_count // 8, 8, KTILE), axis=0)

    total = lax.fori_loop(0, NLON // KTILE, one_tile, jnp.zeros((8, KTILE), F32))
    total = jnp.broadcast_to(jnp.sum(total), (8, LANES))
    joined = [acc_ref[:slots, :group], acc_ref[slots:, :group]]
    if 2 * group < tiles * LANES:
        joined.append(jnp.zeros((slots, tiles * LANES - 2 * group), F32))
    joined = jnp.concatenate(joined, 1)
    for d in range(bands):
        for t in range(tiles):
            part = joined[d * modes : (d + 1) * modes, t * LANES : (t + 1) * LANES]
            out_refs[d][t * modes : (t + 1) * modes, :] = part
        out_refs[d][tiles * modes :, :] = total


VMEM = pl.BlockSpec(memory_space=pltpu.VMEM)
SMEM = pl.BlockSpec(memory_space=pltpu.SMEM)


def per_device(spectrum, capture_rate, row_latitude, slot_wavenumber):
    bands = lax.axis_size("band")
    modes = spectrum.shape[3]
    row_count = capture_rate.shape[1]
    slots = slot_wavenumber.shape[0]
    blocks = modes // BLK
    per_piece = blocks
    tiles = -(-CHAN * row_count // LANES)
    band_index = lax.axis_index("band")
    table = slot_wavenumber.reshape(bands, modes)
    rank = jnp.sum((table[:, None, :] < table[:, :, None]).astype(jnp.int32), 2)
    match = rank[:, None, :] == jnp.arange(modes, dtype=jnp.int32)[None, :, None]
    ordered = jnp.sum(jnp.where(match, table[:, None, :], 0), 2).reshape(slots)
    place_row = jnp.arange(modes, dtype=jnp.int32)[None, None, :]
    places = jnp.sum(jnp.where(match, place_row, 0), 2).reshape(slots)
    rows = jnp.asarray(latitude_rows())
    spread = jnp.asarray(spread_matrix())

    def partner_rows(table):
        partner = band_index ^ jnp.arange(bands, dtype=jnp.int32)
        chosen = partner[:, None] == jnp.arange(bands, dtype=jnp.int32)[None, :]
        return jnp.sum(jnp.where(chosen[:, :, None], table[None], 0), 1)

    latitude = partner_rows(row_latitude.reshape(bands, row_count)).reshape(1, NLAT)
    coeffs = spectrum.reshape(CHAN, modes, DEG)
    params = pltpu.CompilerParams(vmem_limit_bytes=40 * 2**20)
    cost = pl.CostEstimate(
        flops=6 * 10**9 * per_piece, bytes_accessed=2**20, transcendentals=0
    )
    chunk_rows = tiles * per_piece * BLK

    def synth(p):
        dims = (bands, row_count, modes, p * per_piece, per_piece, tiles)
        return pl.pallas_call(
            lambda *refs: synth_kernel(dims, *refs[:6], refs[6 : 6 + bands], *refs[6 + bands :]),
            out_shape=[jax.ShapeDtypeStruct((chunk_rows, LANES), F32)] * bands,
            in_specs=[SMEM, SMEM, VMEM, VMEM, VMEM, VMEM],
            out_specs=[VMEM] * bands,
            scratch_shapes=[
                pltpu.VMEM((BLK, DEG), F32),
                pltpu.VMEM((BLK, DEG), F32),
                pltpu.VMEM((DEG // CHUNK, 2 * ROWS, CHUNK * BLK), BF),
                pltpu.VMEM((2, CHUNK // 2 * BLK, HALF), BF),
                pltpu.VMEM((2, CHUNK // 2 * BLK, HALF), BF),
                pltpu.VMEM((2, CHUNK // 2 * BLK, HALF), BF),
                pltpu.VMEM((2, CHUNK // 2 * BLK, HALF), BF),
                pltpu.VMEM((2, ROWS, HALF), F32),
                pltpu.VMEM((HALF, NLAT), BF),
                pltpu.VMEM((CHAN, BLK, DEG), F32),
            ],
            compiler_params=params,
            cost_estimate=cost,
            name="synth",
        )(
            ordered, places, coeffs, rows, spread, latitude,
        )

    def analyze(p, data):
        dims = (bands, row_count, modes, p * per_piece, per_piece, tiles)
        return pl.pallas_call(
            lambda *refs: analyze_kernel(dims, chunk_rows, refs[:bands], *refs[bands:]),
            out_shape=jax.ShapeDtypeStruct((CHAN, per_piece * BLK, DEG), F32),
            in_specs=[VMEM] * bands + [SMEM, SMEM, VMEM, VMEM],
            out_specs=VMEM,
            scratch_shapes=[
                pltpu.VMEM((BLK, DEG), F32),
                pltpu.VMEM((BLK, DEG), F32),
                pltpu.VMEM((CHUNK * BLK, HALF), BF),
                pltpu.VMEM((CHUNK * BLK, HALF), BF),
                pltpu.VMEM((CHUNK * BLK, HALF), BF),
                pltpu.VMEM((CHUNK * BLK, HALF), BF),
                pltpu.VMEM((HALF, 2 * LANES), BF),
                pltpu.VMEM((DEG, LANES), F32),
                pltpu.VMEM((HALF, NLAT), BF),
                pltpu.VMEM((CHAN, BLK, DEG), F32),
            ],
            compiler_params=params,
            cost_estimate=cost,
            name="analyze",
        )(*data, ordered, places, rows, latitude)

    def exchange(chunks):
        received = [chunks[0]]
        for k in range(1, bands):
            pairs = [(i, i ^ k) for i in range(bands)]
            received.append(lax.ppermute(chunks[k], "band", pairs))
        return received

    received = exchange(synth(0))

    my_latitudes = lax.dynamic_slice_in_dim(row_latitude, band_index * row_count, row_count)
    row_sine = jnp.sin(jnp.pi * (my_latitudes.astype(F32) + 0.5) / NLAT)
    row_sine = jnp.broadcast_to(row_sine[:, None], (row_count, LANES))
    orders = partner_rows(ordered.reshape(bands, modes)).reshape(slots, 1)
    orders = jnp.broadcast_to(orders, (slots, LANES))
    group = FIELDS * row_count
    padded = -(-group // LANES) * LANES
    dims = (bands, row_count, modes, tiles, slots)
    outs = pl.pallas_call(
        lambda *refs: grid_kernel(dims, *refs),
        out_shape=[jax.ShapeDtypeStruct((chunk_rows + 8, LANES), F32)] * bands,
        in_specs=[VMEM] * (bands + 3),
        out_specs=[VMEM] * bands,
        scratch_shapes=[
            pltpu.VMEM((2 * group, 2 * slots), BF),
            pltpu.VMEM((slots, KTILE), F32),
            pltpu.VMEM((slots, KTILE), F32),
            pltpu.VMEM((slots, LANES), F32),
            pltpu.VMEM((slots, LANES), F32),
            pltpu.VMEM((2 * slots, KTILE), BF),
            pltpu.VMEM((2 * slots, KTILE), BF),
            pltpu.VMEM((2 * padded, KTILE), BF),
            pltpu.VMEM((2 * slots, padded), F32),
        ],
        compiler_params=params,
        name="grid",
    )(*received, orders, capture_rate.reshape(row_count, NLON), row_sine)
    result = analyze(0, exchange(outs))
    return result.reshape(1, FIELDS, 2, modes, DEG)


def solution(mesh):
    return jax.shard_map(
        per_device,
        mesh=mesh,
        in_specs=(P("shell", None, None, "band", None), P("shell", "band", None), P(), P()),
        out_specs=P("shell", None, None, "band", None),
        check_vma=False,
    )
```

```python
import functools
import math

import jax
import jax.numpy as jnp
import numpy as np
from jax import lax
from jax.experimental import pallas as pl
from jax.experimental.pallas import tpu as pltpu
from jax.sharding import PartitionSpec as P

DEG = 512
NLAT = 1024
NLON = 2048
FIELDS = 3
HALF = NLAT // 2
CHAN = 2 * FIELDS
BLK = 8
ROWS = CHAN * BLK
CHUNK = 64
LANES = 128
KTILE = 256
BF = jnp.bfloat16
F32 = jnp.float32


def split_two(value):
    high = value.astype(BF)
    low = (value - high.astype(F32)).astype(BF)
    return high, low


def dot(lhs, rhs, contract_rhs=0):
    return lax.dot_general(
        lhs, rhs, (((1,), (contract_rhs,)), ((), ())), preferred_element_type=F32
    )


def latitude_rows():
    theta = np.pi * (np.arange(HALF) + 0.5) / NLAT
    index = np.arange(DEG, dtype=np.float64)
    log_terms = np.zeros(DEG)
    log_terms[1:] = 0.5 * np.log2((2.0 * index[1:] + 1.0) / (2.0 * index[1:]))
    rows = np.zeros((8, DEG))
    rows[0], rows[1], rows[2] = np.cos(theta), np.log2(np.sin(theta)), log_terms
    return rows.astype(np.float32)


def spread_matrix():
    spread = np.zeros((LANES, 2, 2, CHUNK // 2, BLK), np.float32)
    for half in range(2):
        for parity in range(2):
            for step in range(CHUNK // 2):
                spread[half * CHUNK + 2 * step + parity, half, parity, step, :] = 1.0
    return spread.reshape(LANES, 2 * 2 * (CHUNK // 2) * BLK).astype(BF)


def block_orders(slots_ref, first):
    sublane = lax.broadcasted_iota(jnp.int32, (BLK, LANES), 0)
    orders = jnp.zeros((BLK, LANES), jnp.int32)
    lowest = jnp.int32(DEG)
    for i in range(BLK):
        order = slots_ref[first + i]
        orders = jnp.where(sublane == i, order, orders)
        lowest = jnp.minimum(lowest, order)
    return orders[:, :1], lowest


def recursion_tables(order, rows_ref, alpha_ref, beta_ref):
    degree = lax.broadcasted_iota(jnp.int32, (BLK, DEG), 1).astype(F32)
    order_sq = order * order
    denominator = degree * degree - order_sq
    safe = jnp.where(denominator > 0, denominator, 1.0)
    alpha = jnp.sqrt((4.0 * degree * degree - 1.0) / safe)
    back = jnp.maximum((degree - 1.0) * (degree - 1.0) - order_sq, 0.0)
    beta = jnp.sqrt(back * (2.0 * degree + 1.0) / (safe * jnp.maximum(2.0 * degree - 3.0, 1.0)))
    alpha_ref[...] = jnp.where(degree > order, alpha, 0.0)
    beta_ref[...] = jnp.where(degree > order, beta, -1.0)
    terms = jnp.where(degree <= order, rows_ref[2:3, :], 0.0)
    norm = jnp.where(order > 0, 0.5 + jnp.sum(terms, axis=1, keepdims=True), 0.0)
    return norm + order * rows_ref[1:2, :]


def run_chunk(step, carry, cosine, alpha_ref, beta_ref, emit, beside):
    current, previous, log_scale = carry
    tile = pl.ds(pl.multiple_of(step // 2 * LANES, LANES), LANES)
    shift = (step % 2) * CHUNK
    alpha = pltpu.roll(alpha_ref[:, tile], shift, 1)
    beta = pltpu.roll(beta_ref[:, tile], shift, 1)
    scale = None
    for i in range(CHUNK):
        if i % 16 == 0:
            large = jnp.abs(current) > 2.0**60
            factor = jnp.where(large, 2.0**-60, 1.0)
            current = current * factor
            previous = previous * factor
            log_scale = jnp.where(large, log_scale + 60.0, log_scale)
            scale = jnp.exp2(jnp.maximum(log_scale, -200.0))
        newest = (alpha[:, i : i + 1] * cosine) * current - beta[:, i : i + 1] * previous
        current, previous = newest, current
        emit(i, newest * scale)
        if beside and i % (CHUNK // len(beside)) == 1:
            beside[i // (CHUNK // len(beside))]()
    return current, previous, log_scale


def start_state(log_start):
    ones = jnp.ones((BLK, HALF), F32)
    return ones, ones, log_start


def fold_matrix(latitude_ref, fold_ref):
    latitude = latitude_ref[...]
    north = jnp.where(latitude < HALF, latitude, NLAT - 1 - latitude)
    sublane = lax.broadcasted_iota(jnp.int32, (HALF, NLAT), 0)
    fold_ref[...] = jnp.where(sublane == north, 1.0, 0.0).astype(BF)


def synth_kernel(
    dims, slots_ref, place_ref, spec_ref, rows_ref, spread_ref, latitude_ref, out_ref,
    alpha_ref, beta_ref, lhs_ref, high_a, low_a, high_b, low_b, acc_ref, fold_ref, coeff_ref,
):
    bands, row_count, modes, blocks, tiles = dims
    fold_matrix(latitude_ref, fold_ref)
    base = lax.axis_index("band") * modes
    south = latitude_ref[...] >= HALF
    spread_width = 4 * (CHUNK // 2) * BLK
    lane = lax.broadcasted_iota(jnp.int32, (2 * ROWS, spread_width), 1)
    sub = lax.broadcasted_iota(jnp.int32, (2 * ROWS, spread_width), 0)
    diagonal = (lane % BLK) == (sub % BLK)
    width = (CHUNK // 2) * BLK

    def one_block(block, unused):
        orders, lowest = block_orders(slots_ref, base + block * BLK)
        order = orders.astype(F32)
        log_start = recursion_tables(order, rows_ref, alpha_ref, beta_ref)
        for i in range(BLK):
            source = pl.ds(place_ref[base + block * BLK + i], 1)
            coeff_ref[:, i : i + 1, :] = spec_ref[:, source, :]
        degree = lax.broadcasted_iota(jnp.int32, (BLK, DEG), 1)
        coeffs = jnp.where((degree >= orders)[None], coeff_ref[...], 0.0)
        coeff_high, coeff_low = split_two(coeffs.reshape(ROWS, DEG))
        stacked = jnp.concatenate([coeff_high, coeff_low], 0)
        for t in range(DEG // LANES):
            wide = dot(stacked[:, t * LANES : (t + 1) * LANES], spread_ref[...])
            wide = jnp.where(diagonal, wide, 0.0).astype(BF)
            for half in range(2):
                lhs_ref[2 * t + half] = wide[:, half * 2 * width : (half + 1) * 2 * width]
        acc_ref[...] = jnp.zeros_like(acc_ref)
        cosine = jnp.broadcast_to(rows_ref[0:1, :], (BLK, HALF))

        def recur(step, carry, high_ref, low_ref, beside):
            held = {}

            def emit(i, value):
                if i % 4 < 2:
                    held[i] = value
                else:
                    pair = jnp.concatenate([held.pop(i - 2), value], 0)
                    high, low = split_two(pair)
                    at = (i // 4) * 2 * BLK
                    high_ref[i % 2, at : at + 2 * BLK, :] = high
                    low_ref[i % 2, at : at + 2 * BLK, :] = low

            return run_chunk(step, carry, cosine, alpha_ref, beta_ref, emit, beside)

        def add_products(step, high_ref, low_ref):
            def part(parity, columns):
                lhs = lhs_ref[step, :, parity * width : (parity + 1) * width]
                first = dot(lhs, high_ref[parity, :, columns])
                second = dot(lhs[:ROWS], low_ref[parity, :, columns])
                acc_ref[parity, :, columns] += first[:ROWS] + first[ROWS:] + second

            return [
                functools.partial(part, parity, slice(at, at + KTILE))
                for parity in range(2)
                for at in range(0, HALF, KTILE)
            ]

        def two_chunks(pair, carry):
            step = 2 * pair
            beside = add_products(jnp.maximum(step - 1, 0), high_b, low_b)
            carry = recur(step, carry, high_a, low_a, beside)
            beside = add_products(step, high_a, low_a)
            return recur(step + 1, carry, high_b, low_b, beside)

        high_b[...] = jnp.zeros_like(high_b)
        low_b[...] = jnp.zeros_like(low_b)
        chunks = DEG // CHUNK
        lax.fori_loop(lowest // (2 * CHUNK), chunks // 2, two_chunks, start_state(log_start))
        for part in add_products(chunks - 1, high_b, low_b):
            part()
        both = acc_ref[...].reshape(2 * ROWS, HALF)
        high, low = split_two(both)
        moved = dot(jnp.concatenate([high, low], 0), fold_ref[...])
        moved = moved[: 2 * ROWS] + moved[2 * ROWS :]
        sign = jnp.tile(1.0 - 2.0 * (orders % 2).astype(F32), (CHAN, 1))
        even, odd = moved[:ROWS], moved[ROWS:]
        values = jnp.where(south, sign * (even - odd), even + odd)
        for d in range(bands):
            parts = []
            for kind in range(2):
                for field in range(FIELDS):
                    c = field * 2 + kind
                    parts.append(
                        values[c * BLK : (c + 1) * BLK, d * row_count : (d + 1) * row_count]
                    )
            if CHAN * row_count < tiles * LANES:
                parts.append(jnp.zeros((BLK, tiles * LANES - CHAN * row_count), F32))
            joined = jnp.concatenate(parts, 1)
            for t in range(tiles):
                at = pl.ds(pl.multiple_of(t * blocks * BLK + block * BLK, BLK), BLK)
                out_ref[d, at, :] = joined[:, t * LANES : (t + 1) * LANES]
        return unused

    lax.fori_loop(0, blocks, one_block, 0)


def table_kernel(
    dims, slots_ref, rows_ref, out_ref, alpha_ref, beta_ref, first_ref, second_ref, sems,
):
    modes, blocks = dims
    base = lax.axis_index("band") * modes
    cosine = jnp.broadcast_to(rows_ref[0:1, :], (BLK, HALF))
    buffers = (first_ref, second_ref)

    def copy_out(which, block, step):
        return pltpu.make_async_copy(buffers[which], out_ref.at[block, step], sems.at[which])

    def one_block(block, unused):
        orders, lowest = block_orders(slots_ref, base + block * BLK)
        log_start = recursion_tables(orders.astype(F32), rows_ref, alpha_ref, beta_ref)
        start = lowest // (2 * CHUNK)

        def recur(which, step, carry, pending):
            buffer = buffers[which]

            @pl.when(pending)
            def _():
                copy_out(which, block, step).wait()

            held = {}

            def emit(i, value):
                if i % 2 == 0:
                    held[i] = value
                else:
                    pair = jnp.concatenate([held.pop(i - 1), value], 0)
                    high, low = split_two(pair)
                    at = (i // 2) * 2 * BLK
                    buffer[at : at + 2 * BLK, :] = high
                    buffer[CHUNK * BLK + at : CHUNK * BLK + at + 2 * BLK, :] = low

            carry = run_chunk(step, carry, cosine, alpha_ref, beta_ref, emit, ())
            copy_out(which, block, step).start()
            return carry

        def two_chunks(pair, carry):
            pending = (block > 0) | (pair > start)
            carry = recur(0, 2 * pair, carry, pending)
            return recur(1, 2 * pair + 1, carry, pending)

        lax.fori_loop(start, DEG // CHUNK // 2, two_chunks, start_state(log_start))
        return unused

    lax.fori_loop(0, blocks, one_block, 0)
    copy_out(0, 0, 0).wait()
    copy_out(1, 0, 0).wait()


def analyze_kernel(
    dims, total_row, slots_ref, place_ref, data_ref, latitude_ref, table_ref, out_ref,
    chunk_ref, weight_ref, result_ref, fold_ref, coeff_ref, sems,
):
    bands, row_count, modes, blocks, tiles = dims
    base = lax.axis_index("band") * modes
    chunks = DEG // CHUNK

    def copy_in(block, step):
        return pltpu.make_async_copy(
            table_ref.at[block, step], chunk_ref.at[block, step], sems.at[block, step]
        )

    def start_block(block, unused):
        orders, lowest = block_orders(slots_ref, base + block * BLK)

        def start_chunk(step, inner):
            copy_in(block, step).start()
            return inner

        return lax.fori_loop(lowest // (2 * CHUNK) * 2, chunks, start_chunk, unused)

    lax.fori_loop(0, blocks, start_block, 0)
    fold_matrix(latitude_ref, fold_ref)
    south = latitude_ref[...] >= HALF
    total = data_ref[0, total_row : total_row + 8]
    for d in range(1, bands):
        total = total + data_ref[d, total_row : total_row + 8]
    inverse = (1.0 / total)[:, :1]
    lane = lax.broadcasted_iota(jnp.int32, (CHUNK * BLK, LANES), 1)
    sub = lax.broadcasted_iota(jnp.int32, (CHUNK * BLK, LANES), 0)
    keep = (lane % BLK == sub % BLK) & (lane // ROWS == sub // BLK % 2)

    def one_block(block, unused):
        orders, lowest = block_orders(slots_ref, base + block * BLK)
        sign = 1.0 - 2.0 * (orders % 2).astype(F32)
        evens, odds = [], []
        for c in range(CHAN):
            offset = ((c % 2) * FIELDS + c // 2) * row_count
            t, at = offset // LANES, offset % LANES
            rows = pl.ds(pl.multiple_of(t * blocks * BLK + block * BLK, BLK), BLK)
            values = jnp.concatenate(
                [data_ref[d, rows, :][:, at : at + row_count] for d in range(bands)], 1
            )
            flipped = sign * values
            evens.append(jnp.where(south, flipped, values))
            odds.append(jnp.where(south, -flipped, values))
        high, low = split_two(jnp.concatenate(evens + odds, 0))
        folded = dot(jnp.concatenate([high, low], 0), fold_ref[...], 1)
        folded = folded[: 2 * ROWS] + folded[2 * ROWS :]
        padded = jnp.concatenate([folded, jnp.zeros((LANES - 2 * ROWS, HALF), F32)], 0)
        high, low = split_two(padded.T)
        weight_ref[:, :LANES] = high
        weight_ref[:, LANES:] = low
        result_ref[...] = jnp.zeros_like(result_ref)

        def one_chunk(step, inner):
            copy_in(block, step).wait()
            first = dot(chunk_ref[block, step, : CHUNK * BLK], weight_ref[...])
            second = dot(chunk_ref[block, step, CHUNK * BLK :], weight_ref[:, :LANES])
            full = first[:, :LANES] + first[:, LANES:] + second
            picked = jnp.where(keep, full, 0.0).reshape(CHUNK, BLK, LANES)
            to = pl.ds(pl.multiple_of(step * CHUNK, CHUNK), CHUNK)
            result_ref[to, :] = jnp.sum(picked, axis=1)
            return inner

        lax.fori_loop(lowest // (2 * CHUNK) * 2, chunks, one_chunk, 0)
        turned = result_ref[...].T
        turned = turned[:ROWS] + turned[ROWS : 2 * ROWS]
        degree = lax.broadcasted_iota(jnp.int32, (BLK, DEG), 1)
        for c in range(CHAN):
            part = jnp.where(degree >= orders, turned[c * BLK : (c + 1) * BLK], 0.0)
            if c // 2 == FIELDS - 1:
                part = part * inverse
            coeff_ref[c] = part
        for i in range(BLK):
            target = pl.ds(place_ref[base + block * BLK + i], 1)
            out_ref[:, target, :] = coeff_ref[:, i : i + 1, :]
        return unused

    lax.fori_loop(0, blocks, one_block, 0)


def base_trig(order, first):
    lane = lax.broadcasted_iota(jnp.int32, order.shape, 1) + first
    phase = (order * lane) & (NLON - 1)
    quarter = (phase + NLON // 8) >> 9
    rest = (phase - quarter * (NLON // 4)).astype(F32) * (2.0 * math.pi / NLON)
    square = rest * rest
    sine = 1.0 / 362880.0
    for coef in (-1.0 / 5040.0, 1.0 / 120.0, -1.0 / 6.0, 1.0):
        sine = sine * square + coef
    sine = sine * rest
    cosine = 1.0 / 40320.0
    for coef in (-1.0 / 720.0, 1.0 / 24.0, -0.5, 1.0):
        cosine = cosine * square + coef
    swap = (quarter & 1) == 1
    cos_out = jnp.where(swap, sine, cosine)
    sin_out = jnp.where(swap, cosine, sine)
    cos_out = jnp.where(((quarter + 1) & 2) == 2, -cos_out, cos_out)
    sin_out = jnp.where((quarter & 2) == 2, -sin_out, sin_out)
    return cos_out, sin_out


def trig_kernel(high_ref, low_ref, cos_ref, sin_ref):
    half = cos_ref.shape[0]
    root = math.sqrt(0.5)
    for parity in range(2):

        def strip(step, unused):
            at = pl.multiple_of(step * 64, 64)
            shape = (64, LANES)
            order = 2 * (lax.broadcasted_iota(jnp.int32, shape, 0) + at) + parity
            eighth = order & 7
            odd = (eighth & 1) == 1
            turn_cos = jnp.where(odd, root, jnp.where((eighth & 2) == 0, 1.0, 0.0))
            turn_sin = jnp.where(odd, root, jnp.where((eighth & 2) == 2, 1.0, 0.0))
            turn_cos = jnp.where((eighth >= 3) & (eighth <= 5), -turn_cos, turn_cos)
            turn_sin = jnp.where(eighth > 4, -turn_sin, turn_sin)
            for t in range(KTILE // LANES):
                cosine, sine = base_trig(order, t * LANES)
                for k in range(t * LANES, NLON // 2, KTILE):
                    columns = slice(k, k + LANES)
                    high, low = split_two(cosine)
                    high_ref[parity, pl.ds(at, 64), columns] = high
                    low_ref[parity, pl.ds(at, 64), columns] = low
                    high, low = split_two(sine)
                    high_ref[parity, pl.ds(half + at, 64), columns] = high
                    low_ref[parity, pl.ds(half + at, 64), columns] = low
                    cosine, sine = (
                        cosine * turn_cos - sine * turn_sin,
                        sine * turn_cos + cosine * turn_sin,
                    )
            return unused

        lax.fori_loop(0, half // 64, strip, 0)


def grid_kernel(
    dims, data_ref, orders_ref, rate_ref, sine_ref, trig_high, trig_low, out_ref,
    move_ref, lhs_ref, weight_ref, acc_ref,
):
    bands, row_count, modes, tiles, slots = dims
    half = slots // 2
    group = FIELDS * row_count
    padded = weight_ref.shape[1] // 2

    order = orders_ref[...]
    natural = (order & 1) * half + (order >> 1)
    for t in range(slots // LANES):
        lane = lax.broadcasted_iota(jnp.int32, (slots, LANES), 1) + t * LANES
        one_hot = jnp.where(natural == lane, 1.0, 0.0).astype(BF)
        move_ref[:, t * LANES : (t + 1) * LANES] = one_hot
    columns = []
    for t in range(tiles):
        part = data_ref[:, t * modes : (t + 1) * modes, :]
        columns.append(part.reshape(slots, LANES).T)
    turned = jnp.concatenate(columns, 0)
    for kind in range(2):
        high, low = split_two(turned[kind * group : (kind + 1) * group])
        moved = dot(jnp.concatenate([high, low], 0), move_ref[...]).astype(BF)
        for parity in range(2):
            part = moved[:, parity * half : (parity + 1) * half]
            lhs_ref[parity, :, kind * half : (kind + 1) * half] = part
    weight_ref[...] = jnp.zeros_like(weight_ref)
    flux_scale = math.pi / (2.0 * NLAT * NLON * DEG)
    weight = jnp.tile(sine_ref[...], (1, KTILE // LANES))
    total = jnp.zeros((8, KTILE), F32)

    for k in range(0, NLON // 2, KTILE):
        tile = slice(k, k + KTILE)
        sums = []
        for parity in range(2):
            first = dot(lhs_ref[parity], trig_high[parity, :, tile])
            second = dot(lhs_ref[parity, :group, :], trig_low[parity, :, tile])
            sums.append(first[:group] + first[group:] + second)
        values = []
        for fields, at in ((sums[0] + sums[1], k), (sums[0] - sums[1], k + NLON // 2)):
            weighted_rate = rate_ref[:, at : at + KTILE] * weight
            total = total + jnp.sum(weighted_rate.reshape(row_count // 8, 8, KTILE), axis=0)
            scaled = fields[:row_count] * (weight * flux_scale)
            values.append(
                jnp.concatenate(
                    [
                        fields[row_count : 2 * row_count] * scaled,
                        fields[2 * row_count :] * scaled,
                        weighted_rate * fields[:row_count],
                    ],
                    0,
                )
            )
        for parity in range(2):
            both = values[0] + values[1] if parity == 0 else values[0] - values[1]
            high, low = split_two(both)
            weight_ref[parity, :group, :] = high
            weight_ref[parity, padded : padded + group, :] = low
            first = dot(trig_high[parity, :, tile], weight_ref[parity], 1)
            second = dot(trig_low[parity, :, tile], weight_ref[parity, :padded, :], 1)
            part = first[:, :padded] + first[:, padded:] + second
            if k == 0:
                acc_ref[parity] = part
            else:
                acc_ref[parity] += part

    joined = []
    for kind in range(2):
        rows = slice(kind * half, (kind + 1) * half)
        joined.append(jnp.concatenate([acc_ref[0, rows, :group], acc_ref[1, rows, :group]], 0))
    if 2 * group < tiles * LANES:
        joined.append(jnp.zeros((slots, tiles * LANES - 2 * group), F32))
    high, low = split_two(jnp.concatenate(joined, 1))
    moved = dot(move_ref[...], jnp.concatenate([high, low], 1))
    moved = moved[:, : tiles * LANES] + moved[:, tiles * LANES :]
    for t in range(tiles):
        part = moved[:, t * LANES : (t + 1) * LANES]
        out_ref[:, t * modes : (t + 1) * modes, :] = part.reshape(bands, modes, LANES)
    out_ref[:, tiles * modes :, :] = jnp.broadcast_to(jnp.sum(total), (bands, 8, LANES))


VMEM = pl.BlockSpec(memory_space=pltpu.VMEM)
SMEM = pl.BlockSpec(memory_space=pltpu.SMEM)
ANY = pl.BlockSpec(memory_space=pl.ANY)


def work(microseconds):
    return pl.CostEstimate(
        flops=microseconds * 10**9, bytes_accessed=2**20, transcendentals=0
    )


def per_device(spectrum, capture_rate, row_latitude, slot_wavenumber):
    bands = lax.axis_size("band")
    modes = spectrum.shape[3]
    row_count = capture_rate.shape[1]
    slots = slot_wavenumber.shape[0]
    blocks = modes // BLK
    chunks = DEG // CHUNK
    tiles = -(-CHAN * row_count // LANES)
    band_index = lax.axis_index("band")
    table = slot_wavenumber.reshape(bands, modes)
    rank = jnp.sum((table[:, None, :] < table[:, :, None]).astype(jnp.int32), 2)
    match = rank[:, None, :] == jnp.arange(modes, dtype=jnp.int32)[None, :, None]
    ordered = jnp.sum(jnp.where(match, table[:, None, :], 0), 2).reshape(slots)
    place_row = jnp.arange(modes, dtype=jnp.int32)[None, None, :]
    places = jnp.sum(jnp.where(match, place_row, 0), 2).reshape(slots)
    rows = jnp.asarray(latitude_rows())
    spread = jnp.asarray(spread_matrix())
    latitude = row_latitude.reshape(1, NLAT)
    coeffs = spectrum.reshape(CHAN, modes, DEG)
    params = pltpu.CompilerParams(vmem_limit_bytes=48 * 2**20)
    chunk_rows = tiles * modes
    dims = (bands, row_count, modes, blocks, tiles)
    recursion_scratch = [pltpu.VMEM((BLK, DEG), F32)] * 2

    def exchange(value):
        return lax.all_to_all(value, "band", split_axis=0, concat_axis=0, tiled=True)

    sent = pl.pallas_call(
        lambda *refs: synth_kernel(dims, *refs),
        out_shape=jax.ShapeDtypeStruct((bands, chunk_rows, LANES), F32),
        in_specs=[SMEM, SMEM, VMEM, VMEM, VMEM, VMEM],
        out_specs=VMEM,
        scratch_shapes=recursion_scratch
        + [pltpu.VMEM((chunks, 2 * ROWS, CHUNK * BLK), BF)]
        + [pltpu.VMEM((2, CHUNK // 2 * BLK, HALF), BF)] * 4
        + [
            pltpu.VMEM((2, ROWS, HALF), F32),
            pltpu.VMEM((HALF, NLAT), BF),
            pltpu.VMEM((CHAN, BLK, DEG), F32),
        ],
        compiler_params=params,
        cost_estimate=work(15),
        name="synth",
    )(ordered, places, coeffs, rows, spread, latitude)
    received = exchange(sent)

    trig_shape = jax.ShapeDtypeStruct((2, slots, NLON // 2), BF)
    trig_high, trig_low = pl.pallas_call(
        trig_kernel,
        out_shape=[trig_shape, trig_shape],
        out_specs=[VMEM, VMEM],
        scratch_shapes=[pltpu.VMEM((slots // 2, LANES), F32)] * 2,
        compiler_params=params,
        cost_estimate=work(4),
        name="trig",
    )()

    my_latitudes = lax.dynamic_slice_in_dim(row_latitude, band_index * row_count, row_count)
    row_sine = jnp.sin(jnp.pi * (my_latitudes.astype(F32) + 0.5) / NLAT)
    row_sine = jnp.broadcast_to(row_sine[:, None], (row_count, LANES))
    orders = jnp.broadcast_to(ordered.reshape(slots, 1), (slots, LANES))
    group = FIELDS * row_count
    padded = -(-group // LANES) * LANES
    grid_dims = (bands, row_count, modes, tiles, slots)
    fluxes = pl.pallas_call(
        lambda *refs: grid_kernel(grid_dims, *refs),
        out_shape=jax.ShapeDtypeStruct((bands, chunk_rows + 8, LANES), F32),
        in_specs=[VMEM] * 6,
        out_specs=VMEM,
        scratch_shapes=[
            pltpu.VMEM((slots, slots), BF),
            pltpu.VMEM((2, 2 * group, slots), BF),
            pltpu.VMEM((2, 2 * padded, KTILE), BF),
            pltpu.VMEM((2, slots, padded), F32),
        ],
        compiler_params=params,
        cost_estimate=work(8),
        name="grid",
    )(received, orders, capture_rate.reshape(row_count, NLON), row_sine, trig_high, trig_low)
    returned = exchange(fluxes)

    chunk_shape = (blocks, chunks, 2 * CHUNK * BLK, HALF)
    legendre = pl.pallas_call(
        lambda *refs: table_kernel((modes, blocks), *refs),
        out_shape=jax.ShapeDtypeStruct(chunk_shape, BF),
        in_specs=[SMEM, VMEM],
        out_specs=ANY,
        scratch_shapes=recursion_scratch
        + [pltpu.VMEM((2 * CHUNK * BLK, HALF), BF)] * 2
        + [pltpu.SemaphoreType.DMA((2,))],
        compiler_params=params,
        cost_estimate=work(12),
        name="table",
    )(ordered, rows)
    result = pl.pallas_call(
        lambda *refs: analyze_kernel(dims, chunk_rows, *refs),
        out_shape=jax.ShapeDtypeStruct((CHAN, modes, DEG), F32),
        in_specs=[SMEM, SMEM, VMEM, VMEM, ANY],
        out_specs=VMEM,
        scratch_shapes=[
            pltpu.VMEM(chunk_shape, BF),
            pltpu.VMEM((HALF, 2 * LANES), BF),
            pltpu.VMEM((DEG, LANES), F32),
            pltpu.VMEM((HALF, NLAT), BF),
            pltpu.VMEM((CHAN, BLK, DEG), F32),
            pltpu.SemaphoreType.DMA((blocks, chunks)),
        ],
        compiler_params=params,
        cost_estimate=work(9),
        name="analyze",
    )(ordered, places, returned, latitude, legendre)
    return result.reshape(1, FIELDS, 2, modes, DEG)


def solution(mesh):
    return jax.shard_map(
        per_device,
        mesh=mesh,
        in_specs=(P("shell", None, None, "band", None), P("shell", "band", None), P(), P()),
        out_specs=P("shell", None, None, "band", None),
        check_vma=False,
    )
```

```python
import functools
import math

import jax
import jax.numpy as jnp
import numpy as np
from jax import lax
from jax.experimental import pallas as pl
from jax.experimental.pallas import tpu as pltpu
from jax.sharding import PartitionSpec as P

DEG = 512
NLAT = 1024
NLON = 2048
FIELDS = 3
HALF = NLAT // 2
CHAN = 2 * FIELDS
BLK = 8
ROWS = CHAN * BLK
CHUNK = 64
CHECK = 16
LANES = 128
KTILE = 256
BF = jnp.bfloat16
F32 = jnp.float32


def split_two(value):
    high = value.astype(BF)
    low = (value - high.astype(F32)).astype(BF)
    return high, low


def dot(lhs, rhs, contract_rhs=0):
    return lax.dot_general(
        lhs, rhs, (((1,), (contract_rhs,)), ((), ())), preferred_element_type=F32
    )


def latitude_rows():
    theta = np.pi * (np.arange(HALF) + 0.5) / NLAT
    index = np.arange(DEG, dtype=np.float64)
    log_terms = np.zeros(DEG)
    log_terms[1:] = 0.5 * np.log2((2.0 * index[1:] + 1.0) / (2.0 * index[1:]))
    rows = np.zeros((8, DEG))
    rows[0], rows[1], rows[2] = np.cos(theta), np.log2(np.sin(theta)), log_terms
    return rows.astype(np.float32)


def spread_matrix():
    spread = np.zeros((LANES, 2, 2, CHUNK // 2, BLK), np.float32)
    for half in range(2):
        for parity in range(2):
            for step in range(CHUNK // 2):
                spread[half * CHUNK + 2 * step + parity, half, parity, step, :] = 1.0
    return spread.reshape(LANES, 2 * 2 * (CHUNK // 2) * BLK).astype(BF)


def degree_scalars():
    before = np.arange(DEG, dtype=np.float64) - 1.0
    square = before * before
    return np.concatenate([square, 4.0 / (4.0 * square - 1.0)]).astype(np.float32)


def block_orders(slots_ref, first):
    sublane = lax.broadcasted_iota(jnp.int32, (BLK, LANES), 0)
    orders = jnp.zeros((BLK, LANES), jnp.int32)
    lowest = jnp.int32(DEG)
    for i in range(BLK):
        order = slots_ref[first + i]
        orders = jnp.where(sublane == i, order, orders)
        lowest = jnp.minimum(lowest, order)
    return orders, lowest


def running_sum(terms, length):
    lane = lax.broadcasted_iota(jnp.int32, terms.shape, 1) & (length - 1)
    shift = 1
    while shift < length:
        moved = pltpu.roll(terms, shift, 1)
        terms = terms + jnp.where(lane >= shift, moved, 0.0)
        shift *= 2
    return terms


def recursion_tables(slots_ref, base, modes, rows_ref, start_ref, before_ref, within_ref):
    orders = [block_orders(slots_ref, base + at)[0][:, :1] for at in range(0, modes, BLK)]
    order = jnp.concatenate(orders, 0).astype(F32)
    position = lax.broadcasted_iota(jnp.int32, (modes, DEG), 1)
    degree = position.astype(F32)
    square = degree * degree
    above = degree > order
    gap = jnp.where(above, square - order * order, 1.0)
    growth = jnp.where(above, 0.5 * jnp.log2((square - 0.25) / gap), 0.0)
    before_ref[...] = running_sum(growth, DEG)
    later = jnp.where(position & (CHECK - 1) == 0, 0.0, growth)
    within_ref[...] = jnp.exp2(running_sum(later, CHECK))
    terms = jnp.where(degree <= order, rows_ref[2:3, :], 0.0)
    norm = jnp.where(order > 0, 0.5 + jnp.sum(terms, axis=1, keepdims=True), 0.0)
    start_ref[...] = norm + order * rows_ref[1:2, :]


def run_chunk(step, carry, double_cosine, orders, before, scalars_ref, emit, beside):
    current, previous, log_scale = carry
    order = orders.astype(F32)
    order_square = order * order
    before = pltpu.roll(before, (step % 2) * CHUNK, 1)
    scale = None
    for i in range(CHUNK):
        if i % CHECK == 0:
            size = jnp.maximum(jnp.abs(current), jnp.abs(previous))
            large, small = size > 2.0**40, size < 2.0**-40
            factor = jnp.where(large, 2.0**-60, jnp.where(small, 2.0**60, 1.0))
            change = jnp.where(large, 60.0, jnp.where(small, -60.0, 0.0))
            current = current * factor
            previous = previous * factor
            log_scale = log_scale + change
            scale = jnp.exp2(jnp.maximum(log_scale + before[:, i : i + 1], -200.0))
        degree = step * CHUNK + i
        factor = (scalars_ref[degree] - order_square) * scalars_ref[DEG + degree]
        factor = jnp.tile(factor, (1, HALF // LANES))
        started = jnp.tile(orders, (1, HALF // LANES)) < degree
        newest = jnp.where(started, double_cosine * current - factor * previous, 1.0)
        current, previous = newest, current
        emit(i, newest * scale)
        if beside and i % (CHUNK // len(beside)) == 1:
            beside[i // (CHUNK // len(beside))]()
    return current, previous, log_scale


def before_tile(before_ref, block, step):
    rows = pl.ds(pl.multiple_of(block * BLK, BLK), BLK)
    return before_ref[rows, pl.ds(pl.multiple_of(step // 2 * LANES, LANES), LANES)]


def start_state(start_ref, block):
    ones = jnp.ones((BLK, HALF), F32)
    return ones, ones, start_ref[pl.ds(pl.multiple_of(block * BLK, BLK), BLK), :]


def fold_matrix(latitude_ref, fold_ref):
    latitude = latitude_ref[...]
    north = jnp.where(latitude < HALF, latitude, NLAT - 1 - latitude)
    sublane = lax.broadcasted_iota(jnp.int32, (HALF, NLAT), 0)
    fold_ref[...] = jnp.where(sublane == north, 1.0, 0.0).astype(BF)


def synth_kernel(
    dims, slots_ref, place_ref, scalars_ref, spec_ref, rows_ref, spread_ref, latitude_ref,
    out_ref, start_ref, before_ref, within_ref, lhs_ref, high_a, low_a, high_b, low_b, acc_ref, fold_ref, coeff_ref,
):
    bands, row_count, modes, blocks, tiles = dims
    fold_matrix(latitude_ref, fold_ref)
    base = lax.axis_index("band") * modes
    recursion_tables(slots_ref, base, modes, rows_ref, start_ref, before_ref, within_ref)
    south = latitude_ref[...] >= HALF
    spread_width = 4 * (CHUNK // 2) * BLK
    lane = lax.broadcasted_iota(jnp.int32, (2 * ROWS, spread_width), 1)
    sub = lax.broadcasted_iota(jnp.int32, (2 * ROWS, spread_width), 0)
    diagonal = (lane % BLK) == (sub % BLK)
    width = (CHUNK // 2) * BLK

    def one_block(block, unused):
        orders, lowest = block_orders(slots_ref, base + block * BLK)
        column = orders[:, :1]
        here = pl.ds(pl.multiple_of(block * BLK, BLK), BLK)
        for i in range(BLK):
            source = pl.ds(place_ref[base + block * BLK + i], 1)
            coeff_ref[:, i : i + 1, :] = spec_ref[:, source, :]
        degree = lax.broadcasted_iota(jnp.int32, (BLK, DEG), 1)
        within = jnp.where(degree >= column, within_ref[here, :], 0.0)
        coeffs = coeff_ref[...] * within[None]
        coeff_high, coeff_low = split_two(coeffs.reshape(ROWS, DEG))
        stacked = jnp.concatenate([coeff_high, coeff_low], 0)
        for t in range(DEG // LANES):
            wide = dot(stacked[:, t * LANES : (t + 1) * LANES], spread_ref[...])
            wide = jnp.where(diagonal, wide, 0.0).astype(BF)
            for half in range(2):
                lhs_ref[2 * t + half] = wide[:, half * 2 * width : (half + 1) * 2 * width]
        acc_ref[...] = jnp.zeros_like(acc_ref)
        cosine = jnp.broadcast_to(2.0 * rows_ref[0:1, :], (BLK, HALF))

        def recur(step, carry, high_ref, low_ref, beside):
            held = {}

            def emit(i, value):
                if i % 4 < 2:
                    held[i] = value
                else:
                    pair = jnp.concatenate([held.pop(i - 2), value], 0)
                    high, low = split_two(pair)
                    at = (i // 4) * 2 * BLK
                    high_ref[i % 2, at : at + 2 * BLK, :] = high
                    low_ref[i % 2, at : at + 2 * BLK, :] = low

            before = before_tile(before_ref, block, step)
            return run_chunk(step, carry, cosine, orders, before, scalars_ref, emit, beside)

        def add_products(step, high_ref, low_ref):
            def part(parity, columns):
                lhs = lhs_ref[step, :, parity * width : (parity + 1) * width]
                first = dot(lhs, high_ref[parity, :, columns])
                second = dot(lhs[:ROWS], low_ref[parity, :, columns])
                acc_ref[parity, :, columns] += first[:ROWS] + first[ROWS:] + second

            return [
                functools.partial(part, parity, slice(at, at + KTILE))
                for parity in range(2)
                for at in range(0, HALF, KTILE)
            ]

        def two_chunks(pair, carry):
            step = 2 * pair
            beside = add_products(jnp.maximum(step - 1, 0), high_b, low_b)
            carry = recur(step, carry, high_a, low_a, beside)
            beside = add_products(step, high_a, low_a)
            return recur(step + 1, carry, high_b, low_b, beside)

        high_b[...] = jnp.zeros_like(high_b)
        low_b[...] = jnp.zeros_like(low_b)
        chunks = DEG // CHUNK
        lax.fori_loop(lowest // (2 * CHUNK), chunks // 2, two_chunks, start_state(start_ref, block))
        for part in add_products(chunks - 1, high_b, low_b):
            part()
        both = acc_ref[...].reshape(2 * ROWS, HALF)
        high, low = split_two(both)
        moved = dot(jnp.concatenate([high, low], 0), fold_ref[...])
        moved = moved[: 2 * ROWS] + moved[2 * ROWS :]
        sign = jnp.tile(1.0 - 2.0 * (column % 2).astype(F32), (CHAN, 1))
        even, odd = moved[:ROWS], moved[ROWS:]
        values = jnp.where(south, sign * (even - odd), even + odd)
        for d in range(bands):
            parts = []
            for kind in range(2):
                for field in range(FIELDS):
                    c = field * 2 + kind
                    parts.append(
                        values[c * BLK : (c + 1) * BLK, d * row_count : (d + 1) * row_count]
                    )
            if CHAN * row_count < tiles * LANES:
                parts.append(jnp.zeros((BLK, tiles * LANES - CHAN * row_count), F32))
            joined = jnp.concatenate(parts, 1)
            for t in range(tiles):
                at = pl.ds(pl.multiple_of(t * blocks * BLK + block * BLK, BLK), BLK)
                out_ref[d, at, :] = joined[:, t * LANES : (t + 1) * LANES]
        return unused

    lax.fori_loop(0, blocks, one_block, 0)


def table_kernel(
    dims, slots_ref, scalars_ref, rows_ref, out_ref, within_out, start_ref, before_ref,
    first_ref, second_ref, sems,
):
    modes, blocks = dims
    base = lax.axis_index("band") * modes
    cosine = jnp.broadcast_to(2.0 * rows_ref[0:1, :], (BLK, HALF))
    recursion_tables(slots_ref, base, modes, rows_ref, start_ref, before_ref, within_out)
    buffers = (first_ref, second_ref)

    def copy_out(which, block, step):
        return pltpu.make_async_copy(buffers[which], out_ref.at[block, step], sems.at[which])

    def one_block(block, unused):
        orders, lowest = block_orders(slots_ref, base + block * BLK)
        start = lowest // (2 * CHUNK)

        def recur(which, step, carry, pending):
            buffer = buffers[which]

            @pl.when(pending)
            def _():
                copy_out(which, block, step).wait()

            held = {}

            def emit(i, value):
                if i % 2 == 0:
                    held[i] = value
                else:
                    pair = jnp.concatenate([held.pop(i - 1), value], 0)
                    high, low = split_two(pair)
                    at = (i // 2) * 2 * BLK
                    buffer[at : at + 2 * BLK, :] = high
                    buffer[CHUNK * BLK + at : CHUNK * BLK + at + 2 * BLK, :] = low

            before = before_tile(before_ref, block, step)
            carry = run_chunk(step, carry, cosine, orders, before, scalars_ref, emit, ())
            copy_out(which, block, step).start()
            return carry

        def two_chunks(pair, carry):
            pending = (block > 0) | (pair > start)
            carry = recur(0, 2 * pair, carry, pending)
            return recur(1, 2 * pair + 1, carry, pending)

        lax.fori_loop(start, DEG // CHUNK // 2, two_chunks, start_state(start_ref, block))
        return unused

    lax.fori_loop(0, blocks, one_block, 0)
    copy_out(0, 0, 0).wait()
    copy_out(1, 0, 0).wait()


def analyze_kernel(
    dims, total_row, slots_ref, place_ref, data_ref, latitude_ref, within_ref, table_ref, out_ref,
    chunk_ref, weight_ref, result_ref, fold_ref, coeff_ref, sems,
):
    bands, row_count, modes, blocks, tiles = dims
    base = lax.axis_index("band") * modes
    chunks = DEG // CHUNK

    def copy_in(block, step):
        return pltpu.make_async_copy(
            table_ref.at[block, step], chunk_ref.at[block, step], sems.at[block, step]
        )

    def start_block(block, unused):
        orders, lowest = block_orders(slots_ref, base + block * BLK)

        def start_chunk(step, inner):
            copy_in(block, step).start()
            return inner

        return lax.fori_loop(lowest // (2 * CHUNK) * 2, chunks, start_chunk, unused)

    lax.fori_loop(0, blocks, start_block, 0)
    fold_matrix(latitude_ref, fold_ref)
    south = latitude_ref[...] >= HALF
    total = data_ref[0, total_row : total_row + 8]
    for d in range(1, bands):
        total = total + data_ref[d, total_row : total_row + 8]
    inverse = (1.0 / total)[:, :1]
    lane = lax.broadcasted_iota(jnp.int32, (CHUNK * BLK, LANES), 1)
    sub = lax.broadcasted_iota(jnp.int32, (CHUNK * BLK, LANES), 0)
    keep = (lane % BLK == sub % BLK) & (lane // ROWS == sub // BLK % 2)

    def one_block(block, unused):
        orders, lowest = block_orders(slots_ref, base + block * BLK)
        orders = orders[:, :1]
        here = pl.ds(pl.multiple_of(block * BLK, BLK), BLK)
        sign = 1.0 - 2.0 * (orders % 2).astype(F32)
        evens, odds = [], []
        for c in range(CHAN):
            offset = ((c % 2) * FIELDS + c // 2) * row_count
            t, at = offset // LANES, offset % LANES
            rows = pl.ds(pl.multiple_of(t * blocks * BLK + block * BLK, BLK), BLK)
            values = jnp.concatenate(
                [data_ref[d, rows, :][:, at : at + row_count] for d in range(bands)], 1
            )
            flipped = sign * values
            evens.append(jnp.where(south, flipped, values))
            odds.append(jnp.where(south, -flipped, values))
        high, low = split_two(jnp.concatenate(evens + odds, 0))
        folded = dot(jnp.concatenate([high, low], 0), fold_ref[...], 1)
        folded = folded[: 2 * ROWS] + folded[2 * ROWS :]
        padded = jnp.concatenate([folded, jnp.zeros((LANES - 2 * ROWS, HALF), F32)], 0)
        high, low = split_two(padded.T)
        weight_ref[:, :LANES] = high
        weight_ref[:, LANES:] = low
        result_ref[...] = jnp.zeros_like(result_ref)

        def one_chunk(step, inner):
            copy_in(block, step).wait()
            first = dot(chunk_ref[block, step, : CHUNK * BLK], weight_ref[...])
            second = dot(chunk_ref[block, step, CHUNK * BLK :], weight_ref[:, :LANES])
            full = first[:, :LANES] + first[:, LANES:] + second
            picked = jnp.where(keep, full, 0.0).reshape(CHUNK, BLK, LANES)
            to = pl.ds(pl.multiple_of(step * CHUNK, CHUNK), CHUNK)
            result_ref[to, :] = jnp.sum(picked, axis=1)
            return inner

        lax.fori_loop(lowest // (2 * CHUNK) * 2, chunks, one_chunk, 0)
        turned = result_ref[...].T
        turned = turned[:ROWS] + turned[ROWS : 2 * ROWS]
        degree = lax.broadcasted_iota(jnp.int32, (BLK, DEG), 1)
        within = jnp.where(degree >= orders, within_ref[here, :], 0.0)
        for c in range(CHAN):
            part = turned[c * BLK : (c + 1) * BLK] * within
            if c // 2 == FIELDS - 1:
                part = part * inverse
            coeff_ref[c] = part
        for i in range(BLK):
            target = pl.ds(place_ref[base + block * BLK + i], 1)
            out_ref[:, target, :] = coeff_ref[:, i : i + 1, :]
        return unused

    lax.fori_loop(0, blocks, one_block, 0)


def base_trig(order, first):
    lane = lax.broadcasted_iota(jnp.int32, order.shape, 1) + first
    phase = (order * lane) & (NLON - 1)
    quarter = (phase + NLON // 8) >> 9
    rest = (phase - quarter * (NLON // 4)).astype(F32) * (2.0 * math.pi / NLON)
    square = rest * rest
    sine = 1.0 / 362880.0
    for coef in (-1.0 / 5040.0, 1.0 / 120.0, -1.0 / 6.0, 1.0):
        sine = sine * square + coef
    sine = sine * rest
    cosine = 1.0 / 40320.0
    for coef in (-1.0 / 720.0, 1.0 / 24.0, -0.5, 1.0):
        cosine = cosine * square + coef
    swap = (quarter & 1) == 1
    cos_out = jnp.where(swap, sine, cosine)
    sin_out = jnp.where(swap, cosine, sine)
    cos_out = jnp.where(((quarter + 1) & 2) == 2, -cos_out, cos_out)
    sin_out = jnp.where((quarter & 2) == 2, -sin_out, sin_out)
    return cos_out, sin_out


def trig_kernel(high_ref, low_ref, cos_ref, sin_ref):
    half = cos_ref.shape[0]
    root = math.sqrt(0.5)
    for parity in range(2):

        def strip(step, unused):
            at = pl.multiple_of(step * 64, 64)
            shape = (64, LANES)
            order = 2 * (lax.broadcasted_iota(jnp.int32, shape, 0) + at) + parity
            eighth = order & 7
            odd = (eighth & 1) == 1
            turn_cos = jnp.where(odd, root, jnp.where((eighth & 2) == 0, 1.0, 0.0))
            turn_sin = jnp.where(odd, root, jnp.where((eighth & 2) == 2, 1.0, 0.0))
            turn_cos = jnp.where((eighth >= 3) & (eighth <= 5), -turn_cos, turn_cos)
            turn_sin = jnp.where(eighth > 4, -turn_sin, turn_sin)
            for t in range(KTILE // LANES):
                cosine, sine = base_trig(order, t * LANES)
                for k in range(t * LANES, NLON // 2, KTILE):
                    columns = slice(k, k + LANES)
                    high, low = split_two(cosine)
                    high_ref[parity, pl.ds(at, 64), columns] = high
                    low_ref[parity, pl.ds(at, 64), columns] = low
                    high, low = split_two(sine)
                    high_ref[parity, pl.ds(half + at, 64), columns] = high
                    low_ref[parity, pl.ds(half + at, 64), columns] = low
                    cosine, sine = (
                        cosine * turn_cos - sine * turn_sin,
                        sine * turn_cos + cosine * turn_sin,
                    )
            return unused

        lax.fori_loop(0, half // 64, strip, 0)


def grid_kernel(
    dims, data_ref, orders_ref, rate_ref, sine_ref, trig_high, trig_low, out_ref,
    move_ref, lhs_ref, weight_ref, acc_ref,
):
    bands, row_count, modes, tiles, slots = dims
    half = slots // 2
    group = FIELDS * row_count
    padded = weight_ref.shape[1] // 2

    order = orders_ref[...]
    natural = (order & 1) * half + (order >> 1)
    for t in range(slots // LANES):
        lane = lax.broadcasted_iota(jnp.int32, (slots, LANES), 1) + t * LANES
        one_hot = jnp.where(natural == lane, 1.0, 0.0).astype(BF)
        move_ref[:, t * LANES : (t + 1) * LANES] = one_hot
    columns = []
    for t in range(tiles):
        part = data_ref[:, t * modes : (t + 1) * modes, :]
        columns.append(part.reshape(slots, LANES).T)
    turned = jnp.concatenate(columns, 0)
    for kind in range(2):
        high, low = split_two(turned[kind * group : (kind + 1) * group])
        moved = dot(jnp.concatenate([high, low], 0), move_ref[...]).astype(BF)
        for parity in range(2):
            part = moved[:, parity * half : (parity + 1) * half]
            lhs_ref[parity, :, kind * half : (kind + 1) * half] = part
    weight_ref[...] = jnp.zeros_like(weight_ref)
    flux_scale = math.pi / (2.0 * NLAT * NLON * DEG)
    weight = jnp.tile(sine_ref[...], (1, KTILE // LANES))
    total = jnp.zeros((8, KTILE), F32)

    for k in range(0, NLON // 2, KTILE):
        tile = slice(k, k + KTILE)
        sums = []
        for parity in range(2):
            first = dot(lhs_ref[parity], trig_high[parity, :, tile])
            second = dot(lhs_ref[parity, :group, :], trig_low[parity, :, tile])
            sums.append(first[:group] + first[group:] + second)
        values = []
        for fields, at in ((sums[0] + sums[1], k), (sums[0] - sums[1], k + NLON // 2)):
            weighted_rate = rate_ref[:, at : at + KTILE] * weight
            total = total + jnp.sum(weighted_rate.reshape(row_count // 8, 8, KTILE), axis=0)
            scaled = fields[:row_count] * (weight * flux_scale)
            values.append(
                jnp.concatenate(
                    [
                        fields[row_count : 2 * row_count] * scaled,
                        fields[2 * row_count :] * scaled,
                        weighted_rate * fields[:row_count],
                    ],
                    0,
                )
            )
        for parity in range(2):
            both = values[0] + values[1] if parity == 0 else values[0] - values[1]
            high, low = split_two(both)
            weight_ref[parity, :group, :] = high
            weight_ref[parity, padded : padded + group, :] = low
            first = dot(trig_high[parity, :, tile], weight_ref[parity], 1)
            second = dot(trig_low[parity, :, tile], weight_ref[parity, :padded, :], 1)
            part = first[:, :padded] + first[:, padded:] + second
            if k == 0:
                acc_ref[parity] = part
            else:
                acc_ref[parity] += part

    joined = []
    for kind in range(2):
        rows = slice(kind * half, (kind + 1) * half)
        joined.append(jnp.concatenate([acc_ref[0, rows, :group], acc_ref[1, rows, :group]], 0))
    if 2 * group < tiles * LANES:
        joined.append(jnp.zeros((slots, tiles * LANES - 2 * group), F32))
    high, low = split_two(jnp.concatenate(joined, 1))
    moved = dot(move_ref[...], jnp.concatenate([high, low], 1))
    moved = moved[:, : tiles * LANES] + moved[:, tiles * LANES :]
    for t in range(tiles):
        part = moved[:, t * LANES : (t + 1) * LANES]
        out_ref[:, t * modes : (t + 1) * modes, :] = part.reshape(bands, modes, LANES)
    out_ref[:, tiles * modes :, :] = jnp.broadcast_to(jnp.sum(total), (bands, 8, LANES))


VMEM = pl.BlockSpec(memory_space=pltpu.VMEM)
SMEM = pl.BlockSpec(memory_space=pltpu.SMEM)
ANY = pl.BlockSpec(memory_space=pl.ANY)


def work(microseconds):
    return pl.CostEstimate(
        flops=microseconds * 10**9, bytes_accessed=2**20, transcendentals=0
    )


def per_device(spectrum, capture_rate, row_latitude, slot_wavenumber):
    bands = lax.axis_size("band")
    modes = spectrum.shape[3]
    row_count = capture_rate.shape[1]
    slots = slot_wavenumber.shape[0]
    blocks = modes // BLK
    chunks = DEG // CHUNK
    tiles = -(-CHAN * row_count // LANES)
    band_index = lax.axis_index("band")
    table = slot_wavenumber.reshape(bands, modes)
    rank = jnp.sum((table[:, None, :] < table[:, :, None]).astype(jnp.int32), 2)
    match = rank[:, None, :] == jnp.arange(modes, dtype=jnp.int32)[None, :, None]
    ordered = jnp.sum(jnp.where(match, table[:, None, :], 0), 2).reshape(slots)
    place_row = jnp.arange(modes, dtype=jnp.int32)[None, None, :]
    places = jnp.sum(jnp.where(match, place_row, 0), 2).reshape(slots)
    rows = jnp.asarray(latitude_rows())
    spread = jnp.asarray(spread_matrix())
    latitude = row_latitude.reshape(1, NLAT)
    coeffs = spectrum.reshape(CHAN, modes, DEG)
    params = pltpu.CompilerParams(vmem_limit_bytes=48 * 2**20)
    chunk_rows = tiles * modes
    dims = (bands, row_count, modes, blocks, tiles)
    scalars = jnp.asarray(degree_scalars())
    per_order = pltpu.VMEM((modes, DEG), F32)

    def exchange(value):
        return lax.all_to_all(value, "band", split_axis=0, concat_axis=0, tiled=True)

    sent = pl.pallas_call(
        lambda *refs: synth_kernel(dims, *refs),
        out_shape=jax.ShapeDtypeStruct((bands, chunk_rows, LANES), F32),
        in_specs=[SMEM, SMEM, SMEM, VMEM, VMEM, VMEM, VMEM],
        out_specs=VMEM,
        scratch_shapes=[per_order] * 3
        + [pltpu.VMEM((chunks, 2 * ROWS, CHUNK * BLK), BF)]
        + [pltpu.VMEM((2, CHUNK // 2 * BLK, HALF), BF)] * 4
        + [
            pltpu.VMEM((2, ROWS, HALF), F32),
            pltpu.VMEM((HALF, NLAT), BF),
            pltpu.VMEM((CHAN, BLK, DEG), F32),
        ],
        compiler_params=params,
        cost_estimate=work(15),
        name="synth",
    )(ordered, places, scalars, coeffs, rows, spread, latitude)
    received = exchange(sent)

    trig_shape = jax.ShapeDtypeStruct((2, slots, NLON // 2), BF)
    trig_high, trig_low = pl.pallas_call(
        trig_kernel,
        out_shape=[trig_shape, trig_shape],
        out_specs=[VMEM, VMEM],
        scratch_shapes=[pltpu.VMEM((slots // 2, LANES), F32)] * 2,
        compiler_params=params,
        cost_estimate=work(4),
        name="trig",
    )()

    my_latitudes = lax.dynamic_slice_in_dim(row_latitude, band_index * row_count, row_count)
    row_sine = jnp.sin(jnp.pi * (my_latitudes.astype(F32) + 0.5) / NLAT)
    row_sine = jnp.broadcast_to(row_sine[:, None], (row_count, LANES))
    orders = jnp.broadcast_to(ordered.reshape(slots, 1), (slots, LANES))
    group = FIELDS * row_count
    padded = -(-group // LANES) * LANES
    grid_dims = (bands, row_count, modes, tiles, slots)
    fluxes = pl.pallas_call(
        lambda *refs: grid_kernel(grid_dims, *refs),
        out_shape=jax.ShapeDtypeStruct((bands, chunk_rows + 8, LANES), F32),
        in_specs=[VMEM] * 6,
        out_specs=VMEM,
        scratch_shapes=[
            pltpu.VMEM((slots, slots), BF),
            pltpu.VMEM((2, 2 * group, slots), BF),
            pltpu.VMEM((2, 2 * padded, KTILE), BF),
            pltpu.VMEM((2, slots, padded), F32),
        ],
        compiler_params=params,
        cost_estimate=work(8),
        name="grid",
    )(received, orders, capture_rate.reshape(row_count, NLON), row_sine, trig_high, trig_low)
    returned = exchange(fluxes)

    chunk_shape = (blocks, chunks, 2 * CHUNK * BLK, HALF)
    legendre, within = pl.pallas_call(
        lambda *refs: table_kernel((modes, blocks), *refs),
        out_shape=[
            jax.ShapeDtypeStruct(chunk_shape, BF),
            jax.ShapeDtypeStruct((modes, DEG), F32),
        ],
        in_specs=[SMEM, SMEM, VMEM],
        out_specs=[ANY, VMEM],
        scratch_shapes=[per_order] * 2
        + [pltpu.VMEM((2 * CHUNK * BLK, HALF), BF)] * 2
        + [pltpu.SemaphoreType.DMA((2,))],
        compiler_params=params,
        cost_estimate=work(12),
        name="table",
    )(ordered, scalars, rows)
    result = pl.pallas_call(
        lambda *refs: analyze_kernel(dims, chunk_rows, *refs),
        out_shape=jax.ShapeDtypeStruct((CHAN, modes, DEG), F32),
        in_specs=[SMEM, SMEM, VMEM, VMEM, VMEM, ANY],
        out_specs=VMEM,
        scratch_shapes=[
            pltpu.VMEM(chunk_shape, BF),
            pltpu.VMEM((HALF, 2 * LANES), BF),
            pltpu.VMEM((DEG, LANES), F32),
            pltpu.VMEM((HALF, NLAT), BF),
            pltpu.VMEM((CHAN, BLK, DEG), F32),
            pltpu.SemaphoreType.DMA((blocks, chunks)),
        ],
        compiler_params=params,
        cost_estimate=work(9),
        name="analyze",
    )(ordered, places, returned, latitude, within, legendre)
    return result.reshape(1, FIELDS, 2, modes, DEG)


def solution(mesh):
    return jax.shard_map(
        per_device,
        mesh=mesh,
        in_specs=(P("shell", None, None, "band", None), P("shell", "band", None), P(), P()),
        out_specs=P("shell", None, None, "band", None),
        check_vma=False,
    )
```

```python
import functools
import math

import jax
import jax.numpy as jnp
import numpy as np
from jax import lax
from jax.experimental import pallas as pl
from jax.experimental.pallas import tpu as pltpu
from jax.sharding import PartitionSpec as P

DEG = 512
NLAT = 1024
NLON = 2048
FIELDS = 3
HALF = NLAT // 2
CHAN = 2 * FIELDS
BLK = 8
ROWS = CHAN * BLK
CHUNK = 64
CHECK = 16
LANES = 128
KTILE = 256
BF = jnp.bfloat16
F32 = jnp.float32


def split_two(value):
    high = value.astype(BF)
    low = (value - high.astype(F32)).astype(BF)
    return high, low


def dot(lhs, rhs, contract_rhs=0):
    return lax.dot_general(
        lhs, rhs, (((1,), (contract_rhs,)), ((), ())), preferred_element_type=F32
    )


def latitude_rows():
    theta = np.pi * (np.arange(HALF) + 0.5) / NLAT
    index = np.arange(DEG, dtype=np.float64)
    log_terms = np.zeros(DEG)
    log_terms[1:] = 0.5 * np.log2((2.0 * index[1:] + 1.0) / (2.0 * index[1:]))
    rows = np.zeros((8, DEG))
    rows[0], rows[1], rows[2] = np.cos(theta), np.log2(np.sin(theta)), log_terms
    return rows.astype(np.float32)


def spread_matrix():
    spread = np.zeros((LANES, 2, 2, CHUNK // 2, BLK), np.float32)
    for half in range(2):
        for parity in range(2):
            for step in range(CHUNK // 2):
                spread[half * CHUNK + 2 * step + parity, half, parity, step, :] = 1.0
    return spread.reshape(LANES, 2 * 2 * (CHUNK // 2) * BLK).astype(BF)


def degree_scalars():
    before = np.arange(DEG, dtype=np.float64) - 1.0
    square = before * before
    return np.concatenate([square, 4.0 / (4.0 * square - 1.0)]).astype(np.float32)


def block_orders(slots_ref, first):
    sublane = lax.broadcasted_iota(jnp.int32, (BLK, LANES), 0)
    orders = jnp.zeros((BLK, LANES), jnp.int32)
    lowest = jnp.int32(DEG)
    for i in range(BLK):
        order = slots_ref[first + i]
        orders = jnp.where(sublane == i, order, orders)
        lowest = jnp.minimum(lowest, order)
    return orders, lowest


def running_sum(terms, length):
    lane = lax.broadcasted_iota(jnp.int32, terms.shape, 1) & (length - 1)
    shift = 1
    while shift < length:
        moved = pltpu.roll(terms, shift, 1)
        terms = terms + jnp.where(lane >= shift, moved, 0.0)
        shift *= 2
    return terms


def recursion_tables(slots_ref, base, modes, rows_ref, start_ref, before_ref, within_ref):
    orders = [block_orders(slots_ref, base + at)[0][:, :1] for at in range(0, modes, BLK)]
    order = jnp.concatenate(orders, 0).astype(F32)
    position = lax.broadcasted_iota(jnp.int32, (modes, DEG), 1)
    degree = position.astype(F32)
    square = degree * degree
    above = degree > order
    gap = jnp.where(above, square - order * order, 1.0)
    growth = jnp.where(above, 0.5 * jnp.log2((square - 0.25) / gap), 0.0)
    before_ref[...] = running_sum(growth, DEG)
    later = jnp.where(position & (CHECK - 1) == 0, 0.0, growth)
    within_ref[...] = jnp.exp2(running_sum(later, CHECK))
    terms = jnp.where(degree <= order, rows_ref[2:3, :], 0.0)
    norm = jnp.where(order > 0, 0.5 + jnp.sum(terms, axis=1, keepdims=True), 0.0)
    start_ref[...] = norm + order * rows_ref[1:2, :]


def run_chunk(step, carry, double_cosine, orders, before, scalars_ref, emit, beside):
    current, previous, log_scale = carry
    order = orders.astype(F32)
    order_square = order * order
    before = pltpu.roll(before, (step % 2) * CHUNK, 1)
    scale = None
    for i in range(CHUNK):
        if i % CHECK == 0:
            size = jnp.maximum(jnp.abs(current), jnp.abs(previous))
            large, small = size > 2.0**40, size < 2.0**-40
            factor = jnp.where(large, 2.0**-60, jnp.where(small, 2.0**60, 1.0))
            change = jnp.where(large, 60.0, jnp.where(small, -60.0, 0.0))
            current = current * factor
            previous = previous * factor
            log_scale = log_scale + change
            scale = jnp.exp2(jnp.maximum(log_scale + before[:, i : i + 1], -200.0))
        degree = step * CHUNK + i
        factor = (scalars_ref[degree] - order_square) * scalars_ref[DEG + degree]
        factor = jnp.tile(factor, (1, HALF // LANES))
        started = jnp.tile(orders, (1, HALF // LANES)) < degree
        newest = jnp.where(started, double_cosine * current - factor * previous, 1.0)
        current, previous = newest, current
        emit(i, newest * scale)
        if beside and i % (CHUNK // len(beside)) == 1:
            beside[i // (CHUNK // len(beside))]()
    return current, previous, log_scale


def before_tile(before_ref, block, step):
    rows = pl.ds(pl.multiple_of(block * BLK, BLK), BLK)
    return before_ref[rows, pl.ds(pl.multiple_of(step // 2 * LANES, LANES), LANES)]


def start_state(start_ref, block):
    ones = jnp.ones((BLK, HALF), F32)
    return ones, ones, start_ref[pl.ds(pl.multiple_of(block * BLK, BLK), BLK), :]


def fold_matrix(latitude_ref, fold_ref):
    latitude = latitude_ref[...]
    north = jnp.where(latitude < HALF, latitude, NLAT - 1 - latitude)
    sublane = lax.broadcasted_iota(jnp.int32, (HALF, NLAT), 0)
    fold_ref[...] = jnp.where(sublane == north, 1.0, 0.0).astype(BF)


def synth_kernel(
    dims, slots_ref, place_ref, scalars_ref, spec_ref, rows_ref, spread_ref, latitude_ref,
    out_ref, start_ref, before_ref, within_ref, lhs_ref, high_a, low_a, high_b, low_b, acc_ref, fold_ref, coeff_ref,
):
    bands, row_count, modes, blocks, tiles = dims
    fold_matrix(latitude_ref, fold_ref)
    base = lax.axis_index("band") * modes
    recursion_tables(slots_ref, base, modes, rows_ref, start_ref, before_ref, within_ref)
    south = latitude_ref[...] >= HALF
    spread_width = 4 * (CHUNK // 2) * BLK
    lane = lax.broadcasted_iota(jnp.int32, (2 * ROWS, spread_width), 1)
    sub = lax.broadcasted_iota(jnp.int32, (2 * ROWS, spread_width), 0)
    diagonal = (lane % BLK) == (sub % BLK)
    width = (CHUNK // 2) * BLK

    def one_block(block, unused):
        orders, lowest = block_orders(slots_ref, base + block * BLK)
        column = orders[:, :1]
        here = pl.ds(pl.multiple_of(block * BLK, BLK), BLK)
        for i in range(BLK):
            source = pl.ds(place_ref[base + block * BLK + i], 1)
            coeff_ref[:, i : i + 1, :] = spec_ref[:, source, :]
        degree = lax.broadcasted_iota(jnp.int32, (BLK, DEG), 1)
        within = jnp.where(degree >= column, within_ref[here, :], 0.0)
        coeffs = coeff_ref[...] * within[None]
        coeff_high, coeff_low = split_two(coeffs.reshape(ROWS, DEG))
        stacked = jnp.concatenate([coeff_high, coeff_low], 0)
        for t in range(DEG // LANES):
            wide = dot(stacked[:, t * LANES : (t + 1) * LANES], spread_ref[...])
            wide = jnp.where(diagonal, wide, 0.0).astype(BF)
            for half in range(2):
                lhs_ref[2 * t + half] = wide[:, half * 2 * width : (half + 1) * 2 * width]
        acc_ref[...] = jnp.zeros_like(acc_ref)
        cosine = jnp.broadcast_to(2.0 * rows_ref[0:1, :], (BLK, HALF))

        def recur(step, carry, high_ref, low_ref, beside):
            held = {}

            def emit(i, value):
                if i % 4 < 2:
                    held[i] = value
                else:
                    pair = jnp.concatenate([held.pop(i - 2), value], 0)
                    high, low = split_two(pair)
                    at = (i // 4) * 2 * BLK
                    high_ref[i % 2, at : at + 2 * BLK, :] = high
                    low_ref[i % 2, at : at + 2 * BLK, :] = low

            before = before_tile(before_ref, block, step)
            return run_chunk(step, carry, cosine, orders, before, scalars_ref, emit, beside)

        def add_products(step, high_ref, low_ref):
            def part(parity, columns):
                lhs = lhs_ref[step, :, parity * width : (parity + 1) * width]
                first = dot(lhs, high_ref[parity, :, columns])
                second = dot(lhs[:ROWS], low_ref[parity, :, columns])
                acc_ref[parity, :, columns] += first[:ROWS] + first[ROWS:] + second

            return [
                functools.partial(part, parity, slice(at, at + KTILE))
                for parity in range(2)
                for at in range(0, HALF, KTILE)
            ]

        def two_chunks(pair, carry):
            step = 2 * pair
            beside = add_products(jnp.maximum(step - 1, 0), high_b, low_b)
            carry = recur(step, carry, high_a, low_a, beside)
            beside = add_products(step, high_a, low_a)
            return recur(step + 1, carry, high_b, low_b, beside)

        high_b[...] = jnp.zeros_like(high_b)
        low_b[...] = jnp.zeros_like(low_b)
        chunks = DEG // CHUNK
        lax.fori_loop(lowest // (2 * CHUNK), chunks // 2, two_chunks, start_state(start_ref, block))
        for part in add_products(chunks - 1, high_b, low_b):
            part()
        both = acc_ref[...].reshape(2 * ROWS, HALF)
        high, low = split_two(both)
        moved = dot(jnp.concatenate([high, low], 0), fold_ref[...])
        moved = moved[: 2 * ROWS] + moved[2 * ROWS :]
        sign = jnp.tile(1.0 - 2.0 * (column % 2).astype(F32), (CHAN, 1))
        even, odd = moved[:ROWS], moved[ROWS:]
        values = jnp.where(south, sign * (even - odd), even + odd)
        for d in range(bands):
            parts = []
            for kind in range(2):
                for field in range(FIELDS):
                    c = field * 2 + kind
                    parts.append(
                        values[c * BLK : (c + 1) * BLK, d * row_count : (d + 1) * row_count]
                    )
            if CHAN * row_count < tiles * LANES:
                parts.append(jnp.zeros((BLK, tiles * LANES - CHAN * row_count), F32))
            joined = jnp.concatenate(parts, 1)
            for t in range(tiles):
                at = pl.ds(pl.multiple_of(t * blocks * BLK + block * BLK, BLK), BLK)
                out_ref[d, at, :] = joined[:, t * LANES : (t + 1) * LANES]
        return unused

    lax.fori_loop(0, blocks, one_block, 0)


def table_kernel(
    dims, slots_ref, scalars_ref, rows_ref, *refs,
):
    modes, blocks = dims
    out_refs, (within_out, start_ref, before_ref) = refs[:blocks], refs[blocks:]
    base = lax.axis_index("band") * modes
    cosine = jnp.broadcast_to(2.0 * rows_ref[0:1, :], (BLK, HALF))
    recursion_tables(slots_ref, base, modes, rows_ref, start_ref, before_ref, within_out)

    def one_block(block, unused):
        orders, lowest = block_orders(slots_ref, base + block * BLK)

        def one_chunk(step, carry):
            held = {}

            def emit(i, value):
                if i % 2 == 0:
                    held[i] = value
                else:
                    pair = jnp.concatenate([held.pop(i - 1), value], 0)
                    high, low = split_two(pair)
                    at = (i // 2) * 2 * BLK
                    out_refs[block][step, at : at + 2 * BLK, :] = high
                    at += CHUNK * BLK
                    out_refs[block][step, at : at + 2 * BLK, :] = low

            before = before_tile(before_ref, block, step)
            return run_chunk(step, carry, cosine, orders, before, scalars_ref, emit, ())

        lax.fori_loop(lowest // CHUNK, DEG // CHUNK, one_chunk, start_state(start_ref, block))
        return unused

    for block in range(blocks):
        one_block(block, 0)


def analyze_kernel(
    dims, total_row, slots_ref, place_ref, data_ref, latitude_ref, within_ref, *refs,
):
    bands, row_count, modes, blocks, tiles = dims
    table_refs, (out_ref, weight_ref, result_ref, fold_ref, coeff_ref) = refs[:blocks], refs[blocks:]
    base = lax.axis_index("band") * modes
    chunks = DEG // CHUNK

    fold_matrix(latitude_ref, fold_ref)
    south = latitude_ref[...] >= HALF
    total = data_ref[0, total_row : total_row + 8]
    for d in range(1, bands):
        total = total + data_ref[d, total_row : total_row + 8]
    inverse = (1.0 / total)[:, :1]
    lane = lax.broadcasted_iota(jnp.int32, (CHUNK * BLK, LANES), 1)
    sub = lax.broadcasted_iota(jnp.int32, (CHUNK * BLK, LANES), 0)
    keep = (lane % BLK == sub % BLK) & (lane // ROWS == sub // BLK % 2)

    def one_block(block, unused):
        orders, lowest = block_orders(slots_ref, base + block * BLK)
        orders = orders[:, :1]
        here = pl.ds(pl.multiple_of(block * BLK, BLK), BLK)
        sign = 1.0 - 2.0 * (orders % 2).astype(F32)
        evens, odds = [], []
        for c in range(CHAN):
            offset = ((c % 2) * FIELDS + c // 2) * row_count
            t, at = offset // LANES, offset % LANES
            rows = pl.ds(pl.multiple_of(t * blocks * BLK + block * BLK, BLK), BLK)
            values = jnp.concatenate(
                [data_ref[d, rows, :][:, at : at + row_count] for d in range(bands)], 1
            )
            flipped = sign * values
            evens.append(jnp.where(south, flipped, values))
            odds.append(jnp.where(south, -flipped, values))
        high, low = split_two(jnp.concatenate(evens + odds, 0))
        folded = dot(jnp.concatenate([high, low], 0), fold_ref[...], 1)
        folded = folded[: 2 * ROWS] + folded[2 * ROWS :]
        padded = jnp.concatenate([folded, jnp.zeros((LANES - 2 * ROWS, HALF), F32)], 0)
        high, low = split_two(padded.T)
        weight_ref[:, :LANES] = high
        weight_ref[:, LANES:] = low
        result_ref[...] = jnp.zeros_like(result_ref)

        def one_chunk(step, inner):
            first = dot(table_refs[block][step, : CHUNK * BLK], weight_ref[...])
            second = dot(table_refs[block][step, CHUNK * BLK :], weight_ref[:, :LANES])
            full = first[:, :LANES] + first[:, LANES:] + second
            picked = jnp.where(keep, full, 0.0).reshape(CHUNK, BLK, LANES)
            to = pl.ds(pl.multiple_of(step * CHUNK, CHUNK), CHUNK)
            result_ref[to, :] = jnp.sum(picked, axis=1)
            return inner

        lax.fori_loop(lowest // CHUNK, chunks, one_chunk, 0)
        turned = result_ref[...].T
        turned = turned[:ROWS] + turned[ROWS : 2 * ROWS]
        degree = lax.broadcasted_iota(jnp.int32, (BLK, DEG), 1)
        within = jnp.where(degree >= orders, within_ref[here, :], 0.0)
        for c in range(CHAN):
            part = turned[c * BLK : (c + 1) * BLK] * within
            if c // 2 == FIELDS - 1:
                part = part * inverse
            coeff_ref[c] = part
        for i in range(BLK):
            target = pl.ds(place_ref[base + block * BLK + i], 1)
            out_ref[:, target, :] = coeff_ref[:, i : i + 1, :]
        return unused

    for block in range(blocks):
        one_block(block, 0)


def base_trig(order, first):
    lane = lax.broadcasted_iota(jnp.int32, order.shape, 1) + first
    phase = (order * lane) & (NLON - 1)
    quarter = (phase + NLON // 8) >> 9
    rest = (phase - quarter * (NLON // 4)).astype(F32) * (2.0 * math.pi / NLON)
    square = rest * rest
    sine = 1.0 / 362880.0
    for coef in (-1.0 / 5040.0, 1.0 / 120.0, -1.0 / 6.0, 1.0):
        sine = sine * square + coef
    sine = sine * rest
    cosine = 1.0 / 40320.0
    for coef in (-1.0 / 720.0, 1.0 / 24.0, -0.5, 1.0):
        cosine = cosine * square + coef
    swap = (quarter & 1) == 1
    cos_out = jnp.where(swap, sine, cosine)
    sin_out = jnp.where(swap, cosine, sine)
    cos_out = jnp.where(((quarter + 1) & 2) == 2, -cos_out, cos_out)
    sin_out = jnp.where((quarter & 2) == 2, -sin_out, sin_out)
    return cos_out, sin_out


def trig_kernel(high_ref, low_ref, cos_ref, sin_ref):
    half = cos_ref.shape[0]
    root = math.sqrt(0.5)
    for parity in range(2):

        def strip(step, unused):
            at = pl.multiple_of(step * 64, 64)
            shape = (64, LANES)
            order = 2 * (lax.broadcasted_iota(jnp.int32, shape, 0) + at) + parity
            eighth = order & 7
            odd = (eighth & 1) == 1
            turn_cos = jnp.where(odd, root, jnp.where((eighth & 2) == 0, 1.0, 0.0))
            turn_sin = jnp.where(odd, root, jnp.where((eighth & 2) == 2, 1.0, 0.0))
            turn_cos = jnp.where((eighth >= 3) & (eighth <= 5), -turn_cos, turn_cos)
            turn_sin = jnp.where(eighth > 4, -turn_sin, turn_sin)
            for t in range(KTILE // LANES):
                cosine, sine = base_trig(order, t * LANES)
                for k in range(t * LANES, NLON // 2, KTILE):
                    columns = slice(k, k + LANES)
                    high, low = split_two(cosine)
                    high_ref[parity, pl.ds(at, 64), columns] = high
                    low_ref[parity, pl.ds(at, 64), columns] = low
                    high, low = split_two(sine)
                    high_ref[parity, pl.ds(half + at, 64), columns] = high
                    low_ref[parity, pl.ds(half + at, 64), columns] = low
                    cosine, sine = (
                        cosine * turn_cos - sine * turn_sin,
                        sine * turn_cos + cosine * turn_sin,
                    )
            return unused

        lax.fori_loop(0, half // 64, strip, 0)


def grid_kernel(
    dims, data_ref, orders_ref, rate_ref, sine_ref, trig_high, trig_low, out_ref,
    move_ref, lhs_ref, weight_ref, acc_ref,
):
    bands, row_count, modes, tiles, slots = dims
    half = slots // 2
    group = FIELDS * row_count
    padded = weight_ref.shape[1] // 2

    order = orders_ref[...]
    natural = (order & 1) * half + (order >> 1)
    for t in range(slots // LANES):
        lane = lax.broadcasted_iota(jnp.int32, (slots, LANES), 1) + t * LANES
        one_hot = jnp.where(natural == lane, 1.0, 0.0).astype(BF)
        move_ref[:, t * LANES : (t + 1) * LANES] = one_hot
    columns = []
    for t in range(tiles):
        part = data_ref[:, t * modes : (t + 1) * modes, :]
        columns.append(part.reshape(slots, LANES).T)
    turned = jnp.concatenate(columns, 0)
    for kind in range(2):
        high, low = split_two(turned[kind * group : (kind + 1) * group])
        moved = dot(jnp.concatenate([high, low], 0), move_ref[...]).astype(BF)
        for parity in range(2):
            part = moved[:, parity * half : (parity + 1) * half]
            lhs_ref[parity, :, kind * half : (kind + 1) * half] = part
    weight_ref[...] = jnp.zeros_like(weight_ref)
    flux_scale = math.pi / (2.0 * NLAT * NLON * DEG)
    weight = jnp.tile(sine_ref[...], (1, KTILE // LANES))
    total = jnp.zeros((8, KTILE), F32)

    for k in range(0, NLON // 2, KTILE):
        tile = slice(k, k + KTILE)
        sums = []
        for parity in range(2):
            first = dot(lhs_ref[parity], trig_high[parity, :, tile])
            second = dot(lhs_ref[parity, :group, :], trig_low[parity, :, tile])
            sums.append(first[:group] + first[group:] + second)
        values = []
        for fields, at in ((sums[0] + sums[1], k), (sums[0] - sums[1], k + NLON // 2)):
            weighted_rate = rate_ref[:, at : at + KTILE] * weight
            total = total + jnp.sum(weighted_rate.reshape(row_count // 8, 8, KTILE), axis=0)
            scaled = fields[:row_count] * (weight * flux_scale)
            values.append(
                jnp.concatenate(
                    [
                        fields[row_count : 2 * row_count] * scaled,
                        fields[2 * row_count :] * scaled,
                        weighted_rate * fields[:row_count],
                    ],
                    0,
                )
            )
        for parity in range(2):
            both = values[0] + values[1] if parity == 0 else values[0] - values[1]
            high, low = split_two(both)
            weight_ref[parity, :group, :] = high
            weight_ref[parity, padded : padded + group, :] = low
            first = dot(trig_high[parity, :, tile], weight_ref[parity], 1)
            second = dot(trig_low[parity, :, tile], weight_ref[parity, :padded, :], 1)
            part = first[:, :padded] + first[:, padded:] + second
            if k == 0:
                acc_ref[parity] = part
            else:
                acc_ref[parity] += part

    joined = []
    for kind in range(2):
        rows = slice(kind * half, (kind + 1) * half)
        joined.append(jnp.concatenate([acc_ref[0, rows, :group], acc_ref[1, rows, :group]], 0))
    if 2 * group < tiles * LANES:
        joined.append(jnp.zeros((slots, tiles * LANES - 2 * group), F32))
    high, low = split_two(jnp.concatenate(joined, 1))
    moved = dot(move_ref[...], jnp.concatenate([high, low], 1))
    moved = moved[:, : tiles * LANES] + moved[:, tiles * LANES :]
    for t in range(tiles):
        part = moved[:, t * LANES : (t + 1) * LANES]
        out_ref[:, t * modes : (t + 1) * modes, :] = part.reshape(bands, modes, LANES)
    out_ref[:, tiles * modes :, :] = jnp.broadcast_to(jnp.sum(total), (bands, 8, LANES))


VMEM = pl.BlockSpec(memory_space=pltpu.VMEM)
SMEM = pl.BlockSpec(memory_space=pltpu.SMEM)


def work(microseconds):
    return pl.CostEstimate(
        flops=microseconds * 10**9, bytes_accessed=2**20, transcendentals=0
    )


def per_device(spectrum, capture_rate, row_latitude, slot_wavenumber):
    bands = lax.axis_size("band")
    modes = spectrum.shape[3]
    row_count = capture_rate.shape[1]
    slots = slot_wavenumber.shape[0]
    blocks = modes // BLK
    chunks = DEG // CHUNK
    tiles = -(-CHAN * row_count // LANES)
    band_index = lax.axis_index("band")
    table = slot_wavenumber.reshape(bands, modes)
    rank = jnp.sum((table[:, None, :] < table[:, :, None]).astype(jnp.int32), 2)
    match = rank[:, None, :] == jnp.arange(modes, dtype=jnp.int32)[None, :, None]
    ordered = jnp.sum(jnp.where(match, table[:, None, :], 0), 2).reshape(slots)
    place_row = jnp.arange(modes, dtype=jnp.int32)[None, None, :]
    places = jnp.sum(jnp.where(match, place_row, 0), 2).reshape(slots)
    rows = jnp.asarray(latitude_rows())
    spread = jnp.asarray(spread_matrix())
    latitude = row_latitude.reshape(1, NLAT)
    coeffs = spectrum.reshape(CHAN, modes, DEG)
    params = pltpu.CompilerParams(vmem_limit_bytes=16 * 2**20)
    chunk_rows = tiles * modes
    dims = (bands, row_count, modes, blocks, tiles)
    scalars = jnp.asarray(degree_scalars())
    per_order = pltpu.VMEM((modes, DEG), F32)

    def exchange(value):
        return lax.all_to_all(value, "band", split_axis=0, concat_axis=0, tiled=True)

    sent = pl.pallas_call(
        lambda *refs: synth_kernel(dims, *refs),
        out_shape=jax.ShapeDtypeStruct((bands, chunk_rows, LANES), F32),
        in_specs=[SMEM, SMEM, SMEM, VMEM, VMEM, VMEM, VMEM],
        out_specs=VMEM,
        scratch_shapes=[per_order] * 3
        + [pltpu.VMEM((chunks, 2 * ROWS, CHUNK * BLK), BF)]
        + [pltpu.VMEM((2, CHUNK // 2 * BLK, HALF), BF)] * 4
        + [
            pltpu.VMEM((2, ROWS, HALF), F32),
            pltpu.VMEM((HALF, NLAT), BF),
            pltpu.VMEM((CHAN, BLK, DEG), F32),
        ],
        compiler_params=params,
        cost_estimate=work(15),
        name="synth",
    )(ordered, places, scalars, coeffs, rows, spread, latitude)
    received = exchange(sent)

    trig_shape = jax.ShapeDtypeStruct((2, slots, NLON // 2), BF)
    trig_high, trig_low = pl.pallas_call(
        trig_kernel,
        out_shape=[trig_shape, trig_shape],
        out_specs=[VMEM, VMEM],
        scratch_shapes=[pltpu.VMEM((slots // 2, LANES), F32)] * 2,
        compiler_params=params,
        cost_estimate=work(4),
        name="trig",
    )()

    my_latitudes = lax.dynamic_slice_in_dim(row_latitude, band_index * row_count, row_count)
    row_sine = jnp.sin(jnp.pi * (my_latitudes.astype(F32) + 0.5) / NLAT)
    row_sine = jnp.broadcast_to(row_sine[:, None], (row_count, LANES))
    orders = jnp.broadcast_to(ordered.reshape(slots, 1), (slots, LANES))
    group = FIELDS * row_count
    padded = -(-group // LANES) * LANES
    grid_dims = (bands, row_count, modes, tiles, slots)
    fluxes = pl.pallas_call(
        lambda *refs: grid_kernel(grid_dims, *refs),
        out_shape=jax.ShapeDtypeStruct((bands, chunk_rows + 8, LANES), F32),
        in_specs=[VMEM] * 6,
        out_specs=VMEM,
        scratch_shapes=[
            pltpu.VMEM((slots, slots), BF),
            pltpu.VMEM((2, 2 * group, slots), BF),
            pltpu.VMEM((2, 2 * padded, KTILE), BF),
            pltpu.VMEM((2, slots, padded), F32),
        ],
        compiler_params=params,
        cost_estimate=work(8),
        name="grid",
    )(received, orders, capture_rate.reshape(row_count, NLON), row_sine, trig_high, trig_low)
    returned = exchange(fluxes)

    chunk_shape = (chunks, 2 * CHUNK * BLK, HALF)
    *legendre, within = pl.pallas_call(
        lambda *refs: table_kernel((modes, blocks), *refs),
        out_shape=[jax.ShapeDtypeStruct(chunk_shape, BF)] * blocks
        + [jax.ShapeDtypeStruct((modes, DEG), F32)],
        in_specs=[SMEM, SMEM, VMEM],
        out_specs=[VMEM] * (blocks + 1),
        scratch_shapes=[per_order] * 2,
        compiler_params=params,
        cost_estimate=work(12),
        name="table",
    )(ordered, scalars, rows)
    result = pl.pallas_call(
        lambda *refs: analyze_kernel(dims, chunk_rows, *refs),
        out_shape=jax.ShapeDtypeStruct((CHAN, modes, DEG), F32),
        in_specs=[SMEM, SMEM] + [VMEM] * (3 + blocks),
        out_specs=VMEM,
        scratch_shapes=[
            pltpu.VMEM((HALF, 2 * LANES), BF),
            pltpu.VMEM((DEG, LANES), F32),
            pltpu.VMEM((HALF, NLAT), BF),
            pltpu.VMEM((CHAN, BLK, DEG), F32),
        ],
        compiler_params=params,
        cost_estimate=work(9),
        name="analyze",
    )(ordered, places, returned, latitude, within, *legendre)
    return result.reshape(1, FIELDS, 2, modes, DEG)


def solution(mesh):
    return jax.shard_map(
        per_device,
        mesh=mesh,
        in_specs=(P("shell", None, None, "band", None), P("shell", "band", None), P(), P()),
        out_specs=P("shell", None, None, "band", None),
        check_vma=False,
    )
```

```python
import functools
import math

import jax
import jax.numpy as jnp
import numpy as np
from jax import lax
from jax.experimental import pallas as pl
from jax.experimental.pallas import tpu as pltpu
from jax.sharding import PartitionSpec as P

DEG = 512
NLAT = 1024
NLON = 2048
FIELDS = 3
HALF = NLAT // 2
CHAN = 2 * FIELDS
BLK = 8
ROWS = CHAN * BLK
CHUNK = 64
CHECK = 16
LANES = 128
KTILE = 256
BF = jnp.bfloat16
F32 = jnp.float32


def split_two(value):
    high = value.astype(BF)
    low = (value - high.astype(F32)).astype(BF)
    return high, low


def dot(lhs, rhs, contract_rhs=0):
    return lax.dot_general(
        lhs, rhs, (((1,), (contract_rhs,)), ((), ())), preferred_element_type=F32
    )


def latitude_rows():
    theta = np.pi * (np.arange(HALF) + 0.5) / NLAT
    index = np.arange(DEG, dtype=np.float64)
    log_terms = np.zeros(DEG)
    log_terms[1:] = 0.5 * np.log2((2.0 * index[1:] + 1.0) / (2.0 * index[1:]))
    rows = np.zeros((8, DEG))
    rows[0], rows[1], rows[2] = np.cos(theta), np.log2(np.sin(theta)), log_terms
    return rows.astype(np.float32)


def spread_matrix():
    spread = np.zeros((LANES, 2, 2, CHUNK // 2, BLK), np.float32)
    for half in range(2):
        for parity in range(2):
            for step in range(CHUNK // 2):
                spread[half * CHUNK + 2 * step + parity, half, parity, step, :] = 1.0
    return spread.reshape(LANES, 2 * 2 * (CHUNK // 2) * BLK).astype(BF)


def degree_scalars():
    before = np.arange(DEG, dtype=np.float64) - 1.0
    square = before * before
    return np.concatenate([square, 4.0 / (4.0 * square - 1.0)]).astype(np.float32)


def block_orders(slots_ref, first):
    sublane = lax.broadcasted_iota(jnp.int32, (BLK, LANES), 0)
    orders = jnp.zeros((BLK, LANES), jnp.int32)
    lowest = jnp.int32(DEG)
    for i in range(BLK):
        order = slots_ref[first + i]
        orders = jnp.where(sublane == i, order, orders)
        lowest = jnp.minimum(lowest, order)
    return orders, lowest


def running_sum(terms, length):
    lane = lax.broadcasted_iota(jnp.int32, terms.shape, 1) & (length - 1)
    shift = 1
    while shift < length:
        moved = pltpu.roll(terms, shift, 1)
        terms = terms + jnp.where(lane >= shift, moved, 0.0)
        shift *= 2
    return terms


def recursion_tables(slots_ref, modes, rows_ref, start_ref, before_ref, within_ref):
    orders = [block_orders(slots_ref, at)[0][:, :1] for at in range(0, modes, BLK)]
    order = jnp.concatenate(orders, 0).astype(F32)
    position = lax.broadcasted_iota(jnp.int32, (modes, DEG), 1)
    degree = position.astype(F32)
    square = degree * degree
    above = degree > order
    gap = jnp.where(above, square - order * order, 1.0)
    growth = jnp.where(above, 0.5 * jnp.log2((square - 0.25) / gap), 0.0)
    before_ref[...] = running_sum(growth, DEG)
    later = jnp.where(position & (CHECK - 1) == 0, 0.0, growth)
    within_ref[...] = jnp.exp2(running_sum(later, CHECK))
    terms = jnp.where(degree <= order, rows_ref[2:3, :], 0.0)
    norm = jnp.where(order > 0, 0.5 + jnp.sum(terms, axis=1, keepdims=True), 0.0)
    start_ref[...] = norm + order * rows_ref[1:2, :]


def run_chunk(step, carry, double_cosine, orders, before, scalars_ref, emit, beside):
    current, previous, log_scale = carry
    order = orders.astype(F32)
    order_square = order * order
    before = pltpu.roll(before, (step % 2) * CHUNK, 1)
    scale = None
    for i in range(CHUNK):
        if i % CHECK == 0:
            size = jnp.maximum(jnp.abs(current), jnp.abs(previous))
            large, small = size > 2.0**40, size < 2.0**-40
            factor = jnp.where(large, 2.0**-60, jnp.where(small, 2.0**60, 1.0))
            change = jnp.where(large, 60.0, jnp.where(small, -60.0, 0.0))
            current = current * factor
            previous = previous * factor
            log_scale = log_scale + change
            scale = jnp.exp2(jnp.maximum(log_scale + before[:, i : i + 1], -200.0))
        degree = step * CHUNK + i
        factor = (scalars_ref[degree] - order_square) * scalars_ref[DEG + degree]
        factor = jnp.tile(factor, (1, HALF // LANES))
        started = jnp.tile(orders, (1, HALF // LANES)) < degree
        newest = jnp.where(started, double_cosine * current - factor * previous, 1.0)
        current, previous = newest, current
        emit(i, newest * scale)
        if beside and i % (CHUNK // len(beside)) == 1:
            beside[i // (CHUNK // len(beside))]()
    return current, previous, log_scale


def before_tile(before_ref, block, step):
    rows = pl.ds(pl.multiple_of(block * BLK, BLK), BLK)
    return before_ref[rows, pl.ds(pl.multiple_of(step // 2 * LANES, LANES), LANES)]


def start_state(start_ref, block):
    ones = jnp.ones((BLK, HALF), F32)
    return ones, ones, start_ref[pl.ds(pl.multiple_of(block * BLK, BLK), BLK), :]


def fold_matrix(latitude_ref, fold_ref):
    latitude = latitude_ref[...]
    north = jnp.where(latitude < HALF, latitude, NLAT - 1 - latitude)
    sublane = lax.broadcasted_iota(jnp.int32, (HALF, NLAT), 0)
    fold_ref[...] = jnp.where(sublane == north, 1.0, 0.0).astype(BF)


def synth_kernel(
    dims, slots_ref, scalars_ref, spec_ref, rows_ref, spread_ref, latitude_ref,
    out_ref, start_ref, before_ref, within_ref, lhs_ref, high_a, low_a, high_b, low_b, acc_ref, fold_ref, coeff_ref,
):
    bands, row_count, modes, blocks, tiles = dims
    fold_matrix(latitude_ref, fold_ref)
    recursion_tables(slots_ref, modes, rows_ref, start_ref, before_ref, within_ref)
    south = latitude_ref[...] >= HALF
    spread_width = 4 * (CHUNK // 2) * BLK
    lane = lax.broadcasted_iota(jnp.int32, (2 * ROWS, spread_width), 1)
    sub = lax.broadcasted_iota(jnp.int32, (2 * ROWS, spread_width), 0)
    diagonal = (lane % BLK) == (sub % BLK)
    width = (CHUNK // 2) * BLK

    def one_block(block, unused):
        orders, lowest = block_orders(slots_ref, block * BLK)
        column = orders[:, :1]
        here = pl.ds(pl.multiple_of(block * BLK, BLK), BLK)
        for i in range(BLK):
            source = pl.ds(slots_ref[modes + block * BLK + i], 1)
            coeff_ref[:, i : i + 1, :] = spec_ref[:, source, :]
        degree = lax.broadcasted_iota(jnp.int32, (BLK, DEG), 1)
        within = jnp.where(degree >= column, within_ref[here, :], 0.0)
        coeffs = coeff_ref[...] * within[None]
        coeff_high, coeff_low = split_two(coeffs.reshape(ROWS, DEG))
        stacked = jnp.concatenate([coeff_high, coeff_low], 0)
        for t in range(DEG // LANES):
            wide = dot(stacked[:, t * LANES : (t + 1) * LANES], spread_ref[...])
            wide = jnp.where(diagonal, wide, 0.0).astype(BF)
            for half in range(2):
                lhs_ref[2 * t + half] = wide[:, half * 2 * width : (half + 1) * 2 * width]
        acc_ref[block] = jnp.zeros((2, ROWS, HALF), F32)
        cosine = jnp.broadcast_to(2.0 * rows_ref[0:1, :], (BLK, HALF))

        def recur(step, carry, high_ref, low_ref, beside):
            held = {}

            def emit(i, value):
                if i % 4 < 2:
                    held[i] = value
                else:
                    pair = jnp.concatenate([held.pop(i - 2), value], 0)
                    high, low = split_two(pair)
                    at = (i // 4) * 2 * BLK
                    high_ref[i % 2, at : at + 2 * BLK, :] = high
                    low_ref[i % 2, at : at + 2 * BLK, :] = low

            before = before_tile(before_ref, block, step)
            return run_chunk(step, carry, cosine, orders, before, scalars_ref, emit, beside)

        def add_products(step, high_ref, low_ref):
            def part(parity, columns):
                lhs = lhs_ref[step, :, parity * width : (parity + 1) * width]
                first = dot(lhs, high_ref[parity, :, columns])
                second = dot(lhs[:ROWS], low_ref[parity, :, columns])
                acc_ref[block, parity, :, columns] += first[:ROWS] + first[ROWS:] + second

            return [
                functools.partial(part, parity, slice(at, at + KTILE))
                for parity in range(2)
                for at in range(0, HALF, KTILE)
            ]

        def two_chunks(pair, carry):
            step = 2 * pair
            beside = add_products(jnp.maximum(step - 1, 0), high_b, low_b)
            carry = recur(step, carry, high_a, low_a, beside)
            beside = add_products(step, high_a, low_a)
            return recur(step + 1, carry, high_b, low_b, beside)

        high_b[...] = jnp.zeros_like(high_b)
        low_b[...] = jnp.zeros_like(low_b)
        chunks = DEG // CHUNK
        lax.fori_loop(lowest // (2 * CHUNK), chunks // 2, two_chunks, start_state(start_ref, block))
        for part in add_products(chunks - 1, high_b, low_b):
            part()
        return unused

    lax.fori_loop(0, blocks, one_block, 0)
    high, low = split_two(acc_ref[...].reshape(blocks * 2 * ROWS, HALF))
    moved = dot(jnp.concatenate([high, low], 0), fold_ref[...])
    moved = moved[: blocks * 2 * ROWS] + moved[blocks * 2 * ROWS :]
    for block in range(blocks):
        orders = block_orders(slots_ref, block * BLK)[0][:, :1]
        sign = jnp.tile(1.0 - 2.0 * (orders % 2).astype(F32), (CHAN, 1))
        even = moved[block * 2 * ROWS : block * 2 * ROWS + ROWS]
        odd = moved[block * 2 * ROWS + ROWS : (block + 1) * 2 * ROWS]
        values = jnp.where(south, sign * (even - odd), even + odd)
        for d in range(bands):
            parts = []
            for kind in range(2):
                for field in range(FIELDS):
                    c = field * 2 + kind
                    parts.append(
                        values[c * BLK : (c + 1) * BLK, d * row_count : (d + 1) * row_count]
                    )
            if CHAN * row_count < tiles * LANES:
                parts.append(jnp.zeros((BLK, tiles * LANES - CHAN * row_count), F32))
            joined = jnp.concatenate(parts, 1)
            for t in range(tiles):
                at = slice((t * blocks + block) * BLK, (t * blocks + block + 1) * BLK)
                out_ref[d, at, :] = joined[:, t * LANES : (t + 1) * LANES]


def table_kernel(
    blocks, slots_ref, scalars_ref, rows_ref, out_ref, within_out, start_ref, before_ref,
    chunk_ref, sems,
):
    modes = blocks * BLK
    cosine = jnp.broadcast_to(2.0 * rows_ref[0:1, :], (BLK, HALF))
    recursion_tables(slots_ref, modes, rows_ref, start_ref, before_ref, within_out)

    def copy_out(block, step):
        return pltpu.make_async_copy(
            chunk_ref.at[block, step], out_ref.at[block, step], sems.at[block, step]
        )

    def one_block(block, unused):
        orders, lowest = block_orders(slots_ref, block * BLK)

        def one_chunk(step, carry):
            held = {}

            def emit(i, value):
                if i % 2 == 0:
                    held[i] = value
                else:
                    pair = jnp.concatenate([held.pop(i - 1), value], 0)
                    high, low = split_two(pair)
                    at = (i // 2) * 2 * BLK
                    chunk_ref[block, step, at : at + 2 * BLK, :HALF] = high
                    chunk_ref[block, step, at : at + 2 * BLK, HALF:] = low

            before = before_tile(before_ref, block, step)
            carry = run_chunk(step, carry, cosine, orders, before, scalars_ref, emit, ())
            copy_out(block, step).start()
            return carry

        first = lowest // (2 * CHUNK) * 2
        lax.fori_loop(first, DEG // CHUNK, one_chunk, start_state(start_ref, block))
        return unused

    def finish_block(block, unused):
        orders, lowest = block_orders(slots_ref, block * BLK)

        def finish_chunk(step, inner):
            copy_out(block, step).wait()
            return inner

        return lax.fori_loop(lowest // (2 * CHUNK) * 2, DEG // CHUNK, finish_chunk, unused)

    lax.fori_loop(0, blocks, one_block, 0)
    lax.fori_loop(0, blocks, finish_block, 0)


def analyze_kernel(
    dims, total_row, slots_ref, data_ref, column_ref, latitude_ref, within_ref, table_ref,
    out_ref, chunk_ref, weight_ref, stack_ref, result_ref, fold_ref, coeff_ref, sems,
):
    bands, row_count, modes, blocks, tiles = dims
    chunks = DEG // CHUNK

    def copy_in(block, step):
        return pltpu.make_async_copy(
            table_ref.at[block, step], chunk_ref.at[block, step], sems.at[block, step]
        )

    def start_block(block, unused):
        orders, lowest = block_orders(slots_ref, block * BLK)

        def start_chunk(step, inner):
            copy_in(block, step).start()
            return inner

        return lax.fori_loop(lowest // (2 * CHUNK) * 2, chunks, start_chunk, unused)

    lax.fori_loop(0, blocks, start_block, 0)
    latitude = column_ref[...]
    north = jnp.where(latitude < HALF, latitude, NLAT - 1 - latitude)
    lane = lax.broadcasted_iota(jnp.int32, (NLAT, LANES), 1)
    for t in range(HALF // LANES):
        one_hot = jnp.where(north == lane + t * LANES, 1.0, 0.0).astype(BF)
        fold_ref[:, t * LANES : (t + 1) * LANES] = one_hot
    south = latitude_ref[...] >= HALF
    for block in range(blocks):
        orders = block_orders(slots_ref, block * BLK)[0][:, :1]
        sign = 1.0 - 2.0 * (orders % 2).astype(F32)
        evens, odds = [], []
        for c in range(CHAN):
            offset = ((c % 2) * FIELDS + c // 2) * row_count
            t, at = offset // LANES, offset % LANES
            rows = slice((t * blocks + block) * BLK, (t * blocks + block + 1) * BLK)
            values = jnp.concatenate(
                [data_ref[d, rows, :][:, at : at + row_count] for d in range(bands)], 1
            )
            flipped = sign * values
            evens.append(jnp.where(south, flipped, values))
            odds.append(jnp.where(south, -flipped, values))
        high, low = split_two(jnp.concatenate(evens + odds, 0))
        stack_ref[block * 4 * ROWS : block * 4 * ROWS + 2 * ROWS, :] = high
        stack_ref[block * 4 * ROWS + 2 * ROWS : (block + 1) * 4 * ROWS, :] = low
    folded = dot(stack_ref[...], fold_ref[...])
    for block in range(blocks):
        at = block * 4 * ROWS
        part = folded[at : at + 2 * ROWS] + folded[at + 2 * ROWS : at + 4 * ROWS]
        part = jnp.concatenate([part, jnp.zeros((LANES - 2 * ROWS, HALF), F32)], 0)
        high, low = split_two(part.T)
        weight_ref[block, :HALF, :LANES] = high
        weight_ref[block, :HALF, LANES:] = low
        weight_ref[block, HALF:, :LANES] = high
        weight_ref[block, HALF:, LANES:] = jnp.zeros_like(low)

    total = data_ref[0, total_row : total_row + 8]
    for d in range(1, bands):
        total = total + data_ref[d, total_row : total_row + 8]
    inverse = (1.0 / total)[:, :1]
    lane = lax.broadcasted_iota(jnp.int32, (CHUNK * BLK, LANES), 1)
    sub = lax.broadcasted_iota(jnp.int32, (CHUNK * BLK, LANES), 0)
    keep = (lane % BLK == sub % BLK) & (lane // ROWS == sub // BLK % 2)

    def one_block(block, unused):
        orders, lowest = block_orders(slots_ref, block * BLK)
        orders = orders[:, :1]
        here = pl.ds(pl.multiple_of(block * BLK, BLK), BLK)
        result_ref[...] = jnp.zeros_like(result_ref)

        def two_chunks(pair, inner):
            for step in (2 * pair, 2 * pair + 1):
                copy_in(block, step).wait()
            for step in (2 * pair, 2 * pair + 1):
                full = dot(chunk_ref[block, step], weight_ref[block])
                full = full[:, :LANES] + full[:, LANES:]
                picked = jnp.where(keep, full, 0.0).reshape(CHUNK, BLK, LANES)
                to = pl.ds(pl.multiple_of(step * CHUNK, CHUNK), CHUNK)
                result_ref[to, :] = jnp.sum(picked, axis=1)
            return inner

        lax.fori_loop(lowest // (2 * CHUNK), chunks // 2, two_chunks, 0)
        turned = result_ref[...].T
        turned = turned[:ROWS] + turned[ROWS : 2 * ROWS]
        degree = lax.broadcasted_iota(jnp.int32, (BLK, DEG), 1)
        within = jnp.where(degree >= orders, within_ref[here, :], 0.0)
        for c in range(CHAN):
            part = turned[c * BLK : (c + 1) * BLK] * within
            if c // 2 == FIELDS - 1:
                part = part * inverse
            coeff_ref[c] = part
        for i in range(BLK):
            target = pl.ds(slots_ref[modes + block * BLK + i], 1)
            out_ref[:, target, :] = coeff_ref[:, i : i + 1, :]
        return unused

    lax.fori_loop(0, blocks, one_block, 0)


def base_trig(order, first):
    lane = lax.broadcasted_iota(jnp.int32, order.shape, 1) + first
    phase = (order * lane) & (NLON - 1)
    quarter = (phase + NLON // 8) >> 9
    rest = (phase - quarter * (NLON // 4)).astype(F32) * (2.0 * math.pi / NLON)
    square = rest * rest
    sine = 1.0 / 362880.0
    for coef in (-1.0 / 5040.0, 1.0 / 120.0, -1.0 / 6.0, 1.0):
        sine = sine * square + coef
    sine = sine * rest
    cosine = 1.0 / 40320.0
    for coef in (-1.0 / 720.0, 1.0 / 24.0, -0.5, 1.0):
        cosine = cosine * square + coef
    swap = (quarter & 1) == 1
    cos_out = jnp.where(swap, sine, cosine)
    sin_out = jnp.where(swap, cosine, sine)
    cos_out = jnp.where(((quarter + 1) & 2) == 2, -cos_out, cos_out)
    sin_out = jnp.where((quarter & 2) == 2, -sin_out, sin_out)
    return cos_out, sin_out


def trig_kernel(out_ref, trig_ref, sem):
    half = trig_ref.shape[2] // 2
    high_ref, low_ref = trig_ref.at[0], trig_ref.at[1]
    root = math.sqrt(0.5)
    for parity in range(2):

        def strip(step, unused):
            at = pl.multiple_of(step * 64, 64)
            shape = (64, LANES)
            order = 2 * (lax.broadcasted_iota(jnp.int32, shape, 0) + at) + parity
            eighth = order & 7
            odd = (eighth & 1) == 1
            turn_cos = jnp.where(odd, root, jnp.where((eighth & 2) == 0, 1.0, 0.0))
            turn_sin = jnp.where(odd, root, jnp.where((eighth & 2) == 2, 1.0, 0.0))
            turn_cos = jnp.where((eighth >= 3) & (eighth <= 5), -turn_cos, turn_cos)
            turn_sin = jnp.where(eighth > 4, -turn_sin, turn_sin)
            for t in range(KTILE // LANES):
                cosine, sine = base_trig(order, t * LANES)
                for k in range(t * LANES, NLON // 2, KTILE):
                    columns = slice(k, k + LANES)
                    high, low = split_two(cosine)
                    high_ref[parity, pl.ds(at, 64), columns] = high
                    low_ref[parity, pl.ds(at, 64), columns] = low
                    high, low = split_two(sine)
                    high_ref[parity, pl.ds(half + at, 64), columns] = high
                    low_ref[parity, pl.ds(half + at, 64), columns] = low
                    cosine, sine = (
                        cosine * turn_cos - sine * turn_sin,
                        sine * turn_cos + cosine * turn_sin,
                    )
            return unused

        lax.fori_loop(0, half // 64, strip, 0)
    copy = pltpu.make_async_copy(trig_ref, out_ref, sem)
    copy.start()
    copy.wait()


def grid_kernel(
    dims, data_ref, orders_ref, rate_ref, sine_ref, trig_in, out_ref,
    move_ref, lhs_ref, weight_ref, acc_ref, trig_ref, sem,
):
    bands, row_count, modes, tiles, slots = dims
    half = slots // 2
    group = FIELDS * row_count
    padded = weight_ref.shape[1] // 2

    copy = pltpu.make_async_copy(trig_in, trig_ref, sem)
    copy.start()
    trig_high, trig_low = trig_ref.at[0], trig_ref.at[1]
    order = orders_ref[...]
    natural = (order & 1) * half + (order >> 1)
    for t in range(slots // LANES):
        lane = lax.broadcasted_iota(jnp.int32, (slots, LANES), 1) + t * LANES
        one_hot = jnp.where(natural == lane, 1.0, 0.0).astype(BF)
        move_ref[:, t * LANES : (t + 1) * LANES] = one_hot
    columns = []
    for t in range(tiles):
        part = data_ref[:, t * modes : (t + 1) * modes, :]
        columns.append(part.reshape(slots, LANES).T)
    turned = jnp.concatenate(columns, 0)
    for kind in range(2):
        high, low = split_two(turned[kind * group : (kind + 1) * group])
        moved = dot(jnp.concatenate([high, low], 0), move_ref[...]).astype(BF)
        for parity in range(2):
            part = moved[:, parity * half : (parity + 1) * half]
            lhs_ref[parity, :, kind * half : (kind + 1) * half] = part
    weight_ref[...] = jnp.zeros_like(weight_ref)
    flux_scale = math.pi / (2.0 * NLAT * NLON * DEG)
    weight = jnp.tile(sine_ref[...], (1, KTILE // LANES))
    total = jnp.zeros((8, KTILE), F32)
    copy.wait()

    for k in range(0, NLON // 2, KTILE):
        tile = slice(k, k + KTILE)
        sums = []
        for parity in range(2):
            first = dot(lhs_ref[parity], trig_high[parity, :, tile])
            second = dot(lhs_ref[parity, :group, :], trig_low[parity, :, tile])
            sums.append(first[:group] + first[group:] + second)
        values = []
        for fields, at in ((sums[0] + sums[1], k), (sums[0] - sums[1], k + NLON // 2)):
            weighted_rate = rate_ref[:, at : at + KTILE] * weight
            total = total + jnp.sum(weighted_rate.reshape(row_count // 8, 8, KTILE), axis=0)
            scaled = fields[:row_count] * (weight * flux_scale)
            values.append(
                jnp.concatenate(
                    [
                        fields[row_count : 2 * row_count] * scaled,
                        fields[2 * row_count :] * scaled,
                        weighted_rate * fields[:row_count],
                    ],
                    0,
                )
            )
        for parity in range(2):
            both = values[0] + values[1] if parity == 0 else values[0] - values[1]
            high, low = split_two(both)
            weight_ref[parity, :group, :] = high
            weight_ref[parity, padded : padded + group, :] = low
            first = dot(trig_high[parity, :, tile], weight_ref[parity], 1)
            second = dot(trig_low[parity, :, tile], weight_ref[parity, :padded, :], 1)
            part = first[:, :padded] + first[:, padded:] + second
            if k == 0:
                acc_ref[parity] = part
            else:
                acc_ref[parity] += part

    joined = []
    for kind in range(2):
        rows = slice(kind * half, (kind + 1) * half)
        joined.append(jnp.concatenate([acc_ref[0, rows, :group], acc_ref[1, rows, :group]], 0))
    if 2 * group < tiles * LANES:
        joined.append(jnp.zeros((slots, tiles * LANES - 2 * group), F32))
    high, low = split_two(jnp.concatenate(joined, 1))
    moved = dot(move_ref[...], jnp.concatenate([high, low], 1))
    moved = moved[:, : tiles * LANES] + moved[:, tiles * LANES :]
    for t in range(tiles):
        part = moved[:, t * LANES : (t + 1) * LANES]
        out_ref[:, t * modes : (t + 1) * modes, :] = part.reshape(bands, modes, LANES)
    out_ref[:, tiles * modes :, :] = jnp.broadcast_to(jnp.sum(total), (bands, 8, LANES))


VMEM = pl.BlockSpec(memory_space=pltpu.VMEM)
SMEM = pl.BlockSpec(memory_space=pltpu.SMEM)
ANY = pl.BlockSpec(memory_space=pl.ANY)


def work(microseconds):
    return pl.CostEstimate(
        flops=microseconds * 10**9, bytes_accessed=2**20, transcendentals=0
    )


def per_device(spectrum, capture_rate, row_latitude, slot_wavenumber):
    bands = lax.axis_size("band")
    modes = spectrum.shape[3]
    row_count = capture_rate.shape[1]
    slots = slot_wavenumber.shape[0]
    blocks = modes // BLK
    chunks = DEG // CHUNK
    tiles = -(-CHAN * row_count // LANES)
    band_index = lax.axis_index("band")

    def sort_rows(table):
        rank = jnp.sum((table[:, None, :] < table[:, :, None]).astype(jnp.int32), 2)
        match = rank[:, None, :] == jnp.arange(modes, dtype=jnp.int32)[None, :, None]
        places = jnp.arange(modes, dtype=jnp.int32)[None, None, :]
        return [
            jnp.sum(jnp.where(match, values, 0), 2).reshape(-1)
            for values in (table[:, None, :], places)
        ]

    own = lax.dynamic_slice_in_dim(slot_wavenumber, band_index * modes, modes)
    local = jnp.concatenate(sort_rows(own.reshape(1, modes)))
    ordered = sort_rows(slot_wavenumber.reshape(bands, modes))[0]
    rows = jnp.asarray(latitude_rows())
    spread = jnp.asarray(spread_matrix())
    latitude = row_latitude.reshape(1, NLAT)
    coeffs = spectrum.reshape(CHAN, modes, DEG)
    params = pltpu.CompilerParams(vmem_limit_bytes=48 * 2**20)
    chunk_rows = tiles * modes
    dims = (bands, row_count, modes, blocks, tiles)
    scalars = jnp.asarray(degree_scalars())
    per_order = pltpu.VMEM((modes, DEG), F32)

    def exchange(value):
        return lax.all_to_all(value, "band", split_axis=0, concat_axis=0, tiled=True)

    sent = pl.pallas_call(
        lambda *refs: synth_kernel(dims, *refs),
        out_shape=jax.ShapeDtypeStruct((bands, chunk_rows, LANES), F32),
        in_specs=[SMEM, SMEM, VMEM, VMEM, VMEM, VMEM],
        out_specs=VMEM,
        scratch_shapes=[per_order] * 3
        + [pltpu.VMEM((chunks, 2 * ROWS, CHUNK * BLK), BF)]
        + [pltpu.VMEM((2, CHUNK // 2 * BLK, HALF), BF)] * 4
        + [
            pltpu.VMEM((blocks, 2, ROWS, HALF), F32),
            pltpu.VMEM((HALF, NLAT), BF),
            pltpu.VMEM((CHAN, BLK, DEG), F32),
        ],
        compiler_params=params,
        cost_estimate=work(15),
        name="synth",
    )(local, scalars, coeffs, rows, spread, latitude)
    received = exchange(sent)

    trig_shape = (2, 2, slots, NLON // 2)
    trig_scratch = [pltpu.VMEM(trig_shape, BF), pltpu.SemaphoreType.DMA(())]
    trig = pl.pallas_call(
        trig_kernel,
        out_shape=jax.ShapeDtypeStruct(trig_shape, BF),
        out_specs=ANY,
        scratch_shapes=trig_scratch,
        compiler_params=params,
        cost_estimate=work(4),
        name="trig",
    )()

    my_latitudes = lax.dynamic_slice_in_dim(row_latitude, band_index * row_count, row_count)
    row_sine = jnp.sin(jnp.pi * (my_latitudes.astype(F32) + 0.5) / NLAT)
    row_sine = jnp.broadcast_to(row_sine[:, None], (row_count, LANES))
    orders = jnp.broadcast_to(ordered.reshape(slots, 1), (slots, LANES))
    group = FIELDS * row_count
    padded = -(-group // LANES) * LANES
    grid_dims = (bands, row_count, modes, tiles, slots)
    fluxes = pl.pallas_call(
        lambda *refs: grid_kernel(grid_dims, *refs),
        out_shape=jax.ShapeDtypeStruct((bands, chunk_rows + 8, LANES), F32),
        in_specs=[VMEM] * 4 + [ANY],
        out_specs=VMEM,
        scratch_shapes=[
            pltpu.VMEM((slots, slots), BF),
            pltpu.VMEM((2, 2 * group, slots), BF),
            pltpu.VMEM((2, 2 * padded, KTILE), BF),
            pltpu.VMEM((2, slots, padded), F32),
        ]
        + trig_scratch,
        compiler_params=params,
        cost_estimate=work(8),
        name="grid",
    )(received, orders, capture_rate.reshape(row_count, NLON), row_sine, trig)
    returned = exchange(fluxes)

    chunk_shape = (blocks, chunks, CHUNK * BLK, 2 * HALF)
    legendre, within = pl.pallas_call(
        lambda *refs: table_kernel(blocks, *refs),
        out_shape=[
            jax.ShapeDtypeStruct(chunk_shape, BF),
            jax.ShapeDtypeStruct((modes, DEG), F32),
        ],
        in_specs=[SMEM, SMEM, VMEM],
        out_specs=[ANY, VMEM],
        scratch_shapes=[per_order] * 2
        + [pltpu.VMEM(chunk_shape, BF), pltpu.SemaphoreType.DMA((blocks, chunks))],
        compiler_params=params,
        cost_estimate=work(12),
        name="table",
    )(local, scalars, rows)
    column = jnp.broadcast_to(row_latitude[:, None], (NLAT, LANES))
    result = pl.pallas_call(
        lambda *refs: analyze_kernel(dims, chunk_rows, *refs),
        out_shape=jax.ShapeDtypeStruct((CHAN, modes, DEG), F32),
        in_specs=[SMEM, VMEM, VMEM, VMEM, VMEM, ANY],
        out_specs=VMEM,
        scratch_shapes=[
            pltpu.VMEM(chunk_shape, BF),
            pltpu.VMEM((blocks, 2 * HALF, 2 * LANES), BF),
            pltpu.VMEM((blocks * 4 * ROWS, NLAT), BF),
            pltpu.VMEM((DEG, LANES), F32),
            pltpu.VMEM((NLAT, HALF), BF),
            pltpu.VMEM((CHAN, BLK, DEG), F32),
            pltpu.SemaphoreType.DMA((blocks, chunks)),
        ],
        compiler_params=params,
        cost_estimate=work(9),
        name="analyze",
    )(local, returned, column, latitude, within, legendre)
    return result.reshape(1, FIELDS, 2, modes, DEG)


def solution(mesh):
    return jax.shard_map(
        per_device,
        mesh=mesh,
        in_specs=(P("shell", None, None, "band", None), P("shell", "band", None), P(), P()),
        out_specs=P("shell", None, None, "band", None),
        check_vma=False,
    )
```

```python
import functools
import math

import jax
import jax.numpy as jnp
import numpy as np
from jax import lax
from jax.experimental import pallas as pl
from jax.experimental.pallas import tpu as pltpu
from jax.sharding import PartitionSpec as P

DEG = 512
NLAT = 1024
NLON = 2048
FIELDS = 3
HALF = NLAT // 2
CHAN = 2 * FIELDS
BLK = 8
ROWS = CHAN * BLK
CHUNK = 64
CHECK = 16
LANES = 128
KTILE = 256
BF = jnp.bfloat16
F32 = jnp.float32


def split_two(value):
    high = value.astype(BF)
    low = (value - high.astype(F32)).astype(BF)
    return high, low


def dot(lhs, rhs, contract_rhs=0):
    return lax.dot_general(
        lhs, rhs, (((1,), (contract_rhs,)), ((), ())), preferred_element_type=F32
    )


def latitude_rows():
    theta = np.pi * (np.arange(HALF) + 0.5) / NLAT
    index = np.arange(DEG, dtype=np.float64)
    log_terms = np.zeros(DEG)
    log_terms[1:] = 0.5 * np.log2((2.0 * index[1:] + 1.0) / (2.0 * index[1:]))
    rows = np.zeros((8, DEG))
    rows[0], rows[1], rows[2] = np.cos(theta), np.log2(np.sin(theta)), log_terms
    return rows.astype(np.float32)


def spread_matrix():
    spread = np.zeros((LANES, 2, 2, CHUNK // 2, BLK), np.float32)
    for half in range(2):
        for parity in range(2):
            for step in range(CHUNK // 2):
                spread[half * CHUNK + 2 * step + parity, half, parity, step, :] = 1.0
    return spread.reshape(LANES, 2 * 2 * (CHUNK // 2) * BLK).astype(BF)


def degree_scalars():
    before = np.arange(DEG, dtype=np.float64) - 1.0
    square = before * before
    return np.concatenate([square, 4.0 / (4.0 * square - 1.0)]).astype(np.float32)


def block_orders(slots_ref, first):
    sublane = lax.broadcasted_iota(jnp.int32, (BLK, LANES), 0)
    orders = jnp.zeros((BLK, LANES), jnp.int32)
    lowest, highest = jnp.int32(DEG), jnp.int32(0)
    for i in range(BLK):
        order = slots_ref[first + i]
        orders = jnp.where(sublane == i, order, orders)
        lowest, highest = jnp.minimum(lowest, order), jnp.maximum(highest, order)
    return orders, lowest // CHUNK, highest // CHUNK + 1


def running_sum(terms, length):
    lane = lax.broadcasted_iota(jnp.int32, terms.shape, 1) & (length - 1)
    shift = 1
    while shift < length:
        moved = pltpu.roll(terms, shift, 1)
        terms = terms + jnp.where(lane >= shift, moved, 0.0)
        shift *= 2
    return terms


def recursion_tables(slots_ref, modes, rows_ref, start_ref, before_ref, within_ref):
    orders = [block_orders(slots_ref, at)[0][:, :1] for at in range(0, modes, BLK)]
    order = jnp.concatenate(orders, 0).astype(F32)
    position = lax.broadcasted_iota(jnp.int32, (modes, DEG), 1)
    degree = position.astype(F32)
    square = degree * degree
    above = degree > order
    gap = jnp.where(above, square - order * order, 1.0)
    growth = jnp.where(above, 0.5 * jnp.log2((square - 0.25) / gap), 0.0)
    before_ref[...] = running_sum(growth, DEG)
    later = jnp.where(position & (CHECK - 1) == 0, 0.0, growth)
    within_ref[...] = jnp.exp2(running_sum(later, CHECK))
    terms = jnp.where(degree <= order, rows_ref[2:3, :], 0.0)
    norm = jnp.where(order > 0, 0.5 + jnp.sum(terms, axis=1, keepdims=True), 0.0)
    start_ref[...] = norm + order * rows_ref[1:2, :]


def run_chunk(step, carry, double_cosine, orders, before, scalars_ref, emit, beside, guard):
    current, previous, log_scale = carry
    order = orders.astype(F32)
    order_square = order * order
    before = pltpu.roll(before, (step % 2) * CHUNK, 1)
    scale = None
    for i in range(CHUNK):
        if i % CHECK == 0:
            size = jnp.maximum(jnp.abs(current), jnp.abs(previous))
            large, small = size > 2.0**40, size < 2.0**-40
            factor = jnp.where(large, 2.0**-60, jnp.where(small, 2.0**60, 1.0))
            change = jnp.where(large, 60.0, jnp.where(small, -60.0, 0.0))
            current = current * factor
            previous = previous * factor
            log_scale = log_scale + change
            scale = jnp.exp2(jnp.maximum(log_scale + before[:, i : i + 1], -200.0))
        degree = step * CHUNK + i
        factor = (scalars_ref[degree] - order_square) * scalars_ref[DEG + degree]
        factor = jnp.tile(factor, (1, HALF // LANES))
        newest = double_cosine * current - factor * previous
        if guard:
            started = jnp.tile(orders, (1, HALF // LANES)) < degree
            newest = jnp.where(started, newest, 1.0)
        current, previous = newest, current
        emit(i, newest * scale)
        if beside and i % (CHUNK // len(beside)) == 1:
            beside[i // (CHUNK // len(beside))]()
    return current, previous, log_scale


def before_tile(before_ref, block, step):
    rows = pl.ds(pl.multiple_of(block * BLK, BLK), BLK)
    return before_ref[rows, pl.ds(pl.multiple_of(step // 2 * LANES, LANES), LANES)]


def start_state(start_ref, block):
    ones = jnp.ones((BLK, HALF), F32)
    return ones, ones, start_ref[pl.ds(pl.multiple_of(block * BLK, BLK), BLK), :]


def fold_matrix(latitude_ref, fold_ref):
    latitude = latitude_ref[...]
    north = jnp.where(latitude < HALF, latitude, NLAT - 1 - latitude)
    sublane = lax.broadcasted_iota(jnp.int32, (HALF, NLAT), 0)
    fold_ref[...] = jnp.where(sublane == north, 1.0, 0.0).astype(BF)


def synth_kernel(
    dims, slots_ref, scalars_in, spec_in, rows_in, spread_in, latitude_in,
    out_ref, scalars_ref, spec_ref, rows_ref, spread_ref, latitude_ref, sems,
    start_ref, before_ref, within_ref, lhs_ref, high_a, low_a, high_b, low_b, acc_ref, fold_ref, coeff_ref,
):
    bands, row_count, modes, blocks, tiles = dims
    pairs = (
        (rows_in, rows_ref), (scalars_in, scalars_ref), (latitude_in, latitude_ref),
        (spread_in, spread_ref), (spec_in, spec_ref),
    )
    copies = []
    for index, (source, target) in enumerate(pairs):
        copies.append(pltpu.make_async_copy(source, target, sems.at[index]))
        copies[-1].start()
    for copy in copies:
        copy.wait()
    fold_matrix(latitude_ref, fold_ref)
    recursion_tables(slots_ref, modes, rows_ref, start_ref, before_ref, within_ref)
    south = latitude_ref[...] >= HALF
    spread_width = 4 * (CHUNK // 2) * BLK
    lane = lax.broadcasted_iota(jnp.int32, (2 * ROWS, spread_width), 1)
    sub = lax.broadcasted_iota(jnp.int32, (2 * ROWS, spread_width), 0)
    diagonal = (lane % BLK) == (sub % BLK)
    width = (CHUNK // 2) * BLK

    def one_block(block, unused):
        orders, first, last = block_orders(slots_ref, block * BLK)
        column = orders[:, :1]
        here = pl.ds(pl.multiple_of(block * BLK, BLK), BLK)
        for i in range(BLK):
            source = pl.ds(slots_ref[modes + block * BLK + i], 1)
            coeff_ref[:, i : i + 1, :] = spec_ref[:, source, :]
        degree = lax.broadcasted_iota(jnp.int32, (BLK, DEG), 1)
        within = jnp.where(degree >= column, within_ref[here, :], 0.0)
        coeffs = coeff_ref[...] * within[None]
        coeff_high, coeff_low = split_two(coeffs.reshape(ROWS, DEG))
        stacked = jnp.concatenate([coeff_high, coeff_low], 0)
        for t in range(DEG // LANES):
            wide = dot(stacked[:, t * LANES : (t + 1) * LANES], spread_ref[...])
            wide = jnp.where(diagonal, wide, 0.0).astype(BF)
            for half in range(2):
                lhs_ref[2 * t + half] = wide[:, half * 2 * width : (half + 1) * 2 * width]
        acc_ref[block] = jnp.zeros((2, ROWS, HALF), F32)
        cosine = jnp.broadcast_to(2.0 * rows_ref[0:1, :], (BLK, HALF))

        def recur(step, carry, high_ref, low_ref, beside, guard):
            held = {}

            def emit(i, value):
                if i % 4 < 2:
                    held[i] = value
                else:
                    pair = jnp.concatenate([held.pop(i - 2), value], 0)
                    high, low = split_two(pair)
                    at = (i // 4) * 2 * BLK
                    high_ref[i % 2, at : at + 2 * BLK, :] = high
                    low_ref[i % 2, at : at + 2 * BLK, :] = low

            before = before_tile(before_ref, block, step)
            return run_chunk(
                step, carry, cosine, orders, before, scalars_ref, emit, beside, guard
            )

        def add_products(step, high_ref, low_ref):
            def part(parity, columns):
                lhs = lhs_ref[step, :, parity * width : (parity + 1) * width]
                first = dot(lhs, high_ref[parity, :, columns])
                second = dot(lhs[:ROWS], low_ref[parity, :, columns])
                acc_ref[block, parity, :, columns] += first[:ROWS] + first[ROWS:] + second

            return [
                functools.partial(part, parity, slice(at, at + KTILE))
                for parity in range(2)
                for at in range(0, HALF, KTILE)
            ]

        def two_chunks(guard, pair, carry):
            step = 2 * pair
            beside = add_products(jnp.maximum(step - 1, 0), high_b, low_b)
            carry = recur(step, carry, high_a, low_a, beside, guard)
            beside = add_products(step, high_a, low_a)
            return recur(step + 1, carry, high_b, low_b, beside, guard)

        high_b[...] = jnp.zeros_like(high_b)
        low_b[...] = jnp.zeros_like(low_b)
        chunks = DEG // CHUNK
        state = lax.fori_loop(
            0,
            first & 1,
            lambda unused, carry: recur(first, carry, high_b, low_b, (), True),
            start_state(start_ref, block),
        )
        middle = (last + 1) // 2
        state = lax.fori_loop(
            (first + 1) // 2, middle, functools.partial(two_chunks, True), state
        )
        lax.fori_loop(middle, chunks // 2, functools.partial(two_chunks, False), state)
        for part in add_products(chunks - 1, high_b, low_b):
            part()
        return unused

    lax.fori_loop(0, blocks, one_block, 0)
    high, low = split_two(acc_ref[...].reshape(blocks * 2 * ROWS, HALF))
    moved = dot(jnp.concatenate([high, low], 0), fold_ref[...])
    moved = moved[: blocks * 2 * ROWS] + moved[blocks * 2 * ROWS :]
    for block in range(blocks):
        orders = block_orders(slots_ref, block * BLK)[0][:, :1]
        sign = jnp.tile(1.0 - 2.0 * (orders % 2).astype(F32), (CHAN, 1))
        even = moved[block * 2 * ROWS : block * 2 * ROWS + ROWS]
        odd = moved[block * 2 * ROWS + ROWS : (block + 1) * 2 * ROWS]
        values = jnp.where(south, sign * (even - odd), even + odd)
        for d in range(bands):
            parts = []
            for kind in range(2):
                for field in range(FIELDS):
                    c = field * 2 + kind
                    parts.append(
                        values[c * BLK : (c + 1) * BLK, d * row_count : (d + 1) * row_count]
                    )
            if CHAN * row_count < tiles * LANES:
                parts.append(jnp.zeros((BLK, tiles * LANES - CHAN * row_count), F32))
            joined = jnp.concatenate(parts, 1)
            for t in range(tiles):
                at = slice((t * blocks + block) * BLK, (t * blocks + block + 1) * BLK)
                out_ref[d, at, :] = joined[:, t * LANES : (t + 1) * LANES]


def table_kernel(
    blocks, slots_ref, scalars_ref, rows_ref, out_ref, within_out, start_ref, before_ref,
    chunk_ref, sems,
):
    modes = blocks * BLK
    cosine = jnp.broadcast_to(2.0 * rows_ref[0:1, :], (BLK, HALF))
    recursion_tables(slots_ref, modes, rows_ref, start_ref, before_ref, within_out)

    def copy_out(block, step):
        return pltpu.make_async_copy(
            chunk_ref.at[block, step], out_ref.at[block, step], sems.at[block, step]
        )

    def one_block(block, unused):
        orders, first, last = block_orders(slots_ref, block * BLK)

        def one_chunk(guard, step, carry):
            held = {}

            def emit(i, value):
                if i % 2 == 0:
                    held[i] = value
                else:
                    pair = jnp.concatenate([held.pop(i - 1), value], 0)
                    high, low = split_two(pair)
                    at = (i // 2) * 2 * BLK
                    chunk_ref[block, step, at : at + 2 * BLK, :HALF] = high
                    chunk_ref[block, step, at : at + 2 * BLK, HALF:] = low

            before = before_tile(before_ref, block, step)
            carry = run_chunk(
                step, carry, cosine, orders, before, scalars_ref, emit, (), guard
            )
            copy_out(block, step).start()
            return carry

        state = start_state(start_ref, block)
        state = lax.fori_loop(first, last, functools.partial(one_chunk, True), state)
        lax.fori_loop(last, DEG // CHUNK, functools.partial(one_chunk, False), state)
        return unused

    def finish_block(block, unused):
        orders, first, last = block_orders(slots_ref, block * BLK)

        def finish_chunk(step, inner):
            copy_out(block, step).wait()
            return inner

        return lax.fori_loop(first, DEG // CHUNK, finish_chunk, unused)

    lax.fori_loop(0, blocks, one_block, 0)
    lax.fori_loop(0, blocks, finish_block, 0)


def analyze_kernel(
    dims, total_row, slots_ref, data_ref, column_ref, latitude_ref, within_ref, table_ref,
    out_ref, chunk_ref, weight_ref, stack_ref, result_ref, fold_ref, coeff_ref, sems,
):
    bands, row_count, modes, blocks, tiles = dims
    chunks = DEG // CHUNK

    def copy_in(block, step):
        return pltpu.make_async_copy(
            table_ref.at[block, step], chunk_ref.at[block, step], sems.at[block, step]
        )

    def start_block(block, unused):
        orders, first, last = block_orders(slots_ref, block * BLK)

        def start_chunk(step, inner):
            copy_in(block, step).start()
            return inner

        return lax.fori_loop(first, chunks, start_chunk, unused)

    lax.fori_loop(0, blocks, start_block, 0)
    latitude = column_ref[...]
    north = jnp.where(latitude < HALF, latitude, NLAT - 1 - latitude)
    lane = lax.broadcasted_iota(jnp.int32, (NLAT, LANES), 1)
    for t in range(HALF // LANES):
        one_hot = jnp.where(north == lane + t * LANES, 1.0, 0.0).astype(BF)
        fold_ref[:, t * LANES : (t + 1) * LANES] = one_hot
    south = latitude_ref[...] >= HALF
    for block in range(blocks):
        orders = block_orders(slots_ref, block * BLK)[0][:, :1]
        sign = 1.0 - 2.0 * (orders % 2).astype(F32)
        evens, odds = [], []
        for c in range(CHAN):
            offset = ((c % 2) * FIELDS + c // 2) * row_count
            t, at = offset // LANES, offset % LANES
            rows = slice((t * blocks + block) * BLK, (t * blocks + block + 1) * BLK)
            values = jnp.concatenate(
                [data_ref[d, rows, :][:, at : at + row_count] for d in range(bands)], 1
            )
            flipped = sign * values
            evens.append(jnp.where(south, flipped, values))
            odds.append(jnp.where(south, -flipped, values))
        high, low = split_two(jnp.concatenate(evens + odds, 0))
        stack_ref[block * 4 * ROWS : block * 4 * ROWS + 2 * ROWS, :] = high
        stack_ref[block * 4 * ROWS + 2 * ROWS : (block + 1) * 4 * ROWS, :] = low
    folded = dot(stack_ref[...], fold_ref[...])
    for block in range(blocks):
        at = block * 4 * ROWS
        part = folded[at : at + 2 * ROWS] + folded[at + 2 * ROWS : at + 4 * ROWS]
        part = jnp.concatenate([part, jnp.zeros((LANES - 2 * ROWS, HALF), F32)], 0)
        high, low = split_two(part.T)
        weight_ref[block, :HALF, :LANES] = high
        weight_ref[block, :HALF, LANES:] = low
        weight_ref[block, HALF:, :LANES] = high
        weight_ref[block, HALF:, LANES:] = jnp.zeros_like(low)

    total = data_ref[0, total_row : total_row + 8]
    for d in range(1, bands):
        total = total + data_ref[d, total_row : total_row + 8]
    inverse = (1.0 / total)[:, :1]
    lane = lax.broadcasted_iota(jnp.int32, (CHUNK * BLK, LANES), 1)
    sub = lax.broadcasted_iota(jnp.int32, (CHUNK * BLK, LANES), 0)
    keep = (lane % BLK == sub % BLK) & (lane // ROWS == sub // BLK % 2)

    def one_block(block, unused):
        orders, first, last = block_orders(slots_ref, block * BLK)
        orders = orders[:, :1]
        here = pl.ds(pl.multiple_of(block * BLK, BLK), BLK)
        result_ref[...] = jnp.zeros_like(result_ref)

        def some_chunks(steps, inner):
            for step in steps:
                copy_in(block, step).wait()
            for step in steps:
                full = dot(chunk_ref[block, step], weight_ref[block])
                full = full[:, :LANES] + full[:, LANES:]
                picked = jnp.where(keep, full, 0.0).reshape(CHUNK, BLK, LANES)
                to = pl.ds(pl.multiple_of(step * CHUNK, CHUNK), CHUNK)
                result_ref[to, :] = jnp.sum(picked, axis=1)
            return inner

        lax.fori_loop(0, first & 1, lambda unused, inner: some_chunks((first,), inner), 0)
        lax.fori_loop(
            (first + 1) // 2,
            chunks // 2,
            lambda pair, inner: some_chunks((2 * pair, 2 * pair + 1), inner),
            0,
        )
        turned = result_ref[...].T
        turned = turned[:ROWS] + turned[ROWS : 2 * ROWS]
        degree = lax.broadcasted_iota(jnp.int32, (BLK, DEG), 1)
        within = jnp.where(degree >= orders, within_ref[here, :], 0.0)
        for c in range(CHAN):
            part = turned[c * BLK : (c + 1) * BLK] * within
            if c // 2 == FIELDS - 1:
                part = part * inverse
            coeff_ref[c] = part
        for i in range(BLK):
            target = pl.ds(slots_ref[modes + block * BLK + i], 1)
            out_ref[:, target, :] = coeff_ref[:, i : i + 1, :]
        return unused

    lax.fori_loop(0, blocks, one_block, 0)


def base_trig(order, first):
    lane = lax.broadcasted_iota(jnp.int32, order.shape, 1) + first
    phase = (order * lane) & (NLON - 1)
    quarter = (phase + NLON // 8) >> 9
    rest = (phase - quarter * (NLON // 4)).astype(F32) * (2.0 * math.pi / NLON)
    square = rest * rest
    sine = 1.0 / 362880.0
    for coef in (-1.0 / 5040.0, 1.0 / 120.0, -1.0 / 6.0, 1.0):
        sine = sine * square + coef
    sine = sine * rest
    cosine = 1.0 / 40320.0
    for coef in (-1.0 / 720.0, 1.0 / 24.0, -0.5, 1.0):
        cosine = cosine * square + coef
    swap = (quarter & 1) == 1
    cos_out = jnp.where(swap, sine, cosine)
    sin_out = jnp.where(swap, cosine, sine)
    cos_out = jnp.where(((quarter + 1) & 2) == 2, -cos_out, cos_out)
    sin_out = jnp.where((quarter & 2) == 2, -sin_out, sin_out)
    return cos_out, sin_out


def trig_kernel(out_ref, trig_ref, sem):
    half = trig_ref.shape[3] // 2
    root = math.sqrt(0.5)
    for parity in range(2):

        def strip(step, unused):
            at = pl.multiple_of(step * 64, 64)
            shape = (64, LANES)
            order = 2 * (lax.broadcasted_iota(jnp.int32, shape, 0) + at) + parity
            eighth = order & 7
            odd = (eighth & 1) == 1
            turn_cos = jnp.where(odd, root, jnp.where((eighth & 2) == 0, 1.0, 0.0))
            turn_sin = jnp.where(odd, root, jnp.where((eighth & 2) == 2, 1.0, 0.0))
            turn_cos = jnp.where((eighth >= 3) & (eighth <= 5), -turn_cos, turn_cos)
            turn_sin = jnp.where(eighth > 4, -turn_sin, turn_sin)
            for t in range(KTILE // LANES):
                cosine, sine = base_trig(order, t * LANES)
                for k in range(t * LANES, NLON // 2, KTILE):
                    columns = slice(t * LANES, (t + 1) * LANES)
                    for values, start in ((cosine, at), (sine, half + at)):
                        high, low = split_two(values)
                        trig_ref[k // KTILE, 0, parity, pl.ds(start, 64), columns] = high
                        trig_ref[k // KTILE, 1, parity, pl.ds(start, 64), columns] = low
                    cosine, sine = (
                        cosine * turn_cos - sine * turn_sin,
                        sine * turn_cos + cosine * turn_sin,
                    )
            return unused

        lax.fori_loop(0, half // 64, strip, 0)
    copy = pltpu.make_async_copy(trig_ref, out_ref, sem)
    copy.start()
    copy.wait()


def grid_kernel(
    dims, data_ref, orders_ref, rate_ref, sine_ref, trig_in, out_ref,
    move_ref, lhs_ref, weight_ref, acc_ref, trig_ref, sems,
):
    bands, row_count, modes, tiles, slots = dims
    half = slots // 2
    group = FIELDS * row_count
    padded = weight_ref.shape[1] // 2

    copies = []
    for tile in range(NLON // 2 // KTILE):
        copy = pltpu.make_async_copy(trig_in.at[tile], trig_ref.at[tile], sems.at[tile])
        copy.start()
        copies.append(copy)
    order = orders_ref[...]
    natural = (order & 1) * half + (order >> 1)
    for t in range(slots // LANES):
        lane = lax.broadcasted_iota(jnp.int32, (slots, LANES), 1) + t * LANES
        one_hot = jnp.where(natural == lane, 1.0, 0.0).astype(BF)
        move_ref[:, t * LANES : (t + 1) * LANES] = one_hot
    columns = []
    for t in range(tiles):
        part = data_ref[:, t * modes : (t + 1) * modes, :]
        columns.append(part.reshape(slots, LANES).T)
    turned = jnp.concatenate(columns, 0)
    for kind in range(2):
        high, low = split_two(turned[kind * group : (kind + 1) * group])
        moved = dot(jnp.concatenate([high, low], 0), move_ref[...]).astype(BF)
        for parity in range(2):
            part = moved[:, parity * half : (parity + 1) * half]
            lhs_ref[parity, :, kind * half : (kind + 1) * half] = part
    weight_ref[...] = jnp.zeros_like(weight_ref)
    flux_scale = math.pi / (2.0 * NLAT * NLON * DEG)
    weight = jnp.tile(sine_ref[...], (1, KTILE // LANES))
    total = jnp.zeros((8, KTILE), F32)

    for k in range(0, NLON // 2, KTILE):
        copies[k // KTILE].wait()
        trig_high, trig_low = trig_ref.at[k // KTILE, 0], trig_ref.at[k // KTILE, 1]
        sums = []
        for parity in range(2):
            first = dot(lhs_ref[parity], trig_high[parity])
            second = dot(lhs_ref[parity, :group, :], trig_low[parity])
            sums.append(first[:group] + first[group:] + second)
        values = []
        for fields, at in ((sums[0] + sums[1], k), (sums[0] - sums[1], k + NLON // 2)):
            weighted_rate = rate_ref[:, at : at + KTILE] * weight
            total = total + jnp.sum(weighted_rate.reshape(row_count // 8, 8, KTILE), axis=0)
            scaled = fields[:row_count] * (weight * flux_scale)
            values.append(
                jnp.concatenate(
                    [
                        fields[row_count : 2 * row_count] * scaled,
                        fields[2 * row_count :] * scaled,
                        weighted_rate * fields[:row_count],
                    ],
                    0,
                )
            )
        for parity in range(2):
            both = values[0] + values[1] if parity == 0 else values[0] - values[1]
            high, low = split_two(both)
            weight_ref[parity, :group, :] = high
            weight_ref[parity, padded : padded + group, :] = low
            first = dot(trig_high[parity], weight_ref[parity], 1)
            second = dot(trig_low[parity], weight_ref[parity, :padded, :], 1)
            part = first[:, :padded] + first[:, padded:] + second
            if k == 0:
                acc_ref[parity] = part
            else:
                acc_ref[parity] += part

    joined = []
    for kind in range(2):
        rows = slice(kind * half, (kind + 1) * half)
        joined.append(jnp.concatenate([acc_ref[0, rows, :group], acc_ref[1, rows, :group]], 0))
    if 2 * group < tiles * LANES:
        joined.append(jnp.zeros((slots, tiles * LANES - 2 * group), F32))
    high, low = split_two(jnp.concatenate(joined, 1))
    moved = dot(move_ref[...], jnp.concatenate([high, low], 1))
    moved = moved[:, : tiles * LANES] + moved[:, tiles * LANES :]
    for t in range(tiles):
        part = moved[:, t * LANES : (t + 1) * LANES]
        out_ref[:, t * modes : (t + 1) * modes, :] = part.reshape(bands, modes, LANES)
    out_ref[:, tiles * modes :, :] = jnp.broadcast_to(jnp.sum(total), (bands, 8, LANES))


VMEM = pl.BlockSpec(memory_space=pltpu.VMEM)
SMEM = pl.BlockSpec(memory_space=pltpu.SMEM)
HBM = pl.BlockSpec(memory_space=pltpu.HBM)


def work(microseconds):
    return pl.CostEstimate(
        flops=microseconds * 10**9, bytes_accessed=2**20, transcendentals=0
    )


def per_device(spectrum, capture_rate, row_latitude, slot_wavenumber):
    bands = lax.axis_size("band")
    modes = spectrum.shape[3]
    row_count = capture_rate.shape[1]
    slots = slot_wavenumber.shape[0]
    blocks = modes // BLK
    chunks = DEG // CHUNK
    tiles = -(-CHAN * row_count // LANES)
    band_index = lax.axis_index("band")

    def sort_rows(table):
        rank = jnp.sum((table[:, None, :] < table[:, :, None]).astype(jnp.int32), 2)
        match = rank[:, None, :] == jnp.arange(modes, dtype=jnp.int32)[None, :, None]
        places = jnp.arange(modes, dtype=jnp.int32)[None, None, :]
        return [
            jnp.sum(jnp.where(match, values, 0), 2).reshape(-1)
            for values in (table[:, None, :], places)
        ]

    own = lax.dynamic_slice_in_dim(slot_wavenumber, band_index * modes, modes)
    local = jnp.concatenate(sort_rows(own.reshape(1, modes)))
    ordered = sort_rows(slot_wavenumber.reshape(bands, modes))[0]
    rows = jnp.asarray(latitude_rows())
    spread = jnp.asarray(spread_matrix())
    latitude = row_latitude.reshape(1, NLAT)
    coeffs = spectrum.reshape(CHAN, modes, DEG)
    params = pltpu.CompilerParams(vmem_limit_bytes=48 * 2**20)
    chunk_rows = tiles * modes
    dims = (bands, row_count, modes, blocks, tiles)
    scalars = jnp.asarray(degree_scalars())
    per_order = pltpu.VMEM((modes, DEG), F32)

    def exchange(value):
        return lax.all_to_all(value, "band", split_axis=0, concat_axis=0, tiled=True)

    sent = pl.pallas_call(
        lambda *refs: synth_kernel(dims, *refs),
        out_shape=jax.ShapeDtypeStruct((bands, chunk_rows, LANES), F32),
        in_specs=[SMEM] + [HBM] * 5,
        out_specs=VMEM,
        scratch_shapes=[
            pltpu.SMEM(scalars.shape, F32),
            pltpu.VMEM(coeffs.shape, F32),
            pltpu.VMEM(rows.shape, F32),
            pltpu.VMEM(spread.shape, BF),
            pltpu.VMEM(latitude.shape, jnp.int32),
            pltpu.SemaphoreType.DMA((5,)),
        ]
        + [per_order] * 3
        + [pltpu.VMEM((chunks, 2 * ROWS, CHUNK * BLK), BF)]
        + [pltpu.VMEM((2, CHUNK // 2 * BLK, HALF), BF)] * 4
        + [
            pltpu.VMEM((blocks, 2, ROWS, HALF), F32),
            pltpu.VMEM((HALF, NLAT), BF),
            pltpu.VMEM((CHAN, BLK, DEG), F32),
        ],
        compiler_params=pltpu.CompilerParams(vmem_limit_bytes=62 * 2**20),
        cost_estimate=work(15),
        name="synth",
    )(local, scalars, coeffs, rows, spread, latitude)
    received = exchange(sent)

    trig_tiles = NLON // 2 // KTILE
    trig_shape = (trig_tiles, 2, 2, slots, KTILE)
    trig_scratch = pltpu.VMEM(trig_shape, BF)
    trig = pl.pallas_call(
        trig_kernel,
        out_shape=jax.ShapeDtypeStruct(trig_shape, BF),
        out_specs=HBM,
        scratch_shapes=[trig_scratch, pltpu.SemaphoreType.DMA(())],
        compiler_params=params,
        cost_estimate=work(4),
        name="trig",
    )()

    my_latitudes = lax.dynamic_slice_in_dim(row_latitude, band_index * row_count, row_count)
    row_sine = jnp.sin(jnp.pi * (my_latitudes.astype(F32) + 0.5) / NLAT)
    row_sine = jnp.broadcast_to(row_sine[:, None], (row_count, LANES))
    orders = jnp.broadcast_to(ordered.reshape(slots, 1), (slots, LANES))
    group = FIELDS * row_count
    padded = -(-group // LANES) * LANES
    grid_dims = (bands, row_count, modes, tiles, slots)
    fluxes = pl.pallas_call(
        lambda *refs: grid_kernel(grid_dims, *refs),
        out_shape=jax.ShapeDtypeStruct((bands, chunk_rows + 8, LANES), F32),
        in_specs=[VMEM] * 4 + [HBM],
        out_specs=VMEM,
        scratch_shapes=[
            pltpu.VMEM((slots, slots), BF),
            pltpu.VMEM((2, 2 * group, slots), BF),
            pltpu.VMEM((2, 2 * padded, KTILE), BF),
            pltpu.VMEM((2, slots, padded), F32),
            trig_scratch,
            pltpu.SemaphoreType.DMA((trig_tiles,)),
        ],
        compiler_params=params,
        cost_estimate=work(8),
        name="grid",
    )(received, orders, capture_rate.reshape(row_count, NLON), row_sine, trig)
    returned = exchange(fluxes)

    chunk_shape = (blocks, chunks, CHUNK * BLK, 2 * HALF)
    legendre, within = pl.pallas_call(
        lambda *refs: table_kernel(blocks, *refs),
        out_shape=[
            jax.ShapeDtypeStruct(chunk_shape, BF),
            jax.ShapeDtypeStruct((modes, DEG), F32),
        ],
        in_specs=[SMEM, SMEM, VMEM],
        out_specs=[HBM, VMEM],
        scratch_shapes=[per_order] * 2
        + [pltpu.VMEM(chunk_shape, BF), pltpu.SemaphoreType.DMA((blocks, chunks))],
        compiler_params=params,
        cost_estimate=work(12),
        name="table",
    )(local, scalars, rows)
    column = jnp.broadcast_to(row_latitude[:, None], (NLAT, LANES))
    result = pl.pallas_call(
        lambda *refs: analyze_kernel(dims, chunk_rows, *refs),
        out_shape=jax.ShapeDtypeStruct((CHAN, modes, DEG), F32),
        in_specs=[SMEM, VMEM, VMEM, VMEM, VMEM, HBM],
        out_specs=VMEM,
        scratch_shapes=[
            pltpu.VMEM(chunk_shape, BF),
            pltpu.VMEM((blocks, 2 * HALF, 2 * LANES), BF),
            pltpu.VMEM((blocks * 4 * ROWS, NLAT), BF),
            pltpu.VMEM((DEG, LANES), F32),
            pltpu.VMEM((NLAT, HALF), BF),
            pltpu.VMEM((CHAN, BLK, DEG), F32),
            pltpu.SemaphoreType.DMA((blocks, chunks)),
        ],
        compiler_params=params,
        cost_estimate=work(9),
        name="analyze",
    )(local, returned, column, latitude, within, legendre)
    return result.reshape(1, FIELDS, 2, modes, DEG)


def solution(mesh):
    return jax.shard_map(
        per_device,
        mesh=mesh,
        in_specs=(P("shell", None, None, "band", None), P("shell", "band", None), P(), P()),
        out_specs=P("shell", None, None, "band", None),
        check_vma=False,
    )
```

```python
import functools
import math

import jax
import jax.numpy as jnp
import numpy as np
from jax import lax
from jax.experimental import pallas as pl
from jax.experimental.pallas import tpu as pltpu
from jax.sharding import PartitionSpec as P

DEG = 512
NLAT = 1024
NLON = 2048
FIELDS = 3
HALF = NLAT // 2
CHAN = 2 * FIELDS
BLK = 8
ROWS = CHAN * BLK
CHUNK = 64
CHECK = 16
PLACES = 1024
LANES = 128
KTILE = 256
BF = jnp.bfloat16
F32 = jnp.float32


def split_two(value):
    high = value.astype(BF)
    low = (value - high.astype(F32)).astype(BF)
    return high, low


def dot(lhs, rhs, contract_rhs=0):
    return lax.dot_general(
        lhs, rhs, (((1,), (contract_rhs,)), ((), ())), preferred_element_type=F32
    )


def latitude_rows():
    theta = np.pi * (np.arange(HALF) + 0.5) / NLAT
    index = np.arange(DEG, dtype=np.float64)
    log_terms = np.zeros(DEG)
    log_terms[1:] = 0.5 * np.log2((2.0 * index[1:] + 1.0) / (2.0 * index[1:]))
    rows = np.zeros((8, DEG))
    rows[0], rows[1], rows[2] = np.cos(theta), np.log2(np.sin(theta)), log_terms
    return rows.astype(np.float32)


def spread_matrix():
    spread = np.zeros((LANES, 2, 2, CHUNK // 2, BLK), np.float32)
    for half in range(2):
        for parity in range(2):
            for step in range(CHUNK // 2):
                spread[half * CHUNK + 2 * step + parity, half, parity, step, :] = 1.0
    return spread.reshape(LANES, 2 * 2 * (CHUNK // 2) * BLK).astype(BF)


def degree_scalars():
    before = np.arange(DEG, dtype=np.float64) - 1.0
    square = before * before
    return np.concatenate([square, 4.0 / (4.0 * square - 1.0)]).astype(np.float32)


def block_orders(slots_ref, first):
    sublane = lax.broadcasted_iota(jnp.int32, (BLK, LANES), 0)
    orders = jnp.zeros((BLK, LANES), jnp.int32)
    lowest, highest = jnp.int32(DEG), jnp.int32(0)
    for i in range(BLK):
        order = slots_ref[first + i] // PLACES
        orders = jnp.where(sublane == i, order, orders)
        lowest, highest = jnp.minimum(lowest, order), jnp.maximum(highest, order)
    return orders, lowest // CHUNK, highest // CHUNK + 1


def running_sum(terms, length):
    lane = lax.broadcasted_iota(jnp.int32, terms.shape, 1) & (length - 1)
    shift = 1
    while shift < length:
        moved = pltpu.roll(terms, shift, 1)
        terms = terms + jnp.where(lane >= shift, moved, 0.0)
        shift *= 2
    return terms


def recursion_tables(slots_ref, modes, rows_ref, start_ref, before_ref, within_ref):
    orders = [block_orders(slots_ref, at)[0][:, :1] for at in range(0, modes, BLK)]
    order = jnp.concatenate(orders, 0).astype(F32)
    position = lax.broadcasted_iota(jnp.int32, (modes, DEG), 1)
    degree = position.astype(F32)
    square = degree * degree
    above = degree > order
    gap = jnp.where(above, square - order * order, 1.0)
    growth = jnp.where(above, 0.5 * jnp.log2((square - 0.25) / gap), 0.0)
    before_ref[...] = running_sum(growth, DEG)
    later = jnp.where(position & (CHECK - 1) == 0, 0.0, growth)
    within_ref[...] = jnp.exp2(running_sum(later, CHECK))
    terms = jnp.where(degree <= order, rows_ref[2:3, :], 0.0)
    norm = jnp.where(order > 0, 0.5 + jnp.sum(terms, axis=1, keepdims=True), 0.0)
    start_ref[...] = norm + order * rows_ref[1:2, :]


def run_chunk(step, carry, double_cosine, orders, before, scalars_ref, emit, beside, guard):
    current, previous, log_scale = carry
    order = orders.astype(F32)
    order_square = order * order
    before = pltpu.roll(before, (step % 2) * CHUNK, 1)
    scale = None
    for i in range(CHUNK):
        if i % CHECK == 0:
            size = jnp.maximum(jnp.abs(current), jnp.abs(previous))
            large, small = size > 2.0**40, size < 2.0**-40
            factor = jnp.where(large, 2.0**-60, jnp.where(small, 2.0**60, 1.0))
            change = jnp.where(large, 60.0, jnp.where(small, -60.0, 0.0))
            current = current * factor
            previous = previous * factor
            log_scale = log_scale + change
            scale = jnp.exp2(jnp.maximum(log_scale + before[:, i : i + 1], -200.0))
        degree = step * CHUNK + i
        factor = (scalars_ref[degree] - order_square) * scalars_ref[DEG + degree]
        factor = jnp.tile(factor, (1, HALF // LANES))
        newest = double_cosine * current - factor * previous
        if guard:
            started = jnp.tile(orders, (1, HALF // LANES)) < degree
            newest = jnp.where(started, newest, 1.0)
        current, previous = newest, current
        emit(i, newest * scale)
        if beside and i % (CHUNK // len(beside)) == 1:
            beside[i // (CHUNK // len(beside))]()
    return current, previous, log_scale


def before_tile(before_ref, block, step):
    rows = pl.ds(pl.multiple_of(block * BLK, BLK), BLK)
    return before_ref[rows, pl.ds(pl.multiple_of(step // 2 * LANES, LANES), LANES)]


def start_state(start_ref, block):
    ones = jnp.ones((BLK, HALF), F32)
    return ones, ones, start_ref[pl.ds(pl.multiple_of(block * BLK, BLK), BLK), :]


def fold_matrix(latitude_ref, fold_ref):
    latitude = latitude_ref[...]
    north = jnp.where(latitude < HALF, latitude, NLAT - 1 - latitude)
    sublane = lax.broadcasted_iota(jnp.int32, (HALF, NLAT), 0)
    fold_ref[...] = jnp.where(sublane == north, 1.0, 0.0).astype(BF)


def synth_kernel(
    dims, slots_ref, scalars_in, spec_in, rows_in, spread_in, latitude_in,
    out_ref, scalars_ref, spec_ref, rows_ref, spread_ref, latitude_ref, sems,
    start_ref, before_ref, within_ref, lhs_ref, high_a, low_a, high_b, low_b, acc_ref, fold_ref, coeff_ref,
):
    bands, row_count, modes, blocks, tiles = dims
    pairs = (
        (rows_in, rows_ref), (scalars_in, scalars_ref), (latitude_in, latitude_ref),
        (spread_in, spread_ref), (spec_in, spec_ref),
    )
    copies = []
    for index, (source, target) in enumerate(pairs):
        copies.append(pltpu.make_async_copy(source, target, sems.at[index]))
        copies[-1].start()
    for copy in copies:
        copy.wait()
    fold_matrix(latitude_ref, fold_ref)
    recursion_tables(slots_ref, modes, rows_ref, start_ref, before_ref, within_ref)
    south = latitude_ref[...] >= HALF
    spread_width = 4 * (CHUNK // 2) * BLK
    lane = lax.broadcasted_iota(jnp.int32, (2 * ROWS, spread_width), 1)
    sub = lax.broadcasted_iota(jnp.int32, (2 * ROWS, spread_width), 0)
    diagonal = (lane % BLK) == (sub % BLK)
    width = (CHUNK // 2) * BLK

    def one_block(block, unused):
        orders, first, last = block_orders(slots_ref, block * BLK)
        column = orders[:, :1]
        here = pl.ds(pl.multiple_of(block * BLK, BLK), BLK)
        for i in range(BLK):
            source = pl.ds(slots_ref[block * BLK + i] % PLACES, 1)
            coeff_ref[:, i : i + 1, :] = spec_ref[:, source, :]
        degree = lax.broadcasted_iota(jnp.int32, (BLK, DEG), 1)
        within = jnp.where(degree >= column, within_ref[here, :], 0.0)
        coeffs = coeff_ref[...] * within[None]
        coeff_high, coeff_low = split_two(coeffs.reshape(ROWS, DEG))
        stacked = jnp.concatenate([coeff_high, coeff_low], 0)
        for t in range(DEG // LANES):
            wide = dot(stacked[:, t * LANES : (t + 1) * LANES], spread_ref[...])
            wide = jnp.where(diagonal, wide, 0.0).astype(BF)
            for half in range(2):
                lhs_ref[2 * t + half] = wide[:, half * 2 * width : (half + 1) * 2 * width]
        acc_ref[block] = jnp.zeros((2, ROWS, HALF), F32)
        cosine = jnp.broadcast_to(2.0 * rows_ref[0:1, :], (BLK, HALF))

        def recur(step, carry, high_ref, low_ref, beside, guard):
            held = {}

            def emit(i, value):
                if i % 4 < 2:
                    held[i] = value
                else:
                    pair = jnp.concatenate([held.pop(i - 2), value], 0)
                    high, low = split_two(pair)
                    at = (i // 4) * 2 * BLK
                    high_ref[i % 2, at : at + 2 * BLK, :] = high
                    low_ref[i % 2, at : at + 2 * BLK, :] = low

            before = before_tile(before_ref, block, step)
            return run_chunk(
                step, carry, cosine, orders, before, scalars_ref, emit, beside, guard
            )

        def add_products(step, high_ref, low_ref):
            def high_part(parity, columns):
                lhs = lhs_ref[step, :, parity * width : (parity + 1) * width]
                first = dot(lhs, high_ref[parity, :, columns])
                acc_ref[block, parity, :, columns] += first[:ROWS] + first[ROWS:]

            def low_part(parity, columns):
                lhs = lhs_ref[step, :ROWS, parity * width : (parity + 1) * width]
                acc_ref[block, parity, :, columns] += dot(lhs, low_ref[parity, :, columns])

            return [
                functools.partial(part, parity, slice(at, at + KTILE))
                for parity in range(2)
                for at in range(0, HALF, KTILE)
                for part in (high_part, low_part)
            ]

        def two_chunks(guard, pair, carry):
            step = 2 * pair
            beside = add_products(jnp.maximum(step - 1, 0), high_b, low_b)
            carry = recur(step, carry, high_a, low_a, beside, guard)
            beside = add_products(step, high_a, low_a)
            return recur(step + 1, carry, high_b, low_b, beside, guard)

        high_b[...] = jnp.zeros_like(high_b)
        low_b[...] = jnp.zeros_like(low_b)
        chunks = DEG // CHUNK
        state = lax.fori_loop(
            0,
            first & 1,
            lambda unused, carry: recur(first, carry, high_b, low_b, (), True),
            start_state(start_ref, block),
        )
        middle = (last + 1) // 2
        state = lax.fori_loop(
            (first + 1) // 2, middle, functools.partial(two_chunks, True), state
        )
        lax.fori_loop(middle, chunks // 2, functools.partial(two_chunks, False), state)
        for part in add_products(chunks - 1, high_b, low_b):
            part()
        return unused

    lax.fori_loop(0, blocks, one_block, 0)
    high, low = split_two(acc_ref[...].reshape(blocks * 2 * ROWS, HALF))
    moved = dot(jnp.concatenate([high, low], 0), fold_ref[...])
    moved = moved[: blocks * 2 * ROWS] + moved[blocks * 2 * ROWS :]
    for block in range(blocks):
        orders = block_orders(slots_ref, block * BLK)[0][:, :1]
        sign = jnp.tile(1.0 - 2.0 * (orders % 2).astype(F32), (CHAN, 1))
        even = moved[block * 2 * ROWS : block * 2 * ROWS + ROWS]
        odd = moved[block * 2 * ROWS + ROWS : (block + 1) * 2 * ROWS]
        values = jnp.where(south, sign * (even - odd), even + odd)
        for d in range(bands):
            parts = []
            for kind in range(2):
                for field in range(FIELDS):
                    c = field * 2 + kind
                    parts.append(
                        values[c * BLK : (c + 1) * BLK, d * row_count : (d + 1) * row_count]
                    )
            if CHAN * row_count < tiles * LANES:
                parts.append(jnp.zeros((BLK, tiles * LANES - CHAN * row_count), F32))
            joined = jnp.concatenate(parts, 1)
            for t in range(tiles):
                at = slice((t * blocks + block) * BLK, (t * blocks + block + 1) * BLK)
                out_ref[d, at, :] = joined[:, t * LANES : (t + 1) * LANES]


def table_kernel(
    blocks, slots_ref, scalars_ref, rows_ref, out_ref, within_out, start_ref, before_ref,
    chunk_ref, sems,
):
    modes = blocks * BLK
    cosine = jnp.broadcast_to(2.0 * rows_ref[0:1, :], (BLK, HALF))
    recursion_tables(slots_ref, modes, rows_ref, start_ref, before_ref, within_out)

    def copy_out(block, step):
        return pltpu.make_async_copy(
            chunk_ref.at[block, step], out_ref.at[block, step], sems.at[block, step]
        )

    def one_block(block, unused):
        orders, first, last = block_orders(slots_ref, block * BLK)

        def one_chunk(guard, step, carry):
            held = {}

            def emit(i, value):
                if i % 2 == 0:
                    held[i] = value
                else:
                    pair = jnp.concatenate([held.pop(i - 1), value], 0)
                    high, low = split_two(pair)
                    at = (i // 2) * 2 * BLK
                    chunk_ref[block, step, at : at + 2 * BLK, :HALF] = high
                    chunk_ref[block, step, at : at + 2 * BLK, HALF:] = low

            before = before_tile(before_ref, block, step)
            carry = run_chunk(
                step, carry, cosine, orders, before, scalars_ref, emit, (), guard
            )
            copy_out(block, step).start()
            return carry

        state = start_state(start_ref, block)
        state = lax.fori_loop(first, last, functools.partial(one_chunk, True), state)
        lax.fori_loop(last, DEG // CHUNK, functools.partial(one_chunk, False), state)
        return unused

    def finish_block(block, unused):
        orders, first, last = block_orders(slots_ref, block * BLK)

        def finish_chunk(step, inner):
            copy_out(block, step).wait()
            return inner

        return lax.fori_loop(first, DEG // CHUNK, finish_chunk, unused)

    lax.fori_loop(0, blocks, one_block, 0)
    lax.fori_loop(0, blocks, finish_block, 0)


def analyze_kernel(
    dims, total_row, slots_ref, data_ref, column_ref, latitude_ref, within_ref, table_ref,
    out_ref, chunk_ref, weight_ref, stack_ref, result_ref, fold_ref, coeff_ref, sems,
):
    bands, row_count, modes, blocks, tiles = dims
    chunks = DEG // CHUNK

    def copy_in(block, step):
        return pltpu.make_async_copy(
            table_ref.at[block, step], chunk_ref.at[block, step], sems.at[block, step]
        )

    def start_block(block, unused):
        orders, first, last = block_orders(slots_ref, block * BLK)

        def start_chunk(step, inner):
            copy_in(block, step).start()
            return inner

        return lax.fori_loop(first, chunks, start_chunk, unused)

    lax.fori_loop(0, blocks, start_block, 0)
    latitude = column_ref[...]
    north = jnp.where(latitude < HALF, latitude, NLAT - 1 - latitude)
    lane = lax.broadcasted_iota(jnp.int32, (NLAT, LANES), 1)
    for t in range(HALF // LANES):
        one_hot = jnp.where(north == lane + t * LANES, 1.0, 0.0).astype(BF)
        fold_ref[:, t * LANES : (t + 1) * LANES] = one_hot
    south = latitude_ref[...] >= HALF
    for block in range(blocks):
        orders = block_orders(slots_ref, block * BLK)[0][:, :1]
        sign = 1.0 - 2.0 * (orders % 2).astype(F32)
        evens, odds = [], []
        for c in range(CHAN):
            offset = ((c % 2) * FIELDS + c // 2) * row_count
            t, at = offset // LANES, offset % LANES
            rows = slice((t * blocks + block) * BLK, (t * blocks + block + 1) * BLK)
            values = jnp.concatenate(
                [data_ref[d, rows, :][:, at : at + row_count] for d in range(bands)], 1
            )
            flipped = sign * values
            evens.append(jnp.where(south, flipped, values))
            odds.append(jnp.where(south, -flipped, values))
        high, low = split_two(jnp.concatenate(evens + odds, 0))
        stack_ref[block * 4 * ROWS : block * 4 * ROWS + 2 * ROWS, :] = high
        stack_ref[block * 4 * ROWS + 2 * ROWS : (block + 1) * 4 * ROWS, :] = low
    folded = dot(stack_ref[...], fold_ref[...])
    for block in range(blocks):
        at = block * 4 * ROWS
        part = folded[at : at + 2 * ROWS] + folded[at + 2 * ROWS : at + 4 * ROWS]
        part = jnp.concatenate([part, jnp.zeros((LANES - 2 * ROWS, HALF), F32)], 0)
        high, low = split_two(part.T)
        weight_ref[block, :HALF, :LANES] = high
        weight_ref[block, :HALF, LANES:] = low
        weight_ref[block, HALF:, :LANES] = high
        weight_ref[block, HALF:, LANES:] = jnp.zeros_like(low)

    total = data_ref[0, total_row : total_row + 8]
    for d in range(1, bands):
        total = total + data_ref[d, total_row : total_row + 8]
    inverse = (1.0 / total)[:, :1]
    lane = lax.broadcasted_iota(jnp.int32, (CHUNK * BLK, LANES), 1)
    sub = lax.broadcasted_iota(jnp.int32, (CHUNK * BLK, LANES), 0)
    keep = (lane % BLK == sub % BLK) & (lane // ROWS == sub // BLK % 2)

    def one_block(block, unused):
        orders, first, last = block_orders(slots_ref, block * BLK)
        orders = orders[:, :1]
        here = pl.ds(pl.multiple_of(block * BLK, BLK), BLK)
        result_ref[block] = jnp.zeros((DEG, LANES), F32)

        def some_chunks(steps, inner):
            for step in steps:
                copy_in(block, step).wait()
            for step in steps:
                full = dot(chunk_ref[block, step], weight_ref[block])
                full = full[:, :LANES] + full[:, LANES:]
                picked = jnp.where(keep, full, 0.0).reshape(CHUNK, BLK, LANES)
                to = pl.ds(pl.multiple_of(step * CHUNK, CHUNK), CHUNK)
                result_ref[block, to, :] = jnp.sum(picked, axis=1)
            return inner

        lax.fori_loop(0, first & 1, lambda unused, inner: some_chunks((first,), inner), 0)
        lax.fori_loop(
            (first + 1) // 2,
            chunks // 2,
            lambda pair, inner: some_chunks((2 * pair, 2 * pair + 1), inner),
            0,
        )
        return unused

    lax.fori_loop(0, blocks, one_block, 0)
    for block in range(blocks):
        orders = block_orders(slots_ref, block * BLK)[0][:, :1]
        turned = result_ref[block].T
        turned = turned[:ROWS] + turned[ROWS : 2 * ROWS]
        degree = lax.broadcasted_iota(jnp.int32, (BLK, DEG), 1)
        within = jnp.where(degree >= orders, within_ref[block * BLK : (block + 1) * BLK, :], 0.0)
        for c in range(CHAN):
            part = turned[c * BLK : (c + 1) * BLK] * within
            if c // 2 == FIELDS - 1:
                part = part * inverse
            coeff_ref[block, c] = part
        for i in range(BLK):
            target = pl.ds(slots_ref[block * BLK + i] % PLACES, 1)
            out_ref[:, target, :] = coeff_ref[block, :, i : i + 1, :]


def base_trig(order, first):
    lane = lax.broadcasted_iota(jnp.int32, order.shape, 1) + first
    phase = (order * lane) & (NLON - 1)
    quarter = (phase + NLON // 8) >> 9
    rest = (phase - quarter * (NLON // 4)).astype(F32) * (2.0 * math.pi / NLON)
    square = rest * rest
    sine = 1.0 / 362880.0
    for coef in (-1.0 / 5040.0, 1.0 / 120.0, -1.0 / 6.0, 1.0):
        sine = sine * square + coef
    sine = sine * rest
    cosine = 1.0 / 40320.0
    for coef in (-1.0 / 720.0, 1.0 / 24.0, -0.5, 1.0):
        cosine = cosine * square + coef
    swap = (quarter & 1) == 1
    cos_out = jnp.where(swap, sine, cosine)
    sin_out = jnp.where(swap, cosine, sine)
    cos_out = jnp.where(((quarter + 1) & 2) == 2, -cos_out, cos_out)
    sin_out = jnp.where((quarter & 2) == 2, -sin_out, sin_out)
    return cos_out, sin_out


def trig_kernel(out_ref, trig_ref, sem):
    half = trig_ref.shape[3] // 2
    root = math.sqrt(0.5)
    for parity in range(2):

        def strip(step, unused):
            at = pl.multiple_of(step * 64, 64)
            shape = (64, LANES)
            order = 2 * (lax.broadcasted_iota(jnp.int32, shape, 0) + at) + parity
            eighth = order & 7
            odd = (eighth & 1) == 1
            turn_cos = jnp.where(odd, root, jnp.where((eighth & 2) == 0, 1.0, 0.0))
            turn_sin = jnp.where(odd, root, jnp.where((eighth & 2) == 2, 1.0, 0.0))
            turn_cos = jnp.where((eighth >= 3) & (eighth <= 5), -turn_cos, turn_cos)
            turn_sin = jnp.where(eighth > 4, -turn_sin, turn_sin)
            for t in range(KTILE // LANES):
                cosine, sine = base_trig(order, t * LANES)
                for k in range(t * LANES, NLON // 2, KTILE):
                    columns = slice(t * LANES, (t + 1) * LANES)
                    for values, start in ((cosine, at), (sine, half + at)):
                        high, low = split_two(values)
                        trig_ref[k // KTILE, 0, parity, pl.ds(start, 64), columns] = high
                        trig_ref[k // KTILE, 1, parity, pl.ds(start, 64), columns] = low
                    cosine, sine = (
                        cosine * turn_cos - sine * turn_sin,
                        sine * turn_cos + cosine * turn_sin,
                    )
            return unused

        lax.fori_loop(0, half // 64, strip, 0)
    copy = pltpu.make_async_copy(trig_ref, out_ref, sem)
    copy.start()
    copy.wait()


def grid_kernel(
    dims, data_ref, orders_ref, rate_ref, sine_ref, trig_in, out_ref,
    move_ref, lhs_ref, weight_ref, acc_ref, trig_ref, sems,
):
    bands, row_count, modes, tiles, slots = dims
    half = slots // 2
    group = FIELDS * row_count
    padded = weight_ref.shape[1] // 2

    copies = []
    for tile in range(NLON // 2 // KTILE):
        copy = pltpu.make_async_copy(trig_in.at[tile], trig_ref.at[tile], sems.at[tile])
        copy.start()
        copies.append(copy)
    order = orders_ref[...]
    natural = (order & 1) * half + (order >> 1)
    for t in range(slots // LANES):
        lane = lax.broadcasted_iota(jnp.int32, (slots, LANES), 1) + t * LANES
        one_hot = jnp.where(natural == lane, 1.0, 0.0).astype(BF)
        move_ref[:, t * LANES : (t + 1) * LANES] = one_hot
    columns = []
    for t in range(tiles):
        part = data_ref[:, t * modes : (t + 1) * modes, :]
        columns.append(part.reshape(slots, LANES).T)
    turned = jnp.concatenate(columns, 0)
    for kind in range(2):
        high, low = split_two(turned[kind * group : (kind + 1) * group])
        moved = dot(jnp.concatenate([high, low], 0), move_ref[...]).astype(BF)
        for parity in range(2):
            part = moved[:, parity * half : (parity + 1) * half]
            lhs_ref[parity, :, kind * half : (kind + 1) * half] = part
    weight_ref[...] = jnp.zeros_like(weight_ref)
    flux_scale = math.pi / (2.0 * NLAT * NLON * DEG)
    weight = jnp.tile(sine_ref[...], (1, KTILE // LANES))
    total = jnp.zeros((8, KTILE), F32)

    for k in range(0, NLON // 2, KTILE):
        copies[k // KTILE].wait()
        trig_high, trig_low = trig_ref.at[k // KTILE, 0], trig_ref.at[k // KTILE, 1]
        sums = []
        for parity in range(2):
            first = dot(lhs_ref[parity], trig_high[parity])
            second = dot(lhs_ref[parity, :group, :], trig_low[parity])
            sums.append(first[:group] + first[group:] + second)
        values = []
        for fields, at in ((sums[0] + sums[1], k), (sums[0] - sums[1], k + NLON // 2)):
            weighted_rate = rate_ref[:, at : at + KTILE] * weight
            total = total + jnp.sum(weighted_rate.reshape(row_count // 8, 8, KTILE), axis=0)
            scaled = fields[:row_count] * (weight * flux_scale)
            values.append(
                jnp.concatenate(
                    [
                        fields[row_count : 2 * row_count] * scaled,
                        fields[2 * row_count :] * scaled,
                        weighted_rate * fields[:row_count],
                    ],
                    0,
                )
            )
        for parity in range(2):
            both = values[0] + values[1] if parity == 0 else values[0] - values[1]
            high, low = split_two(both)
            weight_ref[parity, :group, :] = high
            weight_ref[parity, padded : padded + group, :] = low
            first = dot(trig_high[parity], weight_ref[parity], 1)
            second = dot(trig_low[parity], weight_ref[parity, :padded, :], 1)
            part = first[:, :padded] + first[:, padded:] + second
            if k == 0:
                acc_ref[parity] = part
            else:
                acc_ref[parity] += part

    joined = []
    for kind in range(2):
        rows = slice(kind * half, (kind + 1) * half)
        joined.append(jnp.concatenate([acc_ref[0, rows, :group], acc_ref[1, rows, :group]], 0))
    if 2 * group < tiles * LANES:
        joined.append(jnp.zeros((slots, tiles * LANES - 2 * group), F32))
    high, low = split_two(jnp.concatenate(joined, 1))
    moved = dot(move_ref[...], jnp.concatenate([high, low], 1))
    moved = moved[:, : tiles * LANES] + moved[:, tiles * LANES :]
    for t in range(tiles):
        part = moved[:, t * LANES : (t + 1) * LANES]
        out_ref[:, t * modes : (t + 1) * modes, :] = part.reshape(bands, modes, LANES)
    out_ref[:, tiles * modes :, :] = jnp.broadcast_to(jnp.sum(total), (bands, 8, LANES))


VMEM = pl.BlockSpec(memory_space=pltpu.VMEM)
SMEM = pl.BlockSpec(memory_space=pltpu.SMEM)
HBM = pl.BlockSpec(memory_space=pltpu.HBM)


def work(microseconds):
    return pl.CostEstimate(
        flops=microseconds * 10**9, bytes_accessed=2**20, transcendentals=0
    )


def per_device(spectrum, capture_rate, row_latitude, slot_wavenumber):
    bands = lax.axis_size("band")
    modes = spectrum.shape[3]
    row_count = capture_rate.shape[1]
    slots = slot_wavenumber.shape[0]
    blocks = modes // BLK
    chunks = DEG // CHUNK
    tiles = -(-CHAN * row_count // LANES)
    band_index = lax.axis_index("band")

    def sort_rows(table):
        rank = jnp.sum((table[:, None, :] < table[:, :, None]).astype(jnp.int32), 2)
        match = rank[:, None, :] == jnp.arange(modes, dtype=jnp.int32)[None, :, None]
        keys = table * PLACES + jnp.arange(modes, dtype=jnp.int32)[None, :]
        return jnp.sum(jnp.where(match, keys[:, None, :], 0), 2).reshape(-1)

    own = lax.dynamic_slice_in_dim(slot_wavenumber, band_index * modes, modes)
    local = sort_rows(own.reshape(1, modes))
    ordered = sort_rows(slot_wavenumber.reshape(bands, modes)) // PLACES
    rows = jnp.asarray(latitude_rows())
    spread = jnp.asarray(spread_matrix())
    latitude = row_latitude.reshape(1, NLAT)
    coeffs = spectrum.reshape(CHAN, modes, DEG)
    params = pltpu.CompilerParams(vmem_limit_bytes=48 * 2**20)
    chunk_rows = tiles * modes
    dims = (bands, row_count, modes, blocks, tiles)
    scalars = jnp.asarray(degree_scalars())
    per_order = pltpu.VMEM((modes, DEG), F32)

    def exchange(value):
        return lax.all_to_all(value, "band", split_axis=0, concat_axis=0, tiled=True)

    sent = pl.pallas_call(
        lambda *refs: synth_kernel(dims, *refs),
        out_shape=jax.ShapeDtypeStruct((bands, chunk_rows, LANES), F32),
        in_specs=[SMEM] + [HBM] * 5,
        out_specs=VMEM,
        scratch_shapes=[
            pltpu.SMEM(scalars.shape, F32),
            pltpu.VMEM(coeffs.shape, F32),
            pltpu.VMEM(rows.shape, F32),
            pltpu.VMEM(spread.shape, BF),
            pltpu.VMEM(latitude.shape, jnp.int32),
            pltpu.SemaphoreType.DMA((5,)),
        ]
        + [per_order] * 3
        + [pltpu.VMEM((chunks, 2 * ROWS, CHUNK * BLK), BF)]
        + [pltpu.VMEM((2, CHUNK // 2 * BLK, HALF), BF)] * 4
        + [
            pltpu.VMEM((blocks, 2, ROWS, HALF), F32),
            pltpu.VMEM((HALF, NLAT), BF),
            pltpu.VMEM((CHAN, BLK, DEG), F32),
        ],
        compiler_params=pltpu.CompilerParams(vmem_limit_bytes=62 * 2**20),
        cost_estimate=work(15),
        name="synth",
    )(local, scalars, coeffs, rows, spread, latitude)
    received = exchange(sent)

    trig_tiles = NLON // 2 // KTILE
    trig_shape = (trig_tiles, 2, 2, slots, KTILE)
    trig_scratch = pltpu.VMEM(trig_shape, BF)
    trig = pl.pallas_call(
        trig_kernel,
        out_shape=jax.ShapeDtypeStruct(trig_shape, BF),
        out_specs=HBM,
        scratch_shapes=[trig_scratch, pltpu.SemaphoreType.DMA(())],
        compiler_params=params,
        cost_estimate=work(4),
        name="trig",
    )()

    my_latitudes = lax.dynamic_slice_in_dim(row_latitude, band_index * row_count, row_count)
    row_sine = jnp.sin(jnp.pi * (my_latitudes.astype(F32) + 0.5) / NLAT)
    row_sine = jnp.broadcast_to(row_sine[:, None], (row_count, LANES))
    orders = jnp.broadcast_to(ordered.reshape(slots, 1), (slots, LANES))
    group = FIELDS * row_count
    padded = -(-group // LANES) * LANES
    grid_dims = (bands, row_count, modes, tiles, slots)
    fluxes = pl.pallas_call(
        lambda *refs: grid_kernel(grid_dims, *refs),
        out_shape=jax.ShapeDtypeStruct((bands, chunk_rows + 8, LANES), F32),
        in_specs=[VMEM] * 4 + [HBM],
        out_specs=VMEM,
        scratch_shapes=[
            pltpu.VMEM((slots, slots), BF),
            pltpu.VMEM((2, 2 * group, slots), BF),
            pltpu.VMEM((2, 2 * padded, KTILE), BF),
            pltpu.VMEM((2, slots, padded), F32),
            trig_scratch,
            pltpu.SemaphoreType.DMA((trig_tiles,)),
        ],
        compiler_params=params,
        cost_estimate=work(8),
        name="grid",
    )(received, orders, capture_rate.reshape(row_count, NLON), row_sine, trig)
    returned = exchange(fluxes)

    chunk_shape = (blocks, chunks, CHUNK * BLK, 2 * HALF)
    legendre, within = pl.pallas_call(
        lambda *refs: table_kernel(blocks, *refs),
        out_shape=[
            jax.ShapeDtypeStruct(chunk_shape, BF),
            jax.ShapeDtypeStruct((modes, DEG), F32),
        ],
        in_specs=[SMEM, SMEM, VMEM],
        out_specs=[HBM, VMEM],
        scratch_shapes=[per_order] * 2
        + [pltpu.VMEM(chunk_shape, BF), pltpu.SemaphoreType.DMA((blocks, chunks))],
        compiler_params=params,
        cost_estimate=work(12),
        name="table",
    )(local, scalars, rows)
    column = jnp.broadcast_to(row_latitude[:, None], (NLAT, LANES))
    result = pl.pallas_call(
        lambda *refs: analyze_kernel(dims, chunk_rows, *refs),
        out_shape=jax.ShapeDtypeStruct((CHAN, modes, DEG), F32),
        in_specs=[SMEM, VMEM, VMEM, VMEM, VMEM, HBM],
        out_specs=VMEM,
        scratch_shapes=[
            pltpu.VMEM(chunk_shape, BF),
            pltpu.VMEM((blocks, 2 * HALF, 2 * LANES), BF),
            pltpu.VMEM((blocks * 4 * ROWS, NLAT), BF),
            pltpu.VMEM((blocks, DEG, LANES), F32),
            pltpu.VMEM((NLAT, HALF), BF),
            pltpu.VMEM((blocks, CHAN, BLK, DEG), F32),
            pltpu.SemaphoreType.DMA((blocks, chunks)),
        ],
        compiler_params=params,
        cost_estimate=work(9),
        name="analyze",
    )(local, returned, column, latitude, within, legendre)
    return result.reshape(1, FIELDS, 2, modes, DEG)


def solution(mesh):
    return jax.shard_map(
        per_device,
        mesh=mesh,
        in_specs=(P("shell", None, None, "band", None), P("shell", "band", None), P(), P()),
        out_specs=P("shell", None, None, "band", None),
        check_vma=False,
    )
```

```python
import functools
import math

import jax
import jax.numpy as jnp
import numpy as np
from jax import lax
from jax.experimental import pallas as pl
from jax.experimental.pallas import tpu as pltpu
from jax.sharding import PartitionSpec as P

DEG = 512
NLAT = 1024
NLON = 2048
FIELDS = 3
HALF = NLAT // 2
CHAN = 2 * FIELDS
BLK = 8
ROWS = CHAN * BLK
CHUNK = 64
CHECK = 16
PLACES = 1024
LANES = 128
KTILE = 256
BF = jnp.bfloat16
F32 = jnp.float32


def split_two(value):
    high = value.astype(BF)
    low = (value - high.astype(F32)).astype(BF)
    return high, low


def dot(lhs, rhs, contract_rhs=0):
    return lax.dot_general(
        lhs, rhs, (((1,), (contract_rhs,)), ((), ())), preferred_element_type=F32
    )


def latitude_rows():
    theta = np.pi * (np.arange(HALF) + 0.5) / NLAT
    index = np.arange(DEG, dtype=np.float64)
    log_terms = np.zeros(DEG)
    log_terms[1:] = 0.5 * np.log2((2.0 * index[1:] + 1.0) / (2.0 * index[1:]))
    rows = np.zeros((8, DEG))
    rows[0], rows[1], rows[2] = np.cos(theta), np.log2(np.sin(theta)), log_terms
    return rows.astype(np.float32)


def spread_matrix():
    spread = np.zeros((LANES, 2, 2, CHUNK // 2, BLK), np.float32)
    for half in range(2):
        for parity in range(2):
            for step in range(CHUNK // 2):
                spread[half * CHUNK + 2 * step + parity, half, parity, step, :] = 1.0
    return spread.reshape(LANES, 2 * 2 * (CHUNK // 2) * BLK).astype(BF)


def degree_scalars():
    before = np.arange(DEG, dtype=np.float64) - 1.0
    square = before * before
    return np.concatenate([square, 4.0 / (4.0 * square - 1.0)]).astype(np.float32)


def block_orders(slots_ref, first):
    sublane = lax.broadcasted_iota(jnp.int32, (BLK, LANES), 0)
    orders = jnp.zeros((BLK, LANES), jnp.int32)
    lowest, highest = jnp.int32(DEG), jnp.int32(0)
    for i in range(BLK):
        order = slots_ref[first + i] // PLACES
        orders = jnp.where(sublane == i, order, orders)
        lowest, highest = jnp.minimum(lowest, order), jnp.maximum(highest, order)
    return orders, lowest // CHUNK, highest // CHUNK + 1


def running_sum(terms, length):
    lane = lax.broadcasted_iota(jnp.int32, terms.shape, 1) & (length - 1)
    shift = 1
    while shift < length:
        moved = pltpu.roll(terms, shift, 1)
        terms = terms + jnp.where(lane >= shift, moved, 0.0)
        shift *= 2
    return terms


def recursion_tables(slots_ref, modes, rows_ref, start_ref, before_ref, within_ref):
    orders = [block_orders(slots_ref, at)[0][:, :1] for at in range(0, modes, BLK)]
    order = jnp.concatenate(orders, 0).astype(F32)
    position = lax.broadcasted_iota(jnp.int32, (modes, DEG), 1)
    degree = position.astype(F32)
    square = degree * degree
    above = degree > order
    gap = jnp.where(above, square - order * order, 1.0)
    growth = jnp.where(above, 0.5 * jnp.log2((square - 0.25) / gap), 0.0)
    before_ref[...] = running_sum(growth, DEG)
    later = jnp.where(position & (CHECK - 1) == 0, 0.0, growth)
    within_ref[...] = jnp.exp2(running_sum(later, CHECK))
    terms = jnp.where(degree <= order, rows_ref[2:3, :], 0.0)
    norm = jnp.where(order > 0, 0.5 + jnp.sum(terms, axis=1, keepdims=True), 0.0)
    start_ref[...] = norm + order * rows_ref[1:2, :]


def run_chunk(step, carry, double_cosine, orders, before, scalars_ref, emit, beside, guard):
    current, previous, log_scale = carry
    order = orders.astype(F32)
    order_square = order * order
    before = pltpu.roll(before, (step % 2) * CHUNK, 1)
    scale = None
    for i in range(CHUNK):
        if i % CHECK == 0:
            size = jnp.maximum(jnp.abs(current), jnp.abs(previous))
            large, small = size > 2.0**40, size < 2.0**-40
            factor = jnp.where(large, 2.0**-60, jnp.where(small, 2.0**60, 1.0))
            change = jnp.where(large, 60.0, jnp.where(small, -60.0, 0.0))
            current = current * factor
            previous = previous * factor
            log_scale = log_scale + change
            scale = jnp.exp2(jnp.maximum(log_scale + before[:, i : i + 1], -200.0))
        degree = step * CHUNK + i
        factor = (scalars_ref[degree] - order_square) * scalars_ref[DEG + degree]
        factor = jnp.tile(factor, (1, HALF // LANES))
        newest = double_cosine * current - factor * previous
        if guard:
            started = jnp.tile(orders, (1, HALF // LANES)) < degree
            newest = jnp.where(started, newest, 1.0)
        current, previous = newest, current
        emit(i, newest * scale)
        if beside and i % (CHUNK // len(beside)) == 1:
            beside[i // (CHUNK // len(beside))]()
    return current, previous, log_scale


def before_tile(before_ref, block, step):
    rows = pl.ds(pl.multiple_of(block * BLK, BLK), BLK)
    return before_ref[rows, pl.ds(pl.multiple_of(step // 2 * LANES, LANES), LANES)]


def start_state(start_ref, block):
    ones = jnp.ones((BLK, HALF), F32)
    return ones, ones, start_ref[pl.ds(pl.multiple_of(block * BLK, BLK), BLK), :]


def fold_matrix(latitude_ref, fold_ref):
    latitude = latitude_ref[...]
    north = jnp.where(latitude < HALF, latitude, NLAT - 1 - latitude)
    sublane = lax.broadcasted_iota(jnp.int32, (HALF, NLAT), 0)
    fold_ref[...] = jnp.where(sublane == north, 1.0, 0.0).astype(BF)


def synth_kernel(
    dims, slots_ref, scalars_in, spec_in, rows_in, spread_in, latitude_in,
    out_ref, scalars_ref, spec_ref, rows_ref, spread_ref, latitude_ref, sems,
    start_ref, before_ref, within_ref, lhs_ref, high_a, low_a, high_b, low_b, acc_ref, fold_ref, coeff_ref,
):
    bands, row_count, modes, blocks, tiles = dims
    pairs = (
        (rows_in, rows_ref), (scalars_in, scalars_ref), (latitude_in, latitude_ref),
        (spread_in, spread_ref), (spec_in, spec_ref),
    )
    copies = []
    for index, (source, target) in enumerate(pairs):
        copies.append(pltpu.make_async_copy(source, target, sems.at[index]))
        copies[-1].start()
    copies[0].wait()
    recursion_tables(slots_ref, modes, rows_ref, start_ref, before_ref, within_ref)
    for copy in copies[1:]:
        copy.wait()
    fold_matrix(latitude_ref, fold_ref)
    south = latitude_ref[...] >= HALF
    spread_width = 4 * (CHUNK // 2) * BLK
    lane = lax.broadcasted_iota(jnp.int32, (2 * ROWS, spread_width), 1)
    sub = lax.broadcasted_iota(jnp.int32, (2 * ROWS, spread_width), 0)
    diagonal = (lane % BLK) == (sub % BLK)
    width = (CHUNK // 2) * BLK

    def one_block(block, unused):
        orders, first, last = block_orders(slots_ref, block * BLK)
        column = orders[:, :1]
        here = pl.ds(pl.multiple_of(block * BLK, BLK), BLK)
        for i in range(BLK):
            source = pl.ds(slots_ref[block * BLK + i] % PLACES, 1)
            coeff_ref[:, i : i + 1, :] = spec_ref[:, source, :]
        degree = lax.broadcasted_iota(jnp.int32, (BLK, DEG), 1)
        within = jnp.where(degree >= column, within_ref[here, :], 0.0)
        coeffs = coeff_ref[...] * within[None]
        coeff_high, coeff_low = split_two(coeffs.reshape(ROWS, DEG))
        stacked = jnp.concatenate([coeff_high, coeff_low], 0)
        for t in range(DEG // LANES):
            wide = dot(stacked[:, t * LANES : (t + 1) * LANES], spread_ref[...])
            wide = jnp.where(diagonal, wide, 0.0).astype(BF)
            for half in range(2):
                lhs_ref[2 * t + half] = wide[:, half * 2 * width : (half + 1) * 2 * width]
        acc_ref[block] = jnp.zeros((2, ROWS, HALF), F32)
        cosine = jnp.broadcast_to(2.0 * rows_ref[0:1, :], (BLK, HALF))

        def recur(step, carry, high_ref, low_ref, beside, guard):
            held = {}

            def emit(i, value):
                if i % 4 < 2:
                    held[i] = value
                else:
                    pair = jnp.concatenate([held.pop(i - 2), value], 0)
                    high, low = split_two(pair)
                    at = (i // 4) * 2 * BLK
                    high_ref[i % 2, at : at + 2 * BLK, :] = high
                    low_ref[i % 2, at : at + 2 * BLK, :] = low

            before = before_tile(before_ref, block, step)
            return run_chunk(
                step, carry, cosine, orders, before, scalars_ref, emit, beside, guard
            )

        def add_products(step, high_ref, low_ref):
            def high_part(parity, columns):
                lhs = lhs_ref[step, :, parity * width : (parity + 1) * width]
                first = dot(lhs, high_ref[parity, :, columns])
                acc_ref[block, parity, :, columns] += first[:ROWS] + first[ROWS:]

            def low_part(parity, columns):
                lhs = lhs_ref[step, :ROWS, parity * width : (parity + 1) * width]
                acc_ref[block, parity, :, columns] += dot(lhs, low_ref[parity, :, columns])

            return [
                functools.partial(part, parity, slice(at, at + KTILE))
                for parity in range(2)
                for at in range(0, HALF, KTILE)
                for part in (high_part, low_part)
            ]

        def two_chunks(guard, pair, carry):
            step = 2 * pair
            beside = add_products(jnp.maximum(step - 1, 0), high_b, low_b)
            carry = recur(step, carry, high_a, low_a, beside, guard)
            beside = add_products(step, high_a, low_a)
            return recur(step + 1, carry, high_b, low_b, beside, guard)

        high_b[...] = jnp.zeros_like(high_b)
        low_b[...] = jnp.zeros_like(low_b)
        chunks = DEG // CHUNK
        state = lax.fori_loop(
            0,
            first & 1,
            lambda unused, carry: recur(first, carry, high_b, low_b, (), True),
            start_state(start_ref, block),
        )
        middle = (last + 1) // 2
        state = lax.fori_loop(
            (first + 1) // 2, middle, functools.partial(two_chunks, True), state
        )
        lax.fori_loop(middle, chunks // 2, functools.partial(two_chunks, False), state)
        for part in add_products(chunks - 1, high_b, low_b):
            part()
        return unused

    lax.fori_loop(0, blocks, one_block, 0)
    high, low = split_two(acc_ref[...].reshape(blocks * 2 * ROWS, HALF))
    moved = dot(jnp.concatenate([high, low], 0), fold_ref[...])
    moved = moved[: blocks * 2 * ROWS] + moved[blocks * 2 * ROWS :]
    for block in range(blocks):
        orders = block_orders(slots_ref, block * BLK)[0][:, :1]
        sign = jnp.tile(1.0 - 2.0 * (orders % 2).astype(F32), (CHAN, 1))
        even = moved[block * 2 * ROWS : block * 2 * ROWS + ROWS]
        odd = moved[block * 2 * ROWS + ROWS : (block + 1) * 2 * ROWS]
        values = jnp.where(south, sign * (even - odd), even + odd)
        for d in range(bands):
            parts = []
            for kind in range(2):
                for field in range(FIELDS):
                    c = field * 2 + kind
                    parts.append(
                        values[c * BLK : (c + 1) * BLK, d * row_count : (d + 1) * row_count]
                    )
            if CHAN * row_count < tiles * LANES:
                parts.append(jnp.zeros((BLK, tiles * LANES - CHAN * row_count), F32))
            joined = jnp.concatenate(parts, 1)
            for t in range(tiles):
                at = slice((t * blocks + block) * BLK, (t * blocks + block + 1) * BLK)
                out_ref[d, at, :] = joined[:, t * LANES : (t + 1) * LANES]


def table_kernel(
    blocks, slots_ref, scalars_ref, rows_ref, out_ref, within_out, start_ref, before_ref,
    chunk_ref, sems,
):
    modes = blocks * BLK
    cosine = jnp.broadcast_to(2.0 * rows_ref[0:1, :], (BLK, HALF))
    recursion_tables(slots_ref, modes, rows_ref, start_ref, before_ref, within_out)

    def copy_out(block, step):
        return pltpu.make_async_copy(
            chunk_ref.at[block, step], out_ref.at[block, step], sems.at[block, step]
        )

    def one_block(block, unused):
        orders, first, last = block_orders(slots_ref, block * BLK)

        def one_chunk(guard, step, carry):
            held = {}

            def emit(i, value):
                if i % 2 == 0:
                    held[i] = value
                else:
                    pair = jnp.concatenate([held.pop(i - 1), value], 0)
                    high, low = split_two(pair)
                    at = (i // 2) * 2 * BLK
                    chunk_ref[block, step, at : at + 2 * BLK, :HALF] = high
                    chunk_ref[block, step, at : at + 2 * BLK, HALF:] = low

            before = before_tile(before_ref, block, step)
            carry = run_chunk(
                step, carry, cosine, orders, before, scalars_ref, emit, (), guard
            )
            copy_out(block, step).start()
            return carry

        state = start_state(start_ref, block)
        state = lax.fori_loop(first, last, functools.partial(one_chunk, True), state)
        lax.fori_loop(last, DEG // CHUNK, functools.partial(one_chunk, False), state)
        return unused

    def finish_block(block, unused):
        orders, first, last = block_orders(slots_ref, block * BLK)

        def finish_chunk(step, inner):
            copy_out(block, step).wait()
            return inner

        return lax.fori_loop(first, DEG // CHUNK, finish_chunk, unused)

    lax.fori_loop(0, blocks, one_block, 0)
    lax.fori_loop(0, blocks, finish_block, 0)


def analyze_kernel(
    dims, total_row, slots_ref, data_ref, column_ref, latitude_ref, within_ref, table_ref,
    out_ref, chunk_ref, weight_ref, stack_ref, result_ref, fold_ref, coeff_ref, raw_ref, sems,
):
    bands, row_count, modes, blocks, tiles = dims
    chunks = DEG // CHUNK

    def copy_in(block, step):
        return pltpu.make_async_copy(
            table_ref.at[block, step], chunk_ref.at[block, step], sems.at[block, step]
        )

    def start_block(block, unused):
        orders, first, last = block_orders(slots_ref, block * BLK)

        def start_chunk(step, inner):
            copy_in(block, step).start()
            return inner

        return lax.fori_loop(first, chunks, start_chunk, unused)

    lax.fori_loop(0, blocks, start_block, 0)
    latitude = column_ref[...]
    north = jnp.where(latitude < HALF, latitude, NLAT - 1 - latitude)
    lane = lax.broadcasted_iota(jnp.int32, (NLAT, LANES), 1)
    for t in range(HALF // LANES):
        one_hot = jnp.where(north == lane + t * LANES, 1.0, 0.0).astype(BF)
        fold_ref[:, t * LANES : (t + 1) * LANES] = one_hot
    south = latitude_ref[...] >= HALF
    for block in range(blocks):
        orders = block_orders(slots_ref, block * BLK)[0][:, :1]
        sign = 1.0 - 2.0 * (orders % 2).astype(F32)
        evens, odds = [], []
        for c in range(CHAN):
            offset = ((c % 2) * FIELDS + c // 2) * row_count
            t, at = offset // LANES, offset % LANES
            rows = slice((t * blocks + block) * BLK, (t * blocks + block + 1) * BLK)
            values = jnp.concatenate(
                [data_ref[d, rows, :][:, at : at + row_count] for d in range(bands)], 1
            )
            flipped = sign * values
            evens.append(jnp.where(south, flipped, values))
            odds.append(jnp.where(south, -flipped, values))
        high, low = split_two(jnp.concatenate(evens + odds, 0))
        stack_ref[block * 4 * ROWS : block * 4 * ROWS + 2 * ROWS, :] = high
        stack_ref[block * 4 * ROWS + 2 * ROWS : (block + 1) * 4 * ROWS, :] = low
    folded = dot(stack_ref[...], fold_ref[...])
    for block in range(blocks):
        at = block * 4 * ROWS
        part = folded[at : at + 2 * ROWS] + folded[at + 2 * ROWS : at + 4 * ROWS]
        part = jnp.concatenate([part, jnp.zeros((LANES - 2 * ROWS, HALF), F32)], 0)
        high, low = split_two(part.T)
        weight_ref[block, :HALF, :LANES] = high
        weight_ref[block, :HALF, LANES:] = low
        weight_ref[block, HALF:, :LANES] = high
        weight_ref[block, HALF:, LANES:] = jnp.zeros_like(low)

    total = data_ref[0, total_row : total_row + 8]
    for d in range(1, bands):
        total = total + data_ref[d, total_row : total_row + 8]
    inverse = (1.0 / total)[:, :1]
    lane = lax.broadcasted_iota(jnp.int32, (CHUNK * BLK, LANES), 1)
    sub = lax.broadcasted_iota(jnp.int32, (CHUNK * BLK, LANES), 0)
    keep = (lane % BLK == sub % BLK) & (lane // ROWS == sub // BLK % 2)

    def one_block(block, unused):
        orders, first, last = block_orders(slots_ref, block * BLK)
        orders = orders[:, :1]
        here = pl.ds(pl.multiple_of(block * BLK, BLK), BLK)
        result_ref[block] = jnp.zeros((DEG, LANES), F32)

        def product(step, which):
            full = dot(chunk_ref[block, step], weight_ref[block])
            raw_ref[which] = full[:, :LANES] + full[:, LANES:]

        def pick(step, which):
            picked = jnp.where(keep, raw_ref[which], 0.0).reshape(CHUNK, BLK, LANES)
            to = pl.ds(pl.multiple_of(step * CHUNK, CHUNK), CHUNK)
            result_ref[block, to, :] = jnp.sum(picked, axis=1)

        def lone_chunk(unused, inner):
            copy_in(block, first).wait()
            product(first, 1)
            return inner

        def two_chunks(pair, inner):
            step = 2 * pair
            copy_in(block, step).wait()
            copy_in(block, step + 1).wait()
            product(step, 0)
            pick(jnp.maximum(step - 1, 0), 1)
            product(step + 1, 1)
            pick(step, 0)
            return inner

        raw_ref[1] = jnp.zeros((CHUNK * BLK, LANES), F32)
        lax.fori_loop(0, first & 1, lone_chunk, 0)
        lax.fori_loop((first + 1) // 2, chunks // 2, two_chunks, 0)
        pick(chunks - 1, 1)
        return unused

    lax.fori_loop(0, blocks, one_block, 0)
    for block in range(blocks):
        orders = block_orders(slots_ref, block * BLK)[0][:, :1]
        turned = result_ref[block].T
        turned = turned[:ROWS] + turned[ROWS : 2 * ROWS]
        degree = lax.broadcasted_iota(jnp.int32, (BLK, DEG), 1)
        within = jnp.where(degree >= orders, within_ref[block * BLK : (block + 1) * BLK, :], 0.0)
        for c in range(CHAN):
            part = turned[c * BLK : (c + 1) * BLK] * within
            if c // 2 == FIELDS - 1:
                part = part * inverse
            coeff_ref[block, c] = part
        for i in range(BLK):
            target = pl.ds(slots_ref[block * BLK + i] % PLACES, 1)
            out_ref[:, target, :] = coeff_ref[block, :, i : i + 1, :]


def base_trig(order, first):
    lane = lax.broadcasted_iota(jnp.int32, order.shape, 1) + first
    phase = (order * lane) & (NLON - 1)
    quarter = (phase + NLON // 8) >> 9
    rest = (phase - quarter * (NLON // 4)).astype(F32) * (2.0 * math.pi / NLON)
    square = rest * rest
    sine = 1.0 / 362880.0
    for coef in (-1.0 / 5040.0, 1.0 / 120.0, -1.0 / 6.0, 1.0):
        sine = sine * square + coef
    sine = sine * rest
    cosine = 1.0 / 40320.0
    for coef in (-1.0 / 720.0, 1.0 / 24.0, -0.5, 1.0):
        cosine = cosine * square + coef
    swap = (quarter & 1) == 1
    cos_out = jnp.where(swap, sine, cosine)
    sin_out = jnp.where(swap, cosine, sine)
    cos_out = jnp.where(((quarter + 1) & 2) == 2, -cos_out, cos_out)
    sin_out = jnp.where((quarter & 2) == 2, -sin_out, sin_out)
    return cos_out, sin_out


def trig_kernel(out_ref, trig_ref, sem):
    half = trig_ref.shape[3] // 2
    root = math.sqrt(0.5)
    for parity in range(2):

        def strip(step, unused):
            at = pl.multiple_of(step * 64, 64)
            shape = (64, LANES)
            order = 2 * (lax.broadcasted_iota(jnp.int32, shape, 0) + at) + parity
            eighth = order & 7
            odd = (eighth & 1) == 1
            turn_cos = jnp.where(odd, root, jnp.where((eighth & 2) == 0, 1.0, 0.0))
            turn_sin = jnp.where(odd, root, jnp.where((eighth & 2) == 2, 1.0, 0.0))
            turn_cos = jnp.where((eighth >= 3) & (eighth <= 5), -turn_cos, turn_cos)
            turn_sin = jnp.where(eighth > 4, -turn_sin, turn_sin)
            for t in range(KTILE // LANES):
                cosine, sine = base_trig(order, t * LANES)
                for k in range(t * LANES, NLON // 2, KTILE):
                    columns = slice(t * LANES, (t + 1) * LANES)
                    for values, start in ((cosine, at), (sine, half + at)):
                        high, low = split_two(values)
                        trig_ref[k // KTILE, 0, parity, pl.ds(start, 64), columns] = high
                        trig_ref[k // KTILE, 1, parity, pl.ds(start, 64), columns] = low
                    cosine, sine = (
                        cosine * turn_cos - sine * turn_sin,
                        sine * turn_cos + cosine * turn_sin,
                    )
            return unused

        lax.fori_loop(0, half // 64, strip, 0)
    copy = pltpu.make_async_copy(trig_ref, out_ref, sem)
    copy.start()
    copy.wait()


def grid_kernel(
    dims, data_ref, orders_ref, rate_ref, sine_ref, trig_in, out_ref,
    move_ref, lhs_ref, weight_ref, acc_ref, trig_ref, sems,
):
    bands, row_count, modes, tiles, slots = dims
    half = slots // 2
    group = FIELDS * row_count
    padded = weight_ref.shape[1] // 2

    copies = []
    for tile in range(NLON // 2 // KTILE):
        copy = pltpu.make_async_copy(trig_in.at[tile], trig_ref.at[tile], sems.at[tile])
        copy.start()
        copies.append(copy)
    order = orders_ref[...]
    natural = (order & 1) * half + (order >> 1)
    for t in range(slots // LANES):
        lane = lax.broadcasted_iota(jnp.int32, (slots, LANES), 1) + t * LANES
        one_hot = jnp.where(natural == lane, 1.0, 0.0).astype(BF)
        move_ref[:, t * LANES : (t + 1) * LANES] = one_hot
    columns = []
    for t in range(tiles):
        part = data_ref[:, t * modes : (t + 1) * modes, :]
        columns.append(part.reshape(slots, LANES).T)
    turned = jnp.concatenate(columns, 0)
    for kind in range(2):
        high, low = split_two(turned[kind * group : (kind + 1) * group])
        moved = dot(jnp.concatenate([high, low], 0), move_ref[...]).astype(BF)
        for parity in range(2):
            part = moved[:, parity * half : (parity + 1) * half]
            lhs_ref[parity, :, kind * half : (kind + 1) * half] = part
    weight_ref[...] = jnp.zeros_like(weight_ref)
    flux_scale = math.pi / (2.0 * NLAT * NLON * DEG)
    weight = jnp.tile(sine_ref[...], (1, KTILE // LANES))
    total = jnp.zeros((8, KTILE), F32)

    for k in range(0, NLON // 2, KTILE):
        copies[k // KTILE].wait()
        trig_high, trig_low = trig_ref.at[k // KTILE, 0], trig_ref.at[k // KTILE, 1]
        sums = []
        for parity in range(2):
            first = dot(lhs_ref[parity], trig_high[parity])
            second = dot(lhs_ref[parity, :group, :], trig_low[parity])
            sums.append(first[:group] + first[group:] + second)
        values = []
        for fields, at in ((sums[0] + sums[1], k), (sums[0] - sums[1], k + NLON // 2)):
            weighted_rate = rate_ref[:, at : at + KTILE] * weight
            total = total + jnp.sum(weighted_rate.reshape(row_count // 8, 8, KTILE), axis=0)
            scaled = fields[:row_count] * (weight * flux_scale)
            values.append(
                jnp.concatenate(
                    [
                        fields[row_count : 2 * row_count] * scaled,
                        fields[2 * row_count :] * scaled,
                        weighted_rate * fields[:row_count],
                    ],
                    0,
                )
            )
        for parity in range(2):
            both = values[0] + values[1] if parity == 0 else values[0] - values[1]
            high, low = split_two(both)
            columns = slice(k, k + KTILE)
            weight_ref[parity, :group, columns] = high
            weight_ref[parity, padded : padded + group, columns] = low
    for parity in range(2):
        trig_high, trig_low = [
            jnp.concatenate([trig_ref[t, part, parity] for t in range(len(copies))], 1)
            for part in range(2)
        ]
        first = dot(trig_high, weight_ref[parity], 1)
        second = dot(trig_low, weight_ref[parity, :padded, :], 1)
        acc_ref[parity] = first[:, :padded] + first[:, padded:] + second

    joined = []
    for kind in range(2):
        rows = slice(kind * half, (kind + 1) * half)
        joined.append(jnp.concatenate([acc_ref[0, rows, :group], acc_ref[1, rows, :group]], 0))
    if 2 * group < tiles * LANES:
        joined.append(jnp.zeros((slots, tiles * LANES - 2 * group), F32))
    high, low = split_two(jnp.concatenate(joined, 1))
    moved = dot(move_ref[...], jnp.concatenate([high, low], 1))
    moved = moved[:, : tiles * LANES] + moved[:, tiles * LANES :]
    for t in range(tiles):
        part = moved[:, t * LANES : (t + 1) * LANES]
        out_ref[:, t * modes : (t + 1) * modes, :] = part.reshape(bands, modes, LANES)
    out_ref[:, tiles * modes :, :] = jnp.broadcast_to(jnp.sum(total), (bands, 8, LANES))


VMEM = pl.BlockSpec(memory_space=pltpu.VMEM)
SMEM = pl.BlockSpec(memory_space=pltpu.SMEM)
HBM = pl.BlockSpec(memory_space=pltpu.HBM)


def work(microseconds):
    return pl.CostEstimate(
        flops=microseconds * 10**9, bytes_accessed=2**20, transcendentals=0
    )


def per_device(spectrum, capture_rate, row_latitude, slot_wavenumber):
    bands = lax.axis_size("band")
    modes = spectrum.shape[3]
    row_count = capture_rate.shape[1]
    slots = slot_wavenumber.shape[0]
    blocks = modes // BLK
    chunks = DEG // CHUNK
    tiles = -(-CHAN * row_count // LANES)
    band_index = lax.axis_index("band")

    def sort_rows(table):
        rank = jnp.sum((table[:, None, :] < table[:, :, None]).astype(jnp.int32), 2)
        match = rank[:, None, :] == jnp.arange(modes, dtype=jnp.int32)[None, :, None]
        keys = table * PLACES + jnp.arange(modes, dtype=jnp.int32)[None, :]
        return jnp.sum(jnp.where(match, keys[:, None, :], 0), 2).reshape(-1)

    own = lax.dynamic_slice_in_dim(slot_wavenumber, band_index * modes, modes)
    local = sort_rows(own.reshape(1, modes))
    ordered = sort_rows(slot_wavenumber.reshape(bands, modes)) // PLACES
    rows = jnp.asarray(latitude_rows())
    spread = jnp.asarray(spread_matrix())
    latitude = row_latitude.reshape(1, NLAT)
    coeffs = spectrum.reshape(CHAN, modes, DEG)
    params = pltpu.CompilerParams(vmem_limit_bytes=48 * 2**20)
    chunk_rows = tiles * modes
    dims = (bands, row_count, modes, blocks, tiles)
    scalars = jnp.asarray(degree_scalars())
    per_order = pltpu.VMEM((modes, DEG), F32)

    def exchange(value):
        return lax.all_to_all(value, "band", split_axis=0, concat_axis=0, tiled=True)

    sent = pl.pallas_call(
        lambda *refs: synth_kernel(dims, *refs),
        out_shape=jax.ShapeDtypeStruct((bands, chunk_rows, LANES), F32),
        in_specs=[SMEM] + [HBM] * 5,
        out_specs=VMEM,
        scratch_shapes=[
            pltpu.SMEM(scalars.shape, F32),
            pltpu.VMEM(coeffs.shape, F32),
            pltpu.VMEM(rows.shape, F32),
            pltpu.VMEM(spread.shape, BF),
            pltpu.VMEM(latitude.shape, jnp.int32),
            pltpu.SemaphoreType.DMA((5,)),
        ]
        + [per_order] * 3
        + [pltpu.VMEM((chunks, 2 * ROWS, CHUNK * BLK), BF)]
        + [pltpu.VMEM((2, CHUNK // 2 * BLK, HALF), BF)] * 4
        + [
            pltpu.VMEM((blocks, 2, ROWS, HALF), F32),
            pltpu.VMEM((HALF, NLAT), BF),
            pltpu.VMEM((CHAN, BLK, DEG), F32),
        ],
        compiler_params=pltpu.CompilerParams(vmem_limit_bytes=62 * 2**20),
        cost_estimate=work(15),
        name="synth",
    )(local, scalars, coeffs, rows, spread, latitude)
    received = exchange(sent)

    trig_tiles = NLON // 2 // KTILE
    trig_shape = (trig_tiles, 2, 2, slots, KTILE)
    trig_scratch = pltpu.VMEM(trig_shape, BF)
    trig = pl.pallas_call(
        trig_kernel,
        out_shape=jax.ShapeDtypeStruct(trig_shape, BF),
        out_specs=HBM,
        scratch_shapes=[trig_scratch, pltpu.SemaphoreType.DMA(())],
        compiler_params=params,
        cost_estimate=work(4),
        name="trig",
    )()

    my_latitudes = lax.dynamic_slice_in_dim(row_latitude, band_index * row_count, row_count)
    row_sine = jnp.sin(jnp.pi * (my_latitudes.astype(F32) + 0.5) / NLAT)
    row_sine = jnp.broadcast_to(row_sine[:, None], (row_count, LANES))
    orders = jnp.broadcast_to(ordered.reshape(slots, 1), (slots, LANES))
    group = FIELDS * row_count
    padded = -(-group // LANES) * LANES
    grid_dims = (bands, row_count, modes, tiles, slots)
    fluxes = pl.pallas_call(
        lambda *refs: grid_kernel(grid_dims, *refs),
        out_shape=jax.ShapeDtypeStruct((bands, chunk_rows + 8, LANES), F32),
        in_specs=[VMEM] * 4 + [HBM],
        out_specs=VMEM,
        scratch_shapes=[
            pltpu.VMEM((slots, slots), BF),
            pltpu.VMEM((2, 2 * group, slots), BF),
            pltpu.VMEM((2, 2 * padded, NLON // 2), BF),
            pltpu.VMEM((2, slots, padded), F32),
            trig_scratch,
            pltpu.SemaphoreType.DMA((trig_tiles,)),
        ],
        compiler_params=params,
        cost_estimate=work(8),
        name="grid",
    )(received, orders, capture_rate.reshape(row_count, NLON), row_sine, trig)
    returned = exchange(fluxes)

    chunk_shape = (blocks, chunks, CHUNK * BLK, 2 * HALF)
    legendre, within = pl.pallas_call(
        lambda *refs: table_kernel(blocks, *refs),
        out_shape=[
            jax.ShapeDtypeStruct(chunk_shape, BF),
            jax.ShapeDtypeStruct((modes, DEG), F32),
        ],
        in_specs=[SMEM, SMEM, VMEM],
        out_specs=[HBM, VMEM],
        scratch_shapes=[per_order] * 2
        + [pltpu.VMEM(chunk_shape, BF), pltpu.SemaphoreType.DMA((blocks, chunks))],
        compiler_params=params,
        cost_estimate=work(12),
        name="table",
    )(local, scalars, rows)
    column = jnp.broadcast_to(row_latitude[:, None], (NLAT, LANES))
    result = pl.pallas_call(
        lambda *refs: analyze_kernel(dims, chunk_rows, *refs),
        out_shape=jax.ShapeDtypeStruct((CHAN, modes, DEG), F32),
        in_specs=[SMEM, VMEM, VMEM, VMEM, VMEM, HBM],
        out_specs=VMEM,
        scratch_shapes=[
            pltpu.VMEM(chunk_shape, BF),
            pltpu.VMEM((blocks, 2 * HALF, 2 * LANES), BF),
            pltpu.VMEM((blocks * 4 * ROWS, NLAT), BF),
            pltpu.VMEM((blocks, DEG, LANES), F32),
            pltpu.VMEM((NLAT, HALF), BF),
            pltpu.VMEM((blocks, CHAN, BLK, DEG), F32),
            pltpu.VMEM((2, CHUNK * BLK, LANES), F32),
            pltpu.SemaphoreType.DMA((blocks, chunks)),
        ],
        compiler_params=params,
        cost_estimate=work(9),
        name="analyze",
    )(local, returned, column, latitude, within, legendre)
    return result.reshape(1, FIELDS, 2, modes, DEG)


def solution(mesh):
    return jax.shard_map(
        per_device,
        mesh=mesh,
        in_specs=(P("shell", None, None, "band", None), P("shell", "band", None), P(), P()),
        out_specs=P("shell", None, None, "band", None),
        check_vma=False,
    )
```

```python
import functools
import math

import jax
import jax.numpy as jnp
import numpy as np
from jax import lax
from jax.experimental import pallas as pl
from jax.experimental.pallas import tpu as pltpu
from jax.sharding import PartitionSpec as P

DEG = 512
NLAT = 1024
NLON = 2048
FIELDS = 3
HALF = NLAT // 2
CHAN = 2 * FIELDS
BLK = 8
ROWS = CHAN * BLK
CHUNK = 64
CHECK = 16
PLACES = 1024
LANES = 128
KTILE = 256
BF = jnp.bfloat16
F32 = jnp.float32


def split_two(value):
    high = value.astype(BF)
    low = (value - high.astype(F32)).astype(BF)
    return high, low


def dot(lhs, rhs, contract_rhs=0):
    return lax.dot_general(
        lhs, rhs, (((1,), (contract_rhs,)), ((), ())), preferred_element_type=F32
    )


def latitude_rows():
    theta = np.pi * (np.arange(HALF) + 0.5) / NLAT
    index = np.arange(DEG, dtype=np.float64)
    log_terms = np.zeros(DEG)
    log_terms[1:] = 0.5 * np.log2((2.0 * index[1:] + 1.0) / (2.0 * index[1:]))
    rows = np.zeros((8, DEG))
    rows[0], rows[1], rows[2] = np.cos(theta), np.log2(np.sin(theta)), log_terms
    return rows.astype(np.float32)


def spread_matrix():
    spread = np.zeros((LANES, 2, 2, CHUNK // 2, BLK), np.float32)
    for half in range(2):
        for parity in range(2):
            for step in range(CHUNK // 2):
                spread[half * CHUNK + 2 * step + parity, half, parity, step, :] = 1.0
    return spread.reshape(LANES, 2 * 2 * (CHUNK // 2) * BLK).astype(BF)


def degree_scalars():
    before = np.arange(DEG, dtype=np.float64) - 1.0
    square = before * before
    return np.concatenate([square, 4.0 / (4.0 * square - 1.0)]).astype(np.float32)


def block_orders(slots_ref, first):
    sublane = lax.broadcasted_iota(jnp.int32, (BLK, LANES), 0)
    orders = jnp.zeros((BLK, LANES), jnp.int32)
    lowest, highest = jnp.int32(DEG), jnp.int32(0)
    for i in range(BLK):
        order = slots_ref[first + i] // PLACES
        orders = jnp.where(sublane == i, order, orders)
        lowest, highest = jnp.minimum(lowest, order), jnp.maximum(highest, order)
    return orders, lowest // CHUNK, highest // CHUNK + 1


def running_sum(terms, length):
    lane = lax.broadcasted_iota(jnp.int32, terms.shape, 1) & (length - 1)
    shift = 1
    while shift < length:
        moved = pltpu.roll(terms, shift, 1)
        terms = terms + jnp.where(lane >= shift, moved, 0.0)
        shift *= 2
    return terms


def recursion_tables(slots_ref, modes, rows_ref, start_ref, before_ref, within_ref):
    orders = [block_orders(slots_ref, at)[0][:, :1] for at in range(0, modes, BLK)]
    order = jnp.concatenate(orders, 0).astype(F32)
    position = lax.broadcasted_iota(jnp.int32, (modes, DEG), 1)
    degree = position.astype(F32)
    square = degree * degree
    above = degree > order
    gap = jnp.where(above, square - order * order, 1.0)
    growth = jnp.where(above, 0.5 * jnp.log2((square - 0.25) / gap), 0.0)
    before_ref[...] = running_sum(growth, DEG)
    later = jnp.where(position & (CHECK - 1) == 0, 0.0, growth)
    within_ref[...] = jnp.exp2(running_sum(later, CHECK))
    terms = jnp.where(degree <= order, rows_ref[2:3, :], 0.0)
    norm = jnp.where(order > 0, 0.5 + jnp.sum(terms, axis=1, keepdims=True), 0.0)
    start_ref[...] = norm + order * rows_ref[1:2, :]


def run_chunk(step, carry, double_cosine, orders, before, scalars_ref, emit, beside, guard):
    current, previous, log_scale = carry
    order = orders.astype(F32)
    order_square = order * order
    before = pltpu.roll(before, (step % 2) * CHUNK, 1)
    scale = None
    for i in range(CHUNK):
        if i % CHECK == 0:
            size = jnp.maximum(jnp.abs(current), jnp.abs(previous))
            large, small = size > 2.0**40, size < 2.0**-40
            factor = jnp.where(large, 2.0**-60, jnp.where(small, 2.0**60, 1.0))
            change = jnp.where(large, 60.0, jnp.where(small, -60.0, 0.0))
            current = current * factor
            previous = previous * factor
            log_scale = log_scale + change
            scale = jnp.exp2(jnp.maximum(log_scale + before[:, i : i + 1], -200.0))
        degree = step * CHUNK + i
        factor = (scalars_ref[degree] - order_square) * scalars_ref[DEG + degree]
        factor = jnp.tile(factor, (1, HALF // LANES))
        newest = double_cosine * current - factor * previous
        if guard:
            started = jnp.tile(orders, (1, HALF // LANES)) < degree
            newest = jnp.where(started, newest, 1.0)
        current, previous = newest, current
        emit(i, newest * scale)
        if beside and i % (CHUNK // len(beside)) == 1:
            beside[i // (CHUNK // len(beside))]()
    return current, previous, log_scale


def before_tile(before_ref, block, step):
    rows = pl.ds(pl.multiple_of(block * BLK, BLK), BLK)
    return before_ref[rows, pl.ds(pl.multiple_of(step // 2 * LANES, LANES), LANES)]


def start_state(start_ref, block):
    ones = jnp.ones((BLK, HALF), F32)
    return ones, ones, start_ref[pl.ds(pl.multiple_of(block * BLK, BLK), BLK), :]


def fold_matrix(latitude_ref, fold_ref):
    latitude = latitude_ref[...]
    north = jnp.where(latitude < HALF, latitude, NLAT - 1 - latitude)
    sublane = lax.broadcasted_iota(jnp.int32, (HALF, NLAT), 0)
    fold_ref[...] = jnp.where(sublane == north, 1.0, 0.0).astype(BF)


def synth_kernel(
    dims, slots_ref, scalars_in, spec_in, rows_in, spread_in, latitude_in,
    out_ref, scalars_ref, spec_ref, rows_ref, spread_ref, latitude_ref, sems,
    start_ref, before_ref, within_ref, lhs_ref, high_a, low_a, high_b, low_b, acc_ref, fold_ref, coeff_ref,
):
    bands, row_count, modes, blocks, tiles = dims
    pairs = (
        (rows_in, rows_ref), (scalars_in, scalars_ref), (latitude_in, latitude_ref),
        (spread_in, spread_ref), (spec_in, spec_ref),
    )
    copies = []
    for index, (source, target) in enumerate(pairs):
        copies.append(pltpu.make_async_copy(source, target, sems.at[index]))
        copies[-1].start()
    copies[0].wait()
    recursion_tables(slots_ref, modes, rows_ref, start_ref, before_ref, within_ref)
    for copy in copies[1:]:
        copy.wait()
    fold_matrix(latitude_ref, fold_ref)
    south = latitude_ref[...] >= HALF
    spread_width = 4 * (CHUNK // 2) * BLK
    lane = lax.broadcasted_iota(jnp.int32, (2 * ROWS, spread_width), 1)
    sub = lax.broadcasted_iota(jnp.int32, (2 * ROWS, spread_width), 0)
    diagonal = (lane % BLK) == (sub % BLK)
    width = (CHUNK // 2) * BLK

    def one_block(block, unused):
        orders, first, last = block_orders(slots_ref, block * BLK)
        column = orders[:, :1]
        here = pl.ds(pl.multiple_of(block * BLK, BLK), BLK)
        for i in range(BLK):
            source = pl.ds(slots_ref[block * BLK + i] % PLACES, 1)
            coeff_ref[:, i : i + 1, :] = spec_ref[:, source, :]
        degree = lax.broadcasted_iota(jnp.int32, (BLK, DEG), 1)
        within = jnp.where(degree >= column, within_ref[here, :], 0.0)
        coeffs = coeff_ref[...] * within[None]
        coeff_high, coeff_low = split_two(coeffs.reshape(ROWS, DEG))
        stacked = jnp.concatenate([coeff_high, coeff_low], 0)
        for t in range(DEG // LANES):
            wide = dot(stacked[:, t * LANES : (t + 1) * LANES], spread_ref[...])
            wide = jnp.where(diagonal, wide, 0.0).astype(BF)
            for half in range(2):
                lhs_ref[2 * t + half] = wide[:, half * 2 * width : (half + 1) * 2 * width]
        acc_ref[block] = jnp.zeros((2, ROWS, HALF), F32)
        cosine = jnp.broadcast_to(2.0 * rows_ref[0:1, :], (BLK, HALF))

        def recur(step, carry, high_ref, low_ref, beside, guard):
            held = {}

            def emit(i, value):
                if i % 4 < 2:
                    held[i] = value
                else:
                    pair = jnp.concatenate([held.pop(i - 2), value], 0)
                    high, low = split_two(pair)
                    at = (i // 4) * 2 * BLK
                    high_ref[i % 2, at : at + 2 * BLK, :] = high
                    low_ref[i % 2, at : at + 2 * BLK, :] = low

            before = before_tile(before_ref, block, step)
            return run_chunk(
                step, carry, cosine, orders, before, scalars_ref, emit, beside, guard
            )

        def add_products(step, high_ref, low_ref):
            def high_part(parity, columns):
                lhs = lhs_ref[step, :, parity * width : (parity + 1) * width]
                first = dot(lhs, high_ref[parity, :, columns])
                acc_ref[block, parity, :, columns] += first[:ROWS] + first[ROWS:]

            def low_part(parity, columns):
                lhs = lhs_ref[step, :ROWS, parity * width : (parity + 1) * width]
                acc_ref[block, parity, :, columns] += dot(lhs, low_ref[parity, :, columns])

            return [
                functools.partial(part, parity, slice(at, at + KTILE))
                for parity in range(2)
                for at in range(0, HALF, KTILE)
                for part in (high_part, low_part)
            ]

        def two_chunks(guard, pair, carry):
            step = 2 * pair
            beside = add_products(jnp.maximum(step - 1, 0), high_b, low_b)
            carry = recur(step, carry, high_a, low_a, beside, guard)
            beside = add_products(step, high_a, low_a)
            return recur(step + 1, carry, high_b, low_b, beside, guard)

        high_b[...] = jnp.zeros_like(high_b)
        low_b[...] = jnp.zeros_like(low_b)
        chunks = DEG // CHUNK
        state = lax.fori_loop(
            0,
            first & 1,
            lambda unused, carry: recur(first, carry, high_b, low_b, (), True),
            start_state(start_ref, block),
        )
        middle = (last + 1) // 2
        state = lax.fori_loop(
            (first + 1) // 2, middle, functools.partial(two_chunks, True), state
        )
        lax.fori_loop(middle, chunks // 2, functools.partial(two_chunks, False), state)
        for part in add_products(chunks - 1, high_b, low_b):
            part()
        return unused

    lax.fori_loop(0, blocks, one_block, 0)
    high, low = split_two(acc_ref[...].reshape(blocks * 2 * ROWS, HALF))
    moved = dot(jnp.concatenate([high, low], 0), fold_ref[...])
    moved = moved[: blocks * 2 * ROWS] + moved[blocks * 2 * ROWS :]
    for block in range(blocks):
        orders = block_orders(slots_ref, block * BLK)[0][:, :1]
        sign = jnp.tile(1.0 - 2.0 * (orders % 2).astype(F32), (CHAN, 1))
        even = moved[block * 2 * ROWS : block * 2 * ROWS + ROWS]
        odd = moved[block * 2 * ROWS + ROWS : (block + 1) * 2 * ROWS]
        values = jnp.where(south, sign * (even - odd), even + odd)
        for d in range(bands):
            parts = []
            for kind in range(2):
                for field in range(FIELDS):
                    c = field * 2 + kind
                    parts.append(
                        values[c * BLK : (c + 1) * BLK, d * row_count : (d + 1) * row_count]
                    )
            if CHAN * row_count < tiles * LANES:
                parts.append(jnp.zeros((BLK, tiles * LANES - CHAN * row_count), F32))
            joined = jnp.concatenate(parts, 1)
            for t in range(tiles):
                at = slice((t * blocks + block) * BLK, (t * blocks + block + 1) * BLK)
                out_ref[d, at, :] = joined[:, t * LANES : (t + 1) * LANES]


def table_kernel(
    blocks, slots_ref, scalars_ref, rows_ref, out_ref, within_out, start_ref, before_ref,
    chunk_ref, sems,
):
    modes = blocks * BLK
    cosine = jnp.broadcast_to(2.0 * rows_ref[0:1, :], (BLK, HALF))
    recursion_tables(slots_ref, modes, rows_ref, start_ref, before_ref, within_out)

    def copy_out(block, step):
        return pltpu.make_async_copy(
            chunk_ref.at[block, step], out_ref.at[block, step], sems.at[block, step]
        )

    def one_block(block, unused):
        orders, first, last = block_orders(slots_ref, block * BLK)

        def one_chunk(guard, step, carry):
            held = {}

            def emit(i, value):
                if i % 2 == 0:
                    held[i] = value
                else:
                    pair = jnp.concatenate([held.pop(i - 1), value], 0)
                    high, low = split_two(pair)
                    at = (i // 2) * 2 * BLK
                    chunk_ref[block, step, at : at + 2 * BLK, :HALF] = high
                    chunk_ref[block, step, at : at + 2 * BLK, HALF:] = low

            before = before_tile(before_ref, block, step)
            carry = run_chunk(
                step, carry, cosine, orders, before, scalars_ref, emit, (), guard
            )
            copy_out(block, step).start()
            return carry

        state = start_state(start_ref, block)
        state = lax.fori_loop(first, last, functools.partial(one_chunk, True), state)
        lax.fori_loop(last, DEG // CHUNK, functools.partial(one_chunk, False), state)
        return unused

    def finish_block(block, unused):
        orders, first, last = block_orders(slots_ref, block * BLK)

        def finish_chunk(step, inner):
            copy_out(block, step).wait()
            return inner

        return lax.fori_loop(first, DEG // CHUNK, finish_chunk, unused)

    lax.fori_loop(0, blocks, one_block, 0)
    lax.fori_loop(0, blocks, finish_block, 0)


def analyze_kernel(
    dims, slots_ref, data_ref, total_ref, column_ref, latitude_ref, within_ref, table_ref,
    out_ref, chunk_ref, weight_ref, stack_ref, result_ref, fold_ref, coeff_ref, raw_ref, sems,
):
    bands, row_count, modes, blocks, tiles = dims
    chunks = DEG // CHUNK

    def copy_in(block, step):
        return pltpu.make_async_copy(
            table_ref.at[block, step], chunk_ref.at[block, step], sems.at[block, step]
        )

    def start_block(block, unused):
        orders, first, last = block_orders(slots_ref, block * BLK)

        def start_chunk(step, inner):
            copy_in(block, step).start()
            return inner

        return lax.fori_loop(first, chunks, start_chunk, unused)

    lax.fori_loop(0, blocks, start_block, 0)
    latitude = column_ref[...]
    north = jnp.where(latitude < HALF, latitude, NLAT - 1 - latitude)
    lane = lax.broadcasted_iota(jnp.int32, (NLAT, LANES), 1)
    for t in range(HALF // LANES):
        one_hot = jnp.where(north == lane + t * LANES, 1.0, 0.0).astype(BF)
        fold_ref[:, t * LANES : (t + 1) * LANES] = one_hot
    south = latitude_ref[...] >= HALF
    for block in range(blocks):
        orders = block_orders(slots_ref, block * BLK)[0][:, :1]
        sign = 1.0 - 2.0 * (orders % 2).astype(F32)
        evens, odds = [], []
        for c in range(CHAN):
            offset = ((c % 2) * FIELDS + c // 2) * row_count
            t, at = offset // LANES, offset % LANES
            rows = slice((t * blocks + block) * BLK, (t * blocks + block + 1) * BLK)
            values = jnp.concatenate(
                [data_ref[d, rows, :][:, at : at + row_count] for d in range(bands)], 1
            )
            flipped = sign * values
            evens.append(jnp.where(south, flipped, values))
            odds.append(jnp.where(south, -flipped, values))
        high, low = split_two(jnp.concatenate(evens + odds, 0))
        stack_ref[block * 4 * ROWS : block * 4 * ROWS + 2 * ROWS, :] = high
        stack_ref[block * 4 * ROWS + 2 * ROWS : (block + 1) * 4 * ROWS, :] = low
    folded = dot(stack_ref[...], fold_ref[...])
    for block in range(blocks):
        at = block * 4 * ROWS
        part = folded[at : at + 2 * ROWS] + folded[at + 2 * ROWS : at + 4 * ROWS]
        part = jnp.concatenate([part, jnp.zeros((LANES - 2 * ROWS, HALF), F32)], 0)
        high, low = split_two(part.T)
        weight_ref[block, :HALF, :LANES] = high
        weight_ref[block, :HALF, LANES:] = low
        weight_ref[block, HALF:, :LANES] = high
        weight_ref[block, HALF:, LANES:] = jnp.zeros_like(low)

    inverse = (1.0 / total_ref[...])[:, :1]
    lane = lax.broadcasted_iota(jnp.int32, (CHUNK * BLK, LANES), 1)
    sub = lax.broadcasted_iota(jnp.int32, (CHUNK * BLK, LANES), 0)
    keep = (lane % BLK == sub % BLK) & (lane // ROWS == sub // BLK % 2)

    def one_block(block, unused):
        orders, first, last = block_orders(slots_ref, block * BLK)
        orders = orders[:, :1]
        here = pl.ds(pl.multiple_of(block * BLK, BLK), BLK)
        result_ref[block] = jnp.zeros((DEG, LANES), F32)

        def product(step, which):
            full = dot(chunk_ref[block, step], weight_ref[block])
            raw_ref[which] = full[:, :LANES] + full[:, LANES:]

        def pick(step, which):
            picked = jnp.where(keep, raw_ref[which], 0.0).reshape(CHUNK, BLK, LANES)
            to = pl.ds(pl.multiple_of(step * CHUNK, CHUNK), CHUNK)
            result_ref[block, to, :] = jnp.sum(picked, axis=1)

        def lone_chunk(unused, inner):
            copy_in(block, first).wait()
            product(first, 1)
            return inner

        def two_chunks(pair, inner):
            step = 2 * pair
            copy_in(block, step).wait()
            copy_in(block, step + 1).wait()
            product(step, 0)
            pick(jnp.maximum(step - 1, 0), 1)
            product(step + 1, 1)
            pick(step, 0)
            return inner

        raw_ref[1] = jnp.zeros((CHUNK * BLK, LANES), F32)
        lax.fori_loop(0, first & 1, lone_chunk, 0)
        lax.fori_loop((first + 1) // 2, chunks // 2, two_chunks, 0)
        pick(chunks - 1, 1)
        return unused

    lax.fori_loop(0, blocks, one_block, 0)
    for block in range(blocks):
        orders = block_orders(slots_ref, block * BLK)[0][:, :1]
        turned = result_ref[block].T
        turned = turned[:ROWS] + turned[ROWS : 2 * ROWS]
        degree = lax.broadcasted_iota(jnp.int32, (BLK, DEG), 1)
        within = jnp.where(degree >= orders, within_ref[block * BLK : (block + 1) * BLK, :], 0.0)
        for c in range(CHAN):
            part = turned[c * BLK : (c + 1) * BLK] * within
            if c // 2 == FIELDS - 1:
                part = part * inverse
            coeff_ref[block, c] = part
        for i in range(BLK):
            target = pl.ds(slots_ref[block * BLK + i] % PLACES, 1)
            out_ref[:, target, :] = coeff_ref[block, :, i : i + 1, :]


def base_trig(order, first):
    lane = lax.broadcasted_iota(jnp.int32, order.shape, 1) + first
    phase = (order * lane) & (NLON - 1)
    quarter = (phase + NLON // 8) >> 9
    rest = (phase - quarter * (NLON // 4)).astype(F32) * (2.0 * math.pi / NLON)
    square = rest * rest
    sine = 1.0 / 362880.0
    for coef in (-1.0 / 5040.0, 1.0 / 120.0, -1.0 / 6.0, 1.0):
        sine = sine * square + coef
    sine = sine * rest
    cosine = 1.0 / 40320.0
    for coef in (-1.0 / 720.0, 1.0 / 24.0, -0.5, 1.0):
        cosine = cosine * square + coef
    swap = (quarter & 1) == 1
    cos_out = jnp.where(swap, sine, cosine)
    sin_out = jnp.where(swap, cosine, sine)
    cos_out = jnp.where(((quarter + 1) & 2) == 2, -cos_out, cos_out)
    sin_out = jnp.where((quarter & 2) == 2, -sin_out, sin_out)
    return cos_out, sin_out


def trig_kernel(out_ref, trig_ref, sem):
    half = trig_ref.shape[3] // 2
    root = math.sqrt(0.5)
    for parity in range(2):

        def strip(step, unused):
            at = pl.multiple_of(step * 64, 64)
            shape = (64, LANES)
            order = 2 * (lax.broadcasted_iota(jnp.int32, shape, 0) + at) + parity
            eighth = order & 7
            odd = (eighth & 1) == 1
            turn_cos = jnp.where(odd, root, jnp.where((eighth & 2) == 0, 1.0, 0.0))
            turn_sin = jnp.where(odd, root, jnp.where((eighth & 2) == 2, 1.0, 0.0))
            turn_cos = jnp.where((eighth >= 3) & (eighth <= 5), -turn_cos, turn_cos)
            turn_sin = jnp.where(eighth > 4, -turn_sin, turn_sin)
            for t in range(KTILE // LANES):
                cosine, sine = base_trig(order, t * LANES)
                for k in range(t * LANES, NLON // 2, KTILE):
                    columns = slice(t * LANES, (t + 1) * LANES)
                    for values, start in ((cosine, at), (sine, half + at)):
                        high, low = split_two(values)
                        trig_ref[k // KTILE, 0, parity, pl.ds(start, 64), columns] = high
                        trig_ref[k // KTILE, 1, parity, pl.ds(start, 64), columns] = low
                    cosine, sine = (
                        cosine * turn_cos - sine * turn_sin,
                        sine * turn_cos + cosine * turn_sin,
                    )
            return unused

        lax.fori_loop(0, half // 64, strip, 0)
    copy = pltpu.make_async_copy(trig_ref, out_ref, sem)
    copy.start()
    copy.wait()


def grid_kernel(
    dims, data_ref, orders_ref, rate_ref, sine_ref, trig_in, out_ref,
    move_ref, lhs_ref, weight_ref, acc_ref, trig_ref, sems,
):
    bands, row_count, modes, tiles, slots = dims
    half = slots // 2
    group = FIELDS * row_count
    padded = weight_ref.shape[1] // 2

    copies = []
    for tile in range(NLON // 2 // KTILE):
        copy = pltpu.make_async_copy(trig_in.at[tile], trig_ref.at[tile], sems.at[tile])
        copy.start()
        copies.append(copy)
    order = orders_ref[...]
    natural = (order & 1) * half + (order >> 1)
    for t in range(slots // LANES):
        lane = lax.broadcasted_iota(jnp.int32, (slots, LANES), 1) + t * LANES
        one_hot = jnp.where(natural == lane, 1.0, 0.0).astype(BF)
        move_ref[:, t * LANES : (t + 1) * LANES] = one_hot
    columns = []
    for t in range(tiles):
        part = data_ref[:, t * modes : (t + 1) * modes, :]
        columns.append(part.reshape(slots, LANES).T)
    turned = jnp.concatenate(columns, 0)
    for kind in range(2):
        high, low = split_two(turned[kind * group : (kind + 1) * group])
        moved = dot(jnp.concatenate([high, low], 0), move_ref[...]).astype(BF)
        for parity in range(2):
            part = moved[:, parity * half : (parity + 1) * half]
            lhs_ref[parity, :, kind * half : (kind + 1) * half] = part
    weight_ref[...] = jnp.zeros_like(weight_ref)
    flux_scale = math.pi / (2.0 * NLAT * NLON * DEG)
    weight = jnp.tile(sine_ref[...], (1, KTILE // LANES))

    for k in range(0, NLON // 2, KTILE):
        copies[k // KTILE].wait()
        trig_high, trig_low = trig_ref.at[k // KTILE, 0], trig_ref.at[k // KTILE, 1]
        sums = []
        for parity in range(2):
            first = dot(lhs_ref[parity], trig_high[parity])
            second = dot(lhs_ref[parity, :group, :], trig_low[parity])
            sums.append(first[:group] + first[group:] + second)
        values = []
        for fields, at in ((sums[0] + sums[1], k), (sums[0] - sums[1], k + NLON // 2)):
            weighted_rate = rate_ref[:, at : at + KTILE] * weight
            scaled = fields[:row_count] * (weight * flux_scale)
            values.append(
                jnp.concatenate(
                    [
                        fields[row_count : 2 * row_count] * scaled,
                        fields[2 * row_count :] * scaled,
                        weighted_rate * fields[:row_count],
                    ],
                    0,
                )
            )
        for parity in range(2):
            both = values[0] + values[1] if parity == 0 else values[0] - values[1]
            high, low = split_two(both)
            columns = slice(k, k + KTILE)
            weight_ref[parity, :group, columns] = high
            weight_ref[parity, padded : padded + group, columns] = low
    for parity in range(2):
        trig_high, trig_low = [
            jnp.concatenate([trig_ref[t, part, parity] for t in range(len(copies))], 1)
            for part in range(2)
        ]
        first = dot(trig_high, weight_ref[parity], 1)
        second = dot(trig_low, weight_ref[parity, :padded, :], 1)
        acc_ref[parity] = first[:, :padded] + first[:, padded:] + second

    joined = []
    for kind in range(2):
        rows = slice(kind * half, (kind + 1) * half)
        joined.append(jnp.concatenate([acc_ref[0, rows, :group], acc_ref[1, rows, :group]], 0))
    if 2 * group < tiles * LANES:
        joined.append(jnp.zeros((slots, tiles * LANES - 2 * group), F32))
    high, low = split_two(jnp.concatenate(joined, 1))
    moved = dot(move_ref[...], jnp.concatenate([high, low], 1))
    moved = moved[:, : tiles * LANES] + moved[:, tiles * LANES :]
    for t in range(tiles):
        part = moved[:, t * LANES : (t + 1) * LANES]
        out_ref[:, t * modes : (t + 1) * modes, :] = part.reshape(bands, modes, LANES)


VMEM = pl.BlockSpec(memory_space=pltpu.VMEM)
SMEM = pl.BlockSpec(memory_space=pltpu.SMEM)
HBM = pl.BlockSpec(memory_space=pltpu.HBM)


def work(microseconds):
    return pl.CostEstimate(
        flops=microseconds * 10**9, bytes_accessed=2**20, transcendentals=0
    )


def per_device(spectrum, capture_rate, row_latitude, slot_wavenumber):
    bands = lax.axis_size("band")
    modes = spectrum.shape[3]
    row_count = capture_rate.shape[1]
    slots = slot_wavenumber.shape[0]
    blocks = modes // BLK
    chunks = DEG // CHUNK
    tiles = -(-CHAN * row_count // LANES)
    band_index = lax.axis_index("band")

    def sort_rows(table):
        rank = jnp.sum((table[:, None, :] < table[:, :, None]).astype(jnp.int32), 2)
        match = rank[:, None, :] == jnp.arange(modes, dtype=jnp.int32)[None, :, None]
        keys = table * PLACES + jnp.arange(modes, dtype=jnp.int32)[None, :]
        return jnp.sum(jnp.where(match, keys[:, None, :], 0), 2).reshape(-1)

    own = lax.dynamic_slice_in_dim(slot_wavenumber, band_index * modes, modes)
    local = sort_rows(own.reshape(1, modes))
    ordered = sort_rows(slot_wavenumber.reshape(bands, modes)) // PLACES
    rows = jnp.asarray(latitude_rows())
    spread = jnp.asarray(spread_matrix())
    latitude = row_latitude.reshape(1, NLAT)
    coeffs = spectrum.reshape(CHAN, modes, DEG)
    params = pltpu.CompilerParams(vmem_limit_bytes=48 * 2**20)
    chunk_rows = tiles * modes
    dims = (bands, row_count, modes, blocks, tiles)
    scalars = jnp.asarray(degree_scalars())
    per_order = pltpu.VMEM((modes, DEG), F32)

    def exchange(value):
        return lax.all_to_all(value, "band", split_axis=0, concat_axis=0, tiled=True)

    sent = pl.pallas_call(
        lambda *refs: synth_kernel(dims, *refs),
        out_shape=jax.ShapeDtypeStruct((bands, chunk_rows, LANES), F32),
        in_specs=[SMEM] + [HBM] * 5,
        out_specs=VMEM,
        scratch_shapes=[
            pltpu.SMEM(scalars.shape, F32),
            pltpu.VMEM(coeffs.shape, F32),
            pltpu.VMEM(rows.shape, F32),
            pltpu.VMEM(spread.shape, BF),
            pltpu.VMEM(latitude.shape, jnp.int32),
            pltpu.SemaphoreType.DMA((5,)),
        ]
        + [per_order] * 3
        + [pltpu.VMEM((chunks, 2 * ROWS, CHUNK * BLK), BF)]
        + [pltpu.VMEM((2, CHUNK // 2 * BLK, HALF), BF)] * 4
        + [
            pltpu.VMEM((blocks, 2, ROWS, HALF), F32),
            pltpu.VMEM((HALF, NLAT), BF),
            pltpu.VMEM((CHAN, BLK, DEG), F32),
        ],
        compiler_params=pltpu.CompilerParams(vmem_limit_bytes=62 * 2**20),
        cost_estimate=work(15),
        name="synth",
    )(local, scalars, coeffs, rows, spread, latitude)

    trig_tiles = NLON // 2 // KTILE
    trig_shape = (trig_tiles, 2, 2, slots, KTILE)
    trig_scratch = pltpu.VMEM(trig_shape, BF)
    trig = pl.pallas_call(
        trig_kernel,
        out_shape=jax.ShapeDtypeStruct(trig_shape, BF),
        out_specs=HBM,
        scratch_shapes=[trig_scratch, pltpu.SemaphoreType.DMA(())],
        compiler_params=params,
        cost_estimate=work(4),
        name="trig",
    )()

    my_latitudes = lax.dynamic_slice_in_dim(row_latitude, band_index * row_count, row_count)
    row_sine = jnp.sin(jnp.pi * (my_latitudes.astype(F32) + 0.5) / NLAT)
    later_sine, sent = lax.optimization_barrier((row_sine, sent))
    total = jnp.full((8, LANES), jnp.sum(capture_rate * later_sine[None, :, None]))
    received = exchange(sent)
    step = 1
    while step < bands:
        pairs = [(i, i ^ step) for i in range(bands)]
        total = total + lax.ppermute(total, "band", pairs)
        step *= 2
    row_sine = jnp.broadcast_to(row_sine[:, None], (row_count, LANES))
    orders = jnp.broadcast_to(ordered.reshape(slots, 1), (slots, LANES))
    group = FIELDS * row_count
    padded = -(-group // LANES) * LANES
    grid_dims = (bands, row_count, modes, tiles, slots)
    fluxes = pl.pallas_call(
        lambda *refs: grid_kernel(grid_dims, *refs),
        out_shape=jax.ShapeDtypeStruct((bands, chunk_rows, LANES), F32),
        in_specs=[VMEM] * 4 + [HBM],
        out_specs=VMEM,
        scratch_shapes=[
            pltpu.VMEM((slots, slots), BF),
            pltpu.VMEM((2, 2 * group, slots), BF),
            pltpu.VMEM((2, 2 * padded, NLON // 2), BF),
            pltpu.VMEM((2, slots, padded), F32),
            trig_scratch,
            pltpu.SemaphoreType.DMA((trig_tiles,)),
        ],
        compiler_params=params,
        cost_estimate=work(8),
        name="grid",
    )(received, orders, capture_rate.reshape(row_count, NLON), row_sine, trig)
    returned = exchange(fluxes)

    chunk_shape = (blocks, chunks, CHUNK * BLK, 2 * HALF)
    legendre, within = pl.pallas_call(
        lambda *refs: table_kernel(blocks, *refs),
        out_shape=[
            jax.ShapeDtypeStruct(chunk_shape, BF),
            jax.ShapeDtypeStruct((modes, DEG), F32),
        ],
        in_specs=[SMEM, SMEM, VMEM],
        out_specs=[HBM, VMEM],
        scratch_shapes=[per_order] * 2
        + [pltpu.VMEM(chunk_shape, BF), pltpu.SemaphoreType.DMA((blocks, chunks))],
        compiler_params=params,
        cost_estimate=work(12),
        name="table",
    )(local, scalars, rows)
    column = jnp.broadcast_to(row_latitude[:, None], (NLAT, LANES))
    result = pl.pallas_call(
        lambda *refs: analyze_kernel(dims, *refs),
        out_shape=jax.ShapeDtypeStruct((CHAN, modes, DEG), F32),
        in_specs=[SMEM, VMEM, VMEM, VMEM, VMEM, VMEM, HBM],
        out_specs=VMEM,
        scratch_shapes=[
            pltpu.VMEM(chunk_shape, BF),
            pltpu.VMEM((blocks, 2 * HALF, 2 * LANES), BF),
            pltpu.VMEM((blocks * 4 * ROWS, NLAT), BF),
            pltpu.VMEM((blocks, DEG, LANES), F32),
            pltpu.VMEM((NLAT, HALF), BF),
            pltpu.VMEM((blocks, CHAN, BLK, DEG), F32),
            pltpu.VMEM((2, CHUNK * BLK, LANES), F32),
            pltpu.SemaphoreType.DMA((blocks, chunks)),
        ],
        compiler_params=params,
        cost_estimate=work(9),
        name="analyze",
    )(local, returned, total, column, latitude, within, legendre)
    return result.reshape(1, FIELDS, 2, modes, DEG)


def solution(mesh):
    return jax.shard_map(
        per_device,
        mesh=mesh,
        in_specs=(P("shell", None, None, "band", None), P("shell", "band", None), P(), P()),
        out_specs=P("shell", None, None, "band", None),
        check_vma=False,
    )
```

```python
import functools
import math

import jax
import jax.numpy as jnp
import numpy as np
from jax import lax
from jax.experimental import pallas as pl
from jax.experimental.pallas import tpu as pltpu
from jax.sharding import PartitionSpec as P

DEG = 512
NLAT = 1024
NLON = 2048
FIELDS = 3
HALF = NLAT // 2
CHAN = 2 * FIELDS
BLK = 8
ROWS = CHAN * BLK
CHUNK = 64
CHECK = 16
PLACES = 1024
LANES = 128
KTILE = 256
BF = jnp.bfloat16
F32 = jnp.float32


def split_two(value):
    high = value.astype(BF)
    low = (value - high.astype(F32)).astype(BF)
    return high, low


def dot(lhs, rhs, contract_rhs=0):
    return lax.dot_general(
        lhs, rhs, (((1,), (contract_rhs,)), ((), ())), preferred_element_type=F32
    )


def latitude_rows():
    theta = np.pi * (np.arange(HALF) + 0.5) / NLAT
    index = np.arange(DEG, dtype=np.float64)
    log_terms = np.zeros(DEG)
    log_terms[1:] = 0.5 * np.log2((2.0 * index[1:] + 1.0) / (2.0 * index[1:]))
    rows = np.zeros((8, DEG))
    rows[0], rows[1], rows[2] = np.cos(theta), np.log2(np.sin(theta)), log_terms
    return rows.astype(np.float32)


def spread_matrix():
    spread = np.zeros((LANES, 2, 2, CHUNK // 2, BLK), np.float32)
    for half in range(2):
        for parity in range(2):
            for step in range(CHUNK // 2):
                spread[half * CHUNK + 2 * step + parity, half, parity, step, :] = 1.0
    return spread.reshape(LANES, 2 * 2 * (CHUNK // 2) * BLK).astype(BF)


def degree_scalars():
    before = np.arange(DEG, dtype=np.float64) - 1.0
    square = before * before
    return np.concatenate([square, 4.0 / (4.0 * square - 1.0)]).astype(np.float32)


def block_orders(slots_ref, first):
    sublane = lax.broadcasted_iota(jnp.int32, (BLK, LANES), 0)
    orders = jnp.zeros((BLK, LANES), jnp.int32)
    lowest, highest = jnp.int32(DEG), jnp.int32(0)
    for i in range(BLK):
        order = slots_ref[first + i] // PLACES
        orders = jnp.where(sublane == i, order, orders)
        lowest, highest = jnp.minimum(lowest, order), jnp.maximum(highest, order)
    return orders, lowest // CHUNK, highest // CHUNK + 1


def running_sum(terms, length):
    lane = lax.broadcasted_iota(jnp.int32, terms.shape, 1) & (length - 1)
    shift = 1
    while shift < length:
        moved = pltpu.roll(terms, shift, 1)
        terms = terms + jnp.where(lane >= shift, moved, 0.0)
        shift *= 2
    return terms


def recursion_tables(slots_ref, modes, rows_ref, start_ref, before_ref, within_ref):
    orders = [block_orders(slots_ref, at)[0][:, :1] for at in range(0, modes, BLK)]
    order = jnp.concatenate(orders, 0).astype(F32)
    position = lax.broadcasted_iota(jnp.int32, (modes, DEG), 1)
    degree = position.astype(F32)
    square = degree * degree
    above = degree > order
    gap = jnp.where(above, square - order * order, 1.0)
    growth = jnp.where(above, 0.5 * jnp.log2((square - 0.25) / gap), 0.0)
    before_ref[...] = running_sum(growth, DEG)
    later = jnp.where(position & (CHECK - 1) == 0, 0.0, growth)
    within_ref[...] = jnp.exp2(running_sum(later, CHECK))
    terms = jnp.where(degree <= order, rows_ref[2:3, :], 0.0)
    norm = jnp.where(order > 0, 0.5 + jnp.sum(terms, axis=1, keepdims=True), 0.0)
    start_ref[...] = norm + order * rows_ref[1:2, :]


def run_chunk(step, carry, double_cosine, orders, before, scalars_ref, emit, beside, guard):
    current, previous, log_scale = carry
    order = orders.astype(F32)
    order_square = order * order
    before = pltpu.roll(before, (step % 2) * CHUNK, 1)
    scale = None
    for i in range(CHUNK):
        if i % CHECK == 0:
            size = jnp.maximum(jnp.abs(current), jnp.abs(previous))
            large, small = size > 2.0**40, size < 2.0**-40
            factor = jnp.where(large, 2.0**-60, jnp.where(small, 2.0**60, 1.0))
            change = jnp.where(large, 60.0, jnp.where(small, -60.0, 0.0))
            current = current * factor
            previous = previous * factor
            log_scale = log_scale + change
            scale = jnp.exp2(jnp.maximum(log_scale + before[:, i : i + 1], -200.0))
        degree = step * CHUNK + i
        factor = (scalars_ref[degree] - order_square) * scalars_ref[DEG + degree]
        factor = jnp.tile(factor, (1, HALF // LANES))
        newest = double_cosine * current - factor * previous
        if guard:
            started = jnp.tile(orders, (1, HALF // LANES)) < degree
            newest = jnp.where(started, newest, 1.0)
        current, previous = newest, current
        emit(i, newest * scale)
        if beside and i % (CHUNK // len(beside)) == 1:
            beside[i // (CHUNK // len(beside))]()
    return current, previous, log_scale


def before_tile(before_ref, block, step):
    rows = pl.ds(pl.multiple_of(block * BLK, BLK), BLK)
    return before_ref[rows, pl.ds(pl.multiple_of(step // 2 * LANES, LANES), LANES)]


def start_state(start_ref, block):
    ones = jnp.ones((BLK, HALF), F32)
    return ones, ones, start_ref[pl.ds(pl.multiple_of(block * BLK, BLK), BLK), :]


def fold_matrix(latitude_ref, fold_ref):
    latitude = latitude_ref[...]
    north = jnp.where(latitude < HALF, latitude, NLAT - 1 - latitude)
    sublane = lax.broadcasted_iota(jnp.int32, (HALF, NLAT), 0)
    fold_ref[...] = jnp.where(sublane == north, 1.0, 0.0).astype(BF)


def synth_kernel(
    dims, slots_ref, scalars_in, spec_in, rows_in, spread_in, latitude_in,
    out_ref, scalars_ref, spec_ref, rows_ref, spread_ref, latitude_ref, sems,
    start_ref, before_ref, within_ref, lhs_ref, high_a, low_a, high_b, low_b, acc_ref, fold_ref, coeff_ref,
):
    bands, row_count, modes, blocks, tiles = dims
    pairs = (
        (rows_in, rows_ref), (scalars_in, scalars_ref), (latitude_in, latitude_ref),
        (spread_in, spread_ref), (spec_in, spec_ref),
    )
    copies = []
    for index, (source, target) in enumerate(pairs):
        copies.append(pltpu.make_async_copy(source, target, sems.at[index]))
        copies[-1].start()
    copies[0].wait()
    recursion_tables(slots_ref, modes, rows_ref, start_ref, before_ref, within_ref)
    for copy in copies[1:]:
        copy.wait()
    fold_matrix(latitude_ref, fold_ref)
    south = latitude_ref[...] >= HALF
    spread_width = 4 * (CHUNK // 2) * BLK
    lane = lax.broadcasted_iota(jnp.int32, (2 * ROWS, spread_width), 1)
    sub = lax.broadcasted_iota(jnp.int32, (2 * ROWS, spread_width), 0)
    diagonal = (lane % BLK) == (sub % BLK)
    width = (CHUNK // 2) * BLK

    def one_block(block, unused):
        orders, first, last = block_orders(slots_ref, block * BLK)
        column = orders[:, :1]
        here = pl.ds(pl.multiple_of(block * BLK, BLK), BLK)
        for i in range(BLK):
            source = pl.ds(slots_ref[block * BLK + i] % PLACES, 1)
            coeff_ref[:, i : i + 1, :] = spec_ref[:, source, :]
        degree = lax.broadcasted_iota(jnp.int32, (BLK, DEG), 1)
        within = jnp.where(degree >= column, within_ref[here, :], 0.0)
        coeffs = coeff_ref[...] * within[None]
        coeff_high, coeff_low = split_two(coeffs.reshape(ROWS, DEG))
        stacked = jnp.concatenate([coeff_high, coeff_low], 0)
        for t in range(DEG // LANES):
            wide = dot(stacked[:, t * LANES : (t + 1) * LANES], spread_ref[...])
            wide = jnp.where(diagonal, wide, 0.0).astype(BF)
            for half in range(2):
                lhs_ref[2 * t + half] = wide[:, half * 2 * width : (half + 1) * 2 * width]
        acc_ref[block] = jnp.zeros((2, ROWS, HALF), F32)
        cosine = jnp.broadcast_to(2.0 * rows_ref[0:1, :], (BLK, HALF))

        def recur(step, carry, high_ref, low_ref, beside, guard):
            held = {}

            def emit(i, value):
                if i % 4 < 2:
                    held[i] = value
                else:
                    pair = jnp.concatenate([held.pop(i - 2), value], 0)
                    high, low = split_two(pair)
                    at = (i // 4) * 2 * BLK
                    high_ref[i % 2, at : at + 2 * BLK, :] = high
                    low_ref[i % 2, at : at + 2 * BLK, :] = low

            before = before_tile(before_ref, block, step)
            return run_chunk(
                step, carry, cosine, orders, before, scalars_ref, emit, beside, guard
            )

        def add_products(step, high_ref, low_ref):
            def high_part(parity, columns):
                lhs = lhs_ref[step, :, parity * width : (parity + 1) * width]
                first = dot(lhs, high_ref[parity, :, columns])
                acc_ref[block, parity, :, columns] += first[:ROWS] + first[ROWS:]

            def low_part(parity, columns):
                lhs = lhs_ref[step, :ROWS, parity * width : (parity + 1) * width]
                acc_ref[block, parity, :, columns] += dot(lhs, low_ref[parity, :, columns])

            return [
                functools.partial(part, parity, slice(at, at + KTILE))
                for parity in range(2)
                for at in range(0, HALF, KTILE)
                for part in (high_part, low_part)
            ]

        def two_chunks(guard, pair, carry):
            step = 2 * pair
            beside = add_products(jnp.maximum(step - 1, 0), high_b, low_b)
            carry = recur(step, carry, high_a, low_a, beside, guard)
            beside = add_products(step, high_a, low_a)
            return recur(step + 1, carry, high_b, low_b, beside, guard)

        high_b[...] = jnp.zeros_like(high_b)
        low_b[...] = jnp.zeros_like(low_b)
        chunks = DEG // CHUNK
        state = lax.fori_loop(
            0,
            first & 1,
            lambda unused, carry: recur(first, carry, high_b, low_b, (), True),
            start_state(start_ref, block),
        )
        middle = (last + 1) // 2
        state = lax.fori_loop(
            (first + 1) // 2, middle, functools.partial(two_chunks, True), state
        )
        lax.fori_loop(middle, chunks // 2, functools.partial(two_chunks, False), state)
        for part in add_products(chunks - 1, high_b, low_b):
            part()
        return unused

    lax.fori_loop(0, blocks, one_block, 0)
    high, low = split_two(acc_ref[...].reshape(blocks * 2 * ROWS, HALF))
    moved = dot(jnp.concatenate([high, low], 0), fold_ref[...])
    moved = moved[: blocks * 2 * ROWS] + moved[blocks * 2 * ROWS :]
    for block in range(blocks):
        orders = block_orders(slots_ref, block * BLK)[0][:, :1]
        sign = jnp.tile(1.0 - 2.0 * (orders % 2).astype(F32), (CHAN, 1))
        even = moved[block * 2 * ROWS : block * 2 * ROWS + ROWS]
        odd = moved[block * 2 * ROWS + ROWS : (block + 1) * 2 * ROWS]
        values = jnp.where(south, sign * (even - odd), even + odd)
        for d in range(bands):
            parts = []
            for kind in range(2):
                for field in range(FIELDS):
                    c = field * 2 + kind
                    parts.append(
                        values[c * BLK : (c + 1) * BLK, d * row_count : (d + 1) * row_count]
                    )
            if CHAN * row_count < tiles * LANES:
                parts.append(jnp.zeros((BLK, tiles * LANES - CHAN * row_count), F32))
            joined = jnp.concatenate(parts, 1)
            for t in range(tiles):
                at = slice((t * blocks + block) * BLK, (t * blocks + block + 1) * BLK)
                out_ref[d, at, :] = joined[:, t * LANES : (t + 1) * LANES]


def table_kernel(
    blocks, slots_ref, scalars_ref, rows_ref, out_ref, within_out, start_ref, before_ref,
    chunk_ref, sems,
):
    modes = blocks * BLK
    cosine = jnp.broadcast_to(2.0 * rows_ref[0:1, :], (BLK, HALF))
    recursion_tables(slots_ref, modes, rows_ref, start_ref, before_ref, within_out)

    def copy_out(block, step):
        return pltpu.make_async_copy(
            chunk_ref.at[block, step], out_ref.at[block, step], sems.at[block, step]
        )

    def one_block(block, unused):
        orders, first, last = block_orders(slots_ref, block * BLK)

        def one_chunk(guard, step, carry):
            held = {}

            def emit(i, value):
                if i % 2 == 0:
                    held[i] = value
                else:
                    pair = jnp.concatenate([held.pop(i - 1), value], 0)
                    high, low = split_two(pair)
                    at = (i // 2) * 2 * BLK
                    chunk_ref[block, step, at : at + 2 * BLK, :HALF] = high
                    chunk_ref[block, step, at : at + 2 * BLK, HALF:] = low

            before = before_tile(before_ref, block, step)
            carry = run_chunk(
                step, carry, cosine, orders, before, scalars_ref, emit, (), guard
            )
            copy_out(block, step).start()
            return carry

        state = start_state(start_ref, block)
        state = lax.fori_loop(first, last, functools.partial(one_chunk, True), state)
        lax.fori_loop(last, DEG // CHUNK, functools.partial(one_chunk, False), state)
        return unused

    def finish_block(block, unused):
        orders, first, last = block_orders(slots_ref, block * BLK)

        def finish_chunk(step, inner):
            copy_out(block, step).wait()
            return inner

        return lax.fori_loop(first, DEG // CHUNK, finish_chunk, unused)

    lax.fori_loop(0, blocks, one_block, 0)
    lax.fori_loop(0, blocks, finish_block, 0)


def analyze_kernel(
    dims, total_row, slots_ref, data_ref, column_ref, latitude_ref, within_ref, table_ref,
    out_ref, chunk_ref, weight_ref, stack_ref, result_ref, fold_ref, coeff_ref, sems,
):
    bands, row_count, modes, blocks, tiles = dims
    chunks = DEG // CHUNK

    def copy_in(block, step):
        return pltpu.make_async_copy(
            table_ref.at[block, step], chunk_ref.at[block, step], sems.at[block, step]
        )

    def start_block(block, unused):
        orders, first, last = block_orders(slots_ref, block * BLK)

        def start_chunk(step, inner):
            copy_in(block, step).start()
            return inner

        return lax.fori_loop(first, chunks, start_chunk, unused)

    lax.fori_loop(0, blocks, start_block, 0)
    latitude = column_ref[...]
    north = jnp.where(latitude < HALF, latitude, NLAT - 1 - latitude)
    lane = lax.broadcasted_iota(jnp.int32, (NLAT, LANES), 1)
    for t in range(HALF // LANES):
        one_hot = jnp.where(north == lane + t * LANES, 1.0, 0.0).astype(BF)
        fold_ref[:, t * LANES : (t + 1) * LANES] = one_hot
    south = latitude_ref[...] >= HALF
    for block in range(blocks):
        orders = block_orders(slots_ref, block * BLK)[0][:, :1]
        sign = 1.0 - 2.0 * (orders % 2).astype(F32)
        evens, odds = [], []
        for c in range(CHAN):
            offset = ((c % 2) * FIELDS + c // 2) * row_count
            t, at = offset // LANES, offset % LANES
            rows = slice((t * blocks + block) * BLK, (t * blocks + block + 1) * BLK)
            values = jnp.concatenate(
                [data_ref[d, rows, :][:, at : at + row_count] for d in range(bands)], 1
            )
            flipped = sign * values
            evens.append(jnp.where(south, flipped, values))
            odds.append(jnp.where(south, -flipped, values))
        high, low = split_two(jnp.concatenate(evens + odds, 0))
        stack_ref[block * 4 * ROWS : block * 4 * ROWS + 2 * ROWS, :] = high
        stack_ref[block * 4 * ROWS + 2 * ROWS : (block + 1) * 4 * ROWS, :] = low
    folded = dot(stack_ref[...], fold_ref[...])
    for block in range(blocks):
        at = block * 4 * ROWS
        part = folded[at : at + 2 * ROWS] + folded[at + 2 * ROWS : at + 4 * ROWS]
        part = jnp.concatenate([part, jnp.zeros((LANES - 2 * ROWS, HALF), F32)], 0)
        high, low = split_two(part.T)
        weight_ref[block, :HALF, :LANES] = high
        weight_ref[block, :HALF, LANES:] = low
        weight_ref[block, HALF:, :LANES] = high
        weight_ref[block, HALF:, LANES:] = jnp.zeros_like(low)

    total = data_ref[0, total_row : total_row + 8]
    for d in range(1, bands):
        total = total + data_ref[d, total_row : total_row + 8]
    inverse = (1.0 / total)[:, :1]
    lane = lax.broadcasted_iota(jnp.int32, (CHUNK * BLK, LANES), 1)
    sub = lax.broadcasted_iota(jnp.int32, (CHUNK * BLK, LANES), 0)
    keep = (lane % BLK == sub % BLK) & (lane // ROWS == sub // BLK % 2)

    def one_block(block, unused):
        orders, first, last = block_orders(slots_ref, block * BLK)
        orders = orders[:, :1]
        here = pl.ds(pl.multiple_of(block * BLK, BLK), BLK)
        result_ref[block] = jnp.zeros((DEG, LANES), F32)

        def some_chunks(step, count):
            for k in range(count):
                copy_in(block, step + k).wait()
            values = chunk_ref[block, pl.ds(step, count)].reshape(count * CHUNK * BLK, 2 * HALF)
            full = dot(values, weight_ref[block])
            full = (full[:, :LANES] + full[:, LANES:]).reshape(count, CHUNK * BLK, LANES)
            picked = jnp.where(keep[None], full, 0.0).reshape(count * CHUNK, BLK, LANES)
            to = pl.ds(pl.multiple_of(step * CHUNK, CHUNK), count * CHUNK)
            result_ref[block, to, :] = jnp.sum(picked, axis=1)

        def lone_chunk(unused, inner):
            some_chunks(first, 1)
            return inner

        def two_chunks(pair, inner):
            some_chunks(2 * pair, 2)
            return inner

        lax.fori_loop(0, first & 1, lone_chunk, 0)
        lax.fori_loop((first + 1) // 2, chunks // 2, two_chunks, 0)
        return unused

    lax.fori_loop(0, blocks, one_block, 0)
    for block in range(blocks):
        orders = block_orders(slots_ref, block * BLK)[0][:, :1]
        turned = result_ref[block].T
        turned = turned[:ROWS] + turned[ROWS : 2 * ROWS]
        degree = lax.broadcasted_iota(jnp.int32, (BLK, DEG), 1)
        within = jnp.where(degree >= orders, within_ref[block * BLK : (block + 1) * BLK, :], 0.0)
        for c in range(CHAN):
            part = turned[c * BLK : (c + 1) * BLK] * within
            if c // 2 == FIELDS - 1:
                part = part * inverse
            coeff_ref[block, c] = part
        for i in range(BLK):
            target = pl.ds(slots_ref[block * BLK + i] % PLACES, 1)
            out_ref[:, target, :] = coeff_ref[block, :, i : i + 1, :]


def base_trig(order, first):
    lane = lax.broadcasted_iota(jnp.int32, order.shape, 1) + first
    phase = (order * lane) & (NLON - 1)
    quarter = (phase + NLON // 8) >> 9
    rest = (phase - quarter * (NLON // 4)).astype(F32) * (2.0 * math.pi / NLON)
    square = rest * rest
    sine = 1.0 / 362880.0
    for coef in (-1.0 / 5040.0, 1.0 / 120.0, -1.0 / 6.0, 1.0):
        sine = sine * square + coef
    sine = sine * rest
    cosine = 1.0 / 40320.0
    for coef in (-1.0 / 720.0, 1.0 / 24.0, -0.5, 1.0):
        cosine = cosine * square + coef
    swap = (quarter & 1) == 1
    cos_out = jnp.where(swap, sine, cosine)
    sin_out = jnp.where(swap, cosine, sine)
    cos_out = jnp.where(((quarter + 1) & 2) == 2, -cos_out, cos_out)
    sin_out = jnp.where((quarter & 2) == 2, -sin_out, sin_out)
    return cos_out, sin_out


def trig_kernel(out_ref, trig_ref, sem):
    half = trig_ref.shape[3] // 2
    root = math.sqrt(0.5)
    for parity in range(2):

        def strip(step, unused):
            at = pl.multiple_of(step * 64, 64)
            shape = (64, LANES)
            order = 2 * (lax.broadcasted_iota(jnp.int32, shape, 0) + at) + parity
            eighth = order & 7
            odd = (eighth & 1) == 1
            turn_cos = jnp.where(odd, root, jnp.where((eighth & 2) == 0, 1.0, 0.0))
            turn_sin = jnp.where(odd, root, jnp.where((eighth & 2) == 2, 1.0, 0.0))
            turn_cos = jnp.where((eighth >= 3) & (eighth <= 5), -turn_cos, turn_cos)
            turn_sin = jnp.where(eighth > 4, -turn_sin, turn_sin)
            for t in range(KTILE // LANES):
                cosine, sine = base_trig(order, t * LANES)
                for k in range(t * LANES, NLON // 2, KTILE):
                    columns = slice(t * LANES, (t + 1) * LANES)
                    for values, start in ((cosine, at), (sine, half + at)):
                        high, low = split_two(values)
                        trig_ref[k // KTILE, 0, parity, pl.ds(start, 64), columns] = high
                        trig_ref[k // KTILE, 1, parity, pl.ds(start, 64), columns] = low
                    cosine, sine = (
                        cosine * turn_cos - sine * turn_sin,
                        sine * turn_cos + cosine * turn_sin,
                    )
            return unused

        lax.fori_loop(0, half // 64, strip, 0)
    copy = pltpu.make_async_copy(trig_ref, out_ref, sem)
    copy.start()
    copy.wait()


def grid_kernel(
    dims, data_ref, orders_ref, rate_ref, sine_ref, trig_in, out_ref,
    move_ref, lhs_ref, weight_ref, acc_ref, trig_ref, sems,
):
    bands, row_count, modes, tiles, slots = dims
    half = slots // 2
    group = FIELDS * row_count
    padded = weight_ref.shape[1] // 2

    copies = []
    for tile in range(NLON // 2 // KTILE):
        copy = pltpu.make_async_copy(trig_in.at[tile], trig_ref.at[tile], sems.at[tile])
        copy.start()
        copies.append(copy)
    order = orders_ref[...]
    natural = (order & 1) * half + (order >> 1)
    for t in range(slots // LANES):
        lane = lax.broadcasted_iota(jnp.int32, (slots, LANES), 1) + t * LANES
        one_hot = jnp.where(natural == lane, 1.0, 0.0).astype(BF)
        move_ref[:, t * LANES : (t + 1) * LANES] = one_hot
    columns = []
    for t in range(tiles):
        part = data_ref[:, t * modes : (t + 1) * modes, :]
        columns.append(part.reshape(slots, LANES).T)
    turned = jnp.concatenate(columns, 0)
    for kind in range(2):
        high, low = split_two(turned[kind * group : (kind + 1) * group])
        moved = dot(jnp.concatenate([high, low], 0), move_ref[...]).astype(BF)
        for parity in range(2):
            part = moved[:, parity * half : (parity + 1) * half]
            lhs_ref[parity, :, kind * half : (kind + 1) * half] = part
    weight_ref[...] = jnp.zeros_like(weight_ref)
    flux_scale = math.pi / (2.0 * NLAT * NLON * DEG)
    weight = jnp.tile(sine_ref[...], (1, KTILE // LANES))
    total = jnp.zeros((8, KTILE), F32)

    for k in range(0, NLON // 2, KTILE):
        copies[k // KTILE].wait()
        trig_high, trig_low = trig_ref.at[k // KTILE, 0], trig_ref.at[k // KTILE, 1]
        sums = []
        for parity in range(2):
            first = dot(lhs_ref[parity], trig_high[parity])
            second = dot(lhs_ref[parity, :group, :], trig_low[parity])
            sums.append(first[:group] + first[group:] + second)
        values = []
        for fields, at in ((sums[0] + sums[1], k), (sums[0] - sums[1], k + NLON // 2)):
            weighted_rate = rate_ref[:, at : at + KTILE] * weight
            total = total + jnp.sum(weighted_rate.reshape(row_count // 8, 8, KTILE), axis=0)
            scaled = fields[:row_count] * (weight * flux_scale)
            values.append(
                jnp.concatenate(
                    [
                        fields[row_count : 2 * row_count] * scaled,
                        fields[2 * row_count :] * scaled,
                        weighted_rate * fields[:row_count],
                    ],
                    0,
                )
            )
        for parity in range(2):
            both = values[0] + values[1] if parity == 0 else values[0] - values[1]
            high, low = split_two(both)
            columns = slice(k, k + KTILE)
            weight_ref[parity, :group, columns] = high
            weight_ref[parity, padded : padded + group, columns] = low
    for parity in range(2):
        trig_high, trig_low = [
            jnp.concatenate([trig_ref[t, part, parity] for t in range(len(copies))], 1)
            for part in range(2)
        ]
        first = dot(trig_high, weight_ref[parity], 1)
        second = dot(trig_low, weight_ref[parity, :padded, :], 1)
        acc_ref[parity] = first[:, :padded] + first[:, padded:] + second

    joined = []
    for kind in range(2):
        rows = slice(kind * half, (kind + 1) * half)
        joined.append(jnp.concatenate([acc_ref[0, rows, :group], acc_ref[1, rows, :group]], 0))
    if 2 * group < tiles * LANES:
        joined.append(jnp.zeros((slots, tiles * LANES - 2 * group), F32))
    high, low = split_two(jnp.concatenate(joined, 1))
    moved = dot(move_ref[...], jnp.concatenate([high, low], 1))
    moved = moved[:, : tiles * LANES] + moved[:, tiles * LANES :]
    for t in range(tiles):
        part = moved[:, t * LANES : (t + 1) * LANES]
        out_ref[:, t * modes : (t + 1) * modes, :] = part.reshape(bands, modes, LANES)
    out_ref[:, tiles * modes :, :] = jnp.broadcast_to(jnp.sum(total), (bands, 8, LANES))


VMEM = pl.BlockSpec(memory_space=pltpu.VMEM)
SMEM = pl.BlockSpec(memory_space=pltpu.SMEM)
HBM = pl.BlockSpec(memory_space=pltpu.HBM)


def work(microseconds):
    return pl.CostEstimate(
        flops=microseconds * 10**9, bytes_accessed=2**20, transcendentals=0
    )


def per_device(spectrum, capture_rate, row_latitude, slot_wavenumber):
    bands = lax.axis_size("band")
    modes = spectrum.shape[3]
    row_count = capture_rate.shape[1]
    slots = slot_wavenumber.shape[0]
    blocks = modes // BLK
    chunks = DEG // CHUNK
    tiles = -(-CHAN * row_count // LANES)
    band_index = lax.axis_index("band")

    def sort_rows(table):
        rank = jnp.sum((table[:, None, :] < table[:, :, None]).astype(jnp.int32), 2)
        match = rank[:, None, :] == jnp.arange(modes, dtype=jnp.int32)[None, :, None]
        keys = table * PLACES + jnp.arange(modes, dtype=jnp.int32)[None, :]
        return jnp.sum(jnp.where(match, keys[:, None, :], 0), 2).reshape(-1)

    own = lax.dynamic_slice_in_dim(slot_wavenumber, band_index * modes, modes)
    local = sort_rows(own.reshape(1, modes))
    ordered = sort_rows(slot_wavenumber.reshape(bands, modes)) // PLACES
    rows = jnp.asarray(latitude_rows())
    spread = jnp.asarray(spread_matrix())
    latitude = row_latitude.reshape(1, NLAT)
    coeffs = spectrum.reshape(CHAN, modes, DEG)
    params = pltpu.CompilerParams(vmem_limit_bytes=48 * 2**20)
    chunk_rows = tiles * modes
    dims = (bands, row_count, modes, blocks, tiles)
    scalars = jnp.asarray(degree_scalars())
    per_order = pltpu.VMEM((modes, DEG), F32)

    def exchange(value):
        return lax.all_to_all(value, "band", split_axis=0, concat_axis=0, tiled=True)

    sent = pl.pallas_call(
        lambda *refs: synth_kernel(dims, *refs),
        out_shape=jax.ShapeDtypeStruct((bands, chunk_rows, LANES), F32),
        in_specs=[SMEM] + [HBM] * 5,
        out_specs=VMEM,
        scratch_shapes=[
            pltpu.SMEM(scalars.shape, F32),
            pltpu.VMEM(coeffs.shape, F32),
            pltpu.VMEM(rows.shape, F32),
            pltpu.VMEM(spread.shape, BF),
            pltpu.VMEM(latitude.shape, jnp.int32),
            pltpu.SemaphoreType.DMA((5,)),
        ]
        + [per_order] * 3
        + [pltpu.VMEM((chunks, 2 * ROWS, CHUNK * BLK), BF)]
        + [pltpu.VMEM((2, CHUNK // 2 * BLK, HALF), BF)] * 4
        + [
            pltpu.VMEM((blocks, 2, ROWS, HALF), F32),
            pltpu.VMEM((HALF, NLAT), BF),
            pltpu.VMEM((CHAN, BLK, DEG), F32),
        ],
        compiler_params=pltpu.CompilerParams(vmem_limit_bytes=62 * 2**20),
        cost_estimate=work(15),
        name="synth",
    )(local, scalars, coeffs, rows, spread, latitude)
    received = exchange(sent)

    trig_tiles = NLON // 2 // KTILE
    trig_shape = (trig_tiles, 2, 2, slots, KTILE)
    trig_scratch = pltpu.VMEM(trig_shape, BF)
    trig = pl.pallas_call(
        trig_kernel,
        out_shape=jax.ShapeDtypeStruct(trig_shape, BF),
        out_specs=HBM,
        scratch_shapes=[trig_scratch, pltpu.SemaphoreType.DMA(())],
        compiler_params=params,
        cost_estimate=work(4),
        name="trig",
    )()

    my_latitudes = lax.dynamic_slice_in_dim(row_latitude, band_index * row_count, row_count)
    row_sine = jnp.sin(jnp.pi * (my_latitudes.astype(F32) + 0.5) / NLAT)
    row_sine = jnp.broadcast_to(row_sine[:, None], (row_count, LANES))
    orders = jnp.broadcast_to(ordered.reshape(slots, 1), (slots, LANES))
    group = FIELDS * row_count
    padded = -(-group // LANES) * LANES
    grid_dims = (bands, row_count, modes, tiles, slots)
    fluxes = pl.pallas_call(
        lambda *refs: grid_kernel(grid_dims, *refs),
        out_shape=jax.ShapeDtypeStruct((bands, chunk_rows + 8, LANES), F32),
        in_specs=[VMEM] * 4 + [HBM],
        out_specs=VMEM,
        scratch_shapes=[
            pltpu.VMEM((slots, slots), BF),
            pltpu.VMEM((2, 2 * group, slots), BF),
            pltpu.VMEM((2, 2 * padded, NLON // 2), BF),
            pltpu.VMEM((2, slots, padded), F32),
            trig_scratch,
            pltpu.SemaphoreType.DMA((trig_tiles,)),
        ],
        compiler_params=params,
        cost_estimate=work(8),
        name="grid",
    )(received, orders, capture_rate.reshape(row_count, NLON), row_sine, trig)
    returned = exchange(fluxes)

    chunk_shape = (blocks, chunks, CHUNK * BLK, 2 * HALF)
    legendre, within = pl.pallas_call(
        lambda *refs: table_kernel(blocks, *refs),
        out_shape=[
            jax.ShapeDtypeStruct(chunk_shape, BF),
            jax.ShapeDtypeStruct((modes, DEG), F32),
        ],
        in_specs=[SMEM, SMEM, VMEM],
        out_specs=[HBM, VMEM],
        scratch_shapes=[per_order] * 2
        + [pltpu.VMEM(chunk_shape, BF), pltpu.SemaphoreType.DMA((blocks, chunks))],
        compiler_params=params,
        cost_estimate=work(12),
        name="table",
    )(local, scalars, rows)
    column = jnp.broadcast_to(row_latitude[:, None], (NLAT, LANES))
    result = pl.pallas_call(
        lambda *refs: analyze_kernel(dims, chunk_rows, *refs),
        out_shape=jax.ShapeDtypeStruct((CHAN, modes, DEG), F32),
        in_specs=[SMEM, VMEM, VMEM, VMEM, VMEM, HBM],
        out_specs=VMEM,
        scratch_shapes=[
            pltpu.VMEM(chunk_shape, BF),
            pltpu.VMEM((blocks, 2 * HALF, 2 * LANES), BF),
            pltpu.VMEM((blocks * 4 * ROWS, NLAT), BF),
            pltpu.VMEM((blocks, DEG, LANES), F32),
            pltpu.VMEM((NLAT, HALF), BF),
            pltpu.VMEM((blocks, CHAN, BLK, DEG), F32),
            pltpu.SemaphoreType.DMA((blocks, chunks)),
        ],
        compiler_params=params,
        cost_estimate=work(9),
        name="analyze",
    )(local, returned, column, latitude, within, legendre)
    return result.reshape(1, FIELDS, 2, modes, DEG)


def solution(mesh):
    return jax.shard_map(
        per_device,
        mesh=mesh,
        in_specs=(P("shell", None, None, "band", None), P("shell", "band", None), P(), P()),
        out_specs=P("shell", None, None, "band", None),
        check_vma=False,
    )
```

```python
import functools
import math

import jax
import jax.numpy as jnp
import numpy as np
from jax import lax
from jax.experimental import pallas as pl
from jax.experimental.pallas import tpu as pltpu
from jax.sharding import PartitionSpec as P

DEG = 512
NLAT = 1024
NLON = 2048
FIELDS = 3
HALF = NLAT // 2
CHAN = 2 * FIELDS
BLK = 8
ROWS = CHAN * BLK
CHUNK = 64
CHECK = 16
PLACES = 1024
LANES = 128
KTILE = 256
BF = jnp.bfloat16
F32 = jnp.float32


def split_two(value):
    high = value.astype(BF)
    low = (value - high.astype(F32)).astype(BF)
    return high, low


def dot(lhs, rhs, contract_rhs=0):
    return lax.dot_general(
        lhs, rhs, (((1,), (contract_rhs,)), ((), ())), preferred_element_type=F32
    )


def latitude_rows():
    theta = np.pi * (np.arange(HALF) + 0.5) / NLAT
    index = np.arange(DEG, dtype=np.float64)
    log_terms = np.zeros(DEG)
    log_terms[1:] = 0.5 * np.log2((2.0 * index[1:] + 1.0) / (2.0 * index[1:]))
    rows = np.zeros((8, DEG))
    rows[0], rows[1], rows[2] = np.cos(theta), np.log2(np.sin(theta)), log_terms
    return rows.astype(np.float32)


def spread_matrix():
    spread = np.zeros((LANES, 2, 2, CHUNK // 2, BLK), np.float32)
    for half in range(2):
        for parity in range(2):
            for step in range(CHUNK // 2):
                spread[half * CHUNK + 2 * step + parity, half, parity, step, :] = 1.0
    return spread.reshape(LANES, 2 * 2 * (CHUNK // 2) * BLK).astype(BF)


def degree_scalars():
    before = np.arange(DEG, dtype=np.float64) - 1.0
    square = before * before
    return np.concatenate([square, 4.0 / (4.0 * square - 1.0)]).astype(np.float32)


def block_orders(slots_ref, first):
    sublane = lax.broadcasted_iota(jnp.int32, (BLK, LANES), 0)
    orders = jnp.zeros((BLK, LANES), jnp.int32)
    lowest, highest = jnp.int32(DEG), jnp.int32(0)
    for i in range(BLK):
        order = slots_ref[first + i] // PLACES
        orders = jnp.where(sublane == i, order, orders)
        lowest, highest = jnp.minimum(lowest, order), jnp.maximum(highest, order)
    return orders, lowest // CHUNK, highest // CHUNK + 1


def running_sum(terms, length):
    lane = lax.broadcasted_iota(jnp.int32, terms.shape, 1) & (length - 1)
    shift = 1
    while shift < length:
        moved = pltpu.roll(terms, shift, 1)
        terms = terms + jnp.where(lane >= shift, moved, 0.0)
        shift *= 2
    return terms


def recursion_tables(slots_ref, modes, rows_ref, start_ref, before_ref, within_ref):
    orders = [block_orders(slots_ref, at)[0][:, :1] for at in range(0, modes, BLK)]
    order = jnp.concatenate(orders, 0).astype(F32)
    position = lax.broadcasted_iota(jnp.int32, (modes, DEG), 1)
    degree = position.astype(F32)
    square = degree * degree
    above = degree > order
    gap = jnp.where(above, square - order * order, 1.0)
    growth = jnp.where(above, 0.5 * jnp.log2((square - 0.25) / gap), 0.0)
    before_ref[...] = running_sum(growth, DEG)
    later = jnp.where(position & (CHECK - 1) == 0, 0.0, growth)
    within_ref[...] = jnp.exp2(running_sum(later, CHECK))
    terms = jnp.where(degree <= order, rows_ref[2:3, :], 0.0)
    norm = jnp.where(order > 0, 0.5 + jnp.sum(terms, axis=1, keepdims=True), 0.0)
    start_ref[...] = norm + order * rows_ref[1:2, :]


def run_chunk(step, carry, double_cosine, orders, before, scalars_ref, emit, beside, guard):
    current, previous, log_scale = carry
    order = orders.astype(F32)
    order_square = order * order
    before = pltpu.roll(before, (step % 2) * CHUNK, 1)
    scale = None
    for i in range(CHUNK):
        if i % CHECK == 0:
            size = jnp.maximum(jnp.abs(current), jnp.abs(previous))
            large, small = size > 2.0**40, size < 2.0**-40
            factor = jnp.where(large, 2.0**-60, jnp.where(small, 2.0**60, 1.0))
            change = jnp.where(large, 60.0, jnp.where(small, -60.0, 0.0))
            current = current * factor
            previous = previous * factor
            log_scale = log_scale + change
            scale = jnp.exp2(jnp.maximum(log_scale + before[:, i : i + 1], -200.0))
        degree = step * CHUNK + i
        factor = (scalars_ref[degree] - order_square) * scalars_ref[DEG + degree]
        factor = jnp.tile(factor, (1, HALF // LANES))
        newest = double_cosine * current - factor * previous
        if guard:
            started = jnp.tile(orders, (1, HALF // LANES)) < degree
            newest = jnp.where(started, newest, 1.0)
        current, previous = newest, current
        emit(i, newest * scale)
        if beside and i % (CHUNK // len(beside)) == 1:
            beside[i // (CHUNK // len(beside))]()
    return current, previous, log_scale


def before_tile(before_ref, block, step):
    rows = pl.ds(pl.multiple_of(block * BLK, BLK), BLK)
    return before_ref[rows, pl.ds(pl.multiple_of(step // 2 * LANES, LANES), LANES)]


def start_state(start_ref, block):
    ones = jnp.ones((BLK, HALF), F32)
    return ones, ones, start_ref[pl.ds(pl.multiple_of(block * BLK, BLK), BLK), :]


def fold_matrix(latitude_ref, fold_ref):
    latitude = latitude_ref[...]
    north = jnp.where(latitude < HALF, latitude, NLAT - 1 - latitude)
    sublane = lax.broadcasted_iota(jnp.int32, (HALF, NLAT), 0)
    fold_ref[...] = jnp.where(sublane == north, 1.0, 0.0).astype(BF)


def synth_kernel(
    dims, slots_ref, scalars_in, spec_in, rows_in, spread_in, latitude_in,
    out_ref, scalars_ref, spec_ref, rows_ref, spread_ref, latitude_ref, sems,
    start_ref, before_ref, within_ref, lhs_ref, high_a, low_a, high_b, low_b, acc_ref, fold_ref, coeff_ref,
):
    bands, row_count, modes, blocks, tiles = dims
    pairs = (
        (rows_in, rows_ref), (scalars_in, scalars_ref), (latitude_in, latitude_ref),
        (spread_in, spread_ref), (spec_in, spec_ref),
    )
    copies = []
    for index, (source, target) in enumerate(pairs):
        copies.append(pltpu.make_async_copy(source, target, sems.at[index]))
        copies[-1].start()
    copies[0].wait()
    recursion_tables(slots_ref, modes, rows_ref, start_ref, before_ref, within_ref)
    for copy in copies[1:]:
        copy.wait()
    fold_matrix(latitude_ref, fold_ref)
    south = latitude_ref[...] >= HALF
    spread_width = 4 * (CHUNK // 2) * BLK
    lane = lax.broadcasted_iota(jnp.int32, (2 * ROWS, spread_width), 1)
    sub = lax.broadcasted_iota(jnp.int32, (2 * ROWS, spread_width), 0)
    diagonal = (lane % BLK) == (sub % BLK)
    width = (CHUNK // 2) * BLK

    def one_block(block, unused):
        orders, first, last = block_orders(slots_ref, block * BLK)
        column = orders[:, :1]
        here = pl.ds(pl.multiple_of(block * BLK, BLK), BLK)
        for i in range(BLK):
            source = pl.ds(slots_ref[block * BLK + i] % PLACES, 1)
            coeff_ref[:, i : i + 1, :] = spec_ref[:, source, :]
        degree = lax.broadcasted_iota(jnp.int32, (BLK, DEG), 1)
        within = jnp.where(degree >= column, within_ref[here, :], 0.0)
        coeffs = coeff_ref[...] * within[None]
        coeff_high, coeff_low = split_two(coeffs.reshape(ROWS, DEG))
        stacked = jnp.concatenate([coeff_high, coeff_low], 0)
        for t in range(DEG // LANES):
            wide = dot(stacked[:, t * LANES : (t + 1) * LANES], spread_ref[...])
            wide = jnp.where(diagonal, wide, 0.0).astype(BF)
            for half in range(2):
                lhs_ref[2 * t + half] = wide[:, half * 2 * width : (half + 1) * 2 * width]
        acc_ref[block] = jnp.zeros((2, ROWS, HALF), F32)
        cosine = jnp.broadcast_to(2.0 * rows_ref[0:1, :], (BLK, HALF))

        def recur(step, carry, high_ref, low_ref, beside, guard):
            held = {}

            def emit(i, value):
                if i % 4 < 2:
                    held[i] = value
                else:
                    pair = jnp.concatenate([held.pop(i - 2), value], 0)
                    high, low = split_two(pair)
                    at = (i // 4) * 2 * BLK
                    high_ref[i % 2, at : at + 2 * BLK, :] = high
                    low_ref[i % 2, at : at + 2 * BLK, :] = low

            before = before_tile(before_ref, block, step)
            return run_chunk(
                step, carry, cosine, orders, before, scalars_ref, emit, beside, guard
            )

        def add_products(step, high_ref, low_ref):
            def part(parity, columns):
                lhs = lhs_ref[step, :, parity * width : (parity + 1) * width]
                first = dot(lhs, high_ref[parity, :, columns])
                second = dot(lhs[:ROWS], low_ref[parity, :, columns])
                acc_ref[block, parity, :, columns] += first[:ROWS] + first[ROWS:] + second

            return [
                functools.partial(part, parity, slice(at, at + KTILE))
                for parity in range(2)
                for at in range(0, HALF, KTILE)
            ]

        def two_chunks(guard, pair, carry):
            step = 2 * pair
            beside = add_products(jnp.maximum(step - 1, 0), high_b, low_b)
            carry = recur(step, carry, high_a, low_a, beside, guard)
            beside = add_products(step, high_a, low_a)
            return recur(step + 1, carry, high_b, low_b, beside, guard)

        high_b[...] = jnp.zeros_like(high_b)
        low_b[...] = jnp.zeros_like(low_b)
        chunks = DEG // CHUNK
        state = lax.fori_loop(
            0,
            first & 1,
            lambda unused, carry: recur(first, carry, high_b, low_b, (), True),
            start_state(start_ref, block),
        )
        middle = (last + 1) // 2
        state = lax.fori_loop(
            (first + 1) // 2, middle, functools.partial(two_chunks, True), state
        )
        lax.fori_loop(middle, chunks // 2, functools.partial(two_chunks, False), state)
        for part in add_products(chunks - 1, high_b, low_b):
            part()
        return unused

    lax.fori_loop(0, blocks, one_block, 0)
    high, low = split_two(acc_ref[...].reshape(blocks * 2 * ROWS, HALF))
    moved = dot(jnp.concatenate([high, low], 0), fold_ref[...])
    moved = moved[: blocks * 2 * ROWS] + moved[blocks * 2 * ROWS :]
    for block in range(blocks):
        orders = block_orders(slots_ref, block * BLK)[0][:, :1]
        sign = jnp.tile(1.0 - 2.0 * (orders % 2).astype(F32), (CHAN, 1))
        even = moved[block * 2 * ROWS : block * 2 * ROWS + ROWS]
        odd = moved[block * 2 * ROWS + ROWS : (block + 1) * 2 * ROWS]
        values = jnp.where(south, sign * (even - odd), even + odd)
        for d in range(bands):
            parts = []
            for kind in range(2):
                for field in range(FIELDS):
                    c = field * 2 + kind
                    parts.append(
                        values[c * BLK : (c + 1) * BLK, d * row_count : (d + 1) * row_count]
                    )
            if CHAN * row_count < tiles * LANES:
                parts.append(jnp.zeros((BLK, tiles * LANES - CHAN * row_count), F32))
            joined = jnp.concatenate(parts, 1)
            for t in range(tiles):
                at = slice((t * blocks + block) * BLK, (t * blocks + block + 1) * BLK)
                out_ref[d, at, :] = joined[:, t * LANES : (t + 1) * LANES]


def table_kernel(
    blocks, slots_ref, scalars_ref, rows_ref, out_ref, within_out, start_ref, before_ref,
    chunk_ref, sems,
):
    modes = blocks * BLK
    cosine = jnp.broadcast_to(2.0 * rows_ref[0:1, :], (BLK, HALF))
    recursion_tables(slots_ref, modes, rows_ref, start_ref, before_ref, within_out)

    def copy_out(block, step):
        return pltpu.make_async_copy(
            chunk_ref.at[block, step], out_ref.at[block, step], sems.at[block, step]
        )

    def one_block(block, unused):
        orders, first, last = block_orders(slots_ref, block * BLK)

        def one_chunk(guard, step, carry):
            held = {}

            def emit(i, value):
                if i % 2 == 0:
                    held[i] = value
                else:
                    pair = jnp.concatenate([held.pop(i - 1), value], 0)
                    high, low = split_two(pair)
                    at = (i // 2) * 2 * BLK
                    chunk_ref[block, step, at : at + 2 * BLK, :HALF] = high
                    chunk_ref[block, step, at : at + 2 * BLK, HALF:] = low

            before = before_tile(before_ref, block, step)
            carry = run_chunk(
                step, carry, cosine, orders, before, scalars_ref, emit, (), guard
            )
            copy_out(block, step).start()
            return carry

        state = start_state(start_ref, block)
        state = lax.fori_loop(first, last, functools.partial(one_chunk, True), state)
        lax.fori_loop(last, DEG // CHUNK, functools.partial(one_chunk, False), state)
        return unused

    def finish_block(block, unused):
        orders, first, last = block_orders(slots_ref, block * BLK)

        def finish_chunk(step, inner):
            copy_out(block, step).wait()
            return inner

        return lax.fori_loop(first, DEG // CHUNK, finish_chunk, unused)

    lax.fori_loop(0, blocks, one_block, 0)
    lax.fori_loop(0, blocks, finish_block, 0)


def analyze_kernel(
    dims, total_row, slots_ref, data_ref, column_ref, latitude_ref, within_ref, table_ref,
    out_ref, chunk_ref, weight_ref, stack_ref, result_ref, fold_ref, coeff_ref, sems,
):
    bands, row_count, modes, blocks, tiles = dims
    chunks = DEG // CHUNK

    def copy_in(block, step):
        return pltpu.make_async_copy(
            table_ref.at[block, step], chunk_ref.at[block, step], sems.at[block, step]
        )

    def start_block(block, unused):
        orders, first, last = block_orders(slots_ref, block * BLK)

        def start_chunk(step, inner):
            copy_in(block, step).start()
            return inner

        return lax.fori_loop(first, chunks, start_chunk, unused)

    lax.fori_loop(0, blocks, start_block, 0)
    latitude = column_ref[...]
    north = jnp.where(latitude < HALF, latitude, NLAT - 1 - latitude)
    lane = lax.broadcasted_iota(jnp.int32, (NLAT, LANES), 1)
    for t in range(HALF // LANES):
        one_hot = jnp.where(north == lane + t * LANES, 1.0, 0.0).astype(BF)
        fold_ref[:, t * LANES : (t + 1) * LANES] = one_hot
    south = latitude_ref[...] >= HALF
    for block in range(blocks):
        orders = block_orders(slots_ref, block * BLK)[0][:, :1]
        sign = 1.0 - 2.0 * (orders % 2).astype(F32)
        evens, odds = [], []
        for c in range(CHAN):
            offset = ((c % 2) * FIELDS + c // 2) * row_count
            t, at = offset // LANES, offset % LANES
            rows = slice((t * blocks + block) * BLK, (t * blocks + block + 1) * BLK)
            values = jnp.concatenate(
                [data_ref[d, rows, :][:, at : at + row_count] for d in range(bands)], 1
            )
            flipped = sign * values
            evens.append(jnp.where(south, flipped, values))
            odds.append(jnp.where(south, -flipped, values))
        high, low = split_two(jnp.concatenate(evens + odds, 0))
        stack_ref[block * 4 * ROWS : block * 4 * ROWS + 2 * ROWS, :] = high
        stack_ref[block * 4 * ROWS + 2 * ROWS : (block + 1) * 4 * ROWS, :] = low
    folded = dot(stack_ref[...], fold_ref[...])
    for block in range(blocks):
        at = block * 4 * ROWS
        part = folded[at : at + 2 * ROWS] + folded[at + 2 * ROWS : at + 4 * ROWS]
        part = jnp.concatenate([part, jnp.zeros((LANES - 2 * ROWS, HALF), F32)], 0)
        high, low = split_two(part.T)
        weight_ref[block, :HALF, :LANES] = high
        weight_ref[block, :HALF, LANES:] = low
        weight_ref[block, HALF:, :LANES] = high
        weight_ref[block, HALF:, LANES:] = jnp.zeros_like(low)

    total = data_ref[0, total_row : total_row + 8]
    for d in range(1, bands):
        total = total + data_ref[d, total_row : total_row + 8]
    inverse = (1.0 / total)[:, :1]
    lane = lax.broadcasted_iota(jnp.int32, (CHUNK * BLK, LANES), 1)
    sub = lax.broadcasted_iota(jnp.int32, (CHUNK * BLK, LANES), 0)
    keep = (lane % BLK == sub % BLK) & (lane // ROWS == sub // BLK % 2)

    def one_block(block, unused):
        orders, first, last = block_orders(slots_ref, block * BLK)
        orders = orders[:, :1]
        here = pl.ds(pl.multiple_of(block * BLK, BLK), BLK)
        result_ref[block] = jnp.zeros((DEG, LANES), F32)

        def some_chunks(step, count):
            for k in range(count):
                copy_in(block, step + k).wait()
            values = chunk_ref[block, pl.ds(step, count)].reshape(count * CHUNK * BLK, 2 * HALF)
            full = dot(values, weight_ref[block])
            full = (full[:, :LANES] + full[:, LANES:]).reshape(count, CHUNK * BLK, LANES)
            picked = jnp.where(keep[None], full, 0.0).reshape(count * CHUNK, BLK, LANES)
            to = pl.ds(pl.multiple_of(step * CHUNK, CHUNK), count * CHUNK)
            result_ref[block, to, :] = jnp.sum(picked, axis=1)

        def lone_chunk(unused, inner):
            some_chunks(first, 1)
            return inner

        even = (first + 1) // 2

        def two_chunks(unused, inner):
            some_chunks(2 * even, 2)
            return inner

        def four_chunks(group, inner):
            some_chunks(4 * group, 4)
            return inner

        lax.fori_loop(0, first & 1, lone_chunk, 0)
        lax.fori_loop(0, even & 1, two_chunks, 0)
        lax.fori_loop((even + 1) // 2, chunks // 4, four_chunks, 0)
        return unused

    lax.fori_loop(0, blocks, one_block, 0)
    for block in range(blocks):
        orders = block_orders(slots_ref, block * BLK)[0][:, :1]
        turned = result_ref[block].T
        turned = turned[:ROWS] + turned[ROWS : 2 * ROWS]
        degree = lax.broadcasted_iota(jnp.int32, (BLK, DEG), 1)
        within = jnp.where(degree >= orders, within_ref[block * BLK : (block + 1) * BLK, :], 0.0)
        for c in range(CHAN):
            part = turned[c * BLK : (c + 1) * BLK] * within
            if c // 2 == FIELDS - 1:
                part = part * inverse
            coeff_ref[block, c] = part
        for i in range(BLK):
            target = pl.ds(slots_ref[block * BLK + i] % PLACES, 1)
            out_ref[:, target, :] = coeff_ref[block, :, i : i + 1, :]


def base_trig(order, first):
    lane = lax.broadcasted_iota(jnp.int32, order.shape, 1) + first
    phase = (order * lane) & (NLON - 1)
    quarter = (phase + NLON // 8) >> 9
    rest = (phase - quarter * (NLON // 4)).astype(F32) * (2.0 * math.pi / NLON)
    square = rest * rest
    sine = 1.0 / 362880.0
    for coef in (-1.0 / 5040.0, 1.0 / 120.0, -1.0 / 6.0, 1.0):
        sine = sine * square + coef
    sine = sine * rest
    cosine = 1.0 / 40320.0
    for coef in (-1.0 / 720.0, 1.0 / 24.0, -0.5, 1.0):
        cosine = cosine * square + coef
    swap = (quarter & 1) == 1
    cos_out = jnp.where(swap, sine, cosine)
    sin_out = jnp.where(swap, cosine, sine)
    cos_out = jnp.where(((quarter + 1) & 2) == 2, -cos_out, cos_out)
    sin_out = jnp.where((quarter & 2) == 2, -sin_out, sin_out)
    return cos_out, sin_out


def trig_kernel(out_ref, trig_ref, sem):
    half = trig_ref.shape[3] // 2
    root = math.sqrt(0.5)
    for parity in range(2):

        def strip(step, unused):
            at = pl.multiple_of(step * 64, 64)
            shape = (64, LANES)
            order = 2 * (lax.broadcasted_iota(jnp.int32, shape, 0) + at) + parity
            eighth = order & 7
            odd = (eighth & 1) == 1
            turn_cos = jnp.where(odd, root, jnp.where((eighth & 2) == 0, 1.0, 0.0))
            turn_sin = jnp.where(odd, root, jnp.where((eighth & 2) == 2, 1.0, 0.0))
            turn_cos = jnp.where((eighth >= 3) & (eighth <= 5), -turn_cos, turn_cos)
            turn_sin = jnp.where(eighth > 4, -turn_sin, turn_sin)
            for t in range(KTILE // LANES):
                cosine, sine = base_trig(order, t * LANES)
                for k in range(t * LANES, NLON // 2, KTILE):
                    columns = slice(t * LANES, (t + 1) * LANES)
                    for values, start in ((cosine, at), (sine, half + at)):
                        high, low = split_two(values)
                        trig_ref[k // KTILE, 0, parity, pl.ds(start, 64), columns] = high
                        trig_ref[k // KTILE, 1, parity, pl.ds(start, 64), columns] = low
                    cosine, sine = (
                        cosine * turn_cos - sine * turn_sin,
                        sine * turn_cos + cosine * turn_sin,
                    )
            return unused

        lax.fori_loop(0, half // 64, strip, 0)
    copy = pltpu.make_async_copy(trig_ref, out_ref, sem)
    copy.start()
    copy.wait()


def grid_kernel(
    dims, data_ref, orders_ref, rate_ref, sine_ref, trig_in, out_ref,
    move_ref, lhs_ref, weight_ref, acc_ref, trig_ref, sems,
):
    bands, row_count, modes, tiles, slots = dims
    half = slots // 2
    group = FIELDS * row_count
    padded = weight_ref.shape[1] // 2

    copies = []
    for tile in range(NLON // 2 // KTILE):
        copy = pltpu.make_async_copy(trig_in.at[tile], trig_ref.at[tile], sems.at[tile])
        copy.start()
        copies.append(copy)
    order = orders_ref[...]
    natural = (order & 1) * half + (order >> 1)
    for t in range(slots // LANES):
        lane = lax.broadcasted_iota(jnp.int32, (slots, LANES), 1) + t * LANES
        one_hot = jnp.where(natural == lane, 1.0, 0.0).astype(BF)
        move_ref[:, t * LANES : (t + 1) * LANES] = one_hot
    columns = []
    for t in range(tiles):
        part = data_ref[:, t * modes : (t + 1) * modes, :]
        columns.append(part.reshape(slots, LANES).T)
    turned = jnp.concatenate(columns, 0)
    for kind in range(2):
        high, low = split_two(turned[kind * group : (kind + 1) * group])
        moved = dot(jnp.concatenate([high, low], 0), move_ref[...]).astype(BF)
        for parity in range(2):
            part = moved[:, parity * half : (parity + 1) * half]
            lhs_ref[parity, :, kind * half : (kind + 1) * half] = part
    weight_ref[...] = jnp.zeros_like(weight_ref)
    flux_scale = math.pi / (2.0 * NLAT * NLON * DEG)
    weight = jnp.tile(sine_ref[...], (1, KTILE // LANES))
    total = jnp.zeros((8, KTILE), F32)

    for k in range(0, NLON // 2, KTILE):
        copies[k // KTILE].wait()
        trig_high, trig_low = trig_ref.at[k // KTILE, 0], trig_ref.at[k // KTILE, 1]
        sums = []
        for parity in range(2):
            first = dot(lhs_ref[parity], trig_high[parity])
            second = dot(lhs_ref[parity, :group, :], trig_low[parity])
            sums.append(first[:group] + first[group:] + second)
        values = []
        for fields, at in ((sums[0] + sums[1], k), (sums[0] - sums[1], k + NLON // 2)):
            weighted_rate = rate_ref[:, at : at + KTILE] * weight
            total = total + jnp.sum(weighted_rate.reshape(row_count // 8, 8, KTILE), axis=0)
            scaled = fields[:row_count] * (weight * flux_scale)
            values.append(
                jnp.concatenate(
                    [
                        fields[row_count : 2 * row_count] * scaled,
                        fields[2 * row_count :] * scaled,
                        weighted_rate * fields[:row_count],
                    ],
                    0,
                )
            )
        for parity in range(2):
            both = values[0] + values[1] if parity == 0 else values[0] - values[1]
            high, low = split_two(both)
            columns = slice(k, k + KTILE)
            weight_ref[parity, :group, columns] = high
            weight_ref[parity, padded : padded + group, columns] = low
    for parity in range(2):
        trig_high, trig_low = [
            jnp.concatenate([trig_ref[t, part, parity] for t in range(len(copies))], 1)
            for part in range(2)
        ]
        first = dot(trig_high, weight_ref[parity], 1)
        second = dot(trig_low, weight_ref[parity, :padded, :], 1)
        acc_ref[parity] = first[:, :padded] + first[:, padded:] + second

    joined = []
    for kind in range(2):
        rows = slice(kind * half, (kind + 1) * half)
        joined.append(jnp.concatenate([acc_ref[0, rows, :group], acc_ref[1, rows, :group]], 0))
    if 2 * group < tiles * LANES:
        joined.append(jnp.zeros((slots, tiles * LANES - 2 * group), F32))
    high, low = split_two(jnp.concatenate(joined, 1))
    moved = dot(move_ref[...], jnp.concatenate([high, low], 1))
    moved = moved[:, : tiles * LANES] + moved[:, tiles * LANES :]
    for t in range(tiles):
        part = moved[:, t * LANES : (t + 1) * LANES]
        out_ref[:, t * modes : (t + 1) * modes, :] = part.reshape(bands, modes, LANES)
    out_ref[:, tiles * modes :, :] = jnp.broadcast_to(jnp.sum(total), (bands, 8, LANES))


VMEM = pl.BlockSpec(memory_space=pltpu.VMEM)
SMEM = pl.BlockSpec(memory_space=pltpu.SMEM)
HBM = pl.BlockSpec(memory_space=pltpu.HBM)


def work(microseconds):
    return pl.CostEstimate(
        flops=microseconds * 10**9, bytes_accessed=2**20, transcendentals=0
    )


def per_device(spectrum, capture_rate, row_latitude, slot_wavenumber):
    bands = lax.axis_size("band")
    modes = spectrum.shape[3]
    row_count = capture_rate.shape[1]
    slots = slot_wavenumber.shape[0]
    blocks = modes // BLK
    chunks = DEG // CHUNK
    tiles = -(-CHAN * row_count // LANES)
    band_index = lax.axis_index("band")

    def sort_rows(table):
        rank = jnp.sum((table[:, None, :] < table[:, :, None]).astype(jnp.int32), 2)
        match = rank[:, None, :] == jnp.arange(modes, dtype=jnp.int32)[None, :, None]
        keys = table * PLACES + jnp.arange(modes, dtype=jnp.int32)[None, :]
        return jnp.sum(jnp.where(match, keys[:, None, :], 0), 2).reshape(-1)

    own = lax.dynamic_slice_in_dim(slot_wavenumber, band_index * modes, modes)
    local = sort_rows(own.reshape(1, modes))
    ordered = sort_rows(slot_wavenumber.reshape(bands, modes)) // PLACES
    rows = jnp.asarray(latitude_rows())
    spread = jnp.asarray(spread_matrix())
    latitude = row_latitude.reshape(1, NLAT)
    coeffs = spectrum.reshape(CHAN, modes, DEG)
    params = pltpu.CompilerParams(vmem_limit_bytes=48 * 2**20)
    chunk_rows = tiles * modes
    dims = (bands, row_count, modes, blocks, tiles)
    scalars = jnp.asarray(degree_scalars())
    per_order = pltpu.VMEM((modes, DEG), F32)

    def exchange(value):
        return lax.all_to_all(value, "band", split_axis=0, concat_axis=0, tiled=True)

    sent = pl.pallas_call(
        lambda *refs: synth_kernel(dims, *refs),
        out_shape=jax.ShapeDtypeStruct((bands, chunk_rows, LANES), F32),
        in_specs=[SMEM] + [HBM] * 5,
        out_specs=VMEM,
        scratch_shapes=[
            pltpu.SMEM(scalars.shape, F32),
            pltpu.VMEM(coeffs.shape, F32),
            pltpu.VMEM(rows.shape, F32),
            pltpu.VMEM(spread.shape, BF),
            pltpu.VMEM(latitude.shape, jnp.int32),
            pltpu.SemaphoreType.DMA((5,)),
        ]
        + [per_order] * 3
        + [pltpu.VMEM((chunks, 2 * ROWS, CHUNK * BLK), BF)]
        + [pltpu.VMEM((2, CHUNK // 2 * BLK, HALF), BF)] * 4
        + [
            pltpu.VMEM((blocks, 2, ROWS, HALF), F32),
            pltpu.VMEM((HALF, NLAT), BF),
            pltpu.VMEM((CHAN, BLK, DEG), F32),
        ],
        compiler_params=pltpu.CompilerParams(vmem_limit_bytes=62 * 2**20),
        cost_estimate=work(15),
        name="synth",
    )(local, scalars, coeffs, rows, spread, latitude)
    received = exchange(sent)

    trig_tiles = NLON // 2 // KTILE
    trig_shape = (trig_tiles, 2, 2, slots, KTILE)
    trig_scratch = pltpu.VMEM(trig_shape, BF)
    trig = pl.pallas_call(
        trig_kernel,
        out_shape=jax.ShapeDtypeStruct(trig_shape, BF),
        out_specs=HBM,
        scratch_shapes=[trig_scratch, pltpu.SemaphoreType.DMA(())],
        compiler_params=params,
        cost_estimate=work(4),
        name="trig",
    )()

    my_latitudes = lax.dynamic_slice_in_dim(row_latitude, band_index * row_count, row_count)
    row_sine = jnp.sin(jnp.pi * (my_latitudes.astype(F32) + 0.5) / NLAT)
    row_sine = jnp.broadcast_to(row_sine[:, None], (row_count, LANES))
    orders = jnp.broadcast_to(ordered.reshape(slots, 1), (slots, LANES))
    group = FIELDS * row_count
    padded = -(-group // LANES) * LANES
    grid_dims = (bands, row_count, modes, tiles, slots)
    fluxes = pl.pallas_call(
        lambda *refs: grid_kernel(grid_dims, *refs),
        out_shape=jax.ShapeDtypeStruct((bands, chunk_rows + 8, LANES), F32),
        in_specs=[VMEM] * 4 + [HBM],
        out_specs=VMEM,
        scratch_shapes=[
            pltpu.VMEM((slots, slots), BF),
            pltpu.VMEM((2, 2 * group, slots), BF),
            pltpu.VMEM((2, 2 * padded, NLON // 2), BF),
            pltpu.VMEM((2, slots, padded), F32),
            trig_scratch,
            pltpu.SemaphoreType.DMA((trig_tiles,)),
        ],
        compiler_params=params,
        cost_estimate=work(8),
        name="grid",
    )(received, orders, capture_rate.reshape(row_count, NLON), row_sine, trig)
    returned = exchange(fluxes)

    chunk_shape = (blocks, chunks, CHUNK * BLK, 2 * HALF)
    legendre, within = pl.pallas_call(
        lambda *refs: table_kernel(blocks, *refs),
        out_shape=[
            jax.ShapeDtypeStruct(chunk_shape, BF),
            jax.ShapeDtypeStruct((modes, DEG), F32),
        ],
        in_specs=[SMEM, SMEM, VMEM],
        out_specs=[HBM, VMEM],
        scratch_shapes=[per_order] * 2
        + [pltpu.VMEM(chunk_shape, BF), pltpu.SemaphoreType.DMA((blocks, chunks))],
        compiler_params=params,
        cost_estimate=work(12),
        name="table",
    )(local, scalars, rows)
    column = jnp.broadcast_to(row_latitude[:, None], (NLAT, LANES))
    result = pl.pallas_call(
        lambda *refs: analyze_kernel(dims, chunk_rows, *refs),
        out_shape=jax.ShapeDtypeStruct((CHAN, modes, DEG), F32),
        in_specs=[SMEM, VMEM, VMEM, VMEM, VMEM, HBM],
        out_specs=VMEM,
        scratch_shapes=[
            pltpu.VMEM(chunk_shape, BF),
            pltpu.VMEM((blocks, 2 * HALF, 2 * LANES), BF),
            pltpu.VMEM((blocks * 4 * ROWS, NLAT), BF),
            pltpu.VMEM((blocks, DEG, LANES), F32),
            pltpu.VMEM((NLAT, HALF), BF),
            pltpu.VMEM((blocks, CHAN, BLK, DEG), F32),
            pltpu.SemaphoreType.DMA((blocks, chunks)),
        ],
        compiler_params=params,
        cost_estimate=work(9),
        name="analyze",
    )(local, returned, column, latitude, within, legendre)
    return result.reshape(1, FIELDS, 2, modes, DEG)


def solution(mesh):
    return jax.shard_map(
        per_device,
        mesh=mesh,
        in_specs=(P("shell", None, None, "band", None), P("shell", "band", None), P(), P()),
        out_specs=P("shell", None, None, "band", None),
        check_vma=False,
    )
```

```python
import functools
import math

import jax
import jax.numpy as jnp
import numpy as np
from jax import lax
from jax.experimental import pallas as pl
from jax.experimental.pallas import tpu as pltpu
from jax.sharding import PartitionSpec as P

DEG = 512
NLAT = 1024
NLON = 2048
FIELDS = 3
HALF = NLAT // 2
CHAN = 2 * FIELDS
BLK = 8
ROWS = CHAN * BLK
CHUNK = 64
CHECK = 16
PLACES = 1024
LANES = 128
KTILE = 256
BF = jnp.bfloat16
F32 = jnp.float32


def split_two(value):
    high = value.astype(BF)
    low = (value - high.astype(F32)).astype(BF)
    return high, low


def dot(lhs, rhs, contract_rhs=0):
    return lax.dot_general(
        lhs, rhs, (((1,), (contract_rhs,)), ((), ())), preferred_element_type=F32
    )


def latitude_rows():
    theta = np.pi * (np.arange(HALF) + 0.5) / NLAT
    index = np.arange(DEG, dtype=np.float64)
    log_terms = np.zeros(DEG)
    log_terms[1:] = 0.5 * np.log2((2.0 * index[1:] + 1.0) / (2.0 * index[1:]))
    rows = np.zeros((8, DEG))
    rows[0], rows[1], rows[2] = np.cos(theta), np.log2(np.sin(theta)), log_terms
    return rows.astype(np.float32)


def spread_matrix():
    spread = np.zeros((LANES, 2, 2, CHUNK // 2, BLK), np.float32)
    for half in range(2):
        for parity in range(2):
            for step in range(CHUNK // 2):
                spread[half * CHUNK + 2 * step + parity, half, parity, step, :] = 1.0
    return spread.reshape(LANES, 2 * 2 * (CHUNK // 2) * BLK).astype(BF)


def degree_scalars():
    before = np.arange(DEG, dtype=np.float64) - 1.0
    square = before * before
    return np.concatenate([square, 4.0 / (4.0 * square - 1.0)]).astype(np.float32)


def block_orders(slots_ref, first):
    sublane = lax.broadcasted_iota(jnp.int32, (BLK, LANES), 0)
    orders = jnp.zeros((BLK, LANES), jnp.int32)
    lowest, highest = jnp.int32(DEG), jnp.int32(0)
    for i in range(BLK):
        order = slots_ref[first + i] // PLACES
        orders = jnp.where(sublane == i, order, orders)
        lowest, highest = jnp.minimum(lowest, order), jnp.maximum(highest, order)
    return orders, lowest // CHUNK, highest // CHUNK + 1


def running_sum(terms, length):
    lane = lax.broadcasted_iota(jnp.int32, terms.shape, 1) & (length - 1)
    shift = 1
    while shift < length:
        moved = pltpu.roll(terms, shift, 1)
        terms = terms + jnp.where(lane >= shift, moved, 0.0)
        shift *= 2
    return terms


def recursion_tables(slots_ref, modes, rows_ref, start_ref, before_ref, within_ref):
    orders = [block_orders(slots_ref, at)[0][:, :1] for at in range(0, modes, BLK)]
    order = jnp.concatenate(orders, 0).astype(F32)
    position = lax.broadcasted_iota(jnp.int32, (modes, DEG), 1)
    degree = position.astype(F32)
    square = degree * degree
    above = degree > order
    gap = jnp.where(above, square - order * order, 1.0)
    growth = jnp.where(above, 0.5 * jnp.log2((square - 0.25) / gap), 0.0)
    before_ref[...] = running_sum(growth, DEG)
    later = jnp.where(position & (CHECK - 1) == 0, 0.0, growth)
    within_ref[...] = jnp.exp2(running_sum(later, CHECK))
    terms = jnp.where(degree <= order, rows_ref[2:3, :], 0.0)
    norm = jnp.where(order > 0, 0.5 + jnp.sum(terms, axis=1, keepdims=True), 0.0)
    start_ref[...] = norm + order * rows_ref[1:2, :]


def run_chunk(step, carry, double_cosine, orders, before, scalars_ref, emit, beside, guard):
    current, previous, log_scale = carry
    order = orders.astype(F32)
    order_square = order * order
    before = pltpu.roll(before, (step % 2) * CHUNK, 1)
    scale = None
    for i in range(CHUNK):
        if i % CHECK == 0:
            size = jnp.maximum(jnp.abs(current), jnp.abs(previous))
            large, small = size > 2.0**40, size < 2.0**-40
            factor = jnp.where(large, 2.0**-60, jnp.where(small, 2.0**60, 1.0))
            change = jnp.where(large, 60.0, jnp.where(small, -60.0, 0.0))
            current = current * factor
            previous = previous * factor
            log_scale = log_scale + change
            scale = jnp.exp2(jnp.maximum(log_scale + before[:, i : i + 1], -200.0))
        degree = step * CHUNK + i
        factor = (scalars_ref[degree] - order_square) * scalars_ref[DEG + degree]
        factor = jnp.tile(factor, (1, HALF // LANES))
        newest = double_cosine * current - factor * previous
        if guard:
            started = jnp.tile(orders, (1, HALF // LANES)) < degree
            newest = jnp.where(started, newest, 1.0)
        current, previous = newest, current
        emit(i, newest * scale)
        if beside and i % (CHUNK // len(beside)) == 1:
            beside[i // (CHUNK // len(beside))]()
    return current, previous, log_scale


def before_tile(before_ref, block, step):
    rows = pl.ds(pl.multiple_of(block * BLK, BLK), BLK)
    return before_ref[rows, pl.ds(pl.multiple_of(step // 2 * LANES, LANES), LANES)]


def start_state(start_ref, block):
    ones = jnp.ones((BLK, HALF), F32)
    return ones, ones, start_ref[pl.ds(pl.multiple_of(block * BLK, BLK), BLK), :]


def fold_matrix(latitude_ref, fold_ref):
    latitude = latitude_ref[...]
    north = jnp.where(latitude < HALF, latitude, NLAT - 1 - latitude)
    sublane = lax.broadcasted_iota(jnp.int32, (HALF, NLAT), 0)
    fold_ref[...] = jnp.where(sublane == north, 1.0, 0.0).astype(BF)


def synth_kernel(
    dims, slots_ref, scalars_in, spec_in, rows_in, spread_in, latitude_in,
    out_ref, scalars_ref, spec_ref, rows_ref, spread_ref, latitude_ref, sems,
    start_ref, before_ref, within_ref, lhs_ref, high_a, low_a, high_b, low_b, acc_ref, fold_ref, coeff_ref, sent_ref, out_sems,
):
    bands, row_count, modes, blocks, tiles = dims
    pairs = (
        (rows_in, rows_ref), (scalars_in, scalars_ref), (latitude_in, latitude_ref),
        (spread_in, spread_ref), (spec_in, spec_ref),
    )
    copies = []
    for index, (source, target) in enumerate(pairs):
        copies.append(pltpu.make_async_copy(source, target, sems.at[index]))
        copies[-1].start()
    copies[0].wait()
    recursion_tables(slots_ref, modes, rows_ref, start_ref, before_ref, within_ref)
    for copy in copies[1:]:
        copy.wait()
    fold_matrix(latitude_ref, fold_ref)
    south = latitude_ref[...] >= HALF
    spread_width = 4 * (CHUNK // 2) * BLK
    lane = lax.broadcasted_iota(jnp.int32, (2 * ROWS, spread_width), 1)
    sub = lax.broadcasted_iota(jnp.int32, (2 * ROWS, spread_width), 0)
    diagonal = (lane % BLK) == (sub % BLK)
    width = (CHUNK // 2) * BLK

    def one_block(block, unused):
        orders, first, last = block_orders(slots_ref, block * BLK)
        column = orders[:, :1]
        here = pl.ds(pl.multiple_of(block * BLK, BLK), BLK)
        for i in range(BLK):
            source = pl.ds(slots_ref[block * BLK + i] % PLACES, 1)
            coeff_ref[:, i : i + 1, :] = spec_ref[:, source, :]
        degree = lax.broadcasted_iota(jnp.int32, (BLK, DEG), 1)
        within = jnp.where(degree >= column, within_ref[here, :], 0.0)
        coeffs = coeff_ref[...] * within[None]
        coeff_high, coeff_low = split_two(coeffs.reshape(ROWS, DEG))
        stacked = jnp.concatenate([coeff_high, coeff_low], 0)
        for t in range(DEG // LANES):
            wide = dot(stacked[:, t * LANES : (t + 1) * LANES], spread_ref[...])
            wide = jnp.where(diagonal, wide, 0.0).astype(BF)
            for half in range(2):
                lhs_ref[2 * t + half] = wide[:, half * 2 * width : (half + 1) * 2 * width]
        acc_ref[block] = jnp.zeros((2, ROWS, HALF), F32)
        cosine = jnp.broadcast_to(2.0 * rows_ref[0:1, :], (BLK, HALF))

        def recur(step, carry, high_ref, low_ref, beside, guard):
            held = {}

            def emit(i, value):
                if i % 4 < 2:
                    held[i] = value
                else:
                    pair = jnp.concatenate([held.pop(i - 2), value], 0)
                    high, low = split_two(pair)
                    at = (i // 4) * 2 * BLK
                    high_ref[i % 2, at : at + 2 * BLK, :] = high
                    low_ref[i % 2, at : at + 2 * BLK, :] = low

            before = before_tile(before_ref, block, step)
            return run_chunk(
                step, carry, cosine, orders, before, scalars_ref, emit, beside, guard
            )

        def add_products(step, high_ref, low_ref):
            def part(parity, columns):
                lhs = lhs_ref[step, :, parity * width : (parity + 1) * width]
                first = dot(lhs, high_ref[parity, :, columns])
                second = dot(lhs[:ROWS], low_ref[parity, :, columns])
                acc_ref[block, parity, :, columns] += first[:ROWS] + first[ROWS:] + second

            return [
                functools.partial(part, parity, slice(at, at + KTILE))
                for parity in range(2)
                for at in range(0, HALF, KTILE)
            ]

        def two_chunks(guard, pair, carry):
            step = 2 * pair
            beside = add_products(jnp.maximum(step - 1, 0), high_b, low_b)
            carry = recur(step, carry, high_a, low_a, beside, guard)
            beside = add_products(step, high_a, low_a)
            return recur(step + 1, carry, high_b, low_b, beside, guard)

        high_b[...] = jnp.zeros_like(high_b)
        low_b[...] = jnp.zeros_like(low_b)
        chunks = DEG // CHUNK
        state = lax.fori_loop(
            0,
            first & 1,
            lambda unused, carry: recur(first, carry, high_b, low_b, (), True),
            start_state(start_ref, block),
        )
        middle = (last + 1) // 2
        state = lax.fori_loop(
            (first + 1) // 2, middle, functools.partial(two_chunks, True), state
        )
        lax.fori_loop(middle, chunks // 2, functools.partial(two_chunks, False), state)
        for part in add_products(chunks - 1, high_b, low_b):
            part()
        return unused

    lax.fori_loop(0, blocks, one_block, 0)
    high, low = split_two(acc_ref[...].reshape(blocks * 2 * ROWS, HALF))
    moved = dot(jnp.concatenate([high, low], 0), fold_ref[...])
    moved = moved[: blocks * 2 * ROWS] + moved[blocks * 2 * ROWS :]
    lanes = []
    for block in range(blocks):
        orders = block_orders(slots_ref, block * BLK)[0][:, :1]
        sign = jnp.tile(1.0 - 2.0 * (orders % 2).astype(F32), (CHAN, 1))
        even = moved[block * 2 * ROWS : block * 2 * ROWS + ROWS]
        odd = moved[block * 2 * ROWS + ROWS : (block + 1) * 2 * ROWS]
        lanes.append(jnp.where(south, sign * (even - odd), even + odd))
    copies = []
    for d in range(bands):
        columns = slice(d * row_count, (d + 1) * row_count)
        for block in range(blocks):
            parts = []
            for kind in range(2):
                for field in range(FIELDS):
                    c = field * 2 + kind
                    parts.append(lanes[block][c * BLK : (c + 1) * BLK, columns])
            if CHAN * row_count < tiles * LANES:
                parts.append(jnp.zeros((BLK, tiles * LANES - CHAN * row_count), F32))
            joined = jnp.concatenate(parts, 1)
            for t in range(tiles):
                at = slice((t * blocks + block) * BLK, (t * blocks + block + 1) * BLK)
                sent_ref[d, at, :] = joined[:, t * LANES : (t + 1) * LANES]
        copies.append(pltpu.make_async_copy(sent_ref.at[d], out_ref.at[d], out_sems.at[d]))
        copies[-1].start()
    for copy in copies:
        copy.wait()


def table_kernel(
    blocks, slots_ref, scalars_ref, rows_ref, out_ref, within_out, start_ref, before_ref,
    chunk_ref, sems,
):
    modes = blocks * BLK
    cosine = jnp.broadcast_to(2.0 * rows_ref[0:1, :], (BLK, HALF))
    recursion_tables(slots_ref, modes, rows_ref, start_ref, before_ref, within_out)

    def copy_out(block, step):
        return pltpu.make_async_copy(
            chunk_ref.at[block, step], out_ref.at[block, step], sems.at[block, step]
        )

    def one_block(block, unused):
        orders, first, last = block_orders(slots_ref, block * BLK)

        def one_chunk(guard, step, carry):
            held = {}

            def emit(i, value):
                if i % 2 == 0:
                    held[i] = value
                else:
                    pair = jnp.concatenate([held.pop(i - 1), value], 0)
                    high, low = split_two(pair)
                    at = (i // 2) * 2 * BLK
                    chunk_ref[block, step, at : at + 2 * BLK, :HALF] = high
                    chunk_ref[block, step, at : at + 2 * BLK, HALF:] = low

            before = before_tile(before_ref, block, step)
            carry = run_chunk(
                step, carry, cosine, orders, before, scalars_ref, emit, (), guard
            )
            copy_out(block, step).start()
            return carry

        state = start_state(start_ref, block)
        state = lax.fori_loop(first, last, functools.partial(one_chunk, True), state)
        lax.fori_loop(last, DEG // CHUNK, functools.partial(one_chunk, False), state)
        return unused

    def finish_block(block, unused):
        orders, first, last = block_orders(slots_ref, block * BLK)

        def finish_chunk(step, inner):
            copy_out(block, step).wait()
            return inner

        return lax.fori_loop(first, DEG // CHUNK, finish_chunk, unused)

    lax.fori_loop(0, blocks, one_block, 0)
    lax.fori_loop(0, blocks, finish_block, 0)


def analyze_kernel(
    dims, total_row, slots_ref, data_ref, column_ref, latitude_ref, within_ref, table_ref,
    out_ref, chunk_ref, weight_ref, stack_ref, result_ref, fold_ref, coeff_ref, sems,
):
    bands, row_count, modes, blocks, tiles = dims
    chunks = DEG // CHUNK

    def copy_in(block, step):
        return pltpu.make_async_copy(
            table_ref.at[block, step], chunk_ref.at[block, step], sems.at[block, step]
        )

    def start_block(block, unused):
        orders, first, last = block_orders(slots_ref, block * BLK)

        def start_chunk(step, inner):
            copy_in(block, step).start()
            return inner

        return lax.fori_loop(first, chunks, start_chunk, unused)

    lax.fori_loop(0, blocks, start_block, 0)
    latitude = column_ref[...]
    north = jnp.where(latitude < HALF, latitude, NLAT - 1 - latitude)
    lane = lax.broadcasted_iota(jnp.int32, (NLAT, LANES), 1)
    for t in range(HALF // LANES):
        one_hot = jnp.where(north == lane + t * LANES, 1.0, 0.0).astype(BF)
        fold_ref[:, t * LANES : (t + 1) * LANES] = one_hot
    south = latitude_ref[...] >= HALF
    for block in range(blocks):
        orders = block_orders(slots_ref, block * BLK)[0][:, :1]
        sign = 1.0 - 2.0 * (orders % 2).astype(F32)
        evens, odds = [], []
        for c in range(CHAN):
            offset = ((c % 2) * FIELDS + c // 2) * row_count
            t, at = offset // LANES, offset % LANES
            rows = slice((t * blocks + block) * BLK, (t * blocks + block + 1) * BLK)
            values = jnp.concatenate(
                [data_ref[d, rows, :][:, at : at + row_count] for d in range(bands)], 1
            )
            flipped = sign * values
            evens.append(jnp.where(south, flipped, values))
            odds.append(jnp.where(south, -flipped, values))
        high, low = split_two(jnp.concatenate(evens + odds, 0))
        stack_ref[block * 4 * ROWS : block * 4 * ROWS + 2 * ROWS, :] = high
        stack_ref[block * 4 * ROWS + 2 * ROWS : (block + 1) * 4 * ROWS, :] = low
    folded = dot(stack_ref[...], fold_ref[...])
    for block in range(blocks):
        at = block * 4 * ROWS
        part = folded[at : at + 2 * ROWS] + folded[at + 2 * ROWS : at + 4 * ROWS]
        part = jnp.concatenate([part, jnp.zeros((LANES - 2 * ROWS, HALF), F32)], 0)
        high, low = split_two(part.T)
        weight_ref[block, :HALF, :LANES] = high
        weight_ref[block, :HALF, LANES:] = low
        weight_ref[block, HALF:, :LANES] = high
        weight_ref[block, HALF:, LANES:] = jnp.zeros_like(low)

    total = data_ref[0, total_row : total_row + 8]
    for d in range(1, bands):
        total = total + data_ref[d, total_row : total_row + 8]
    inverse = (1.0 / total)[:, :1]
    lane = lax.broadcasted_iota(jnp.int32, (CHUNK * BLK, LANES), 1)
    sub = lax.broadcasted_iota(jnp.int32, (CHUNK * BLK, LANES), 0)
    keep = (lane % BLK == sub % BLK) & (lane // ROWS == sub // BLK % 2)

    def one_block(block, unused):
        orders, first, last = block_orders(slots_ref, block * BLK)
        orders = orders[:, :1]
        here = pl.ds(pl.multiple_of(block * BLK, BLK), BLK)
        result_ref[block] = jnp.zeros((DEG, LANES), F32)

        def some_chunks(step, count):
            for k in range(count):
                copy_in(block, step + k).wait()
            values = chunk_ref[block, pl.ds(step, count)].reshape(count * CHUNK * BLK, 2 * HALF)
            full = dot(values, weight_ref[block])
            full = (full[:, :LANES] + full[:, LANES:]).reshape(count, CHUNK * BLK, LANES)
            picked = jnp.where(keep[None], full, 0.0).reshape(count * CHUNK, BLK, LANES)
            to = pl.ds(pl.multiple_of(step * CHUNK, CHUNK), count * CHUNK)
            result_ref[block, to, :] = jnp.sum(picked, axis=1)

        def lone_chunk(unused, inner):
            some_chunks(first, 1)
            return inner

        even = (first + 1) // 2

        def two_chunks(unused, inner):
            some_chunks(2 * even, 2)
            return inner

        def four_chunks(group, inner):
            some_chunks(4 * group, 4)
            return inner

        lax.fori_loop(0, first & 1, lone_chunk, 0)
        lax.fori_loop(0, even & 1, two_chunks, 0)
        lax.fori_loop((even + 1) // 2, chunks // 4, four_chunks, 0)
        return unused

    lax.fori_loop(0, blocks, one_block, 0)
    for block in range(blocks):
        orders = block_orders(slots_ref, block * BLK)[0][:, :1]
        turned = result_ref[block].T
        turned = turned[:ROWS] + turned[ROWS : 2 * ROWS]
        degree = lax.broadcasted_iota(jnp.int32, (BLK, DEG), 1)
        within = jnp.where(degree >= orders, within_ref[block * BLK : (block + 1) * BLK, :], 0.0)
        for c in range(CHAN):
            part = turned[c * BLK : (c + 1) * BLK] * within
            if c // 2 == FIELDS - 1:
                part = part * inverse
            coeff_ref[block, c] = part
        for i in range(BLK):
            target = pl.ds(slots_ref[block * BLK + i] % PLACES, 1)
            out_ref[:, target, :] = coeff_ref[block, :, i : i + 1, :]


def base_trig(order, first):
    lane = lax.broadcasted_iota(jnp.int32, order.shape, 1) + first
    phase = (order * lane) & (NLON - 1)
    quarter = (phase + NLON // 8) >> 9
    rest = (phase - quarter * (NLON // 4)).astype(F32) * (2.0 * math.pi / NLON)
    square = rest * rest
    sine = 1.0 / 362880.0
    for coef in (-1.0 / 5040.0, 1.0 / 120.0, -1.0 / 6.0, 1.0):
        sine = sine * square + coef
    sine = sine * rest
    cosine = 1.0 / 40320.0
    for coef in (-1.0 / 720.0, 1.0 / 24.0, -0.5, 1.0):
        cosine = cosine * square + coef
    swap = (quarter & 1) == 1
    cos_out = jnp.where(swap, sine, cosine)
    sin_out = jnp.where(swap, cosine, sine)
    cos_out = jnp.where(((quarter + 1) & 2) == 2, -cos_out, cos_out)
    sin_out = jnp.where((quarter & 2) == 2, -sin_out, sin_out)
    return cos_out, sin_out


def trig_kernel(out_ref, trig_ref, sem):
    half = trig_ref.shape[3] // 2
    root = math.sqrt(0.5)
    for parity in range(2):

        def strip(step, unused):
            at = pl.multiple_of(step * 64, 64)
            shape = (64, LANES)
            order = 2 * (lax.broadcasted_iota(jnp.int32, shape, 0) + at) + parity
            eighth = order & 7
            odd = (eighth & 1) == 1
            turn_cos = jnp.where(odd, root, jnp.where((eighth & 2) == 0, 1.0, 0.0))
            turn_sin = jnp.where(odd, root, jnp.where((eighth & 2) == 2, 1.0, 0.0))
            turn_cos = jnp.where((eighth >= 3) & (eighth <= 5), -turn_cos, turn_cos)
            turn_sin = jnp.where(eighth > 4, -turn_sin, turn_sin)
            for t in range(KTILE // LANES):
                cosine, sine = base_trig(order, t * LANES)
                for k in range(t * LANES, NLON // 2, KTILE):
                    columns = slice(t * LANES, (t + 1) * LANES)
                    for values, start in ((cosine, at), (sine, half + at)):
                        high, low = split_two(values)
                        trig_ref[k // KTILE, 0, parity, pl.ds(start, 64), columns] = high
                        trig_ref[k // KTILE, 1, parity, pl.ds(start, 64), columns] = low
                    cosine, sine = (
                        cosine * turn_cos - sine * turn_sin,
                        sine * turn_cos + cosine * turn_sin,
                    )
            return unused

        lax.fori_loop(0, half // 64, strip, 0)
    copy = pltpu.make_async_copy(trig_ref, out_ref, sem)
    copy.start()
    copy.wait()


def grid_kernel(
    dims, data_ref, orders_ref, rate_ref, sine_ref, trig_in, out_ref,
    move_ref, lhs_ref, weight_ref, acc_ref, trig_ref, sems,
):
    bands, row_count, modes, tiles, slots = dims
    half = slots // 2
    group = FIELDS * row_count
    padded = weight_ref.shape[1] // 2

    copies = []
    for tile in range(NLON // 2 // KTILE):
        copy = pltpu.make_async_copy(trig_in.at[tile], trig_ref.at[tile], sems.at[tile])
        copy.start()
        copies.append(copy)
    order = orders_ref[...]
    natural = (order & 1) * half + (order >> 1)
    for t in range(slots // LANES):
        lane = lax.broadcasted_iota(jnp.int32, (slots, LANES), 1) + t * LANES
        one_hot = jnp.where(natural == lane, 1.0, 0.0).astype(BF)
        move_ref[:, t * LANES : (t + 1) * LANES] = one_hot
    columns = []
    for t in range(tiles):
        part = data_ref[:, t * modes : (t + 1) * modes, :]
        columns.append(part.reshape(slots, LANES).T)
    turned = jnp.concatenate(columns, 0)
    for kind in range(2):
        high, low = split_two(turned[kind * group : (kind + 1) * group])
        moved = dot(jnp.concatenate([high, low], 0), move_ref[...]).astype(BF)
        for parity in range(2):
            part = moved[:, parity * half : (parity + 1) * half]
            lhs_ref[parity, :, kind * half : (kind + 1) * half] = part
    weight_ref[...] = jnp.zeros_like(weight_ref)
    flux_scale = math.pi / (2.0 * NLAT * NLON * DEG)
    weight = jnp.tile(sine_ref[...], (1, KTILE // LANES))
    total = jnp.zeros((8, KTILE), F32)

    for k in range(0, NLON // 2, KTILE):
        copies[k // KTILE].wait()
        trig_high, trig_low = trig_ref.at[k // KTILE, 0], trig_ref.at[k // KTILE, 1]
        sums = []
        for parity in range(2):
            first = dot(lhs_ref[parity], trig_high[parity])
            second = dot(lhs_ref[parity, :group, :], trig_low[parity])
            sums.append(first[:group] + first[group:] + second)
        values = []
        for fields, at in ((sums[0] + sums[1], k), (sums[0] - sums[1], k + NLON // 2)):
            weighted_rate = rate_ref[:, at : at + KTILE] * weight
            total = total + jnp.sum(weighted_rate.reshape(row_count // 8, 8, KTILE), axis=0)
            scaled = fields[:row_count] * (weight * flux_scale)
            values.append(
                jnp.concatenate(
                    [
                        fields[row_count : 2 * row_count] * scaled,
                        fields[2 * row_count :] * scaled,
                        weighted_rate * fields[:row_count],
                    ],
                    0,
                )
            )
        for parity in range(2):
            both = values[0] + values[1] if parity == 0 else values[0] - values[1]
            high, low = split_two(both)
            columns = slice(k, k + KTILE)
            weight_ref[parity, :group, columns] = high
            weight_ref[parity, padded : padded + group, columns] = low
    for parity in range(2):
        trig_high, trig_low = [
            jnp.concatenate([trig_ref[t, part, parity] for t in range(len(copies))], 1)
            for part in range(2)
        ]
        first = dot(trig_high, weight_ref[parity], 1)
        second = dot(trig_low, weight_ref[parity, :padded, :], 1)
        acc_ref[parity] = first[:, :padded] + first[:, padded:] + second

    joined = []
    for kind in range(2):
        rows = slice(kind * half, (kind + 1) * half)
        joined.append(jnp.concatenate([acc_ref[0, rows, :group], acc_ref[1, rows, :group]], 0))
    if 2 * group < tiles * LANES:
        joined.append(jnp.zeros((slots, tiles * LANES - 2 * group), F32))
    high, low = split_two(jnp.concatenate(joined, 1))
    moved = dot(move_ref[...], jnp.concatenate([high, low], 1))
    moved = moved[:, : tiles * LANES] + moved[:, tiles * LANES :]
    for t in range(tiles):
        part = moved[:, t * LANES : (t + 1) * LANES]
        out_ref[:, t * modes : (t + 1) * modes, :] = part.reshape(bands, modes, LANES)
    out_ref[:, tiles * modes :, :] = jnp.broadcast_to(jnp.sum(total), (bands, 8, LANES))


VMEM = pl.BlockSpec(memory_space=pltpu.VMEM)
SMEM = pl.BlockSpec(memory_space=pltpu.SMEM)
HBM = pl.BlockSpec(memory_space=pltpu.HBM)


def work(microseconds):
    return pl.CostEstimate(
        flops=microseconds * 10**9, bytes_accessed=2**20, transcendentals=0
    )


def per_device(spectrum, capture_rate, row_latitude, slot_wavenumber):
    bands = lax.axis_size("band")
    modes = spectrum.shape[3]
    row_count = capture_rate.shape[1]
    slots = slot_wavenumber.shape[0]
    blocks = modes // BLK
    chunks = DEG // CHUNK
    tiles = -(-CHAN * row_count // LANES)
    band_index = lax.axis_index("band")

    def sort_rows(table):
        rank = jnp.sum((table[:, None, :] < table[:, :, None]).astype(jnp.int32), 2)
        match = rank[:, None, :] == jnp.arange(modes, dtype=jnp.int32)[None, :, None]
        keys = table * PLACES + jnp.arange(modes, dtype=jnp.int32)[None, :]
        return jnp.sum(jnp.where(match, keys[:, None, :], 0), 2).reshape(-1)

    own = lax.dynamic_slice_in_dim(slot_wavenumber, band_index * modes, modes)
    local = sort_rows(own.reshape(1, modes))
    ordered = sort_rows(slot_wavenumber.reshape(bands, modes)) // PLACES
    rows = jnp.asarray(latitude_rows())
    spread = jnp.asarray(spread_matrix())
    latitude = row_latitude.reshape(1, NLAT)
    coeffs = spectrum.reshape(CHAN, modes, DEG)
    params = pltpu.CompilerParams(vmem_limit_bytes=48 * 2**20)
    chunk_rows = tiles * modes
    dims = (bands, row_count, modes, blocks, tiles)
    scalars = jnp.asarray(degree_scalars())
    per_order = pltpu.VMEM((modes, DEG), F32)

    def exchange(value):
        return lax.all_to_all(value, "band", split_axis=0, concat_axis=0, tiled=True)

    sent = pl.pallas_call(
        lambda *refs: synth_kernel(dims, *refs),
        out_shape=jax.ShapeDtypeStruct((bands, chunk_rows, LANES), F32),
        in_specs=[SMEM] + [HBM] * 5,
        out_specs=HBM,
        scratch_shapes=[
            pltpu.SMEM(scalars.shape, F32),
            pltpu.VMEM(coeffs.shape, F32),
            pltpu.VMEM(rows.shape, F32),
            pltpu.VMEM(spread.shape, BF),
            pltpu.VMEM(latitude.shape, jnp.int32),
            pltpu.SemaphoreType.DMA((5,)),
        ]
        + [per_order] * 3
        + [pltpu.VMEM((chunks, 2 * ROWS, CHUNK * BLK), BF)]
        + [pltpu.VMEM((2, CHUNK // 2 * BLK, HALF), BF)] * 4
        + [
            pltpu.VMEM((blocks, 2, ROWS, HALF), F32),
            pltpu.VMEM((HALF, NLAT), BF),
            pltpu.VMEM((CHAN, BLK, DEG), F32),
            pltpu.VMEM((bands, chunk_rows, LANES), F32),
            pltpu.SemaphoreType.DMA((bands,)),
        ],
        compiler_params=pltpu.CompilerParams(vmem_limit_bytes=62 * 2**20),
        cost_estimate=work(15),
        name="synth",
    )(local, scalars, coeffs, rows, spread, latitude)
    received = exchange(sent)

    trig_tiles = NLON // 2 // KTILE
    trig_shape = (trig_tiles, 2, 2, slots, KTILE)
    trig_scratch = pltpu.VMEM(trig_shape, BF)
    trig = pl.pallas_call(
        trig_kernel,
        out_shape=jax.ShapeDtypeStruct(trig_shape, BF),
        out_specs=HBM,
        scratch_shapes=[trig_scratch, pltpu.SemaphoreType.DMA(())],
        compiler_params=params,
        cost_estimate=work(4),
        name="trig",
    )()

    my_latitudes = lax.dynamic_slice_in_dim(row_latitude, band_index * row_count, row_count)
    row_sine = jnp.sin(jnp.pi * (my_latitudes.astype(F32) + 0.5) / NLAT)
    row_sine = jnp.broadcast_to(row_sine[:, None], (row_count, LANES))
    orders = jnp.broadcast_to(ordered.reshape(slots, 1), (slots, LANES))
    group = FIELDS * row_count
    padded = -(-group // LANES) * LANES
    grid_dims = (bands, row_count, modes, tiles, slots)
    fluxes = pl.pallas_call(
        lambda *refs: grid_kernel(grid_dims, *refs),
        out_shape=jax.ShapeDtypeStruct((bands, chunk_rows + 8, LANES), F32),
        in_specs=[VMEM] * 4 + [HBM],
        out_specs=VMEM,
        scratch_shapes=[
            pltpu.VMEM((slots, slots), BF),
            pltpu.VMEM((2, 2 * group, slots), BF),
            pltpu.VMEM((2, 2 * padded, NLON // 2), BF),
            pltpu.VMEM((2, slots, padded), F32),
            trig_scratch,
            pltpu.SemaphoreType.DMA((trig_tiles,)),
        ],
        compiler_params=params,
        cost_estimate=work(8),
        name="grid",
    )(received, orders, capture_rate.reshape(row_count, NLON), row_sine, trig)
    returned = exchange(fluxes)

    chunk_shape = (blocks, chunks, CHUNK * BLK, 2 * HALF)
    legendre, within = pl.pallas_call(
        lambda *refs: table_kernel(blocks, *refs),
        out_shape=[
            jax.ShapeDtypeStruct(chunk_shape, BF),
            jax.ShapeDtypeStruct((modes, DEG), F32),
        ],
        in_specs=[SMEM, SMEM, VMEM],
        out_specs=[HBM, VMEM],
        scratch_shapes=[per_order] * 2
        + [pltpu.VMEM(chunk_shape, BF), pltpu.SemaphoreType.DMA((blocks, chunks))],
        compiler_params=params,
        cost_estimate=work(12),
        name="table",
    )(local, scalars, rows)
    column = jnp.broadcast_to(row_latitude[:, None], (NLAT, LANES))
    result = pl.pallas_call(
        lambda *refs: analyze_kernel(dims, chunk_rows, *refs),
        out_shape=jax.ShapeDtypeStruct((CHAN, modes, DEG), F32),
        in_specs=[SMEM, VMEM, VMEM, VMEM, VMEM, HBM],
        out_specs=VMEM,
        scratch_shapes=[
            pltpu.VMEM(chunk_shape, BF),
            pltpu.VMEM((blocks, 2 * HALF, 2 * LANES), BF),
            pltpu.VMEM((blocks * 4 * ROWS, NLAT), BF),
            pltpu.VMEM((blocks, DEG, LANES), F32),
            pltpu.VMEM((NLAT, HALF), BF),
            pltpu.VMEM((blocks, CHAN, BLK, DEG), F32),
            pltpu.SemaphoreType.DMA((blocks, chunks)),
        ],
        compiler_params=params,
        cost_estimate=work(9),
        name="analyze",
    )(local, returned, column, latitude, within, legendre)
    return result.reshape(1, FIELDS, 2, modes, DEG)


def solution(mesh):
    return jax.shard_map(
        per_device,
        mesh=mesh,
        in_specs=(P("shell", None, None, "band", None), P("shell", "band", None), P(), P()),
        out_specs=P("shell", None, None, "band", None),
        check_vma=False,
    )
```

```python
import functools
import math

import jax
import jax.numpy as jnp
import numpy as np
from jax import lax
from jax.experimental import pallas as pl
from jax.experimental.pallas import tpu as pltpu
from jax.sharding import PartitionSpec as P

DEG = 512
NLAT = 1024
NLON = 2048
FIELDS = 3
HALF = NLAT // 2
CHAN = 2 * FIELDS
BLK = 8
ROWS = CHAN * BLK
CHUNK = 64
CHECK = 16
PLACES = 1024
LANES = 128
KTILE = 256
BF = jnp.bfloat16
F32 = jnp.float32


def split_two(value):
    high = value.astype(BF)
    low = (value - high.astype(F32)).astype(BF)
    return high, low


def dot(lhs, rhs, contract_rhs=0):
    return lax.dot_general(
        lhs, rhs, (((1,), (contract_rhs,)), ((), ())), preferred_element_type=F32
    )


def latitude_rows():
    theta = np.pi * (np.arange(HALF) + 0.5) / NLAT
    index = np.arange(DEG, dtype=np.float64)
    log_terms = np.zeros(DEG)
    log_terms[1:] = 0.5 * np.log2((2.0 * index[1:] + 1.0) / (2.0 * index[1:]))
    rows = np.zeros((8, DEG))
    rows[0], rows[1], rows[2] = np.cos(theta), np.log2(np.sin(theta)), log_terms
    return rows.astype(np.float32)


def spread_matrix():
    spread = np.zeros((LANES, 2, 2, CHUNK // 2, BLK), np.float32)
    for half in range(2):
        for parity in range(2):
            for step in range(CHUNK // 2):
                spread[half * CHUNK + 2 * step + parity, half, parity, step, :] = 1.0
    return spread.reshape(LANES, 2 * 2 * (CHUNK // 2) * BLK).astype(BF)


def degree_scalars():
    before = np.arange(DEG, dtype=np.float64) - 1.0
    square = before * before
    return np.concatenate([square, 4.0 / (4.0 * square - 1.0)]).astype(np.float32)


def block_orders(slots_ref, first):
    sublane = lax.broadcasted_iota(jnp.int32, (BLK, LANES), 0)
    orders = jnp.zeros((BLK, LANES), jnp.int32)
    lowest, highest = jnp.int32(DEG), jnp.int32(0)
    for i in range(BLK):
        order = slots_ref[first + i] // PLACES
        orders = jnp.where(sublane == i, order, orders)
        lowest, highest = jnp.minimum(lowest, order), jnp.maximum(highest, order)
    return orders, lowest // CHUNK, highest // CHUNK + 1


def running_sum(terms, length):
    lane = lax.broadcasted_iota(jnp.int32, terms.shape, 1) & (length - 1)
    shift = 1
    while shift < length:
        moved = pltpu.roll(terms, shift, 1)
        terms = terms + jnp.where(lane >= shift, moved, 0.0)
        shift *= 2
    return terms


def recursion_tables(slots_ref, modes, rows_ref, start_ref, before_ref, within_ref):
    orders = [block_orders(slots_ref, at)[0][:, :1] for at in range(0, modes, BLK)]
    order = jnp.concatenate(orders, 0).astype(F32)
    position = lax.broadcasted_iota(jnp.int32, (modes, DEG), 1)
    degree = position.astype(F32)
    square = degree * degree
    above = degree > order
    gap = jnp.where(above, square - order * order, 1.0)
    growth = jnp.where(above, 0.5 * jnp.log2((square - 0.25) / gap), 0.0)
    before_ref[...] = running_sum(growth, DEG)
    later = jnp.where(position & (CHECK - 1) == 0, 0.0, growth)
    within_ref[...] = jnp.exp2(running_sum(later, CHECK))
    terms = jnp.where(degree <= order, rows_ref[2:3, :], 0.0)
    norm = jnp.where(order > 0, 0.5 + jnp.sum(terms, axis=1, keepdims=True), 0.0)
    start_ref[...] = norm + order * rows_ref[1:2, :]


def run_chunk(step, carry, double_cosine, orders, before, scalars_ref, emit, beside, guard):
    current, previous, log_scale = carry
    order = orders.astype(F32)
    order_square = order * order
    before = pltpu.roll(before, (step % 2) * CHUNK, 1)
    scale = None
    for i in range(CHUNK):
        if i % CHECK == 0:
            size = jnp.maximum(jnp.abs(current), jnp.abs(previous))
            large, small = size > 2.0**40, size < 2.0**-40
            factor = jnp.where(large, 2.0**-60, jnp.where(small, 2.0**60, 1.0))
            change = jnp.where(large, 60.0, jnp.where(small, -60.0, 0.0))
            current = current * factor
            previous = previous * factor
            log_scale = log_scale + change
            scale = jnp.exp2(jnp.maximum(log_scale + before[:, i : i + 1], -200.0))
        degree = step * CHUNK + i
        factor = (scalars_ref[degree] - order_square) * scalars_ref[DEG + degree]
        factor = jnp.tile(factor, (1, HALF // LANES))
        newest = double_cosine * current - factor * previous
        if guard:
            started = jnp.tile(orders, (1, HALF // LANES)) < degree
            newest = jnp.where(started, newest, 1.0)
        current, previous = newest, current
        emit(i, newest * scale)
        if beside and i % (CHUNK // len(beside)) == 1:
            beside[i // (CHUNK // len(beside))]()
    return current, previous, log_scale


def before_tile(before_ref, block, step):
    rows = pl.ds(pl.multiple_of(block * BLK, BLK), BLK)
    return before_ref[rows, pl.ds(pl.multiple_of(step // 2 * LANES, LANES), LANES)]


def start_state(start_ref, block):
    ones = jnp.ones((BLK, HALF), F32)
    return ones, ones, start_ref[pl.ds(pl.multiple_of(block * BLK, BLK), BLK), :]


def fold_matrix(latitude_ref, fold_ref):
    latitude = latitude_ref[...]
    north = jnp.where(latitude < HALF, latitude, NLAT - 1 - latitude)
    sublane = lax.broadcasted_iota(jnp.int32, (HALF, NLAT), 0)
    fold_ref[...] = jnp.where(sublane == north, 1.0, 0.0).astype(BF)


def synth_kernel(
    dims, slots_ref, scalars_in, spec_in, rows_in, spread_in, latitude_in,
    out_ref, scalars_ref, spec_ref, rows_ref, spread_ref, latitude_ref, sems,
    start_ref, before_ref, within_ref, lhs_ref, high_a, low_a, high_b, low_b, acc_ref, fold_ref, coeff_ref,
):
    bands, row_count, modes, blocks, tiles = dims
    pairs = (
        (rows_in, rows_ref), (scalars_in, scalars_ref), (latitude_in, latitude_ref),
        (spread_in, spread_ref), (spec_in, spec_ref),
    )
    copies = []
    for index, (source, target) in enumerate(pairs):
        copies.append(pltpu.make_async_copy(source, target, sems.at[index]))
        copies[-1].start()
    copies[0].wait()
    recursion_tables(slots_ref, modes, rows_ref, start_ref, before_ref, within_ref)
    for copy in copies[1:]:
        copy.wait()
    fold_matrix(latitude_ref, fold_ref)
    south = latitude_ref[...] >= HALF
    spread_width = 4 * (CHUNK // 2) * BLK
    lane = lax.broadcasted_iota(jnp.int32, (2 * ROWS, spread_width), 1)
    sub = lax.broadcasted_iota(jnp.int32, (2 * ROWS, spread_width), 0)
    diagonal = (lane % BLK) == (sub % BLK)
    width = (CHUNK // 2) * BLK

    def one_block(block, unused):
        orders, first, last = block_orders(slots_ref, block * BLK)
        column = orders[:, :1]
        here = pl.ds(pl.multiple_of(block * BLK, BLK), BLK)
        for i in range(BLK):
            source = pl.ds(slots_ref[block * BLK + i] % PLACES, 1)
            coeff_ref[:, i : i + 1, :] = spec_ref[:, source, :]
        degree = lax.broadcasted_iota(jnp.int32, (BLK, DEG), 1)
        within = jnp.where(degree >= column, within_ref[here, :], 0.0)
        coeffs = coeff_ref[...] * within[None]
        coeff_high, coeff_low = split_two(coeffs.reshape(ROWS, DEG))
        stacked = jnp.concatenate([coeff_high, coeff_low], 0)
        for t in range(DEG // LANES):
            wide = dot(stacked[:, t * LANES : (t + 1) * LANES], spread_ref[...])
            wide = jnp.where(diagonal, wide, 0.0).astype(BF)
            for half in range(2):
                lhs_ref[2 * t + half] = wide[:, half * 2 * width : (half + 1) * 2 * width]
        acc_ref[block] = jnp.zeros((2, ROWS, HALF), F32)
        cosine = jnp.broadcast_to(2.0 * rows_ref[0:1, :], (BLK, HALF))

        def recur(step, carry, high_ref, low_ref, beside, guard):
            held = {}

            def emit(i, value):
                if i % 4 < 2:
                    held[i] = value
                else:
                    pair = jnp.concatenate([held.pop(i - 2), value], 0)
                    high, low = split_two(pair)
                    at = (i // 4) * 2 * BLK
                    high_ref[i % 2, at : at + 2 * BLK, :] = high
                    low_ref[i % 2, at : at + 2 * BLK, :] = low

            before = before_tile(before_ref, block, step)
            return run_chunk(
                step, carry, cosine, orders, before, scalars_ref, emit, beside, guard
            )

        def add_products(step, high_ref, low_ref):
            def part(parity, columns):
                lhs = lhs_ref[step, :, parity * width : (parity + 1) * width]
                first = dot(lhs, high_ref[parity, :, columns])
                second = dot(lhs[:ROWS], low_ref[parity, :, columns])
                acc_ref[block, parity, :, columns] += first[:ROWS] + first[ROWS:] + second

            return [
                functools.partial(part, parity, slice(at, at + 2 * KTILE))
                for parity in range(2)
                for at in range(0, HALF, 2 * KTILE)
            ]

        def two_chunks(guard, pair, carry):
            step = 2 * pair
            beside = add_products(jnp.maximum(step - 1, 0), high_b, low_b)
            carry = recur(step, carry, high_a, low_a, beside, guard)
            beside = add_products(step, high_a, low_a)
            return recur(step + 1, carry, high_b, low_b, beside, guard)

        high_b[...] = jnp.zeros_like(high_b)
        low_b[...] = jnp.zeros_like(low_b)
        chunks = DEG // CHUNK
        state = lax.fori_loop(
            0,
            first & 1,
            lambda unused, carry: recur(first, carry, high_b, low_b, (), True),
            start_state(start_ref, block),
        )
        middle = (last + 1) // 2
        state = lax.fori_loop(
            (first + 1) // 2, middle, functools.partial(two_chunks, True), state
        )
        lax.fori_loop(middle, chunks // 2, functools.partial(two_chunks, False), state)
        for part in add_products(chunks - 1, high_b, low_b):
            part()
        return unused

    lax.fori_loop(0, blocks, one_block, 0)
    high, low = split_two(acc_ref[...].reshape(blocks * 2 * ROWS, HALF))
    moved = dot(jnp.concatenate([high, low], 0), fold_ref[...])
    moved = moved[: blocks * 2 * ROWS] + moved[blocks * 2 * ROWS :]
    for block in range(blocks):
        orders = block_orders(slots_ref, block * BLK)[0][:, :1]
        sign = jnp.tile(1.0 - 2.0 * (orders % 2).astype(F32), (CHAN, 1))
        even = moved[block * 2 * ROWS : block * 2 * ROWS + ROWS]
        odd = moved[block * 2 * ROWS + ROWS : (block + 1) * 2 * ROWS]
        values = jnp.where(south, sign * (even - odd), even + odd)
        for d in range(bands):
            parts = []
            for kind in range(2):
                for field in range(FIELDS):
                    c = field * 2 + kind
                    parts.append(
                        values[c * BLK : (c + 1) * BLK, d * row_count : (d + 1) * row_count]
                    )
            if CHAN * row_count < tiles * LANES:
                parts.append(jnp.zeros((BLK, tiles * LANES - CHAN * row_count), F32))
            joined = jnp.concatenate(parts, 1)
            for t in range(tiles):
                at = slice((t * blocks + block) * BLK, (t * blocks + block + 1) * BLK)
                out_ref[d, at, :] = joined[:, t * LANES : (t + 1) * LANES]


def table_kernel(
    blocks, slots_ref, scalars_ref, rows_ref, out_ref, within_out, start_ref, before_ref,
    chunk_ref, sems,
):
    modes = blocks * BLK
    cosine = jnp.broadcast_to(2.0 * rows_ref[0:1, :], (BLK, HALF))
    recursion_tables(slots_ref, modes, rows_ref, start_ref, before_ref, within_out)

    def copy_out(block, step):
        return pltpu.make_async_copy(
            chunk_ref.at[block, step], out_ref.at[block, step], sems.at[block, step]
        )

    def one_block(block, unused):
        orders, first, last = block_orders(slots_ref, block * BLK)

        def one_chunk(guard, step, carry):
            held = {}

            def emit(i, value):
                if i % 2 == 0:
                    held[i] = value
                else:
                    pair = jnp.concatenate([held.pop(i - 1), value], 0)
                    high, low = split_two(pair)
                    at = (i // 2) * 2 * BLK
                    chunk_ref[block, step, at : at + 2 * BLK, :HALF] = high
                    chunk_ref[block, step, at : at + 2 * BLK, HALF:] = low

            before = before_tile(before_ref, block, step)
            carry = run_chunk(
                step, carry, cosine, orders, before, scalars_ref, emit, (), guard
            )
            copy_out(block, step).start()
            return carry

        state = start_state(start_ref, block)
        state = lax.fori_loop(first, last, functools.partial(one_chunk, True), state)
        lax.fori_loop(last, DEG // CHUNK, functools.partial(one_chunk, False), state)
        return unused

    def finish_block(block, unused):
        orders, first, last = block_orders(slots_ref, block * BLK)

        def finish_chunk(step, inner):
            copy_out(block, step).wait()
            return inner

        return lax.fori_loop(first, DEG // CHUNK, finish_chunk, unused)

    lax.fori_loop(0, blocks, one_block, 0)
    lax.fori_loop(0, blocks, finish_block, 0)


def analyze_kernel(
    dims, total_row, slots_ref, data_ref, column_ref, latitude_ref, within_ref, table_ref,
    out_ref, chunk_ref, weight_ref, stack_ref, result_ref, fold_ref, coeff_ref, sems,
):
    bands, row_count, modes, blocks, tiles = dims
    chunks = DEG // CHUNK

    def copy_in(block, step):
        return pltpu.make_async_copy(
            table_ref.at[block, step], chunk_ref.at[block, step], sems.at[block, step]
        )

    def start_block(block, unused):
        orders, first, last = block_orders(slots_ref, block * BLK)

        def start_chunk(step, inner):
            copy_in(block, step).start()
            return inner

        return lax.fori_loop(first, chunks, start_chunk, unused)

    lax.fori_loop(0, blocks, start_block, 0)
    latitude = column_ref[...]
    north = jnp.where(latitude < HALF, latitude, NLAT - 1 - latitude)
    lane = lax.broadcasted_iota(jnp.int32, (NLAT, LANES), 1)
    for t in range(HALF // LANES):
        one_hot = jnp.where(north == lane + t * LANES, 1.0, 0.0).astype(BF)
        fold_ref[:, t * LANES : (t + 1) * LANES] = one_hot
    south = latitude_ref[...] >= HALF
    for block in range(blocks):
        orders = block_orders(slots_ref, block * BLK)[0][:, :1]
        sign = 1.0 - 2.0 * (orders % 2).astype(F32)
        evens, odds = [], []
        for c in range(CHAN):
            offset = ((c % 2) * FIELDS + c // 2) * row_count
            t, at = offset // LANES, offset % LANES
            rows = slice((t * blocks + block) * BLK, (t * blocks + block + 1) * BLK)
            values = jnp.concatenate(
                [data_ref[d, rows, :][:, at : at + row_count] for d in range(bands)], 1
            )
            flipped = sign * values
            evens.append(jnp.where(south, flipped, values))
            odds.append(jnp.where(south, -flipped, values))
        high, low = split_two(jnp.concatenate(evens + odds, 0))
        stack_ref[block * 4 * ROWS : block * 4 * ROWS + 2 * ROWS, :] = high
        stack_ref[block * 4 * ROWS + 2 * ROWS : (block + 1) * 4 * ROWS, :] = low
    folded = dot(stack_ref[...], fold_ref[...])
    for block in range(blocks):
        at = block * 4 * ROWS
        part = folded[at : at + 2 * ROWS] + folded[at + 2 * ROWS : at + 4 * ROWS]
        part = jnp.concatenate([part, jnp.zeros((LANES - 2 * ROWS, HALF), F32)], 0)
        high, low = split_two(part.T)
        weight_ref[block, :HALF, :LANES] = high
        weight_ref[block, :HALF, LANES:] = low
        weight_ref[block, HALF:, :LANES] = high
        weight_ref[block, HALF:, LANES:] = jnp.zeros_like(low)

    total = data_ref[0, total_row : total_row + 8]
    for d in range(1, bands):
        total = total + data_ref[d, total_row : total_row + 8]
    inverse = (1.0 / total)[:, :1]
    lane = lax.broadcasted_iota(jnp.int32, (CHUNK * BLK, LANES), 1)
    sub = lax.broadcasted_iota(jnp.int32, (CHUNK * BLK, LANES), 0)
    keep = (lane % BLK == sub % BLK) & (lane // ROWS == sub // BLK % 2)

    def one_block(block, unused):
        orders, first, last = block_orders(slots_ref, block * BLK)
        orders = orders[:, :1]
        here = pl.ds(pl.multiple_of(block * BLK, BLK), BLK)
        result_ref[block] = jnp.zeros((DEG, LANES), F32)

        def some_chunks(step, count):
            for k in range(count):
                copy_in(block, step + k).wait()
            values = chunk_ref[block, pl.ds(step, count)].reshape(count * CHUNK * BLK, 2 * HALF)
            full = dot(values, weight_ref[block])
            full = (full[:, :LANES] + full[:, LANES:]).reshape(count, CHUNK * BLK, LANES)
            picked = jnp.where(keep[None], full, 0.0).reshape(count * CHUNK, BLK, LANES)
            to = pl.ds(pl.multiple_of(step * CHUNK, CHUNK), count * CHUNK)
            result_ref[block, to, :] = jnp.sum(picked, axis=1)

        def lone_chunk(unused, inner):
            some_chunks(first, 1)
            return inner

        even = (first + 1) // 2

        def two_chunks(unused, inner):
            some_chunks(2 * even, 2)
            return inner

        def four_chunks(group, inner):
            some_chunks(4 * group, 4)
            return inner

        lax.fori_loop(0, first & 1, lone_chunk, 0)
        lax.fori_loop(0, even & 1, two_chunks, 0)
        lax.fori_loop((even + 1) // 2, chunks // 4, four_chunks, 0)
        return unused

    lax.fori_loop(0, blocks, one_block, 0)
    for block in range(blocks):
        orders = block_orders(slots_ref, block * BLK)[0][:, :1]
        turned = result_ref[block].T
        turned = turned[:ROWS] + turned[ROWS : 2 * ROWS]
        degree = lax.broadcasted_iota(jnp.int32, (BLK, DEG), 1)
        within = jnp.where(degree >= orders, within_ref[block * BLK : (block + 1) * BLK, :], 0.0)
        for c in range(CHAN):
            part = turned[c * BLK : (c + 1) * BLK] * within
            if c // 2 == FIELDS - 1:
                part = part * inverse
            coeff_ref[block, c] = part
        for i in range(BLK):
            target = pl.ds(slots_ref[block * BLK + i] % PLACES, 1)
            out_ref[:, target, :] = coeff_ref[block, :, i : i + 1, :]


def base_trig(order, first):
    lane = lax.broadcasted_iota(jnp.int32, order.shape, 1) + first
    phase = (order * lane) & (NLON - 1)
    quarter = (phase + NLON // 8) >> 9
    rest = (phase - quarter * (NLON // 4)).astype(F32) * (2.0 * math.pi / NLON)
    square = rest * rest
    sine = 1.0 / 362880.0
    for coef in (-1.0 / 5040.0, 1.0 / 120.0, -1.0 / 6.0, 1.0):
        sine = sine * square + coef
    sine = sine * rest
    cosine = 1.0 / 40320.0
    for coef in (-1.0 / 720.0, 1.0 / 24.0, -0.5, 1.0):
        cosine = cosine * square + coef
    swap = (quarter & 1) == 1
    cos_out = jnp.where(swap, sine, cosine)
    sin_out = jnp.where(swap, cosine, sine)
    cos_out = jnp.where(((quarter + 1) & 2) == 2, -cos_out, cos_out)
    sin_out = jnp.where((quarter & 2) == 2, -sin_out, sin_out)
    return cos_out, sin_out


def trig_kernel(out_ref, trig_ref, sem):
    half = trig_ref.shape[3] // 2
    root = math.sqrt(0.5)
    for parity in range(2):

        def strip(step, unused):
            at = pl.multiple_of(step * 64, 64)
            shape = (64, LANES)
            order = 2 * (lax.broadcasted_iota(jnp.int32, shape, 0) + at) + parity
            eighth = order & 7
            odd = (eighth & 1) == 1
            turn_cos = jnp.where(odd, root, jnp.where((eighth & 2) == 0, 1.0, 0.0))
            turn_sin = jnp.where(odd, root, jnp.where((eighth & 2) == 2, 1.0, 0.0))
            turn_cos = jnp.where((eighth >= 3) & (eighth <= 5), -turn_cos, turn_cos)
            turn_sin = jnp.where(eighth > 4, -turn_sin, turn_sin)
            for t in range(KTILE // LANES):
                cosine, sine = base_trig(order, t * LANES)
                for k in range(t * LANES, NLON // 2, KTILE):
                    columns = slice(t * LANES, (t + 1) * LANES)
                    for values, start in ((cosine, at), (sine, half + at)):
                        high, low = split_two(values)
                        trig_ref[k // KTILE, 0, parity, pl.ds(start, 64), columns] = high
                        trig_ref[k // KTILE, 1, parity, pl.ds(start, 64), columns] = low
                    cosine, sine = (
                        cosine * turn_cos - sine * turn_sin,
                        sine * turn_cos + cosine * turn_sin,
                    )
            return unused

        lax.fori_loop(0, half // 64, strip, 0)
    copy = pltpu.make_async_copy(trig_ref, out_ref, sem)
    copy.start()
    copy.wait()


def grid_kernel(
    dims, data_ref, orders_ref, rate_ref, sine_ref, trig_in, out_ref,
    move_ref, lhs_ref, weight_ref, acc_ref, trig_ref, sems,
):
    bands, row_count, modes, tiles, slots = dims
    half = slots // 2
    group = FIELDS * row_count
    padded = weight_ref.shape[1] // 2

    copies = []
    for tile in range(NLON // 2 // KTILE):
        copy = pltpu.make_async_copy(trig_in.at[tile], trig_ref.at[tile], sems.at[tile])
        copy.start()
        copies.append(copy)
    order = orders_ref[...]
    natural = (order & 1) * half + (order >> 1)
    for t in range(slots // LANES):
        lane = lax.broadcasted_iota(jnp.int32, (slots, LANES), 1) + t * LANES
        one_hot = jnp.where(natural == lane, 1.0, 0.0).astype(BF)
        move_ref[:, t * LANES : (t + 1) * LANES] = one_hot
    columns = []
    for t in range(tiles):
        part = data_ref[:, t * modes : (t + 1) * modes, :]
        columns.append(part.reshape(slots, LANES).T)
    turned = jnp.concatenate(columns, 0)
    for kind in range(2):
        high, low = split_two(turned[kind * group : (kind + 1) * group])
        moved = dot(jnp.concatenate([high, low], 0), move_ref[...]).astype(BF)
        for parity in range(2):
            part = moved[:, parity * half : (parity + 1) * half]
            lhs_ref[parity, :, kind * half : (kind + 1) * half] = part
    weight_ref[...] = jnp.zeros_like(weight_ref)
    flux_scale = math.pi / (2.0 * NLAT * NLON * DEG)
    weight = jnp.tile(sine_ref[...], (1, KTILE // LANES))
    total = jnp.zeros((8, KTILE), F32)

    for k in range(0, NLON // 2, KTILE):
        copies[k // KTILE].wait()
        trig_high, trig_low = trig_ref.at[k // KTILE, 0], trig_ref.at[k // KTILE, 1]
        sums = []
        for parity in range(2):
            first = dot(lhs_ref[parity], trig_high[parity])
            second = dot(lhs_ref[parity, :group, :], trig_low[parity])
            sums.append(first[:group] + first[group:] + second)
        values = []
        for fields, at in ((sums[0] + sums[1], k), (sums[0] - sums[1], k + NLON // 2)):
            weighted_rate = rate_ref[:, at : at + KTILE] * weight
            total = total + jnp.sum(weighted_rate.reshape(row_count // 8, 8, KTILE), axis=0)
            scaled = fields[:row_count] * (weight * flux_scale)
            values.append(
                jnp.concatenate(
                    [
                        fields[row_count : 2 * row_count] * scaled,
                        fields[2 * row_count :] * scaled,
                        weighted_rate * fields[:row_count],
                    ],
                    0,
                )
            )
        for parity in range(2):
            both = values[0] + values[1] if parity == 0 else values[0] - values[1]
            high, low = split_two(both)
            columns = slice(k, k + KTILE)
            weight_ref[parity, :group, columns] = high
            weight_ref[parity, padded : padded + group, columns] = low
    for parity in range(2):
        trig_high, trig_low = [
            jnp.concatenate([trig_ref[t, part, parity] for t in range(len(copies))], 1)
            for part in range(2)
        ]
        first = dot(trig_high, weight_ref[parity], 1)
        second = dot(trig_low, weight_ref[parity, :padded, :], 1)
        acc_ref[parity] = first[:, :padded] + first[:, padded:] + second

    joined = []
    for kind in range(2):
        rows = slice(kind * half, (kind + 1) * half)
        joined.append(jnp.concatenate([acc_ref[0, rows, :group], acc_ref[1, rows, :group]], 0))
    if 2 * group < tiles * LANES:
        joined.append(jnp.zeros((slots, tiles * LANES - 2 * group), F32))
    high, low = split_two(jnp.concatenate(joined, 1))
    moved = dot(move_ref[...], jnp.concatenate([high, low], 1))
    moved = moved[:, : tiles * LANES] + moved[:, tiles * LANES :]
    for t in range(tiles):
        part = moved[:, t * LANES : (t + 1) * LANES]
        out_ref[:, t * modes : (t + 1) * modes, :] = part.reshape(bands, modes, LANES)
    out_ref[:, tiles * modes :, :] = jnp.broadcast_to(jnp.sum(total), (bands, 8, LANES))


VMEM = pl.BlockSpec(memory_space=pltpu.VMEM)
SMEM = pl.BlockSpec(memory_space=pltpu.SMEM)
HBM = pl.BlockSpec(memory_space=pltpu.HBM)


def work(microseconds):
    return pl.CostEstimate(
        flops=microseconds * 10**9, bytes_accessed=2**20, transcendentals=0
    )


def per_device(spectrum, capture_rate, row_latitude, slot_wavenumber):
    bands = lax.axis_size("band")
    modes = spectrum.shape[3]
    row_count = capture_rate.shape[1]
    slots = slot_wavenumber.shape[0]
    blocks = modes // BLK
    chunks = DEG // CHUNK
    tiles = -(-CHAN * row_count // LANES)
    band_index = lax.axis_index("band")

    def sort_rows(table):
        rank = jnp.sum((table[:, None, :] < table[:, :, None]).astype(jnp.int32), 2)
        match = rank[:, None, :] == jnp.arange(modes, dtype=jnp.int32)[None, :, None]
        keys = table * PLACES + jnp.arange(modes, dtype=jnp.int32)[None, :]
        return jnp.sum(jnp.where(match, keys[:, None, :], 0), 2).reshape(-1)

    own = lax.dynamic_slice_in_dim(slot_wavenumber, band_index * modes, modes)
    local = sort_rows(own.reshape(1, modes))
    ordered = sort_rows(slot_wavenumber.reshape(bands, modes)) // PLACES
    rows = jnp.asarray(latitude_rows())
    spread = jnp.asarray(spread_matrix())
    latitude = row_latitude.reshape(1, NLAT)
    coeffs = spectrum.reshape(CHAN, modes, DEG)
    params = pltpu.CompilerParams(vmem_limit_bytes=48 * 2**20)
    chunk_rows = tiles * modes
    dims = (bands, row_count, modes, blocks, tiles)
    scalars = jnp.asarray(degree_scalars())
    per_order = pltpu.VMEM((modes, DEG), F32)

    def exchange(value):
        return lax.all_to_all(value, "band", split_axis=0, concat_axis=0, tiled=True)

    sent = pl.pallas_call(
        lambda *refs: synth_kernel(dims, *refs),
        out_shape=jax.ShapeDtypeStruct((bands, chunk_rows, LANES), F32),
        in_specs=[SMEM] + [HBM] * 5,
        out_specs=VMEM,
        scratch_shapes=[
            pltpu.SMEM(scalars.shape, F32),
            pltpu.VMEM(coeffs.shape, F32),
            pltpu.VMEM(rows.shape, F32),
            pltpu.VMEM(spread.shape, BF),
            pltpu.VMEM(latitude.shape, jnp.int32),
            pltpu.SemaphoreType.DMA((5,)),
        ]
        + [per_order] * 3
        + [pltpu.VMEM((chunks, 2 * ROWS, CHUNK * BLK), BF)]
        + [pltpu.VMEM((2, CHUNK // 2 * BLK, HALF), BF)] * 4
        + [
            pltpu.VMEM((blocks, 2, ROWS, HALF), F32),
            pltpu.VMEM((HALF, NLAT), BF),
            pltpu.VMEM((CHAN, BLK, DEG), F32),
        ],
        compiler_params=pltpu.CompilerParams(vmem_limit_bytes=62 * 2**20),
        cost_estimate=work(15),
        name="synth",
    )(local, scalars, coeffs, rows, spread, latitude)
    received = exchange(sent)

    trig_tiles = NLON // 2 // KTILE
    trig_shape = (trig_tiles, 2, 2, slots, KTILE)
    trig_scratch = pltpu.VMEM(trig_shape, BF)
    trig = pl.pallas_call(
        trig_kernel,
        out_shape=jax.ShapeDtypeStruct(trig_shape, BF),
        out_specs=HBM,
        scratch_shapes=[trig_scratch, pltpu.SemaphoreType.DMA(())],
        compiler_params=params,
        cost_estimate=work(4),
        name="trig",
    )()

    my_latitudes = lax.dynamic_slice_in_dim(row_latitude, band_index * row_count, row_count)
    row_sine = jnp.sin(jnp.pi * (my_latitudes.astype(F32) + 0.5) / NLAT)
    row_sine = jnp.broadcast_to(row_sine[:, None], (row_count, LANES))
    orders = jnp.broadcast_to(ordered.reshape(slots, 1), (slots, LANES))
    group = FIELDS * row_count
    padded = -(-group // LANES) * LANES
    grid_dims = (bands, row_count, modes, tiles, slots)
    fluxes = pl.pallas_call(
        lambda *refs: grid_kernel(grid_dims, *refs),
        out_shape=jax.ShapeDtypeStruct((bands, chunk_rows + 8, LANES), F32),
        in_specs=[VMEM] * 4 + [HBM],
        out_specs=VMEM,
        scratch_shapes=[
            pltpu.VMEM((slots, slots), BF),
            pltpu.VMEM((2, 2 * group, slots), BF),
            pltpu.VMEM((2, 2 * padded, NLON // 2), BF),
            pltpu.VMEM((2, slots, padded), F32),
            trig_scratch,
            pltpu.SemaphoreType.DMA((trig_tiles,)),
        ],
        compiler_params=params,
        cost_estimate=work(8),
        name="grid",
    )(received, orders, capture_rate.reshape(row_count, NLON), row_sine, trig)
    returned = exchange(fluxes)

    chunk_shape = (blocks, chunks, CHUNK * BLK, 2 * HALF)
    legendre, within = pl.pallas_call(
        lambda *refs: table_kernel(blocks, *refs),
        out_shape=[
            jax.ShapeDtypeStruct(chunk_shape, BF),
            jax.ShapeDtypeStruct((modes, DEG), F32),
        ],
        in_specs=[SMEM, SMEM, VMEM],
        out_specs=[HBM, VMEM],
        scratch_shapes=[per_order] * 2
        + [pltpu.VMEM(chunk_shape, BF), pltpu.SemaphoreType.DMA((blocks, chunks))],
        compiler_params=params,
        cost_estimate=work(12),
        name="table",
    )(local, scalars, rows)
    column = jnp.broadcast_to(row_latitude[:, None], (NLAT, LANES))
    result = pl.pallas_call(
        lambda *refs: analyze_kernel(dims, chunk_rows, *refs),
        out_shape=jax.ShapeDtypeStruct((CHAN, modes, DEG), F32),
        in_specs=[SMEM, VMEM, VMEM, VMEM, VMEM, HBM],
        out_specs=VMEM,
        scratch_shapes=[
            pltpu.VMEM(chunk_shape, BF),
            pltpu.VMEM((blocks, 2 * HALF, 2 * LANES), BF),
            pltpu.VMEM((blocks * 4 * ROWS, NLAT), BF),
            pltpu.VMEM((blocks, DEG, LANES), F32),
            pltpu.VMEM((NLAT, HALF), BF),
            pltpu.VMEM((blocks, CHAN, BLK, DEG), F32),
            pltpu.SemaphoreType.DMA((blocks, chunks)),
        ],
        compiler_params=params,
        cost_estimate=work(9),
        name="analyze",
    )(local, returned, column, latitude, within, legendre)
    return result.reshape(1, FIELDS, 2, modes, DEG)


def solution(mesh):
    return jax.shard_map(
        per_device,
        mesh=mesh,
        in_specs=(P("shell", None, None, "band", None), P("shell", "band", None), P(), P()),
        out_specs=P("shell", None, None, "band", None),
        check_vma=False,
    )
```

```python
import functools
import math

import jax
import jax.numpy as jnp
import numpy as np
from jax import lax
from jax.experimental import pallas as pl
from jax.experimental.pallas import tpu as pltpu
from jax.sharding import PartitionSpec as P

DEG = 512
NLAT = 1024
NLON = 2048
FIELDS = 3
HALF = NLAT // 2
CHAN = 2 * FIELDS
BLK = 8
ROWS = CHAN * BLK
CHUNK = 64
CHECK = 16
PLACES = 1024
LANES = 128
KTILE = 256
BF = jnp.bfloat16
F32 = jnp.float32


def split_two(value):
    high = value.astype(BF)
    low = (value - high.astype(F32)).astype(BF)
    return high, low


def dot(lhs, rhs, contract_rhs=0):
    return lax.dot_general(
        lhs, rhs, (((1,), (contract_rhs,)), ((), ())), preferred_element_type=F32
    )


def latitude_rows():
    theta = np.pi * (np.arange(HALF) + 0.5) / NLAT
    index = np.arange(DEG, dtype=np.float64)
    log_terms = np.zeros(DEG)
    log_terms[1:] = 0.5 * np.log2((2.0 * index[1:] + 1.0) / (2.0 * index[1:]))
    rows = np.zeros((8, DEG))
    rows[0], rows[1], rows[2] = np.cos(theta), np.log2(np.sin(theta)), log_terms
    return rows.astype(np.float32)


def spread_matrix():
    spread = np.zeros((LANES, 2, 2, CHUNK // 2, BLK), np.float32)
    for half in range(2):
        for parity in range(2):
            for step in range(CHUNK // 2):
                spread[half * CHUNK + 2 * step + parity, half, parity, step, :] = 1.0
    return spread.reshape(LANES, 2 * 2 * (CHUNK // 2) * BLK).astype(BF)


def degree_scalars():
    before = np.arange(DEG, dtype=np.float64) - 1.0
    square = before * before
    return np.concatenate([square, 4.0 / (4.0 * square - 1.0)]).astype(np.float32)


def block_orders(slots_ref, first):
    sublane = lax.broadcasted_iota(jnp.int32, (BLK, LANES), 0)
    orders = jnp.zeros((BLK, LANES), jnp.int32)
    lowest, highest = jnp.int32(DEG), jnp.int32(0)
    for i in range(BLK):
        order = slots_ref[first + i] // PLACES
        orders = jnp.where(sublane == i, order, orders)
        lowest, highest = jnp.minimum(lowest, order), jnp.maximum(highest, order)
    return orders, lowest // CHUNK, highest // CHUNK + 1


def running_sum(terms, length):
    lane = lax.broadcasted_iota(jnp.int32, terms.shape, 1) & (length - 1)
    shift = 1
    while shift < length:
        moved = pltpu.roll(terms, shift, 1)
        terms = terms + jnp.where(lane >= shift, moved, 0.0)
        shift *= 2
    return terms


def recursion_tables(slots_ref, modes, rows_ref, start_ref, before_ref, within_ref):
    orders = [block_orders(slots_ref, at)[0][:, :1] for at in range(0, modes, BLK)]
    order = jnp.concatenate(orders, 0).astype(F32)
    position = lax.broadcasted_iota(jnp.int32, (modes, DEG), 1)
    degree = position.astype(F32)
    square = degree * degree
    above = degree > order
    gap = jnp.where(above, square - order * order, 1.0)
    growth = jnp.where(above, 0.5 * jnp.log2((square - 0.25) / gap), 0.0)
    before_ref[...] = running_sum(growth, DEG)
    later = jnp.where(position & (CHECK - 1) == 0, 0.0, growth)
    within_ref[...] = jnp.exp2(running_sum(later, CHECK))
    terms = jnp.where(degree <= order, rows_ref[2:3, :], 0.0)
    norm = jnp.where(order > 0, 0.5 + jnp.sum(terms, axis=1, keepdims=True), 0.0)
    start_ref[...] = norm + order * rows_ref[1:2, :]


def run_chunk(step, carry, double_cosine, orders, before, scalars_ref, emit, beside, guard):
    current, previous, log_scale = carry
    order = orders.astype(F32)
    order_square = order * order
    before = pltpu.roll(before, (step % 2) * CHUNK, 1)
    scale = None
    for i in range(CHUNK):
        if i % CHECK == 0:
            size = jnp.maximum(jnp.abs(current), jnp.abs(previous))
            large, small = size > 2.0**40, size < 2.0**-40
            factor = jnp.where(large, 2.0**-60, jnp.where(small, 2.0**60, 1.0))
            change = jnp.where(large, 60.0, jnp.where(small, -60.0, 0.0))
            current = current * factor
            previous = previous * factor
            log_scale = log_scale + change
            scale = jnp.exp2(jnp.maximum(log_scale + before[:, i : i + 1], -200.0))
        degree = step * CHUNK + i
        factor = (scalars_ref[degree] - order_square) * scalars_ref[DEG + degree]
        factor = jnp.tile(factor, (1, HALF // LANES))
        newest = double_cosine * current - factor * previous
        if guard:
            started = jnp.tile(orders, (1, HALF // LANES)) < degree
            newest = jnp.where(started, newest, 1.0)
        current, previous = newest, current
        emit(i, newest * scale)
        if beside and i % (CHUNK // len(beside)) == 1:
            beside[i // (CHUNK // len(beside))]()
    return current, previous, log_scale


def before_tile(before_ref, block, step):
    rows = pl.ds(pl.multiple_of(block * BLK, BLK), BLK)
    return before_ref[rows, pl.ds(pl.multiple_of(step // 2 * LANES, LANES), LANES)]


def start_state(start_ref, block):
    ones = jnp.ones((BLK, HALF), F32)
    return ones, ones, start_ref[pl.ds(pl.multiple_of(block * BLK, BLK), BLK), :]


def fold_matrix(latitude_ref, fold_ref):
    latitude = latitude_ref[...]
    north = jnp.where(latitude < HALF, latitude, NLAT - 1 - latitude)
    sublane = lax.broadcasted_iota(jnp.int32, (HALF, NLAT), 0)
    fold_ref[...] = jnp.where(sublane == north, 1.0, 0.0).astype(BF)


def synth_kernel(
    dims, slots_ref, scalars_in, spec_in, rows_in, spread_in, latitude_in,
    out_ref, scalars_ref, spec_ref, rows_ref, spread_ref, latitude_ref, sems,
    start_ref, before_ref, within_ref, lhs_ref, high_a, low_a, high_b, low_b, acc_ref, fold_ref, coeff_ref,
):
    bands, row_count, modes, blocks, tiles = dims
    pairs = (
        (rows_in, rows_ref), (scalars_in, scalars_ref), (latitude_in, latitude_ref),
        (spread_in, spread_ref), (spec_in, spec_ref),
    )
    copies = []
    for index, (source, target) in enumerate(pairs):
        copies.append(pltpu.make_async_copy(source, target, sems.at[index]))
        copies[-1].start()
    copies[0].wait()
    recursion_tables(slots_ref, modes, rows_ref, start_ref, before_ref, within_ref)
    for copy in copies[1:]:
        copy.wait()
    fold_matrix(latitude_ref, fold_ref)
    south = latitude_ref[...] >= HALF
    spread_width = 4 * (CHUNK // 2) * BLK
    lane = lax.broadcasted_iota(jnp.int32, (2 * ROWS, spread_width), 1)
    sub = lax.broadcasted_iota(jnp.int32, (2 * ROWS, spread_width), 0)
    diagonal = (lane % BLK) == (sub % BLK)
    width = (CHUNK // 2) * BLK

    chunks = DEG // CHUNK
    high_b[...] = jnp.zeros_like(high_b)
    low_b[...] = jnp.zeros_like(low_b)
    lhs_ref[chunks] = jnp.zeros((2 * ROWS, CHUNK * BLK), BF)

    def one_block(block, unused):
        orders, first, last = block_orders(slots_ref, block * BLK)
        column = orders[:, :1]
        here = pl.ds(pl.multiple_of(block * BLK, BLK), BLK)
        for i in range(BLK):
            source = pl.ds(slots_ref[block * BLK + i] % PLACES, 1)
            coeff_ref[:, i : i + 1, :] = spec_ref[:, source, :]
        degree = lax.broadcasted_iota(jnp.int32, (BLK, DEG), 1)
        within = jnp.where(degree >= column, within_ref[here, :], 0.0)
        coeffs = coeff_ref[...] * within[None]
        coeff_high, coeff_low = split_two(coeffs.reshape(ROWS, DEG))
        stacked = jnp.concatenate([coeff_high, coeff_low], 0)
        for t in range(DEG // LANES):
            wide = dot(stacked[:, t * LANES : (t + 1) * LANES], spread_ref[...])
            wide = jnp.where(diagonal, wide, 0.0).astype(BF)
            for half in range(2):
                lhs_ref[2 * t + half] = wide[:, half * 2 * width : (half + 1) * 2 * width]
        acc_ref[block] = jnp.zeros((2, ROWS, HALF), F32)
        cosine = jnp.broadcast_to(2.0 * rows_ref[0:1, :], (BLK, HALF))

        def recur(step, carry, high_ref, low_ref, beside, guard):
            held = {}

            def emit(i, value):
                if i % 4 < 2:
                    held[i] = value
                else:
                    pair = jnp.concatenate([held.pop(i - 2), value], 0)
                    high, low = split_two(pair)
                    at = (i // 4) * 2 * BLK
                    high_ref[i % 2, at : at + 2 * BLK, :] = high
                    low_ref[i % 2, at : at + 2 * BLK, :] = low

            before = before_tile(before_ref, block, step)
            return run_chunk(
                step, carry, cosine, orders, before, scalars_ref, emit, beside, guard
            )

        def add_products(step, high_ref, low_ref):
            def part(parity, columns):
                lhs = lhs_ref[step, :, parity * width : (parity + 1) * width]
                first = dot(lhs, high_ref[parity, :, columns])
                second = dot(lhs[:ROWS], low_ref[parity, :, columns])
                acc_ref[block, parity, :, columns] += first[:ROWS] + first[ROWS:] + second

            return [
                functools.partial(part, parity, slice(at, at + 2 * KTILE))
                for parity in range(2)
                for at in range(0, HALF, 2 * KTILE)
            ]

        def two_chunks(guard, pair, carry):
            step = 2 * pair
            beside = add_products(jnp.where(step == 0, chunks, step - 1), high_b, low_b)
            carry = recur(step, carry, high_a, low_a, beside, guard)
            beside = add_products(step, high_a, low_a)
            return recur(step + 1, carry, high_b, low_b, beside, guard)

        state = lax.fori_loop(
            0,
            first & 1,
            lambda unused, carry: recur(first, carry, high_b, low_b, (), True),
            start_state(start_ref, block),
        )
        middle = (last + 1) // 2
        state = lax.fori_loop(
            (first + 1) // 2, middle, functools.partial(two_chunks, True), state
        )
        lax.fori_loop(middle, chunks // 2, functools.partial(two_chunks, False), state)
        for part in add_products(chunks - 1, high_b, low_b):
            part()
        return unused

    lax.fori_loop(0, blocks, one_block, 0)
    high, low = split_two(acc_ref[...].reshape(blocks * 2 * ROWS, HALF))
    moved = dot(jnp.concatenate([high, low], 0), fold_ref[...])
    moved = moved[: blocks * 2 * ROWS] + moved[blocks * 2 * ROWS :]
    for block in range(blocks):
        orders = block_orders(slots_ref, block * BLK)[0][:, :1]
        sign = jnp.tile(1.0 - 2.0 * (orders % 2).astype(F32), (CHAN, 1))
        even = moved[block * 2 * ROWS : block * 2 * ROWS + ROWS]
        odd = moved[block * 2 * ROWS + ROWS : (block + 1) * 2 * ROWS]
        values = jnp.where(south, sign * (even - odd), even + odd)
        for d in range(bands):
            parts = []
            for kind in range(2):
                for field in range(FIELDS):
                    c = field * 2 + kind
                    parts.append(
                        values[c * BLK : (c + 1) * BLK, d * row_count : (d + 1) * row_count]
                    )
            if CHAN * row_count < tiles * LANES:
                parts.append(jnp.zeros((BLK, tiles * LANES - CHAN * row_count), F32))
            joined = jnp.concatenate(parts, 1)
            for t in range(tiles):
                at = slice((t * blocks + block) * BLK, (t * blocks + block + 1) * BLK)
                out_ref[d, at, :] = joined[:, t * LANES : (t + 1) * LANES]


def table_kernel(
    blocks, slots_ref, scalars_ref, rows_ref, out_ref, within_out, start_ref, before_ref,
    chunk_ref, sems,
):
    modes = blocks * BLK
    cosine = jnp.broadcast_to(2.0 * rows_ref[0:1, :], (BLK, HALF))
    recursion_tables(slots_ref, modes, rows_ref, start_ref, before_ref, within_out)

    def copy_out(block, step):
        return pltpu.make_async_copy(
            chunk_ref.at[block, step], out_ref.at[block, step], sems.at[block, step]
        )

    def one_block(block, unused):
        orders, first, last = block_orders(slots_ref, block * BLK)

        def one_chunk(guard, step, carry):
            held = {}

            def emit(i, value):
                if i % 2 == 0:
                    held[i] = value
                else:
                    pair = jnp.concatenate([held.pop(i - 1), value], 0)
                    high, low = split_two(pair)
                    at = (i // 2) * 2 * BLK
                    chunk_ref[block, step, at : at + 2 * BLK, :HALF] = high
                    chunk_ref[block, step, at : at + 2 * BLK, HALF:] = low

            before = before_tile(before_ref, block, step)
            carry = run_chunk(
                step, carry, cosine, orders, before, scalars_ref, emit, (), guard
            )
            copy_out(block, step).start()
            return carry

        state = start_state(start_ref, block)
        state = lax.fori_loop(first, last, functools.partial(one_chunk, True), state)
        lax.fori_loop(last, DEG // CHUNK, functools.partial(one_chunk, False), state)
        return unused

    def finish_block(block, unused):
        orders, first, last = block_orders(slots_ref, block * BLK)

        def finish_chunk(step, inner):
            copy_out(block, step).wait()
            return inner

        return lax.fori_loop(first, DEG // CHUNK, finish_chunk, unused)

    lax.fori_loop(0, blocks, one_block, 0)
    lax.fori_loop(0, blocks, finish_block, 0)


def analyze_kernel(
    dims, total_row, slots_ref, data_ref, column_ref, latitude_ref, within_ref, table_ref,
    out_ref, chunk_ref, weight_ref, stack_ref, result_ref, fold_ref, coeff_ref, sems,
):
    bands, row_count, modes, blocks, tiles = dims
    chunks = DEG // CHUNK

    def copy_in(block, step):
        return pltpu.make_async_copy(
            table_ref.at[block, step], chunk_ref.at[block, step], sems.at[block, step]
        )

    def start_block(block, unused):
        orders, first, last = block_orders(slots_ref, block * BLK)

        def start_chunk(step, inner):
            copy_in(block, step).start()
            return inner

        return lax.fori_loop(first, chunks, start_chunk, unused)

    lax.fori_loop(0, blocks, start_block, 0)
    latitude = column_ref[...]
    north = jnp.where(latitude < HALF, latitude, NLAT - 1 - latitude)
    lane = lax.broadcasted_iota(jnp.int32, (NLAT, LANES), 1)
    for t in range(HALF // LANES):
        one_hot = jnp.where(north == lane + t * LANES, 1.0, 0.0).astype(BF)
        fold_ref[:, t * LANES : (t + 1) * LANES] = one_hot
    south = latitude_ref[...] >= HALF
    for block in range(blocks):
        orders = block_orders(slots_ref, block * BLK)[0][:, :1]
        sign = 1.0 - 2.0 * (orders % 2).astype(F32)
        evens, odds = [], []
        for c in range(CHAN):
            offset = ((c % 2) * FIELDS + c // 2) * row_count
            t, at = offset // LANES, offset % LANES
            rows = slice((t * blocks + block) * BLK, (t * blocks + block + 1) * BLK)
            values = jnp.concatenate(
                [data_ref[d, rows, :][:, at : at + row_count] for d in range(bands)], 1
            )
            flipped = sign * values
            evens.append(jnp.where(south, flipped, values))
            odds.append(jnp.where(south, -flipped, values))
        high, low = split_two(jnp.concatenate(evens + odds, 0))
        stack_ref[block * 4 * ROWS : block * 4 * ROWS + 2 * ROWS, :] = high
        stack_ref[block * 4 * ROWS + 2 * ROWS : (block + 1) * 4 * ROWS, :] = low
    folded = dot(stack_ref[...], fold_ref[...])
    for block in range(blocks):
        at = block * 4 * ROWS
        part = folded[at : at + 2 * ROWS] + folded[at + 2 * ROWS : at + 4 * ROWS]
        part = jnp.concatenate([part, jnp.zeros((LANES - 2 * ROWS, HALF), F32)], 0)
        high, low = split_two(part.T)
        weight_ref[block, :HALF, :LANES] = high
        weight_ref[block, :HALF, LANES:] = low
        weight_ref[block, HALF:, :LANES] = high
        weight_ref[block, HALF:, LANES:] = jnp.zeros_like(low)

    total = data_ref[0, total_row : total_row + 8]
    for d in range(1, bands):
        total = total + data_ref[d, total_row : total_row + 8]
    inverse = (1.0 / total)[:, :1]
    lane = lax.broadcasted_iota(jnp.int32, (CHUNK * BLK, LANES), 1)
    sub = lax.broadcasted_iota(jnp.int32, (CHUNK * BLK, LANES), 0)
    keep = (lane % BLK == sub % BLK) & (lane // ROWS == sub // BLK % 2)

    def one_block(block, unused):
        orders, first, last = block_orders(slots_ref, block * BLK)
        orders = orders[:, :1]
        here = pl.ds(pl.multiple_of(block * BLK, BLK), BLK)
        result_ref[block] = jnp.zeros((DEG, LANES), F32)

        def some_chunks(step, count):
            for k in range(count):
                copy_in(block, step + k).wait()
            values = chunk_ref[block, pl.ds(step, count)].reshape(count * CHUNK * BLK, 2 * HALF)
            full = dot(values, weight_ref[block])
            full = (full[:, :LANES] + full[:, LANES:]).reshape(count, CHUNK * BLK, LANES)
            picked = jnp.where(keep[None], full, 0.0).reshape(count * CHUNK, BLK, LANES)
            to = pl.ds(pl.multiple_of(step * CHUNK, CHUNK), count * CHUNK)
            result_ref[block, to, :] = jnp.sum(picked, axis=1)

        def lone_chunk(unused, inner):
            some_chunks(first, 1)
            return inner

        even = (first + 1) // 2

        def two_chunks(unused, inner):
            some_chunks(2 * even, 2)
            return inner

        def four_chunks(group, inner):
            some_chunks(4 * group, 4)
            return inner

        lax.fori_loop(0, first & 1, lone_chunk, 0)
        lax.fori_loop(0, even & 1, two_chunks, 0)
        lax.fori_loop((even + 1) // 2, chunks // 4, four_chunks, 0)
        return unused

    lax.fori_loop(0, blocks, one_block, 0)
    for block in range(blocks):
        orders = block_orders(slots_ref, block * BLK)[0][:, :1]
        turned = result_ref[block].T
        turned = turned[:ROWS] + turned[ROWS : 2 * ROWS]
        degree = lax.broadcasted_iota(jnp.int32, (BLK, DEG), 1)
        within = jnp.where(degree >= orders, within_ref[block * BLK : (block + 1) * BLK, :], 0.0)
        for c in range(CHAN):
            part = turned[c * BLK : (c + 1) * BLK] * within
            if c // 2 == FIELDS - 1:
                part = part * inverse
            coeff_ref[block, c] = part
        for i in range(BLK):
            target = pl.ds(slots_ref[block * BLK + i] % PLACES, 1)
            out_ref[:, target, :] = coeff_ref[block, :, i : i + 1, :]


def base_trig(order, first):
    lane = lax.broadcasted_iota(jnp.int32, order.shape, 1) + first
    phase = (order * lane) & (NLON - 1)
    quarter = (phase + NLON // 8) >> 9
    rest = (phase - quarter * (NLON // 4)).astype(F32) * (2.0 * math.pi / NLON)
    square = rest * rest
    sine = 1.0 / 362880.0
    for coef in (-1.0 / 5040.0, 1.0 / 120.0, -1.0 / 6.0, 1.0):
        sine = sine * square + coef
    sine = sine * rest
    cosine = 1.0 / 40320.0
    for coef in (-1.0 / 720.0, 1.0 / 24.0, -0.5, 1.0):
        cosine = cosine * square + coef
    swap = (quarter & 1) == 1
    cos_out = jnp.where(swap, sine, cosine)
    sin_out = jnp.where(swap, cosine, sine)
    cos_out = jnp.where(((quarter + 1) & 2) == 2, -cos_out, cos_out)
    sin_out = jnp.where((quarter & 2) == 2, -sin_out, sin_out)
    return cos_out, sin_out


def trig_kernel(out_ref, trig_ref, sem):
    half = trig_ref.shape[3] // 2
    root = math.sqrt(0.5)
    for parity in range(2):

        def strip(step, unused):
            at = pl.multiple_of(step * 64, 64)
            shape = (64, LANES)
            order = 2 * (lax.broadcasted_iota(jnp.int32, shape, 0) + at) + parity
            eighth = order & 7
            odd = (eighth & 1) == 1
            turn_cos = jnp.where(odd, root, jnp.where((eighth & 2) == 0, 1.0, 0.0))
            turn_sin = jnp.where(odd, root, jnp.where((eighth & 2) == 2, 1.0, 0.0))
            turn_cos = jnp.where((eighth >= 3) & (eighth <= 5), -turn_cos, turn_cos)
            turn_sin = jnp.where(eighth > 4, -turn_sin, turn_sin)
            for t in range(KTILE // LANES):
                cosine, sine = base_trig(order, t * LANES)
                for k in range(t * LANES, NLON // 2, KTILE):
                    columns = slice(t * LANES, (t + 1) * LANES)
                    for values, start in ((cosine, at), (sine, half + at)):
                        high, low = split_two(values)
                        trig_ref[k // KTILE, 0, parity, pl.ds(start, 64), columns] = high
                        trig_ref[k // KTILE, 1, parity, pl.ds(start, 64), columns] = low
                    cosine, sine = (
                        cosine * turn_cos - sine * turn_sin,
                        sine * turn_cos + cosine * turn_sin,
                    )
            return unused

        lax.fori_loop(0, half // 64, strip, 0)
    copy = pltpu.make_async_copy(trig_ref, out_ref, sem)
    copy.start()
    copy.wait()


def grid_kernel(
    dims, data_ref, orders_ref, rate_ref, sine_ref, trig_in, out_ref,
    move_ref, lhs_ref, weight_ref, acc_ref, trig_ref, sems,
):
    bands, row_count, modes, tiles, slots = dims
    half = slots // 2
    group = FIELDS * row_count
    padded = weight_ref.shape[1] // 2

    copies = []
    for tile in range(NLON // 2 // KTILE):
        copy = pltpu.make_async_copy(trig_in.at[tile], trig_ref.at[tile], sems.at[tile])
        copy.start()
        copies.append(copy)
    order = orders_ref[...]
    natural = (order & 1) * half + (order >> 1)
    for t in range(slots // LANES):
        lane = lax.broadcasted_iota(jnp.int32, (slots, LANES), 1) + t * LANES
        one_hot = jnp.where(natural == lane, 1.0, 0.0).astype(BF)
        move_ref[:, t * LANES : (t + 1) * LANES] = one_hot
    columns = []
    for t in range(tiles):
        part = data_ref[:, t * modes : (t + 1) * modes, :]
        columns.append(part.reshape(slots, LANES).T)
    turned = jnp.concatenate(columns, 0)
    for kind in range(2):
        high, low = split_two(turned[kind * group : (kind + 1) * group])
        moved = dot(jnp.concatenate([high, low], 0), move_ref[...]).astype(BF)
        for parity in range(2):
            part = moved[:, parity * half : (parity + 1) * half]
            lhs_ref[parity, :, kind * half : (kind + 1) * half] = part
    weight_ref[...] = jnp.zeros_like(weight_ref)
    flux_scale = math.pi / (2.0 * NLAT * NLON * DEG)
    weight = jnp.tile(sine_ref[...], (1, KTILE // LANES))
    total = jnp.zeros((8, KTILE), F32)

    for k in range(0, NLON // 2, KTILE):
        copies[k // KTILE].wait()
        trig_high, trig_low = trig_ref.at[k // KTILE, 0], trig_ref.at[k // KTILE, 1]
        sums = []
        for parity in range(2):
            first = dot(lhs_ref[parity], trig_high[parity])
            second = dot(lhs_ref[parity, :group, :], trig_low[parity])
            sums.append(first[:group] + first[group:] + second)
        values = []
        for fields, at in ((sums[0] + sums[1], k), (sums[0] - sums[1], k + NLON // 2)):
            weighted_rate = rate_ref[:, at : at + KTILE] * weight
            total = total + jnp.sum(weighted_rate.reshape(row_count // 8, 8, KTILE), axis=0)
            scaled = fields[:row_count] * (weight * flux_scale)
            values.append(
                jnp.concatenate(
                    [
                        fields[row_count : 2 * row_count] * scaled,
                        fields[2 * row_count :] * scaled,
                        weighted_rate * fields[:row_count],
                    ],
                    0,
                )
            )
        for parity in range(2):
            both = values[0] + values[1] if parity == 0 else values[0] - values[1]
            high, low = split_two(both)
            columns = slice(k, k + KTILE)
            weight_ref[parity, :group, columns] = high
            weight_ref[parity, padded : padded + group, columns] = low
    for parity in range(2):
        trig_high, trig_low = [
            jnp.concatenate([trig_ref[t, part, parity] for t in range(len(copies))], 1)
            for part in range(2)
        ]
        first = dot(trig_high, weight_ref[parity], 1)
        second = dot(trig_low, weight_ref[parity, :padded, :], 1)
        acc_ref[parity] = first[:, :padded] + first[:, padded:] + second

    joined = []
    for kind in range(2):
        rows = slice(kind * half, (kind + 1) * half)
        joined.append(jnp.concatenate([acc_ref[0, rows, :group], acc_ref[1, rows, :group]], 0))
    if 2 * group < tiles * LANES:
        joined.append(jnp.zeros((slots, tiles * LANES - 2 * group), F32))
    high, low = split_two(jnp.concatenate(joined, 1))
    moved = dot(move_ref[...], jnp.concatenate([high, low], 1))
    moved = moved[:, : tiles * LANES] + moved[:, tiles * LANES :]
    for t in range(tiles):
        part = moved[:, t * LANES : (t + 1) * LANES]
        out_ref[:, t * modes : (t + 1) * modes, :] = part.reshape(bands, modes, LANES)
    out_ref[:, tiles * modes :, :] = jnp.broadcast_to(jnp.sum(total), (bands, 8, LANES))


VMEM = pl.BlockSpec(memory_space=pltpu.VMEM)
SMEM = pl.BlockSpec(memory_space=pltpu.SMEM)
HBM = pl.BlockSpec(memory_space=pltpu.HBM)


def work(microseconds):
    return pl.CostEstimate(
        flops=microseconds * 10**9, bytes_accessed=2**20, transcendentals=0
    )


def per_device(spectrum, capture_rate, row_latitude, slot_wavenumber):
    bands = lax.axis_size("band")
    modes = spectrum.shape[3]
    row_count = capture_rate.shape[1]
    slots = slot_wavenumber.shape[0]
    blocks = modes // BLK
    chunks = DEG // CHUNK
    tiles = -(-CHAN * row_count // LANES)
    band_index = lax.axis_index("band")

    def sort_rows(table):
        rank = jnp.sum((table[:, None, :] < table[:, :, None]).astype(jnp.int32), 2)
        match = rank[:, None, :] == jnp.arange(modes, dtype=jnp.int32)[None, :, None]
        keys = table * PLACES + jnp.arange(modes, dtype=jnp.int32)[None, :]
        return jnp.sum(jnp.where(match, keys[:, None, :], 0), 2).reshape(-1)

    own = lax.dynamic_slice_in_dim(slot_wavenumber, band_index * modes, modes)
    local = sort_rows(own.reshape(1, modes))
    ordered = sort_rows(slot_wavenumber.reshape(bands, modes)) // PLACES
    rows = jnp.asarray(latitude_rows())
    spread = jnp.asarray(spread_matrix())
    latitude = row_latitude.reshape(1, NLAT)
    coeffs = spectrum.reshape(CHAN, modes, DEG)
    params = pltpu.CompilerParams(vmem_limit_bytes=48 * 2**20)
    chunk_rows = tiles * modes
    dims = (bands, row_count, modes, blocks, tiles)
    scalars = jnp.asarray(degree_scalars())
    per_order = pltpu.VMEM((modes, DEG), F32)

    def exchange(value):
        return lax.all_to_all(value, "band", split_axis=0, concat_axis=0, tiled=True)

    sent = pl.pallas_call(
        lambda *refs: synth_kernel(dims, *refs),
        out_shape=jax.ShapeDtypeStruct((bands, chunk_rows, LANES), F32),
        in_specs=[SMEM] + [HBM] * 5,
        out_specs=VMEM,
        scratch_shapes=[
            pltpu.SMEM(scalars.shape, F32),
            pltpu.VMEM(coeffs.shape, F32),
            pltpu.VMEM(rows.shape, F32),
            pltpu.VMEM(spread.shape, BF),
            pltpu.VMEM(latitude.shape, jnp.int32),
            pltpu.SemaphoreType.DMA((5,)),
        ]
        + [per_order] * 3
        + [pltpu.VMEM((chunks + 1, 2 * ROWS, CHUNK * BLK), BF)]
        + [pltpu.VMEM((2, CHUNK // 2 * BLK, HALF), BF)] * 4
        + [
            pltpu.VMEM((blocks, 2, ROWS, HALF), F32),
            pltpu.VMEM((HALF, NLAT), BF),
            pltpu.VMEM((CHAN, BLK, DEG), F32),
        ],
        compiler_params=pltpu.CompilerParams(vmem_limit_bytes=62 * 2**20),
        cost_estimate=work(15),
        name="synth",
    )(local, scalars, coeffs, rows, spread, latitude)
    received = exchange(sent)

    trig_tiles = NLON // 2 // KTILE
    trig_shape = (trig_tiles, 2, 2, slots, KTILE)
    trig_scratch = pltpu.VMEM(trig_shape, BF)
    trig = pl.pallas_call(
        trig_kernel,
        out_shape=jax.ShapeDtypeStruct(trig_shape, BF),
        out_specs=HBM,
        scratch_shapes=[trig_scratch, pltpu.SemaphoreType.DMA(())],
        compiler_params=params,
        cost_estimate=work(4),
        name="trig",
    )()

    my_latitudes = lax.dynamic_slice_in_dim(row_latitude, band_index * row_count, row_count)
    row_sine = jnp.sin(jnp.pi * (my_latitudes.astype(F32) + 0.5) / NLAT)
    row_sine = jnp.broadcast_to(row_sine[:, None], (row_count, LANES))
    orders = jnp.broadcast_to(ordered.reshape(slots, 1), (slots, LANES))
    group = FIELDS * row_count
    padded = -(-group // LANES) * LANES
    grid_dims = (bands, row_count, modes, tiles, slots)
    fluxes = pl.pallas_call(
        lambda *refs: grid_kernel(grid_dims, *refs),
        out_shape=jax.ShapeDtypeStruct((bands, chunk_rows + 8, LANES), F32),
        in_specs=[VMEM] * 4 + [HBM],
        out_specs=VMEM,
        scratch_shapes=[
            pltpu.VMEM((slots, slots), BF),
            pltpu.VMEM((2, 2 * group, slots), BF),
            pltpu.VMEM((2, 2 * padded, NLON // 2), BF),
            pltpu.VMEM((2, slots, padded), F32),
            trig_scratch,
            pltpu.SemaphoreType.DMA((trig_tiles,)),
        ],
        compiler_params=params,
        cost_estimate=work(8),
        name="grid",
    )(received, orders, capture_rate.reshape(row_count, NLON), row_sine, trig)
    returned = exchange(fluxes)

    chunk_shape = (blocks, chunks, CHUNK * BLK, 2 * HALF)
    legendre, within = pl.pallas_call(
        lambda *refs: table_kernel(blocks, *refs),
        out_shape=[
            jax.ShapeDtypeStruct(chunk_shape, BF),
            jax.ShapeDtypeStruct((modes, DEG), F32),
        ],
        in_specs=[SMEM, SMEM, VMEM],
        out_specs=[HBM, VMEM],
        scratch_shapes=[per_order] * 2
        + [pltpu.VMEM(chunk_shape, BF), pltpu.SemaphoreType.DMA((blocks, chunks))],
        compiler_params=params,
        cost_estimate=work(12),
        name="table",
    )(local, scalars, rows)
    column = jnp.broadcast_to(row_latitude[:, None], (NLAT, LANES))
    result = pl.pallas_call(
        lambda *refs: analyze_kernel(dims, chunk_rows, *refs),
        out_shape=jax.ShapeDtypeStruct((CHAN, modes, DEG), F32),
        in_specs=[SMEM, VMEM, VMEM, VMEM, VMEM, HBM],
        out_specs=VMEM,
        scratch_shapes=[
            pltpu.VMEM(chunk_shape, BF),
            pltpu.VMEM((blocks, 2 * HALF, 2 * LANES), BF),
            pltpu.VMEM((blocks * 4 * ROWS, NLAT), BF),
            pltpu.VMEM((blocks, DEG, LANES), F32),
            pltpu.VMEM((NLAT, HALF), BF),
            pltpu.VMEM((blocks, CHAN, BLK, DEG), F32),
            pltpu.SemaphoreType.DMA((blocks, chunks)),
        ],
        compiler_params=params,
        cost_estimate=work(9),
        name="analyze",
    )(local, returned, column, latitude, within, legendre)
    return result.reshape(1, FIELDS, 2, modes, DEG)


def solution(mesh):
    return jax.shard_map(
        per_device,
        mesh=mesh,
        in_specs=(P("shell", None, None, "band", None), P("shell", "band", None), P(), P()),
        out_specs=P("shell", None, None, "band", None),
        check_vma=False,
    )
```

```python
import functools
import math

import jax
import jax.numpy as jnp
import numpy as np
from jax import lax
from jax.experimental import pallas as pl
from jax.experimental.pallas import tpu as pltpu
from jax.sharding import PartitionSpec as P

DEG = 512
NLAT = 1024
NLON = 2048
FIELDS = 3
HALF = NLAT // 2
CHAN = 2 * FIELDS
BLK = 8
ROWS = CHAN * BLK
CHUNK = 64
CHECK = 16
PLACES = 1024
LANES = 128
KTILE = 256
BF = jnp.bfloat16
F32 = jnp.float32


def split_two(value):
    high = value.astype(BF)
    low = (value - high.astype(F32)).astype(BF)
    return high, low


def dot(lhs, rhs, contract_rhs=0):
    return lax.dot_general(
        lhs, rhs, (((1,), (contract_rhs,)), ((), ())), preferred_element_type=F32
    )


def latitude_rows():
    theta = np.pi * (np.arange(HALF) + 0.5) / NLAT
    index = np.arange(DEG, dtype=np.float64)
    log_terms = np.zeros(DEG)
    log_terms[1:] = 0.5 * np.log2((2.0 * index[1:] + 1.0) / (2.0 * index[1:]))
    rows = np.zeros((8, DEG))
    rows[0], rows[1], rows[2] = np.cos(theta), np.log2(np.sin(theta)), log_terms
    return rows.astype(np.float32)


def spread_matrix():
    spread = np.zeros((LANES, 2, 2, CHUNK // 2, BLK), np.float32)
    for half in range(2):
        for parity in range(2):
            for step in range(CHUNK // 2):
                spread[half * CHUNK + 2 * step + parity, half, parity, step, :] = 1.0
    return spread.reshape(LANES, 2 * 2 * (CHUNK // 2) * BLK).astype(BF)


def degree_scalars():
    before = np.arange(DEG, dtype=np.float64) - 1.0
    square = before * before
    return np.concatenate([square, 4.0 / (4.0 * square - 1.0)]).astype(np.float32)


def block_orders(slots_ref, first):
    sublane = lax.broadcasted_iota(jnp.int32, (BLK, LANES), 0)
    orders = jnp.zeros((BLK, LANES), jnp.int32)
    lowest, highest = jnp.int32(DEG), jnp.int32(0)
    for i in range(BLK):
        order = slots_ref[first + i] // PLACES
        orders = jnp.where(sublane == i, order, orders)
        lowest, highest = jnp.minimum(lowest, order), jnp.maximum(highest, order)
    return orders, lowest // CHUNK, highest // CHUNK + 1


def running_sum(terms, length):
    lane = lax.broadcasted_iota(jnp.int32, terms.shape, 1) & (length - 1)
    shift = 1
    while shift < length:
        moved = pltpu.roll(terms, shift, 1)
        terms = terms + jnp.where(lane >= shift, moved, 0.0)
        shift *= 2
    return terms


def recursion_tables(slots_ref, modes, rows_ref, start_ref, before_ref, within_ref):
    orders = [block_orders(slots_ref, at)[0][:, :1] for at in range(0, modes, BLK)]
    order = jnp.concatenate(orders, 0).astype(F32)
    position = lax.broadcasted_iota(jnp.int32, (modes, DEG), 1)
    degree = position.astype(F32)
    square = degree * degree
    above = degree > order
    gap = jnp.where(above, square - order * order, 1.0)
    growth = jnp.where(above, 0.5 * jnp.log2((square - 0.25) / gap), 0.0)
    before_ref[...] = running_sum(growth, DEG)
    later = jnp.where(position & (CHECK - 1) == 0, 0.0, growth)
    within_ref[...] = jnp.exp2(running_sum(later, CHECK))
    terms = jnp.where(degree <= order, rows_ref[2:3, :], 0.0)
    norm = jnp.where(order > 0, 0.5 + jnp.sum(terms, axis=1, keepdims=True), 0.0)
    start_ref[...] = norm + order * rows_ref[1:2, :]


def run_chunk(step, carry, double_cosine, orders, before, scalars_ref, emit, beside, guard):
    current, previous, log_scale = carry
    order = orders.astype(F32)
    order_square = order * order
    before = pltpu.roll(before, (step % 2) * CHUNK, 1)
    scale = None
    for i in range(CHUNK):
        if i % CHECK == 0:
            size = jnp.maximum(jnp.abs(current), jnp.abs(previous))
            large, small = size > 2.0**40, size < 2.0**-40
            factor = jnp.where(large, 2.0**-60, jnp.where(small, 2.0**60, 1.0))
            change = jnp.where(large, 60.0, jnp.where(small, -60.0, 0.0))
            current = current * factor
            previous = previous * factor
            log_scale = log_scale + change
            scale = jnp.exp2(jnp.maximum(log_scale + before[:, i : i + 1], -200.0))
        degree = step * CHUNK + i
        factor = (scalars_ref[degree] - order_square) * scalars_ref[DEG + degree]
        factor = jnp.tile(factor, (1, HALF // LANES))
        newest = double_cosine * current - factor * previous
        if guard:
            started = jnp.tile(orders, (1, HALF // LANES)) < degree
            newest = jnp.where(started, newest, 1.0)
        current, previous = newest, current
        emit(i, newest * scale)
        if beside and i % (CHUNK // len(beside)) == 1:
            beside[i // (CHUNK // len(beside))]()
    return current, previous, log_scale


def before_tile(before_ref, block, step):
    rows = pl.ds(pl.multiple_of(block * BLK, BLK), BLK)
    return before_ref[rows, pl.ds(pl.multiple_of(step // 2 * LANES, LANES), LANES)]


def start_state(start_ref, block):
    ones = jnp.ones((BLK, HALF), F32)
    return ones, ones, start_ref[pl.ds(pl.multiple_of(block * BLK, BLK), BLK), :]


def fold_matrix(latitude_ref, fold_ref):
    latitude = latitude_ref[...]
    north = jnp.where(latitude < HALF, latitude, NLAT - 1 - latitude)
    sublane = lax.broadcasted_iota(jnp.int32, (HALF, NLAT), 0)
    fold_ref[...] = jnp.where(sublane == north, 1.0, 0.0).astype(BF)


def synth_kernel(
    dims, slots_ref, scalars_in, spec_in, rows_in, spread_in, latitude_in,
    out_ref, scalars_ref, spec_ref, rows_ref, spread_ref, latitude_ref, sems,
    start_ref, before_ref, within_ref, lhs_ref, high_a, low_a, high_b, low_b, acc_ref, fold_ref, coeff_ref,
):
    bands, row_count, modes, blocks, tiles = dims
    pairs = (
        (rows_in, rows_ref), (scalars_in, scalars_ref), (latitude_in, latitude_ref),
        (spread_in, spread_ref), (spec_in, spec_ref),
    )
    copies = []
    for index, (source, target) in enumerate(pairs):
        copies.append(pltpu.make_async_copy(source, target, sems.at[index]))
        copies[-1].start()
    copies[0].wait()
    recursion_tables(slots_ref, modes, rows_ref, start_ref, before_ref, within_ref)
    for copy in copies[1:]:
        copy.wait()
    fold_matrix(latitude_ref, fold_ref)
    south = latitude_ref[...] >= HALF
    spread_width = 4 * (CHUNK // 2) * BLK
    lane = lax.broadcasted_iota(jnp.int32, (2 * ROWS, spread_width), 1)
    sub = lax.broadcasted_iota(jnp.int32, (2 * ROWS, spread_width), 0)
    diagonal = (lane % BLK) == (sub % BLK)
    width = (CHUNK // 2) * BLK

    def one_block(block, unused):
        orders, first, last = block_orders(slots_ref, block * BLK)
        column = orders[:, :1]
        here = pl.ds(pl.multiple_of(block * BLK, BLK), BLK)
        for i in range(BLK):
            source = pl.ds(slots_ref[block * BLK + i] % PLACES, 1)
            coeff_ref[:, i : i + 1, :] = spec_ref[:, source, :]
        degree = lax.broadcasted_iota(jnp.int32, (BLK, DEG), 1)
        within = jnp.where(degree >= column, within_ref[here, :], 0.0)
        coeffs = coeff_ref[...] * within[None]
        coeff_high, coeff_low = split_two(coeffs.reshape(ROWS, DEG))
        stacked = jnp.concatenate([coeff_high, coeff_low], 0)
        for t in range(DEG // LANES):
            wide = dot(stacked[:, t * LANES : (t + 1) * LANES], spread_ref[...])
            wide = jnp.where(diagonal, wide, 0.0).astype(BF)
            for half in range(2):
                lhs_ref[2 * t + half] = wide[:, half * 2 * width : (half + 1) * 2 * width]
        acc_ref[block] = jnp.zeros((2, ROWS, HALF), F32)
        cosine = jnp.broadcast_to(2.0 * rows_ref[0:1, :], (BLK, HALF))

        def recur(step, carry, high_ref, low_ref, beside, guard):
            held = {}

            def emit(i, value):
                if i % 4 < 2:
                    held[i] = value
                else:
                    pair = jnp.concatenate([held.pop(i - 2), value], 0)
                    high, low = split_two(pair)
                    at = (i // 4) * 2 * BLK
                    high_ref[i % 2, at : at + 2 * BLK, :] = high
                    low_ref[i % 2, at : at + 2 * BLK, :] = low

            before = before_tile(before_ref, block, step)
            return run_chunk(
                step, carry, cosine, orders, before, scalars_ref, emit, beside, guard
            )

        def add_products(step, high_ref, low_ref):
            def part(parity, columns):
                lhs = lhs_ref[step, :, parity * width : (parity + 1) * width]
                first = dot(lhs, high_ref[parity, :, columns])
                second = dot(lhs[:ROWS], low_ref[parity, :, columns])
                acc_ref[block, parity, :, columns] += first[:ROWS] + first[ROWS:] + second

            return [
                functools.partial(part, parity, slice(at, at + 2 * KTILE))
                for parity in range(2)
                for at in range(0, HALF, 2 * KTILE)
            ]

        def two_chunks(guard, pair, carry):
            step = 2 * pair
            beside = add_products(jnp.maximum(step - 1, 0), high_b, low_b)
            carry = recur(step, carry, high_a, low_a, beside, guard)
            beside = add_products(step, high_a, low_a)
            return recur(step + 1, carry, high_b, low_b, beside, guard)

        high_b[...] = jnp.zeros_like(high_b)
        low_b[...] = jnp.zeros_like(low_b)
        chunks = DEG // CHUNK
        state = lax.fori_loop(
            0,
            first & 1,
            lambda unused, carry: recur(first, carry, high_b, low_b, (), True),
            start_state(start_ref, block),
        )
        middle = (last + 1) // 2
        state = lax.fori_loop(
            (first + 1) // 2, middle, functools.partial(two_chunks, True), state
        )
        lax.fori_loop(middle, chunks // 2, functools.partial(two_chunks, False), state)
        for part in add_products(chunks - 1, high_b, low_b):
            part()
        return unused

    lax.fori_loop(0, blocks, one_block, 0)
    high, low = split_two(acc_ref[...].reshape(blocks * 2 * ROWS, HALF))
    moved = dot(jnp.concatenate([high, low], 0), fold_ref[...])
    moved = moved[: blocks * 2 * ROWS] + moved[blocks * 2 * ROWS :]
    for block in range(blocks):
        orders = block_orders(slots_ref, block * BLK)[0][:, :1]
        sign = jnp.tile(1.0 - 2.0 * (orders % 2).astype(F32), (CHAN, 1))
        even = moved[block * 2 * ROWS : block * 2 * ROWS + ROWS]
        odd = moved[block * 2 * ROWS + ROWS : (block + 1) * 2 * ROWS]
        values = jnp.where(south, sign * (even - odd), even + odd)
        for d in range(bands):
            parts = []
            for kind in range(2):
                for field in range(FIELDS):
                    c = field * 2 + kind
                    parts.append(
                        values[c * BLK : (c + 1) * BLK, d * row_count : (d + 1) * row_count]
                    )
            if CHAN * row_count < tiles * LANES:
                parts.append(jnp.zeros((BLK, tiles * LANES - CHAN * row_count), F32))
            joined = jnp.concatenate(parts, 1)
            for t in range(tiles):
                at = slice((t * blocks + block) * BLK, (t * blocks + block + 1) * BLK)
                out_ref[d, at, :] = joined[:, t * LANES : (t + 1) * LANES]


def table_kernel(
    blocks, slots_ref, scalars_ref, rows_ref, out_ref, within_out, start_ref, before_ref,
    chunk_ref, sems,
):
    modes = blocks * BLK
    cosine = jnp.broadcast_to(2.0 * rows_ref[0:1, :], (BLK, HALF))
    recursion_tables(slots_ref, modes, rows_ref, start_ref, before_ref, within_out)

    def copy_out(block, step):
        return pltpu.make_async_copy(
            chunk_ref.at[block, step], out_ref.at[block, step], sems.at[block, step]
        )

    def one_block(block, unused):
        orders, first, last = block_orders(slots_ref, block * BLK)

        def one_chunk(guard, step, carry):
            held = {}

            def emit(i, value):
                if i % 2 == 0:
                    held[i] = value
                else:
                    pair = jnp.concatenate([held.pop(i - 1), value], 0)
                    high, low = split_two(pair)
                    at = (i // 2) * 2 * BLK
                    chunk_ref[block, step, at : at + 2 * BLK, :HALF] = high
                    chunk_ref[block, step, at : at + 2 * BLK, HALF:] = low

            before = before_tile(before_ref, block, step)
            carry = run_chunk(
                step, carry, cosine, orders, before, scalars_ref, emit, (), guard
            )
            copy_out(block, step).start()
            return carry

        state = start_state(start_ref, block)
        state = lax.fori_loop(first, last, functools.partial(one_chunk, True), state)
        lax.fori_loop(last, DEG // CHUNK, functools.partial(one_chunk, False), state)
        return unused

    def finish_block(block, unused):
        orders, first, last = block_orders(slots_ref, block * BLK)

        def finish_chunk(step, inner):
            copy_out(block, step).wait()
            return inner

        return lax.fori_loop(first, DEG // CHUNK, finish_chunk, unused)

    lax.fori_loop(0, blocks, one_block, 0)
    lax.fori_loop(0, blocks, finish_block, 0)


def analyze_kernel(
    dims, total_row, slots_ref, data_ref, column_ref, latitude_ref, within_ref, table_ref,
    out_ref, chunk_ref, weight_ref, stack_ref, result_ref, fold_ref, coeff_ref, sems,
):
    bands, row_count, modes, blocks, tiles = dims
    chunks = DEG // CHUNK

    def copy_in(block, step):
        return pltpu.make_async_copy(
            table_ref.at[block, step], chunk_ref.at[block, step], sems.at[block, step]
        )

    def start_block(block, unused):
        orders, first, last = block_orders(slots_ref, block * BLK)

        def start_chunk(step, inner):
            copy_in(block, step).start()
            return inner

        return lax.fori_loop(first, chunks, start_chunk, unused)

    lax.fori_loop(0, blocks, start_block, 0)
    latitude = column_ref[...]
    north = jnp.where(latitude < HALF, latitude, NLAT - 1 - latitude)
    lane = lax.broadcasted_iota(jnp.int32, (NLAT, LANES), 1)
    for t in range(HALF // LANES):
        one_hot = jnp.where(north == lane + t * LANES, 1.0, 0.0).astype(BF)
        fold_ref[:, t * LANES : (t + 1) * LANES] = one_hot
    south = latitude_ref[...] >= HALF
    for block in range(blocks):
        orders = block_orders(slots_ref, block * BLK)[0][:, :1]
        sign = 1.0 - 2.0 * (orders % 2).astype(F32)
        evens, odds = [], []
        for c in range(CHAN):
            offset = ((c % 2) * FIELDS + c // 2) * row_count
            t, at = offset // LANES, offset % LANES
            rows = slice((t * blocks + block) * BLK, (t * blocks + block + 1) * BLK)
            values = jnp.concatenate(
                [data_ref[d, rows, :][:, at : at + row_count] for d in range(bands)], 1
            )
            flipped = sign * values
            evens.append(jnp.where(south, flipped, values))
            odds.append(jnp.where(south, -flipped, values))
        high, low = split_two(jnp.concatenate(evens + odds, 0))
        stack_ref[block * 4 * ROWS : block * 4 * ROWS + 2 * ROWS, :] = high
        stack_ref[block * 4 * ROWS + 2 * ROWS : (block + 1) * 4 * ROWS, :] = low
    folded = dot(stack_ref[...], fold_ref[...])
    for block in range(blocks):
        at = block * 4 * ROWS
        part = folded[at : at + 2 * ROWS] + folded[at + 2 * ROWS : at + 4 * ROWS]
        part = jnp.concatenate([part, jnp.zeros((LANES - 2 * ROWS, HALF), F32)], 0)
        high, low = split_two(part.T)
        weight_ref[block, :HALF, :LANES] = high
        weight_ref[block, :HALF, LANES:] = low
        weight_ref[block, HALF:, :LANES] = high
        weight_ref[block, HALF:, LANES:] = jnp.zeros_like(low)

    total = data_ref[0, total_row : total_row + 8]
    for d in range(1, bands):
        total = total + data_ref[d, total_row : total_row + 8]
    inverse = (1.0 / total)[:, :1]
    lane = lax.broadcasted_iota(jnp.int32, (CHUNK * BLK, LANES), 1)
    sub = lax.broadcasted_iota(jnp.int32, (CHUNK * BLK, LANES), 0)
    keep = (lane % BLK == sub % BLK) & (lane // ROWS == sub // BLK % 2)

    def one_block(block, unused):
        orders, first, last = block_orders(slots_ref, block * BLK)
        orders = orders[:, :1]
        here = pl.ds(pl.multiple_of(block * BLK, BLK), BLK)
        result_ref[block] = jnp.zeros((DEG, LANES), F32)

        def some_chunks(step, count):
            for k in range(count):
                copy_in(block, step + k).wait()
            values = chunk_ref[block, pl.ds(step, count)].reshape(count * CHUNK * BLK, 2 * HALF)
            full = dot(values, weight_ref[block])
            full = (full[:, :LANES] + full[:, LANES:]).reshape(count, CHUNK * BLK, LANES)
            picked = jnp.where(keep[None], full, 0.0).reshape(count * CHUNK, BLK, LANES)
            to = pl.ds(pl.multiple_of(step * CHUNK, CHUNK), count * CHUNK)
            result_ref[block, to, :] = jnp.sum(picked, axis=1)

        def lone_chunk(unused, inner):
            some_chunks(first, 1)
            return inner

        even = (first + 1) // 2

        def two_chunks(unused, inner):
            some_chunks(2 * even, 2)
            return inner

        def four_chunks(group, inner):
            some_chunks(4 * group, 4)
            return inner

        lax.fori_loop(0, first & 1, lone_chunk, 0)
        lax.fori_loop(0, even & 1, two_chunks, 0)
        lax.fori_loop((even + 1) // 2, chunks // 4, four_chunks, 0)
        return unused

    lax.fori_loop(0, blocks, one_block, 0)
    for block in range(blocks):
        orders = block_orders(slots_ref, block * BLK)[0][:, :1]
        turned = result_ref[block].T
        turned = turned[:ROWS] + turned[ROWS : 2 * ROWS]
        degree = lax.broadcasted_iota(jnp.int32, (BLK, DEG), 1)
        within = jnp.where(degree >= orders, within_ref[block * BLK : (block + 1) * BLK, :], 0.0)
        for c in range(CHAN):
            part = turned[c * BLK : (c + 1) * BLK] * within
            if c // 2 == FIELDS - 1:
                part = part * inverse
            coeff_ref[block, c] = part
        for i in range(BLK):
            target = pl.ds(slots_ref[block * BLK + i] % PLACES, 1)
            out_ref[:, target, :] = coeff_ref[block, :, i : i + 1, :]


def base_trig(order, first):
    lane = lax.broadcasted_iota(jnp.int32, order.shape, 1) + first
    phase = (order * lane) & (NLON - 1)
    quarter = (phase + NLON // 8) >> 9
    rest = (phase - quarter * (NLON // 4)).astype(F32) * (2.0 * math.pi / NLON)
    square = rest * rest
    sine = 1.0 / 362880.0
    for coef in (-1.0 / 5040.0, 1.0 / 120.0, -1.0 / 6.0, 1.0):
        sine = sine * square + coef
    sine = sine * rest
    cosine = 1.0 / 40320.0
    for coef in (-1.0 / 720.0, 1.0 / 24.0, -0.5, 1.0):
        cosine = cosine * square + coef
    swap = (quarter & 1) == 1
    cos_out = jnp.where(swap, sine, cosine)
    sin_out = jnp.where(swap, cosine, sine)
    cos_out = jnp.where(((quarter + 1) & 2) == 2, -cos_out, cos_out)
    sin_out = jnp.where((quarter & 2) == 2, -sin_out, sin_out)
    return cos_out, sin_out


def trig_kernel(out_ref, trig_ref, sem):
    half = trig_ref.shape[3] // 2
    root = math.sqrt(0.5)
    for parity in range(2):

        def strip(step, unused):
            at = pl.multiple_of(step * 64, 64)
            shape = (64, LANES)
            order = 2 * (lax.broadcasted_iota(jnp.int32, shape, 0) + at) + parity
            eighth = order & 7
            odd = (eighth & 1) == 1
            turn_cos = jnp.where(odd, root, jnp.where((eighth & 2) == 0, 1.0, 0.0))
            turn_sin = jnp.where(odd, root, jnp.where((eighth & 2) == 2, 1.0, 0.0))
            turn_cos = jnp.where((eighth >= 3) & (eighth <= 5), -turn_cos, turn_cos)
            turn_sin = jnp.where(eighth > 4, -turn_sin, turn_sin)
            for t in range(KTILE // LANES):
                cosine, sine = base_trig(order, t * LANES)
                for k in range(t * LANES, NLON // 2, KTILE):
                    columns = slice(t * LANES, (t + 1) * LANES)
                    for values, start in ((cosine, at), (sine, half + at)):
                        high, low = split_two(values)
                        trig_ref[k // KTILE, 0, parity, pl.ds(start, 64), columns] = high
                        trig_ref[k // KTILE, 1, parity, pl.ds(start, 64), columns] = low
                    cosine, sine = (
                        cosine * turn_cos - sine * turn_sin,
                        sine * turn_cos + cosine * turn_sin,
                    )
            return unused

        lax.fori_loop(0, half // 64, strip, 0)
    copy = pltpu.make_async_copy(trig_ref, out_ref, sem)
    copy.start()
    copy.wait()


def grid_kernel(
    dims, data_ref, orders_ref, rate_ref, sine_ref, trig_in, out_ref,
    move_ref, lhs_ref, weight_ref, acc_ref, trig_ref, sems,
):
    bands, row_count, modes, tiles, slots = dims
    half = slots // 2
    group = FIELDS * row_count
    padded = weight_ref.shape[1] // 2

    copies = []
    for tile in range(NLON // 2 // KTILE):
        copy = pltpu.make_async_copy(trig_in.at[tile], trig_ref.at[tile], sems.at[tile])
        copy.start()
        copies.append(copy)
    order = orders_ref[...]
    natural = (order & 1) * half + (order >> 1)
    for t in range(slots // LANES):
        lane = lax.broadcasted_iota(jnp.int32, (slots, LANES), 1) + t * LANES
        one_hot = jnp.where(natural == lane, 1.0, 0.0).astype(BF)
        move_ref[:, t * LANES : (t + 1) * LANES] = one_hot
    columns = []
    for t in range(tiles):
        part = data_ref[:, t * modes : (t + 1) * modes, :]
        columns.append(part.reshape(slots, LANES).T)
    turned = jnp.concatenate(columns, 0)
    for kind in range(2):
        high, low = split_two(turned[kind * group : (kind + 1) * group])
        moved = dot(jnp.concatenate([high, low], 0), move_ref[...]).astype(BF)
        for parity in range(2):
            part = moved[:, parity * half : (parity + 1) * half]
            lhs_ref[parity, :, kind * half : (kind + 1) * half] = part
    if group < padded:
        empty = jnp.zeros((2, padded - group, NLON // 2), BF)
        weight_ref[:, group:padded, :] = empty
        weight_ref[:, padded + group :, :] = empty
    flux_scale = math.pi / (2.0 * NLAT * NLON * DEG)
    weight = jnp.tile(sine_ref[...], (1, KTILE // LANES))
    total = jnp.zeros((8, KTILE), F32)

    for k in range(0, NLON // 2, KTILE):
        copies[k // KTILE].wait()
        trig_high, trig_low = trig_ref.at[k // KTILE, 0], trig_ref.at[k // KTILE, 1]
        sums = []
        for parity in range(2):
            first = dot(lhs_ref[parity], trig_high[parity])
            second = dot(lhs_ref[parity, :group, :], trig_low[parity])
            sums.append(first[:group] + first[group:] + second)
        values = []
        for fields, at in ((sums[0] + sums[1], k), (sums[0] - sums[1], k + NLON // 2)):
            weighted_rate = rate_ref[:, at : at + KTILE] * weight
            total = total + jnp.sum(weighted_rate.reshape(row_count // 8, 8, KTILE), axis=0)
            scaled = fields[:row_count] * (weight * flux_scale)
            values.append(
                jnp.concatenate(
                    [
                        fields[row_count : 2 * row_count] * scaled,
                        fields[2 * row_count :] * scaled,
                        weighted_rate * fields[:row_count],
                    ],
                    0,
                )
            )
        for parity in range(2):
            both = values[0] + values[1] if parity == 0 else values[0] - values[1]
            high, low = split_two(both)
            columns = slice(k, k + KTILE)
            weight_ref[parity, :group, columns] = high
            weight_ref[parity, padded : padded + group, columns] = low
    for parity in range(2):
        trig_high, trig_low = [
            jnp.concatenate([trig_ref[t, part, parity] for t in range(len(copies))], 1)
            for part in range(2)
        ]
        first = dot(trig_high, weight_ref[parity], 1)
        second = dot(trig_low, weight_ref[parity, :padded, :], 1)
        acc_ref[parity] = first[:, :padded] + first[:, padded:] + second

    joined = []
    for kind in range(2):
        rows = slice(kind * half, (kind + 1) * half)
        joined.append(jnp.concatenate([acc_ref[0, rows, :group], acc_ref[1, rows, :group]], 0))
    if 2 * group < tiles * LANES:
        joined.append(jnp.zeros((slots, tiles * LANES - 2 * group), F32))
    high, low = split_two(jnp.concatenate(joined, 1))
    moved = dot(move_ref[...], jnp.concatenate([high, low], 1))
    moved = moved[:, : tiles * LANES] + moved[:, tiles * LANES :]
    for t in range(tiles):
        part = moved[:, t * LANES : (t + 1) * LANES]
        out_ref[:, t * modes : (t + 1) * modes, :] = part.reshape(bands, modes, LANES)
    out_ref[:, tiles * modes :, :] = jnp.broadcast_to(jnp.sum(total), (bands, 8, LANES))


VMEM = pl.BlockSpec(memory_space=pltpu.VMEM)
SMEM = pl.BlockSpec(memory_space=pltpu.SMEM)
HBM = pl.BlockSpec(memory_space=pltpu.HBM)


def work(microseconds):
    return pl.CostEstimate(
        flops=microseconds * 10**9, bytes_accessed=2**20, transcendentals=0
    )


def per_device(spectrum, capture_rate, row_latitude, slot_wavenumber):
    bands = lax.axis_size("band")
    modes = spectrum.shape[3]
    row_count = capture_rate.shape[1]
    slots = slot_wavenumber.shape[0]
    blocks = modes // BLK
    chunks = DEG // CHUNK
    tiles = -(-CHAN * row_count // LANES)
    band_index = lax.axis_index("band")

    def sort_rows(table):
        rank = jnp.sum((table[:, None, :] < table[:, :, None]).astype(jnp.int32), 2)
        match = rank[:, None, :] == jnp.arange(modes, dtype=jnp.int32)[None, :, None]
        keys = table * PLACES + jnp.arange(modes, dtype=jnp.int32)[None, :]
        return jnp.sum(jnp.where(match, keys[:, None, :], 0), 2).reshape(-1)

    own = lax.dynamic_slice_in_dim(slot_wavenumber, band_index * modes, modes)
    local = sort_rows(own.reshape(1, modes))
    ordered = sort_rows(slot_wavenumber.reshape(bands, modes)) // PLACES
    rows = jnp.asarray(latitude_rows())
    spread = jnp.asarray(spread_matrix())
    latitude = row_latitude.reshape(1, NLAT)
    coeffs = spectrum.reshape(CHAN, modes, DEG)
    params = pltpu.CompilerParams(vmem_limit_bytes=48 * 2**20)
    chunk_rows = tiles * modes
    dims = (bands, row_count, modes, blocks, tiles)
    scalars = jnp.asarray(degree_scalars())
    per_order = pltpu.VMEM((modes, DEG), F32)

    def exchange(value):
        return lax.all_to_all(value, "band", split_axis=0, concat_axis=0, tiled=True)

    sent = pl.pallas_call(
        lambda *refs: synth_kernel(dims, *refs),
        out_shape=jax.ShapeDtypeStruct((bands, chunk_rows, LANES), F32),
        in_specs=[SMEM] + [HBM] * 5,
        out_specs=VMEM,
        scratch_shapes=[
            pltpu.SMEM(scalars.shape, F32),
            pltpu.VMEM(coeffs.shape, F32),
            pltpu.VMEM(rows.shape, F32),
            pltpu.VMEM(spread.shape, BF),
            pltpu.VMEM(latitude.shape, jnp.int32),
            pltpu.SemaphoreType.DMA((5,)),
        ]
        + [per_order] * 3
        + [pltpu.VMEM((chunks, 2 * ROWS, CHUNK * BLK), BF)]
        + [pltpu.VMEM((2, CHUNK // 2 * BLK, HALF), BF)] * 4
        + [
            pltpu.VMEM((blocks, 2, ROWS, HALF), F32),
            pltpu.VMEM((HALF, NLAT), BF),
            pltpu.VMEM((CHAN, BLK, DEG), F32),
        ],
        compiler_params=pltpu.CompilerParams(vmem_limit_bytes=62 * 2**20),
        cost_estimate=work(15),
        name="synth",
    )(local, scalars, coeffs, rows, spread, latitude)
    received = exchange(sent)

    trig_tiles = NLON // 2 // KTILE
    trig_shape = (trig_tiles, 2, 2, slots, KTILE)
    trig_scratch = pltpu.VMEM(trig_shape, BF)
    trig = pl.pallas_call(
        trig_kernel,
        out_shape=jax.ShapeDtypeStruct(trig_shape, BF),
        out_specs=HBM,
        scratch_shapes=[trig_scratch, pltpu.SemaphoreType.DMA(())],
        compiler_params=params,
        cost_estimate=work(4),
        name="trig",
    )()

    my_latitudes = lax.dynamic_slice_in_dim(row_latitude, band_index * row_count, row_count)
    row_sine = jnp.sin(jnp.pi * (my_latitudes.astype(F32) + 0.5) / NLAT)
    row_sine = jnp.broadcast_to(row_sine[:, None], (row_count, LANES))
    orders = jnp.broadcast_to(ordered.reshape(slots, 1), (slots, LANES))
    group = FIELDS * row_count
    padded = -(-group // LANES) * LANES
    grid_dims = (bands, row_count, modes, tiles, slots)
    fluxes = pl.pallas_call(
        lambda *refs: grid_kernel(grid_dims, *refs),
        out_shape=jax.ShapeDtypeStruct((bands, chunk_rows + 8, LANES), F32),
        in_specs=[VMEM] * 4 + [HBM],
        out_specs=VMEM,
        scratch_shapes=[
            pltpu.VMEM((slots, slots), BF),
            pltpu.VMEM((2, 2 * group, slots), BF),
            pltpu.VMEM((2, 2 * padded, NLON // 2), BF),
            pltpu.VMEM((2, slots, padded), F32),
            trig_scratch,
            pltpu.SemaphoreType.DMA((trig_tiles,)),
        ],
        compiler_params=params,
        cost_estimate=work(8),
        name="grid",
    )(received, orders, capture_rate.reshape(row_count, NLON), row_sine, trig)
    returned = exchange(fluxes)

    chunk_shape = (blocks, chunks, CHUNK * BLK, 2 * HALF)
    legendre, within = pl.pallas_call(
        lambda *refs: table_kernel(blocks, *refs),
        out_shape=[
            jax.ShapeDtypeStruct(chunk_shape, BF),
            jax.ShapeDtypeStruct((modes, DEG), F32),
        ],
        in_specs=[SMEM, SMEM, VMEM],
        out_specs=[HBM, VMEM],
        scratch_shapes=[per_order] * 2
        + [pltpu.VMEM(chunk_shape, BF), pltpu.SemaphoreType.DMA((blocks, chunks))],
        compiler_params=params,
        cost_estimate=work(12),
        name="table",
    )(local, scalars, rows)
    column = jnp.broadcast_to(row_latitude[:, None], (NLAT, LANES))
    result = pl.pallas_call(
        lambda *refs: analyze_kernel(dims, chunk_rows, *refs),
        out_shape=jax.ShapeDtypeStruct((CHAN, modes, DEG), F32),
        in_specs=[SMEM, VMEM, VMEM, VMEM, VMEM, HBM],
        out_specs=VMEM,
        scratch_shapes=[
            pltpu.VMEM(chunk_shape, BF),
            pltpu.VMEM((blocks, 2 * HALF, 2 * LANES), BF),
            pltpu.VMEM((blocks * 4 * ROWS, NLAT), BF),
            pltpu.VMEM((blocks, DEG, LANES), F32),
            pltpu.VMEM((NLAT, HALF), BF),
            pltpu.VMEM((blocks, CHAN, BLK, DEG), F32),
            pltpu.SemaphoreType.DMA((blocks, chunks)),
        ],
        compiler_params=params,
        cost_estimate=work(9),
        name="analyze",
    )(local, returned, column, latitude, within, legendre)
    return result.reshape(1, FIELDS, 2, modes, DEG)


def solution(mesh):
    return jax.shard_map(
        per_device,
        mesh=mesh,
        in_specs=(P("shell", None, None, "band", None), P("shell", "band", None), P(), P()),
        out_specs=P("shell", None, None, "band", None),
        check_vma=False,
    )
```
